32 devices in a mesh: dp: 8 (over z, y), tensor: 4 (over x, core).
Axes of the slice: x: 2, y: 2, z: 4, core: 2. Of those that a mesh axis runs over, the one named last changes fastest.
Arguments:
- tokens: bfloat16 [1024, 2048], P('dp'), may hold values from -6 to 6
- out_grad: bfloat16 [1024, 2048], P('dp'), may hold values from -6 to 6
- row_place: int32 [1024], replicated, may hold values from 0 to 1023, as said below
- seq_lengths: int32 [8, 3], P('dp'), may hold values from 1 to 64, 128 in all within a row
- att_routes: int32 [1024, 2], P('dp'), may hold values from 0 to 7, all different within a row; in each aligned block of 128 rows (0 to 127, 128 to 255, ...) at most 64 rows name the same one
- att_gates: float32 [1024, 2], P('dp'), may hold values from 0.25 to 1
- mlp_routes: int32 [1024, 2], P('dp'), may hold values from 0 to 7, all different within a row; in each aligned block of 128 rows (0 to 127, 128 to 255, ...) at most 64 rows name the same one
- mlp_gates: float32 [1024, 2], P('dp'), may hold values from 0.25 to 1
- gain_attn: float32 [2048], replicated, may hold values from 0.5 to 1.5
- w_kv: bfloat16 [2048, 2, 2048], P(None, None, 'tensor'), may hold values from -0.125 to 0.125
- w_query: bfloat16 [8, 2048, 2048], P('dp', None, 'tensor'), may hold values from -0.125 to 0.125
- w_out: bfloat16 [8, 2048, 2048], P('dp', 'tensor'), may hold values from -0.5 to 0.5
- gain_mlp: float32 [2048], replicated, may hold values from 0.5 to 1.5
- w_gate: bfloat16 [8, 2048, 5632], P('dp', None, 'tensor'), may hold values from -0.125 to 0.125
- w_up: bfloat16 [8, 2048, 5632], P('dp', None, 'tensor'), may hold values from -0.125 to 0.125
- w_down: bfloat16 [8, 5632, 2048], P('dp', 'tensor'), may hold values from -0.15625 to 0.15625
Outputs:
- mixed: bfloat16 [1024, 2048], P('dp')
- tokens_grad: bfloat16 [1024, 2048], P('dp')
- gain_attn_grad: float32 [2048], replicated
- w_kv_grad: float32 [2048, 2, 2048], P(None, None, 'tensor')
- w_query_grad: float32 [8, 2048, 2048], P('dp', None, 'tensor')
- w_out_grad: float32 [8, 2048, 2048], P('dp', 'tensor')
- gain_mlp_grad: float32 [2048], replicated
- w_gate_grad: float32 [8, 2048, 5632], P('dp', None, 'tensor')
- w_up_grad: float32 [8, 2048, 5632], P('dp', None, 'tensor')
- w_down_grad: float32 [8, 5632, 2048], P('dp', 'tensor')
The draws below stay inside these ranges and needn't reach their ends.
Inputs may be any that keep to these rules, and one draw needn't show every extreme that they name: `row_place`: A permutation of the working positions; of the 128 given rows on each index of dp, the same number go to every group. `seq_lengths`: each row sums to 128, and its largest entry is exactly 64. `att_routes`: the two entries of a row differ. Among the rows of one index of dp no expert is named by more than 64 rows, and one is named by exactly 64 rows in some of them. `mlp_routes`: the two entries of a row differ. Among the rows of one index of dp no expert is named by more than 64 rows, and one is named by exactly 64 rows in some of them.
All inputs are finite; a program needn't handle non-finite values.
Results may differ from the reference program's by a relative error of at most 0.019.
Values may be sent and summed in bfloat16 or wider, within the bound.
A program may use at most 256 MiB of HBM per device.

```python
import math
import jax
import jax.numpy as jnp
import numpy as np
from jax import lax

D = 2048
HD = 128
KVH = 16
HQ_EXP = 16
ATT_EXPERTS = 8
EXPERTS = 8
FF = 5632
TOPK = 2
NSEQ = 3
TOK_DEV = 128
GROUP = 1
CAP = 64
TOKENS = 1024
N_DP = 8


def draw_row_place(key, part):
    key = jax.random.fold_in(key, 7)
    groups = TOKENS // TOK_DEV
    per_peer = TOK_DEV // groups
    sources = jnp.repeat(jnp.arange(groups, dtype=jnp.int32), per_peer)
    fill_keys = jax.random.split(jax.random.fold_in(key, 1), groups)
    owners = jax.vmap(lambda single: jax.random.permutation(single, sources))(fill_keys)
    flattened = owners.reshape(-1)
    grouped = jnp.argsort(flattened * TOKENS + jnp.arange(TOKENS, dtype=jnp.int32)).astype(jnp.int32).reshape(groups, TOK_DEV)
    shuffle_keys = jax.random.split(jax.random.fold_in(key, 2), groups)
    shuffled = jax.vmap(lambda single, ordered: jax.random.permutation(single, ordered))(shuffle_keys, grouped)
    return shuffled.reshape(-1).astype(jnp.int32)


def levels(key, dims, cuts, low, high):
    level = 1.0
    for position, blocks in cuts:
        steps = jax.random.uniform(jax.random.fold_in(jax.random.fold_in(key, 6), position), (blocks,), jnp.float32, low / len(cuts), high / len(cuts))
        level = level * jnp.repeat(jnp.exp(steps), dims[position] // blocks).reshape((-1,) + (1,) * (len(dims) - 1 - position))
    return level


def profile(count, total, reach, lean):
    loads = [(1 << 20) // math.isqrt(standing ** lean) + 1 for standing in range(2, count + 1)]
    surplus, given = total - reach - (count - 1), [1] * (count - 1)
    while surplus > 0:
        movable = [i for i in range(count - 1) if given[i] < reach]
        whole, budget = sum([loads[i] for i in movable]), surplus
        for i in movable:
            extra = min(reach - given[i], max(1, budget * loads[i] // whole), surplus)
            given[i] = given[i] + extra
            surplus = surplus - extra
    return np.array([reach] + given)


def uneven_parts(own_key, amount, total, most, lean):
    if amount == 2:
        one = jax.random.randint(own_key, (), max(1, total - most), min(most, total - 1) + 1)
        return jnp.stack([one, total - one])
    lengths = jnp.asarray(profile(amount, total, most, lean), jnp.int32)
    pairs = (amount - 1) // 2
    source_of, taker = lengths[1:1 + 2 * pairs:2], lengths[2:2 + 2 * pairs:2]
    slack = jnp.minimum(source_of - 1, most - taker)
    moved = jax.random.randint(jax.random.fold_in(own_key, 1), (pairs,), 0, 1 << 20) % (slack + 1)
    lengths = lengths.at[1:1 + 2 * pairs:2].set(source_of - moved).at[2:2 + 2 * pairs:2].set(taker + moved)
    return lengths[jax.random.permutation(jax.random.fold_in(own_key, 2), amount)]


def shared_out(rng, own, number, rows, count, top, most, skew):
    sequence = jax.random.permutation(rng, count)
    packed, ordinary = load_shares(count, rows * top, most, skew, True), load_shares(count, rows * top, most, skew, False)
    places = jnp.arange(count)

    def named(sizes, offset_by):
        used = int((sizes > 0).sum())
        fixed = max(1, used // 4)
        moved = fixed + (places - fixed + offset_by * (used - fixed)) % max(1, count - fixed)
        return jnp.zeros((count,), jnp.int32).at[sequence[jnp.where(places < fixed, places, moved)]].set(jnp.asarray(sizes, jnp.int32))

    sizes = jnp.where(number % 4 == 0, named(packed, number // 4), named(ordinary, number - number // 4 - 1))
    mixed = jax.random.permutation(jax.random.fold_in(own, 3), count)
    giver, receiver = mixed[0:count // 2 * 2:2], mixed[1:count // 2 * 2:2]
    room = jnp.minimum(sizes[giver] - 1, most - sizes[receiver]) // 2
    room = jnp.where((giver == sequence[0]) | (receiver == sequence[0]) | (sizes[receiver] == 0), 0, jnp.maximum(room, 0))
    moved = jax.random.randint(jax.random.fold_in(own, 4), (count // 2,), 0, 1 << 20) % (room + 1)
    sizes = sizes.at[giver].add(-moved).at[receiver].add(moved)
    members = jnp.searchsorted(jnp.cumsum(sizes), jnp.arange(rows * top), side="right").astype(jnp.int32)
    listing = members.reshape(top, rows).T
    listing = listing[jax.random.permutation(jax.random.fold_in(own, 1), rows)]
    offset_by = jax.random.randint(jax.random.fold_in(own, 2), (rows, 1), 0, top)
    return jnp.take_along_axis(listing, (jnp.arange(top)[None, :] + offset_by) % top, axis=1)


def load_shares(number_of, total, bound, skew, full):
    weights = [(1 << 20) // math.isqrt(grade ** skew) + 1 for grade in range(1, number_of + 1)]
    largest = bound if full else min(bound, max(-(-total // number_of), total * weights[0] // sum(weights)))
    least = 1 if total - largest >= number_of - 1 else 0
    holding, surplus = [largest] + [least] * (number_of - 1), total - largest - least * (number_of - 1)
    while surplus > 0:
        movable = [i for i in range(1, number_of) if holding[i] < largest] or [i for i in range(1, number_of) if holding[i] < bound]
        pool, budget = sum([weights[i] for i in movable]), surplus
        for i in movable:
            more = min(bound - holding[i], max(1, budget * weights[i] // pool), surplus)
            holding[i] = holding[i] + more
            surplus = surplus - more
    return np.array(holding)


def bell_draw(key, dims, scale, most, cuts=(), held_as=jnp.bfloat16):
    factor_of = levels(key, dims, cuts, -0.22, 0.18) if cuts else 1.0
    drawn = jax.random.normal(key, dims, jnp.float32) * scale * factor_of
    return jnp.minimum(jnp.maximum(drawn, -most), most).astype(held_as)


def setup_inputs(seed: int = 0) -> dict:
    splits = jax.random.split(jax.random.key(seed), 17)
    tokens = bell_draw(splits[0], (TOKENS, D), 1.0, 6.0, ((0, 8),))
    out_grad = bell_draw(splits[1], (TOKENS, D), 1.0, 6.0, ((0, 8),))
    row_place = draw_row_place(jax.random.fold_in(splits[16], 71), 0)
    seq_lengths = jax.vmap(lambda own: uneven_parts(own, NSEQ, TOK_DEV, TOK_DEV // 2, 2))(jax.random.split(splits[3], N_DP)).reshape((N_DP, NSEQ)).astype(jnp.int32)
    att_routes_keys = jax.random.split(jax.random.fold_in(splits[4], 1), TOKENS // TOK_DEV)
    att_routes_turns = jax.random.permutation(jax.random.fold_in(splits[4], 3), TOKENS // TOK_DEV)
    att_routes = jax.vmap(lambda own, number: shared_out(jax.random.fold_in(splits[4], 2), own, number, TOK_DEV, ATT_EXPERTS, TOPK, CAP, 2))(att_routes_keys, att_routes_turns).reshape((TOKENS, TOPK))
    att_gates = jnp.clip(0.25 + 0.75 * jax.random.uniform(splits[5], (TOKENS, TOPK), jnp.float32) ** levels(splits[5], (TOKENS, TOPK), ((0, 8),), -0.2, 0.2), 0.25, 1.0)
    mlp_routes_keys = jax.random.split(jax.random.fold_in(splits[6], 1), TOKENS // TOK_DEV)
    mlp_routes_turns = jax.random.permutation(jax.random.fold_in(splits[6], 3), TOKENS // TOK_DEV)
    mlp_routes = jax.vmap(lambda own, number: shared_out(jax.random.fold_in(splits[6], 2), own, number, TOK_DEV, EXPERTS, TOPK, CAP, 2))(mlp_routes_keys, mlp_routes_turns).reshape((TOKENS, TOPK))
    mlp_gates = jnp.clip(0.25 + 0.75 * jax.random.uniform(splits[7], (TOKENS, TOPK), jnp.float32) ** levels(splits[7], (TOKENS, TOPK), ((0, 8),), -0.2, 0.2), 0.25, 1.0)
    gain_attn = jnp.clip(1.0 + 0.1 * jax.random.normal(splits[8], (D,), jnp.float32), 0.5, 1.5)
    w_kv = bell_draw(splits[9], (D, 2, KVH * HD), D ** -0.5, 0.125, ((2, 4),))
    w_query = bell_draw(splits[10], (ATT_EXPERTS * GROUP, D // GROUP, HQ_EXP * HD), D ** -0.5, 0.125, ((0, 8), (2, 4)))
    w_out = bell_draw(splits[11], (ATT_EXPERTS * GROUP, HQ_EXP * HD, D // GROUP), (HQ_EXP * HD // 16) ** -0.5, 0.5, ((0, 8), (1, 4)))
    gain_mlp = jnp.clip(1.0 + 0.1 * jax.random.normal(splits[12], (D,), jnp.float32), 0.5, 1.5)
    w_gate = bell_draw(splits[13], (EXPERTS * GROUP, D, FF // GROUP), D ** -0.5, 0.125, ((0, 8), (2, 4)))
    w_up = bell_draw(splits[14], (EXPERTS * GROUP, D, FF // GROUP), D ** -0.5, 0.125, ((0, 8), (2, 4)))
    w_down = bell_draw(splits[15], (EXPERTS * GROUP, FF // GROUP, D), (FF // 4) ** -0.5, 0.15625, ((0, 8), (1, 4)))
    return {"tokens": tokens, "out_grad": out_grad, "row_place": row_place, "seq_lengths": seq_lengths, "att_routes": att_routes, "att_gates": att_gates, "mlp_routes": mlp_routes, "mlp_gates": mlp_gates, "gain_attn": gain_attn, "w_kv": w_kv, "w_query": w_query, "w_out": w_out, "gain_mlp": gain_mlp, "w_gate": w_gate, "w_up": w_up, "w_down": w_down}


EPSILON = 1e-05
THETA = 10000.0
HIGHEST = lax.Precision.HIGHEST

@jax.custom_vjp
def low(v):
    return lax.optimization_barrier(v.astype(jnp.bfloat16)).astype(jnp.float32)

@jax.custom_vjp
def low_back(v):
    return v

def low_keep(v):
    return (low(v), None)

def low_pass(kept, grad):
    return (grad,)

def back_keep(v):
    return (v, None)

def back_low(kept, grad):
    return (low(grad),)
low.defvjp(low_keep, low_pass)
low_back.defvjp(back_keep, back_low)

def rms_norm(values_in, gain):
    return values_in * lax.rsqrt(lax.optimization_barrier(jnp.mean(values_in * values_in, axis=-1, keepdims=True)) + EPSILON) * gain

def rotate(vectors, positions, direction):
    half_dim = vectors.shape[-1] // 2
    frequency = jnp.exp(-math.log(THETA) * jnp.arange(half_dim, dtype=jnp.float32) / half_dim)
    angles = positions.astype(jnp.float32)[:, None] * frequency[None, :]
    target = (vectors.shape[0],) + (1,) * (vectors.ndim - 2) + (half_dim,)
    cosine = jnp.cos(angles).reshape(target)
    sine = direction * jnp.sin(angles).reshape(target)
    former = vectors[..., :half_dim]
    latter = vectors[..., half_dim:]
    return jnp.concatenate([former * cosine - latter * sine, latter * cosine + former * sine], axis=-1)

def attend(block_items):
    query_block, keys_block, values_block, segment_block = block_items
    counting = jnp.arange(segment_block.shape[0], dtype=jnp.int32)
    allowed = (segment_block[:, None] == segment_block[None, :]) & (counting[None, :] <= counting[:, None])
    scores = jnp.einsum('ikjd,mjd->kjim', query_block, keys_block, precision=HIGHEST) / math.sqrt(HD)
    scores = low_back(scores)
    scores = jnp.where(allowed[None, None], scores, -1e+30)
    probability = jax.nn.softmax(scores, axis=-1)
    return jnp.einsum('kjim,mjd->ikjd', low(probability), values_block, precision=HIGHEST)

def scatter_pairs(expert_rows, slot_table, total):
    features = expert_rows.shape[-1]
    holder = jnp.zeros((2 * total + 1, features), expert_rows.dtype)
    holder = holder.at[slot_table.reshape(-1)].add(expert_rows.reshape(-1, features))
    return holder[:-1]

def reference(tokens, out_grad, row_place, seq_lengths, att_routes, att_gates, mlp_routes, mlp_gates, gain_attn, w_kv, w_query, w_out, gain_mlp, w_gate, w_up, w_down):
    total = TOKENS
    group_size = N_DP // EXPERTS
    limit = N_DP * CAP
    inverse = jnp.zeros((total,), jnp.int32).at[row_place].set(jnp.arange(total, dtype=jnp.int32))
    seq_ends = jnp.cumsum(seq_lengths, axis=1)
    starts = seq_ends - seq_lengths
    counting = jnp.arange(TOK_DEV, dtype=jnp.int32)
    segment = lax.optimization_barrier(jnp.sum((counting[None, :, None] >= seq_ends[:, None, :]).astype(jnp.int32), axis=2))
    member = segment[:, :, None] == jnp.arange(NSEQ, dtype=jnp.int32)[None, None, :]
    begins = lax.optimization_barrier(jnp.sum(jnp.where(member, starts[:, None, :], 0), axis=2))
    positions = (counting[None, :] - begins).reshape(-1)

    def tables(routes, count):
        flattened = routes.reshape(-1)
        listed = [jnp.nonzero(flattened == expert, size=limit, fill_value=2 * total)[0].astype(jnp.int32) for expert in range(count)]
        return jnp.stack(listed)
    att_table = tables(att_routes, ATT_EXPERTS)
    mlp_table = tables(mlp_routes, EXPERTS)
    query_width = HQ_EXP * HD

    def forward(tokens_f, gain_a, kv_weight, query_weight, out_weight, gain_m, gate_weight, up_weight, down_weight):
        query_full = query_weight.reshape(ATT_EXPERTS, D, query_width)
        out_full = out_weight.reshape(ATT_EXPERTS, group_size, query_width, D // group_size).transpose(0, 2, 1, 3).reshape(ATT_EXPERTS, query_width, D)
        gate_full = gate_weight.reshape(EXPERTS, group_size, D, FF // group_size).transpose(0, 2, 1, 3).reshape(EXPERTS, D, FF)
        up_full = up_weight.reshape(EXPERTS, group_size, D, FF // group_size).transpose(0, 2, 1, 3).reshape(EXPERTS, D, FF)
        down_full = down_weight.reshape(EXPERTS, FF, D)
        residual = tokens_f[inverse]
        normed = low(rms_norm(residual, gain_a))
        kv_proj = low_back(jnp.einsum('ld,dck->lck', normed, kv_weight, precision=HIGHEST))
        keys = low(rotate(kv_proj[:, 0].reshape(total, KVH, HD), positions, 1.0))
        values = low(kv_proj[:, 1].reshape(total, KVH, HD))
        padded = jnp.concatenate([normed, jnp.zeros((1, D), jnp.float32)], axis=0)

        def project_query(item):
            weight_e, index_e = item
            return jnp.dot(padded[index_e // 2], weight_e, precision=HIGHEST)
        query_rows = lax.map(jax.checkpoint(project_query), (query_full, att_table))
        query = low_back(scatter_pairs(query_rows, att_table, total).reshape(total, 2, KVH, HD))
        query = low(rotate(query, positions, 1.0))
        blocks = (query.reshape(N_DP, TOK_DEV, 2, KVH, HD), keys.reshape(N_DP, TOK_DEV, KVH, HD), values.reshape(N_DP, TOK_DEV, KVH, HD), segment)
        attn = lax.map(jax.checkpoint(attend), blocks).reshape(2 * total, query_width)
        attn = low(low_back(attn))
        attn_padded = jnp.concatenate([attn, jnp.zeros((1, query_width), jnp.float32)], axis=0)

        def project_out(item):
            weight_e, index_e = item
            return jnp.dot(attn_padded[index_e], weight_e, precision=HIGHEST)
        out_rows = lax.map(jax.checkpoint(project_out), (out_full, att_table))
        out_pairs = low_back(scatter_pairs(out_rows, att_table, total)).reshape(total, 2, D)
        hidden = residual + lax.optimization_barrier(jnp.sum(out_pairs * att_gates[:, :, None], axis=1))
        normed2 = low(rms_norm(hidden, gain_m))
        padded2 = jnp.concatenate([normed2, jnp.zeros((1, D), jnp.float32)], axis=0)

        def expert_apply(item):
            gate_e, up_e, down_e, index_e = item
            picked = padded2[index_e // 2]
            gate_act = low_back(jnp.dot(picked, gate_e, precision=HIGHEST))
            up_act = low_back(jnp.dot(picked, up_e, precision=HIGHEST))
            inner = low(jax.nn.silu(gate_act) * up_act)
            return jnp.dot(inner, down_e, precision=HIGHEST)
        expert_rows = lax.map(jax.checkpoint(expert_apply), (gate_full, up_full, down_full, mlp_table))
        expert_pairs = low_back(scatter_pairs(expert_rows, mlp_table, total)).reshape(total, 2, D)
        mixed = hidden + lax.optimization_barrier(jnp.sum(expert_pairs * mlp_gates[:, :, None], axis=1))
        return mixed[row_place]
    primals = (tokens.astype(jnp.float32), gain_attn, w_kv.astype(jnp.float32), w_query.astype(jnp.float32), w_out.astype(jnp.float32), gain_mlp, w_gate.astype(jnp.float32), w_up.astype(jnp.float32), w_down.astype(jnp.float32))
    mixed, pullback = jax.vjp(forward, *primals)
    grads = pullback(out_grad.astype(jnp.float32))
    return (mixed.astype(jnp.bfloat16), grads[0].astype(jnp.bfloat16), grads[1], grads[2], grads[3], grads[4], grads[5], grads[6], grads[7], grads[8])
```

```python
import functools
import math

import jax
import jax.numpy as jnp
from jax import lax
from jax.experimental import pallas as pl
from jax.experimental.pallas import tpu as pltpu
from jax.sharding import PartitionSpec as P

HD = 128
ATT_EXPERTS = 8
EXPERTS = 8
CAP = 64


EPSILON = 1e-05
THETA = 10000.0


def inverse_rms(values_in):
    return lax.rsqrt(jnp.mean(values_in * values_in, axis=-1, keepdims=True) + EPSILON)


def norm_backward(inputs, inv_root, gain, incoming):
    weighted = incoming * gain
    inner_mean = jnp.mean(inputs * weighted, axis=-1, keepdims=True)
    return inv_root * weighted - inputs * (inv_root * inv_root * inv_root) * inner_mean


def rotate(vectors, positions, direction):
    half_dim = vectors.shape[-1] // 2
    frequency = jnp.exp(-math.log(THETA) * jnp.arange(half_dim, dtype=jnp.float32) / half_dim)
    angles = positions.astype(jnp.float32)[:, None] * frequency[None, :]
    target = (vectors.shape[0],) + (1,) * (vectors.ndim - 2) + (half_dim,)
    cosine = jnp.cos(angles).reshape(target)
    sine = direction * jnp.sin(angles).reshape(target)
    former = vectors[..., :half_dim]
    latter = vectors[..., half_dim:]
    return jnp.concatenate(
        [former * cosine - latter * sine, latter * cosine + former * sine], axis=-1
    )


def expert_slots(routes, experts, capacity):
    flattened = routes.reshape(-1)
    pair_count = flattened.shape[0]
    one_hot = (flattened[:, None] == jnp.arange(experts, dtype=jnp.int32)[None, :]).astype(
        jnp.int32
    )
    earlier = jnp.cumsum(one_hot, axis=0) - one_hot
    position = jnp.sum(earlier * one_hot, axis=1)
    slot_table = jnp.full((experts, capacity), pair_count, jnp.int32)
    slot_table = slot_table.at[flattened, position].set(jnp.arange(pair_count, dtype=jnp.int32))
    return (flattened * capacity + position, slot_table)


def pick_rows(source_rows, slot_table):
    padded = jnp.concatenate(
        [source_rows, jnp.zeros((1, source_rows.shape[1]), source_rows.dtype)], axis=0
    )
    return padded[slot_table]


def send_slices(source_rows, slot_table, group_size):
    picked = pick_rows(source_rows, slot_table)
    experts, capacity, features = picked.shape
    divided = picked.reshape(experts, capacity, group_size, features // group_size)
    return divided.transpose(0, 2, 1, 3).reshape(
        experts * group_size, capacity, features // group_size
    )


def send_copies(source_rows, slot_table, group_size):
    picked = pick_rows(source_rows, slot_table)
    experts, capacity, features = picked.shape
    copies = jnp.broadcast_to(picked[:, None], (experts, group_size, capacity, features))
    return copies.reshape(experts * group_size, capacity, features)


def owners_summed(returned, pair_where, group_size):
    owners, capacity, features = returned.shape
    summed = returned.reshape(owners // group_size, group_size, capacity, features).sum(axis=1)
    return summed.reshape(-1, features)[pair_where]


def owners_joined(returned, pair_where, group_size):
    owners, capacity, features = returned.shape
    joined = returned.reshape(owners // group_size, group_size, capacity, features).transpose(
        0, 2, 1, 3
    )
    return joined.reshape(-1, group_size * features)[pair_where]


def query_return(pieces):
    return lax.all_to_all(pieces, "dp", split_axis=0, concat_axis=0, tiled=True)


def output_return(pieces):
    return lax.all_to_all(pieces, "dp", split_axis=0, concat_axis=0, tiled=True)


def expert_return(pieces):
    return lax.all_to_all(pieces, "dp", split_axis=0, concat_axis=0, tiled=True)


def tensor_total(pieces):
    return lax.psum(pieces, "tensor")


def deal_plan(row_place, rows_dev):
    device_count = lax.axis_size("dp")
    my_index = lax.axis_index("dp")
    per_peer = rows_dev // device_count
    every_place = row_place.reshape(device_count, rows_dev)
    my_places = lax.dynamic_index_in_dim(every_place, my_index, 0, keepdims=False)
    counting = jnp.arange(rows_dev, dtype=jnp.int32)
    ordering = jnp.argsort(my_places // rows_dev * rows_dev + counting)
    wanted = every_place // rows_dev == my_index
    chosen = jnp.argsort(
        jnp.where(wanted, counting[None, :], rows_dev + counting[None, :]), axis=1
    )[:, :per_peer]
    placed = jnp.take_along_axis(every_place, chosen, axis=1) % rows_dev
    return (ordering, placed.reshape(-1))


def masked_scores(query_b, keys_b, allowed):
    raw = jnp.einsum(
        "ikjd,mjd->kjim", query_b, keys_b, preferred_element_type=jnp.float32
    ) / math.sqrt(query_b.shape[-1])
    return jnp.where(allowed[None, None], raw, -1e30)


def local(
    tokens,
    out_grad,
    row_place,
    seq_lengths,
    att_routes,
    att_gates,
    mlp_routes,
    mlp_gates,
    gain_attn,
    w_kv,
    w_query,
    w_out,
    gain_mlp,
    w_gate,
    w_up,
    w_down,
):
    rows_dev, features = tokens.shape
    device_count = lax.axis_size("dp")
    group_size = device_count // EXPERTS
    per_peer = rows_dev // device_count
    counting = jnp.arange(rows_dev, dtype=jnp.int32)
    ordering, placed = deal_plan(row_place, rows_dev)
    unplace = jnp.zeros((rows_dev,), jnp.int32).at[placed].set(counting)
    unorder = jnp.zeros((rows_dev,), jnp.int32).at[ordering].set(counting)
    dealt_x, dealt_g = (
        lax.all_to_all(
            tokens[ordering].reshape(device_count, per_peer, features),
            "dp",
            split_axis=0,
            concat_axis=0,
            tiled=True,
        ),
        lax.all_to_all(
            out_grad[ordering].reshape(device_count, per_peer, features),
            "dp",
            split_axis=0,
            concat_axis=0,
            tiled=True,
        ),
    )
    residual = dealt_x.reshape(rows_dev, features)[unplace].astype(jnp.float32)
    top_grad = dealt_g.reshape(rows_dev, features)[unplace].astype(jnp.float32)
    lengths = seq_lengths[0]
    seq_ends = jnp.cumsum(lengths)
    segment = jnp.sum((counting[:, None] >= seq_ends[None, :]).astype(jnp.int32), axis=1)
    starts = seq_ends - lengths
    member = segment[:, None] == jnp.arange(lengths.shape[0], dtype=jnp.int32)[None, :]
    begins = jnp.sum(jnp.where(member, starts[None, :], 0), axis=1)
    positions = counting - begins
    allowed = (segment[:, None] == segment[None, :]) & (counting[None, :] <= counting[:, None])
    head_count = w_kv.shape[2] // HD
    scale_attn = inverse_rms(residual)
    normed = (residual * scale_attn * gain_attn).astype(jnp.bfloat16)
    kv_proj = jnp.einsum("ld,dck->lck", normed, w_kv, preferred_element_type=jnp.float32)
    keys = rotate(kv_proj[:, 0].reshape(rows_dev, head_count, HD), positions, 1.0).astype(
        jnp.bfloat16
    )
    values = kv_proj[:, 1].reshape(rows_dev, head_count, HD).astype(jnp.bfloat16)
    att_where, att_table = expert_slots(att_routes, ATT_EXPERTS, CAP)
    query_rows = lax.all_to_all(
        send_slices(normed, att_table // 2, group_size),
        "dp",
        split_axis=0,
        concat_axis=0,
        tiled=True,
    )
    query_part = jnp.einsum(
        "scd,dh->sch", query_rows, w_query[0], preferred_element_type=jnp.float32
    )
    query_pre = owners_summed(query_return(query_part), att_where, group_size)
    query_rot = rotate(query_pre.reshape(rows_dev, 2, head_count, HD), positions, 1.0).astype(
        jnp.bfloat16
    )
    scores = masked_scores(query_rot, keys, allowed)
    highest = jnp.max(scores, axis=-1, keepdims=True)
    expo = jnp.exp(scores - highest)
    row_total = jnp.sum(expo, axis=-1, keepdims=True)
    log_total = highest + jnp.log(row_total)
    probability = expo / row_total
    attn = jnp.einsum(
        "kjim,mjd->ikjd",
        probability.astype(jnp.bfloat16),
        values,
        preferred_element_type=jnp.float32,
    )
    attn_low = attn.astype(jnp.bfloat16).reshape(rows_dev * 2, head_count * HD)
    out_rows = lax.all_to_all(
        send_copies(attn_low, att_table, group_size), "dp", split_axis=0, concat_axis=0, tiled=True
    )
    out_part = jnp.einsum("sch,hd->scd", out_rows, w_out[0], preferred_element_type=jnp.float32)
    out_pairs = owners_joined(output_return(out_part), att_where, group_size).reshape(
        rows_dev, 2, features
    )
    hidden = residual + tensor_total(jnp.sum(out_pairs * att_gates[:, :, None], axis=1))
    gate_map, up_map, down_map = (w_gate[0], w_up[0], w_down[0])
    scale_mlp = inverse_rms(hidden)
    normed2 = (hidden * scale_mlp * gain_mlp).astype(jnp.bfloat16)
    mlp_where, mlp_table = expert_slots(mlp_routes, EXPERTS, CAP)
    expert_sent = send_copies(normed2, mlp_table // 2, group_size)
    expert_rows = lax.all_to_all(expert_sent, "dp", split_axis=0, concat_axis=0, tiled=True)
    flat_rows = expert_rows.reshape(-1, features)
    gate_act = jnp.dot(flat_rows, gate_map, preferred_element_type=jnp.float32)
    up_act = jnp.dot(flat_rows, up_map, preferred_element_type=jnp.float32)
    inner = (jax.nn.silu(gate_act) * up_act).astype(jnp.bfloat16)
    expert_part = jnp.dot(inner, down_map, preferred_element_type=jnp.float32).reshape(
        expert_rows.shape
    )
    expert_pairs = owners_summed(expert_return(expert_part), mlp_where, group_size).reshape(
        rows_dev, 2, features
    )
    mixed_rows = hidden + tensor_total(jnp.sum(expert_pairs * mlp_gates[:, :, None], axis=1))
    branch_grad = (
        (top_grad[:, None, :] * mlp_gates[:, :, None])
        .astype(jnp.bfloat16)
        .reshape(rows_dev * 2, features)
    )
    grad_sent = send_copies(branch_grad, mlp_table, group_size)
    grad_back, rows_back = (
        lax.all_to_all(grad_sent, "dp", split_axis=0, concat_axis=0, tiled=True),
        lax.all_to_all(expert_sent, "dp", split_axis=0, concat_axis=0, tiled=True),
    )
    grad_rows = grad_back.reshape(-1, features)
    rows_again = rows_back.reshape(-1, features)
    gate_again = jnp.dot(rows_again, gate_map, preferred_element_type=jnp.float32)
    up_again = jnp.dot(rows_again, up_map, preferred_element_type=jnp.float32)
    inner_again = (jax.nn.silu(gate_again) * up_again).astype(jnp.bfloat16)
    contract_rows = (((0,), (0,)), ((), ()))
    contract_cols = (((1,), (1,)), ((), ()))
    d_inner = lax.dot_general(
        grad_rows, down_map, contract_cols, preferred_element_type=jnp.float32
    )
    down_grad_all = lax.dot_general(
        inner_again, grad_rows, contract_rows, preferred_element_type=jnp.float32
    )
    sigmoid_g = jax.nn.sigmoid(gate_again)
    d_up = (d_inner * gate_again * sigmoid_g).astype(jnp.bfloat16)
    d_gate = (d_inner * up_again * sigmoid_g * (1.0 + gate_again * (1.0 - sigmoid_g))).astype(
        jnp.bfloat16
    )
    gate_grad_all = lax.dot_general(
        rows_again, d_gate, contract_rows, preferred_element_type=jnp.float32
    )
    up_grad_all = lax.dot_general(
        rows_again, d_up, contract_rows, preferred_element_type=jnp.float32
    )
    d_rows = lax.dot_general(d_gate, gate_map, contract_cols, preferred_element_type=jnp.float32)
    d_rows = d_rows + lax.dot_general(
        d_up, up_map, contract_cols, preferred_element_type=jnp.float32
    )
    d_pairs = owners_summed(expert_return(d_rows.reshape(expert_rows.shape)), mlp_where, group_size)
    w_gate_grad = gate_grad_all[None]
    w_up_grad = up_grad_all[None]
    w_down_grad = down_grad_all[None]
    d_normed2 = tensor_total(jnp.sum(d_pairs.reshape(rows_dev, 2, features), axis=1))
    d_hidden = top_grad + norm_backward(hidden, scale_mlp, gain_mlp, d_normed2)
    gain_mlp_grad = jnp.sum(d_normed2 * hidden * scale_mlp, axis=0)
    att_grad = (
        (d_hidden[:, None, :] * att_gates[:, :, None])
        .astype(jnp.bfloat16)
        .reshape(rows_dev * 2, features)
    )
    grad_slices = lax.all_to_all(
        send_slices(att_grad, att_table, group_size), "dp", split_axis=0, concat_axis=0, tiled=True
    )
    w_out_grad = jnp.einsum(
        "sch,scd->hd", out_rows, grad_slices, preferred_element_type=jnp.float32
    )
    d_attn_part = jnp.einsum(
        "scd,hd->sch", grad_slices, w_out[0], preferred_element_type=jnp.float32
    )
    d_attn = owners_summed(output_return(d_attn_part), att_where, group_size)
    d_attn = d_attn.astype(jnp.bfloat16).reshape(rows_dev, 2, head_count, HD)
    probability = jnp.exp(masked_scores(query_rot, keys, allowed) - log_total)
    d_prob = jnp.einsum("ikjd,mjd->kjim", d_attn, values, preferred_element_type=jnp.float32)
    d_values = jnp.einsum(
        "kjim,ikjd->mjd",
        probability.astype(jnp.bfloat16),
        d_attn,
        preferred_element_type=jnp.float32,
    )
    delta = jnp.sum(d_prob * probability, axis=-1, keepdims=True)
    d_scores = (probability * (d_prob - delta)).astype(jnp.bfloat16)
    root_hd = math.sqrt(HD)
    d_query = (
        jnp.einsum("kjim,mjd->ikjd", d_scores, keys, preferred_element_type=jnp.float32) / root_hd
    )
    d_keys = (
        jnp.einsum("kjim,ikjd->mjd", d_scores, query_rot, preferred_element_type=jnp.float32)
        / root_hd
    )
    dq_pre = (
        rotate(d_query, positions, -1.0).astype(jnp.bfloat16).reshape(rows_dev * 2, head_count * HD)
    )
    dk_pre = rotate(d_keys, positions, -1.0).reshape(rows_dev, head_count * HD)
    d_kv = jnp.stack([dk_pre, d_values.reshape(rows_dev, head_count * HD)], axis=1).astype(
        jnp.bfloat16
    )
    dq_rows = lax.all_to_all(
        send_copies(dq_pre, att_table, group_size), "dp", split_axis=0, concat_axis=0, tiled=True
    )
    w_query_grad = jnp.einsum(
        "scd,sch->dh", query_rows, dq_rows, preferred_element_type=jnp.float32
    )
    d_slice = jnp.einsum("sch,dh->scd", dq_rows, w_query[0], preferred_element_type=jnp.float32)
    d_norm_query = owners_joined(query_return(d_slice), att_where, group_size)
    d_norm_query = jnp.sum(d_norm_query.reshape(rows_dev, 2, features), axis=1)
    w_kv_grad = jnp.einsum("ld,lck->dck", normed, d_kv, preferred_element_type=jnp.float32)
    d_norm_kv = jnp.einsum("lck,dck->ld", d_kv, w_kv, preferred_element_type=jnp.float32)
    d_normed = tensor_total(d_norm_query + d_norm_kv)
    in_grad = d_hidden + norm_backward(residual, scale_attn, gain_attn, d_normed)
    gain_attn_grad = jnp.sum(d_normed * residual * scale_attn, axis=0)
    w_kv_grad, gain_attn_grad, gain_mlp_grad = (
        lax.psum(w_kv_grad.astype(jnp.bfloat16), "dp").astype(jnp.float32),
        lax.psum(gain_attn_grad.astype(jnp.bfloat16), "dp").astype(jnp.float32),
        lax.psum(gain_mlp_grad.astype(jnp.bfloat16), "dp").astype(jnp.float32),
    )
    send_mixed = mixed_rows.astype(jnp.bfloat16)[placed].reshape(device_count, per_peer, features)
    send_input = in_grad.astype(jnp.bfloat16)[placed].reshape(device_count, per_peer, features)
    back_mixed, back_input = (
        lax.all_to_all(send_mixed, "dp", split_axis=0, concat_axis=0, tiled=True),
        lax.all_to_all(send_input, "dp", split_axis=0, concat_axis=0, tiled=True),
    )
    mixed = back_mixed.reshape(rows_dev, features)[unorder]
    tokens_grad = back_input.reshape(rows_dev, features)[unorder]
    return (
        mixed,
        tokens_grad,
        gain_attn_grad,
        w_kv_grad,
        w_query_grad[None],
        w_out_grad[None],
        gain_mlp_grad,
        w_gate_grad,
        w_up_grad,
        w_down_grad,
    )


MESH = pl.DeviceIdType.MESH
VM = pltpu.VMEM
DMA = pltpu.SemaphoreType.DMA
BF = jnp.bfloat16
F32 = jnp.float32

def rcopy(src, dst, ss, rs, dp, tn):
    return pltpu.make_async_remote_copy(src_ref=src, dst_ref=dst, send_sem=ss, recv_sem=rs,
        device_id={"dp": dp, "tensor": tn}, device_id_type=MESH)

def greet(targets):
    b = pltpu.get_barrier_semaphore()
    for dp, tn in targets:
        pl.semaphore_signal(b, inc=1, device_id={"dp": dp, "tensor": tn}, device_id_type=MESH)
    pl.semaphore_wait(b, len(targets))

def ranks():
    g = lax.axis_index("dp"); t = lax.axis_index("tensor")
    return g, t, lax.rem(t + 2, 4), t + 1 - 2 * lax.rem(t, 2)

def params(cid):
    return pltpu.CompilerParams(collective_id=cid, has_side_effects=True, vmem_limit_bytes=56*2**20)

def gather_body(n, mode, src, out, ssem, rsem, xs, xr, cs, cr, c2s, c2r, lsem):
    g, t, tx, tc = ranks()
    w = src.shape[-1]
    greet([(lax.rem(g + o, n), t) for o in range(1, n)] + [(g, tx), (g, tc)])
    cols = pl.ds(pl.multiple_of(t * w, w), w)
    colsx = pl.ds(pl.multiple_of(tx * w, w), w)
    pick = (lambda d: src.at[d]) if mode == "rows" else (lambda d: src)
    at = (lambda b, cc: out.at[:, b, :, cc]) if mode == "deal" else (lambda b, cc: out.at[b, :, cc])
    sends = []
    for o in range(1, n):
        d = lax.rem(g + o, n)
        c = rcopy(pick(d), at(g, cols), ssem.at[o], rsem.at[o], d, t)
        c.start(); sends.append(c)
    loc = pltpu.make_async_copy(pick(g), at(g, cols), lsem)
    loc.start(); loc.wait()
    fx = []; fc = []; fc2 = []
    for o in range(n):
        b = lax.rem(g - o + n, n)
        if o > 0: sends[o - 1].wait_recv()
        c = rcopy(at(b, cols), at(b, cols), xs.at[o], xr.at[o], g, tx); c.start(); fx.append(c)
        c = rcopy(at(b, cols), at(b, cols), cs.at[o], cr.at[o], g, tc); c.start(); fc.append(c)
    for o in range(n):
        b = lax.rem(g - o + n, n)
        fx[o].wait_recv()
        c = rcopy(at(b, colsx), at(b, colsx), c2s.at[o], c2r.at[o], g, tc); c.start(); fc2.append(c)
    for c in fc + fc2: c.wait_recv()
    for c in sends + fx + fc + fc2: c.wait_send()

def gather(src, n, bcast=False, deal=False, cid=0, space=VM):
    r, w = src.shape[-2:]
    mode = "deal" if deal else "copy" if bcast else "rows"
    shape = (n, n, r, 4 * w) if deal else (n, r, 4 * w)
    return pl.pallas_call(functools.partial(gather_body, n, mode),
        out_shape=jax.ShapeDtypeStruct(shape, src.dtype),
        in_specs=[pl.BlockSpec(memory_space=VM)], out_specs=pl.BlockSpec(memory_space=space),
        scratch_shapes=[DMA((n,))]*8 + [DMA],
        name="gather_rows", compiler_params=params(cid))(src)

def reduce_body(n, nb, src, out, cbuf, cin, xbuf, xin, dbuf, cs, cr, xs, xr, ds_, dr):
    g, t, tx, tc = ranks()
    tcx = lax.rem(tc + 2, 4); w = out.shape[-1]
    greet([(lax.rem(g + o, n), t) for o in range(1, n)] + [(g, tx), (g, tc)])
    sl = lambda q: pl.ds(pl.multiple_of(q * w, w), w)
    order = list(range(1, n)) + [0] + list(range(n, nb))
    at = lambda o: lax.rem(g + o, n) if o < n else o
    C = {}; X = {}; Dd = {}
    for o in order:
        d = at(o)
        cbuf[o, 0] = src[d, :, sl(tc)].astype(BF)
        cbuf[o, 1] = src[d, :, sl(tcx)].astype(BF)
        C[o] = rcopy(cbuf.at[o], cin.at[o], cs.at[o], cr.at[o], g, tc); C[o].start()
    for o in order:
        C[o].wait_recv()
        xbuf[o] = (src[at(o), :, sl(tx)] + cin[o, 1].astype(F32)).astype(BF)
        X[o] = rcopy(xbuf.at[o], xin.at[o], xs.at[o], xr.at[o], g, tx); X[o].start()
    for o in order:
        d = at(o)
        X[o].wait_recv()
        total = (src[d, :, sl(t)] + cin[o, 0].astype(F32) + xin[o].astype(F32)).astype(BF)
        if 0 < o < n:
            dbuf[o] = total
            Dd[o] = rcopy(dbuf.at[o], out.at[g], ds_.at[o], dr.at[o], d, t); Dd[o].start()
        elif o == 0:
            out[g] = total
        else:
            out[o] = total
    for c in Dd.values(): c.wait_recv()
    for c in list(C.values()) + list(X.values()) + list(Dd.values()): c.wait_send()

def reduce(src, n, cid=1):
    nb, r, w = src.shape; w //= 4
    return pl.pallas_call(functools.partial(reduce_body, n, nb),
        out_shape=jax.ShapeDtypeStruct((nb, r, w), BF),
        in_specs=[pl.BlockSpec(memory_space=VM)], out_specs=pl.BlockSpec(memory_space=VM),
        scratch_shapes=[VM((nb,2,r,w),BF), VM((nb,2,r,w),BF), VM((nb,r,w),BF), VM((nb,r,w),BF), VM((n,r,w),BF)] + [DMA((nb,))]*4 + [DMA((n,))]*2,
        name="reduce_rows", compiler_params=params(cid))(src)

def a2a_body(n, src, out, ss, rs):
    g, t, tx, tc = ranks()
    greet([(lax.rem(g + o, n), t) for o in range(1, n)])
    cs = []
    for o in range(1, n):
        d = lax.rem(g + o, n)
        c = rcopy(src.at[d], out.at[g], ss.at[o], rs.at[o], d, t); c.start(); cs.append(c)
    out[g] = src[g]
    for c in cs: c.wait()

def a2a(src, n, cid=2):
    return pl.pallas_call(functools.partial(a2a_body, n),
        out_shape=jax.ShapeDtypeStruct(src.shape, src.dtype),
        in_specs=[pl.BlockSpec(memory_space=VM)], out_specs=pl.BlockSpec(memory_space=VM),
        scratch_shapes=[DMA((n,))]*2,
        name="a2a_rows", compiler_params=params(cid))(src)

def a2a_copy_body(n, src, out, ss, rs):
    g, t, tx, tc = ranks()
    greet([(lax.rem(g + o, n), t) for o in range(1, n)])
    cs = []
    for o in range(1, n):
        d = lax.rem(g + o, n)
        c = rcopy(src, out.at[g], ss.at[o], rs.at[o], d, t); c.start(); cs.append(c)
    out[g] = src[...]
    for c in cs: c.wait()

def a2a_copy(src, n, cid):
    return pl.pallas_call(functools.partial(a2a_copy_body, n),
        out_shape=jax.ShapeDtypeStruct((n,) + src.shape, src.dtype),
        in_specs=[pl.BlockSpec(memory_space=VM)], out_specs=pl.BlockSpec(memory_space=VM),
        scratch_shapes=[DMA((n,))]*2,
        name="copy_rows", compiler_params=params(cid))(src)

def dot(a, b, dims):
    return lax.dot_general(a, b, dims, preferred_element_type=F32)


def mm(a, b):
    return dot(a, b, (((a.ndim - 1,), (0,)), ((), ())))


def mm_t(a, b):
    return dot(a, b, (((1,), (1,)), ((), ())))


def mm_rows(a, b):
    return dot(a, b, (((0,), (0,)), ((), ())))


def slots_of(route_a, route_b, names, cap):
    tokens = route_a.shape[-1]
    member = (route_a == names) | (route_b == names)
    before = (jnp.arange(tokens)[:, None] < jnp.arange(tokens)[None, :]).astype(BF)
    rank = mm(member.astype(BF), before)
    slot = jnp.arange(cap, dtype=F32)[None, :, None]
    return ((rank[:, None, :] == slot) & member[:, None, :]).astype(BF)


def slot_gate(table, route_a, route_b, gate_a, gate_b, names):
    per_token = jnp.where(route_a == names, gate_a, 0.0) + jnp.where(route_b == names, gate_b, 0.0)
    return jnp.sum(table.astype(F32) * per_token[:, None, :], axis=-1)


def weigh(table, gates, rows):
    slots = table.reshape(-1, table.shape[-1])
    scaled = rows.reshape(slots.shape[0], -1).astype(F32) * gates.reshape(-1, 1)
    high = scaled.astype(BF)
    low = (scaled - high.astype(F32)).astype(BF)
    return mm_rows(slots, high) + mm_rows(slots, low)


def angles(positions):
    half = HD // 2
    frequency = jnp.exp(-math.log(THETA) * jnp.arange(half, dtype=F32) / half)
    turned = positions[..., None] * frequency
    return jnp.cos(turned)[..., None, :], jnp.sin(turned)[..., None, :]


def turn(vectors, cosine, sine):
    half = HD // 2
    a, b = vectors[..., :half], vectors[..., half:]
    return jnp.concatenate([a * cosine - b * sine, b * cosine + a * sine], axis=-1)


def fast_local(
    tokens, out_grad, row_place, seq_lengths, att_routes, att_gates, mlp_routes, mlp_gates,
    gain_attn, w_kv, w_query, w_out, gain_mlp, w_gate, w_up, w_down,
):
    rows, features = tokens.shape
    n = lax.axis_size("dp")
    g, t = lax.axis_index("dp"), lax.axis_index("tensor")
    width = features // 4
    per = rows // n
    heads = w_kv.shape[2] // HD
    hw = heads * HD
    part = lambda a: lax.dynamic_slice_in_dim(a, t * width, width, a.ndim - 1)
    counting = jnp.arange(rows, dtype=jnp.int32)

    place = row_place.reshape(n, rows)
    group = place // rows
    earlier = (group[:, :, None] == group[:, None, :]) & (counting[None, :] < counting[:, None])
    arrival = jnp.sum(earlier.astype(jnp.int32), axis=-1)
    mine = lax.dynamic_index_in_dim(group * per + arrival, g, 0, keepdims=False)
    sorter = (mine[None, :] == counting[:, None]).astype(BF)
    x_sorted = mm(sorter, part(tokens)).astype(BF).reshape(n, per, width)
    dy_sorted = mm(sorter, part(out_grad)).astype(BF).reshape(n, per, width)
    x_all = gather(x_sorted, n, deal=True, cid=1).reshape(n, rows, features)

    here = (group == g) & True
    spot = (jnp.arange(n, dtype=jnp.int32)[:, None] * per + arrival)
    work_of = jnp.sum(
        jnp.where(here[None] & (spot[None] == counting[:, None, None]), place[None] % rows, 0), axis=(1, 2)
    )
    ends = jnp.cumsum(seq_lengths[0])
    segment = jnp.sum((counting[:, None] >= ends[None, :]).astype(jnp.int32), axis=1)
    begins = jnp.sum(
        jnp.where(segment[:, None] == jnp.arange(ends.shape[0])[None, :], (ends - seq_lengths[0])[None, :], 0), axis=1
    )
    carried = jnp.stack(
        [v.astype(F32) for v in (
            att_routes[:, 0], att_routes[:, 1], att_gates[:, 0], att_gates[:, 1],
            mlp_routes[:, 0], mlp_routes[:, 1], mlp_gates[:, 0], mlp_gates[:, 1],
            counting - begins, segment, counting)] + [jnp.zeros((rows,), F32)] * 5)
    moved = jnp.sum(
        jnp.where(work_of[None, :, None] == counting[None, None, :], carried[:, None, :], 0.0), axis=2
    )
    meta_all = a2a_copy(moved, n, cid=8)
    ar0, ar1, ag0, ag1, mr0, mr1, mg0, mg1, pos, seg, wpos = [meta_all[:, i] for i in range(11)]
    me = g.astype(F32)
    names = jnp.arange(n, dtype=F32)[:, None]
    own = lambda a: lax.dynamic_index_in_dim(a, g, 0, keepdims=False)

    att_in = slots_of(ar0, ar1, me, CAP)
    att_in_gate = slot_gate(att_in, ar0, ar1, ag0, ag1, me)
    mlp_in = slots_of(mr0, mr1, me, CAP)
    mlp_in_gate = slot_gate(mlp_in, mr0, mr1, mg0, mg1, me)
    o_ar0, o_ar1, o_ag0, o_ag1 = own(ar0)[None], own(ar1)[None], own(ag0)[None], own(ag1)[None]
    o_mr0, o_mr1, o_mg0, o_mg1 = own(mr0)[None], own(mr1)[None], own(mg0)[None], own(mg1)[None]
    att_out = slots_of(o_ar0, o_ar1, names, CAP)
    att_out_gate = slot_gate(att_out, o_ar0, o_ar1, o_ag0, o_ag1, names)
    mlp_out = slots_of(o_mr0, o_mr1, names, CAP)
    mlp_out_gate = slot_gate(mlp_out, o_mr0, o_mr1, o_mg0, o_mg1, names)

    xf = x_all.astype(F32)
    scale_attn = inverse_rms(xf)
    normed = (xf * scale_attn * gain_attn).astype(BF)
    normed_flat = normed.reshape(n * rows, features)
    kv = mm(normed_flat, w_kv.reshape(features, 2 * hw)).reshape(n, rows, 2, heads, HD)
    key_cos, key_sin = angles(pos)
    keys = turn(kv[:, :, 0], key_cos, key_sin).astype(BF)
    values = kv[:, :, 1].astype(BF)
    picked = jnp.einsum("gst,gtd->gsd", att_in, normed, preferred_element_type=F32).astype(BF)
    picked = picked.reshape(n * CAP, features)
    slot_pos = jnp.sum(att_in.astype(F32) * pos[:, None, :], axis=-1)
    slot_seg = jnp.sum(att_in.astype(F32) * seg[:, None, :], axis=-1)
    slot_wpos = jnp.sum(att_in.astype(F32) * wpos[:, None, :], axis=-1)
    q_cos, q_sin = angles(slot_pos)
    query = turn(mm(picked, w_query[0]).reshape(n, CAP, heads, HD), q_cos, q_sin).astype(BF)
    allowed = (slot_seg[:, :, None] == seg[:, None, :]) & (wpos[:, None, :] <= slot_wpos[:, :, None])
    root = math.sqrt(HD)
    scores = jnp.einsum("gshd,gmhd->ghsm", query, keys, preferred_element_type=F32) / root
    scores = jnp.where(allowed[:, None], scores, -1e30)
    probs = jax.nn.softmax(scores, axis=-1)
    probs_low = probs.astype(BF)
    attn = jnp.einsum("ghsm,gmhd->gshd", probs_low, values, preferred_element_type=F32)
    attn = attn.astype(BF).reshape(n * CAP, hw)
    query_back = lax.all_to_all(query.reshape(n, CAP, hw), "dp", split_axis=0, concat_axis=0, tiled=True)
    obr = reduce(mm(attn, w_out[0]).reshape(n, CAP, features), n, cid=2)
    x_own = part(own(x_all)).astype(F32)
    hidden = x_own + weigh(att_out, att_out_gate, obr)

    mlp_rows = mlp_out.reshape(n * CAP, rows)
    hid_rows = gather(mm(mlp_rows, hidden.astype(BF)).astype(BF).reshape(n, CAP, width), n, cid=0)
    dy_all = gather(dy_sorted, n, deal=True, cid=1).reshape(n, rows, features)
    d_mbr = jnp.einsum("gst,gtd->gsd", mlp_in, dy_all, preferred_element_type=F32) * mlp_in_gate[..., None]
    d_mbr = d_mbr.astype(BF).reshape(n * CAP, features)
    hid_rows = hid_rows.reshape(n * CAP, features).astype(F32)
    normed2 = (hid_rows * inverse_rms(hid_rows) * gain_mlp).astype(BF)
    gate_map, up_map, down_map = w_gate[0], w_up[0], w_down[0]
    gate_act = mm(normed2, gate_map)
    up_act = mm(normed2, up_map)
    sigmoid_g = jax.nn.sigmoid(gate_act)
    inner = (gate_act * sigmoid_g * up_act).astype(BF)
    d_inner = mm_t(d_mbr, down_map)
    d_up = (d_inner * gate_act * sigmoid_g).astype(BF)
    d_gate = (d_inner * up_act * sigmoid_g * (1.0 + gate_act * (1.0 - sigmoid_g))).astype(BF)
    d_rows = mm_t(d_gate, gate_map) + mm_t(d_up, up_map)
    d_pairs = reduce(d_rows.reshape(n, CAP, features), n, cid=2)
    mbr = reduce(mm(inner, down_map).reshape(n, CAP, features), n, cid=2)
    mixed_rows = hidden + weigh(mlp_out, mlp_out_gate, mbr)
    w_gate_grad = mm_rows(normed2, d_gate)[None]
    w_up_grad = mm_rows(normed2, d_up)[None]
    w_down_grad = mm_rows(inner, d_mbr)[None]
    d_normed2 = mm_rows(mlp_rows, d_pairs.reshape(n * CAP, width))
    gain_mlp_t, gain_attn_t = part(gain_mlp), part(gain_attn)
    dy_own = part(own(dy_all)).astype(F32)
    e2 = gain_mlp_t * d_normed2
    square, inner_sum = lax.psum(
        (jnp.sum(hidden * hidden, axis=1, keepdims=True), jnp.sum(hidden * e2, axis=1, keepdims=True)), "tensor")
    scale_mlp = lax.rsqrt(square / features + EPSILON)
    d_hidden = dy_own + scale_mlp * e2 - hidden * (scale_mlp * scale_mlp * scale_mlp) * (inner_sum / features)
    gain_mlp_part = jnp.sum(d_normed2 * hidden * scale_mlp, axis=0)

    att_rows = att_out.reshape(n * CAP, rows)
    d_obr = gather(mm(att_rows, d_hidden.astype(BF)).astype(BF).reshape(n, CAP, width), n, cid=0)
    d_obr = (d_obr.astype(F32) * att_in_gate[..., None]).astype(BF).reshape(n * CAP, features)
    d_attn = mm_t(d_obr, w_out[0]).astype(BF).reshape(n, CAP, heads, HD)
    d_attn_back = a2a(d_attn.reshape(n, CAP, hw), n, cid=4)
    w_out_grad = mm_rows(attn, d_obr)[None]
    d_probs = jnp.einsum("gshd,gmhd->ghsm", d_attn, values, preferred_element_type=F32)
    delta = jnp.sum(d_probs * probs, axis=-1, keepdims=True)
    d_scores = (probs * (d_probs - delta)).astype(BF)
    d_query = jnp.einsum("ghsm,gmhd->gshd", d_scores, keys, preferred_element_type=F32) / root
    dq_pre = turn(d_query, q_cos, -q_sin).astype(BF).reshape(n * CAP, hw)
    w_query_grad = mm_rows(picked, dq_pre)[None]
    d_norm_q = mm_t(dq_pre, w_query[0]).reshape(n, CAP, features)

    b_query = query_back.reshape(n * CAP, heads, HD)
    b_d_attn = d_attn_back.reshape(n * CAP, heads, HD)
    b_keys, b_values, b_seg, b_wpos = own(keys), own(values), own(seg), own(wpos)
    r_seg = jnp.sum(att_rows.astype(F32) * b_seg[None, :], axis=-1)
    r_wpos = jnp.sum(att_rows.astype(F32) * b_wpos[None, :], axis=-1)
    b_allowed = (r_seg[:, None] == b_seg[None, :]) & (b_wpos[None, :] <= r_wpos[:, None])
    b_scores = jnp.einsum("shd,mhd->hsm", b_query, b_keys, preferred_element_type=F32) / root
    b_probs = jax.nn.softmax(jnp.where(b_allowed[None], b_scores, -1e30), axis=-1)
    b_d_probs = jnp.einsum("shd,mhd->hsm", b_d_attn, b_values, preferred_element_type=F32)
    b_delta = jnp.sum(b_d_probs * b_probs, axis=-1, keepdims=True)
    b_d_scores = (b_probs * (b_d_probs - b_delta)).astype(BF)
    d_values = jnp.einsum("hsm,shd->mhd", b_probs.astype(BF), b_d_attn, preferred_element_type=F32)
    d_keys = jnp.einsum("hsm,shd->mhd", b_d_scores, b_query, preferred_element_type=F32) / root
    d_keys = turn(d_keys, own(key_cos), -own(key_sin))
    d_kv = jnp.concatenate([d_keys.reshape(rows, hw), d_values.reshape(rows, hw)], axis=1).astype(BF)
    d_kv_all = a2a_copy(d_kv, n, cid=5)
    w_kv_grad = mm_rows(normed_flat, d_kv_all.reshape(n * rows, 2 * hw)).reshape(features, 2, hw)
    d_norm_kv = mm_t(d_kv, w_kv.reshape(features, 2 * hw)).reshape(rows // CAP, CAP, features)

    d_norm = reduce(jnp.concatenate([d_norm_q, d_norm_kv], axis=0), n, cid=3)
    d_normed = mm_rows(att_rows, d_norm[:n].reshape(n * CAP, width))
    d_normed = d_normed + d_norm[n:].reshape(rows, width).astype(F32)
    scale_own = own(scale_attn)
    e1 = gain_attn_t * d_normed
    sum_1 = lax.psum(jnp.sum(x_own * e1, axis=1, keepdims=True), "tensor")
    in_grad = d_hidden + scale_own * e1 - x_own * (scale_own * scale_own * scale_own) * (sum_1 / features)
    gain_attn_part = jnp.sum(d_normed * x_own * scale_own, axis=0)

    gains = jnp.concatenate([gain_mlp_part[None], gain_attn_part[None], jnp.zeros((6, width), F32)], axis=0)
    gains = jnp.sum(gather(gains, n, bcast=True, cid=7), axis=0)
    back = jnp.concatenate(
        [mixed_rows.astype(BF).reshape(n, per, width), in_grad.astype(BF).reshape(n, per, width)], axis=1
    )
    back = gather(back, n, cid=6)
    mixed = mm_rows(sorter, back[:, :per].reshape(rows, features)).astype(BF)
    tokens_grad = mm_rows(sorter, back[:, per:].reshape(rows, features)).astype(BF)
    return (
        mixed, tokens_grad, gains[1], w_kv_grad, w_query_grad, w_out_grad, gains[0],
        w_gate_grad, w_up_grad, w_down_grad,
    )


def solution(mesh):
    placed = (
        P("dp", None),
        P("dp", None),
        P(),
        P("dp", None),
        P("dp", None),
        P("dp", None),
        P("dp", None),
        P("dp", None),
        P(),
        P(None, None, "tensor"),
        P("dp", None, "tensor"),
        P("dp", "tensor", None),
        P(),
        P("dp", None, "tensor"),
        P("dp", None, "tensor"),
        P("dp", "tensor", None),
    )
    dealt = mesh.shape["dp"] == EXPERTS and mesh.shape["tensor"] == 4
    return jax.shard_map(
        fast_local if dealt else local,
        mesh=mesh,
        in_specs=placed,
        out_specs=(
            P("dp", None),
            P("dp", None),
            P(),
            P(None, None, "tensor"),
            P("dp", None, "tensor"),
            P("dp", "tensor", None),
            P(),
            P("dp", None, "tensor"),
            P("dp", None, "tensor"),
            P("dp", "tensor", None),
        ),
        check_vma=False,
    )
```

```python
import functools
import math

import jax
import jax.numpy as jnp
import numpy as np
from jax import lax
from jax.experimental import pallas as pl
from jax.experimental.pallas import tpu as pltpu
from jax.sharding import PartitionSpec as P

HD = 128
ATT_EXPERTS = 8
EXPERTS = 8
CAP = 64


EPSILON = 1e-05
THETA = 10000.0


def inverse_rms(values_in):
    return lax.rsqrt(jnp.mean(values_in * values_in, axis=-1, keepdims=True) + EPSILON)


def norm_backward(inputs, inv_root, gain, incoming):
    weighted = incoming * gain
    inner_mean = jnp.mean(inputs * weighted, axis=-1, keepdims=True)
    return inv_root * weighted - inputs * (inv_root * inv_root * inv_root) * inner_mean


def rotate(vectors, positions, direction):
    half_dim = vectors.shape[-1] // 2
    frequency = jnp.exp(-math.log(THETA) * jnp.arange(half_dim, dtype=jnp.float32) / half_dim)
    angles = positions.astype(jnp.float32)[:, None] * frequency[None, :]
    target = (vectors.shape[0],) + (1,) * (vectors.ndim - 2) + (half_dim,)
    cosine = jnp.cos(angles).reshape(target)
    sine = direction * jnp.sin(angles).reshape(target)
    former = vectors[..., :half_dim]
    latter = vectors[..., half_dim:]
    return jnp.concatenate(
        [former * cosine - latter * sine, latter * cosine + former * sine], axis=-1
    )


def expert_slots(routes, experts, capacity):
    flattened = routes.reshape(-1)
    pair_count = flattened.shape[0]
    one_hot = (flattened[:, None] == jnp.arange(experts, dtype=jnp.int32)[None, :]).astype(
        jnp.int32
    )
    earlier = jnp.cumsum(one_hot, axis=0) - one_hot
    position = jnp.sum(earlier * one_hot, axis=1)
    slot_table = jnp.full((experts, capacity), pair_count, jnp.int32)
    slot_table = slot_table.at[flattened, position].set(jnp.arange(pair_count, dtype=jnp.int32))
    return (flattened * capacity + position, slot_table)


def pick_rows(source_rows, slot_table):
    padded = jnp.concatenate(
        [source_rows, jnp.zeros((1, source_rows.shape[1]), source_rows.dtype)], axis=0
    )
    return padded[slot_table]


def send_slices(source_rows, slot_table, group_size):
    picked = pick_rows(source_rows, slot_table)
    experts, capacity, features = picked.shape
    divided = picked.reshape(experts, capacity, group_size, features // group_size)
    return divided.transpose(0, 2, 1, 3).reshape(
        experts * group_size, capacity, features // group_size
    )


def send_copies(source_rows, slot_table, group_size):
    picked = pick_rows(source_rows, slot_table)
    experts, capacity, features = picked.shape
    copies = jnp.broadcast_to(picked[:, None], (experts, group_size, capacity, features))
    return copies.reshape(experts * group_size, capacity, features)


def owners_summed(returned, pair_where, group_size):
    owners, capacity, features = returned.shape
    summed = returned.reshape(owners // group_size, group_size, capacity, features).sum(axis=1)
    return summed.reshape(-1, features)[pair_where]


def owners_joined(returned, pair_where, group_size):
    owners, capacity, features = returned.shape
    joined = returned.reshape(owners // group_size, group_size, capacity, features).transpose(
        0, 2, 1, 3
    )
    return joined.reshape(-1, group_size * features)[pair_where]


def query_return(pieces):
    return lax.all_to_all(pieces, "dp", split_axis=0, concat_axis=0, tiled=True)


def output_return(pieces):
    return lax.all_to_all(pieces, "dp", split_axis=0, concat_axis=0, tiled=True)


def expert_return(pieces):
    return lax.all_to_all(pieces, "dp", split_axis=0, concat_axis=0, tiled=True)


def tensor_total(pieces):
    return lax.psum(pieces, "tensor")


def deal_plan(row_place, rows_dev):
    device_count = lax.axis_size("dp")
    my_index = lax.axis_index("dp")
    per_peer = rows_dev // device_count
    every_place = row_place.reshape(device_count, rows_dev)
    my_places = lax.dynamic_index_in_dim(every_place, my_index, 0, keepdims=False)
    counting = jnp.arange(rows_dev, dtype=jnp.int32)
    ordering = jnp.argsort(my_places // rows_dev * rows_dev + counting)
    wanted = every_place // rows_dev == my_index
    chosen = jnp.argsort(
        jnp.where(wanted, counting[None, :], rows_dev + counting[None, :]), axis=1
    )[:, :per_peer]
    placed = jnp.take_along_axis(every_place, chosen, axis=1) % rows_dev
    return (ordering, placed.reshape(-1))


def masked_scores(query_b, keys_b, allowed):
    raw = jnp.einsum(
        "ikjd,mjd->kjim", query_b, keys_b, preferred_element_type=jnp.float32
    ) / math.sqrt(query_b.shape[-1])
    return jnp.where(allowed[None, None], raw, -1e30)


def local(
    tokens,
    out_grad,
    row_place,
    seq_lengths,
    att_routes,
    att_gates,
    mlp_routes,
    mlp_gates,
    gain_attn,
    w_kv,
    w_query,
    w_out,
    gain_mlp,
    w_gate,
    w_up,
    w_down,
):
    rows_dev, features = tokens.shape
    device_count = lax.axis_size("dp")
    group_size = device_count // EXPERTS
    per_peer = rows_dev // device_count
    counting = jnp.arange(rows_dev, dtype=jnp.int32)
    ordering, placed = deal_plan(row_place, rows_dev)
    unplace = jnp.zeros((rows_dev,), jnp.int32).at[placed].set(counting)
    unorder = jnp.zeros((rows_dev,), jnp.int32).at[ordering].set(counting)
    dealt_x, dealt_g = (
        lax.all_to_all(
            tokens[ordering].reshape(device_count, per_peer, features),
            "dp",
            split_axis=0,
            concat_axis=0,
            tiled=True,
        ),
        lax.all_to_all(
            out_grad[ordering].reshape(device_count, per_peer, features),
            "dp",
            split_axis=0,
            concat_axis=0,
            tiled=True,
        ),
    )
    residual = dealt_x.reshape(rows_dev, features)[unplace].astype(jnp.float32)
    top_grad = dealt_g.reshape(rows_dev, features)[unplace].astype(jnp.float32)
    lengths = seq_lengths[0]
    seq_ends = jnp.cumsum(lengths)
    segment = jnp.sum((counting[:, None] >= seq_ends[None, :]).astype(jnp.int32), axis=1)
    starts = seq_ends - lengths
    member = segment[:, None] == jnp.arange(lengths.shape[0], dtype=jnp.int32)[None, :]
    begins = jnp.sum(jnp.where(member, starts[None, :], 0), axis=1)
    positions = counting - begins
    allowed = (segment[:, None] == segment[None, :]) & (counting[None, :] <= counting[:, None])
    head_count = w_kv.shape[2] // HD
    scale_attn = inverse_rms(residual)
    normed = (residual * scale_attn * gain_attn).astype(jnp.bfloat16)
    kv_proj = jnp.einsum("ld,dck->lck", normed, w_kv, preferred_element_type=jnp.float32)
    keys = rotate(kv_proj[:, 0].reshape(rows_dev, head_count, HD), positions, 1.0).astype(
        jnp.bfloat16
    )
    values = kv_proj[:, 1].reshape(rows_dev, head_count, HD).astype(jnp.bfloat16)
    att_where, att_table = expert_slots(att_routes, ATT_EXPERTS, CAP)
    query_rows = lax.all_to_all(
        send_slices(normed, att_table // 2, group_size),
        "dp",
        split_axis=0,
        concat_axis=0,
        tiled=True,
    )
    query_part = jnp.einsum(
        "scd,dh->sch", query_rows, w_query[0], preferred_element_type=jnp.float32
    )
    query_pre = owners_summed(query_return(query_part), att_where, group_size)
    query_rot = rotate(query_pre.reshape(rows_dev, 2, head_count, HD), positions, 1.0).astype(
        jnp.bfloat16
    )
    scores = masked_scores(query_rot, keys, allowed)
    highest = jnp.max(scores, axis=-1, keepdims=True)
    expo = jnp.exp(scores - highest)
    row_total = jnp.sum(expo, axis=-1, keepdims=True)
    log_total = highest + jnp.log(row_total)
    probability = expo / row_total
    attn = jnp.einsum(
        "kjim,mjd->ikjd",
        probability.astype(jnp.bfloat16),
        values,
        preferred_element_type=jnp.float32,
    )
    attn_low = attn.astype(jnp.bfloat16).reshape(rows_dev * 2, head_count * HD)
    out_rows = lax.all_to_all(
        send_copies(attn_low, att_table, group_size), "dp", split_axis=0, concat_axis=0, tiled=True
    )
    out_part = jnp.einsum("sch,hd->scd", out_rows, w_out[0], preferred_element_type=jnp.float32)
    out_pairs = owners_joined(output_return(out_part), att_where, group_size).reshape(
        rows_dev, 2, features
    )
    hidden = residual + tensor_total(jnp.sum(out_pairs * att_gates[:, :, None], axis=1))
    gate_map, up_map, down_map = (w_gate[0], w_up[0], w_down[0])
    scale_mlp = inverse_rms(hidden)
    normed2 = (hidden * scale_mlp * gain_mlp).astype(jnp.bfloat16)
    mlp_where, mlp_table = expert_slots(mlp_routes, EXPERTS, CAP)
    expert_sent = send_copies(normed2, mlp_table // 2, group_size)
    expert_rows = lax.all_to_all(expert_sent, "dp", split_axis=0, concat_axis=0, tiled=True)
    flat_rows = expert_rows.reshape(-1, features)
    gate_act = jnp.dot(flat_rows, gate_map, preferred_element_type=jnp.float32)
    up_act = jnp.dot(flat_rows, up_map, preferred_element_type=jnp.float32)
    inner = (jax.nn.silu(gate_act) * up_act).astype(jnp.bfloat16)
    expert_part = jnp.dot(inner, down_map, preferred_element_type=jnp.float32).reshape(
        expert_rows.shape
    )
    expert_pairs = owners_summed(expert_return(expert_part), mlp_where, group_size).reshape(
        rows_dev, 2, features
    )
    mixed_rows = hidden + tensor_total(jnp.sum(expert_pairs * mlp_gates[:, :, None], axis=1))
    branch_grad = (
        (top_grad[:, None, :] * mlp_gates[:, :, None])
        .astype(jnp.bfloat16)
        .reshape(rows_dev * 2, features)
    )
    grad_sent = send_copies(branch_grad, mlp_table, group_size)
    grad_back, rows_back = (
        lax.all_to_all(grad_sent, "dp", split_axis=0, concat_axis=0, tiled=True),
        lax.all_to_all(expert_sent, "dp", split_axis=0, concat_axis=0, tiled=True),
    )
    grad_rows = grad_back.reshape(-1, features)
    rows_again = rows_back.reshape(-1, features)
    gate_again = jnp.dot(rows_again, gate_map, preferred_element_type=jnp.float32)
    up_again = jnp.dot(rows_again, up_map, preferred_element_type=jnp.float32)
    inner_again = (jax.nn.silu(gate_again) * up_again).astype(jnp.bfloat16)
    contract_rows = (((0,), (0,)), ((), ()))
    contract_cols = (((1,), (1,)), ((), ()))
    d_inner = lax.dot_general(
        grad_rows, down_map, contract_cols, preferred_element_type=jnp.float32
    )
    down_grad_all = lax.dot_general(
        inner_again, grad_rows, contract_rows, preferred_element_type=jnp.float32
    )
    sigmoid_g = jax.nn.sigmoid(gate_again)
    d_up = (d_inner * gate_again * sigmoid_g).astype(jnp.bfloat16)
    d_gate = (d_inner * up_again * sigmoid_g * (1.0 + gate_again * (1.0 - sigmoid_g))).astype(
        jnp.bfloat16
    )
    gate_grad_all = lax.dot_general(
        rows_again, d_gate, contract_rows, preferred_element_type=jnp.float32
    )
    up_grad_all = lax.dot_general(
        rows_again, d_up, contract_rows, preferred_element_type=jnp.float32
    )
    d_rows = lax.dot_general(d_gate, gate_map, contract_cols, preferred_element_type=jnp.float32)
    d_rows = d_rows + lax.dot_general(
        d_up, up_map, contract_cols, preferred_element_type=jnp.float32
    )
    d_pairs = owners_summed(expert_return(d_rows.reshape(expert_rows.shape)), mlp_where, group_size)
    w_gate_grad = gate_grad_all[None]
    w_up_grad = up_grad_all[None]
    w_down_grad = down_grad_all[None]
    d_normed2 = tensor_total(jnp.sum(d_pairs.reshape(rows_dev, 2, features), axis=1))
    d_hidden = top_grad + norm_backward(hidden, scale_mlp, gain_mlp, d_normed2)
    gain_mlp_grad = jnp.sum(d_normed2 * hidden * scale_mlp, axis=0)
    att_grad = (
        (d_hidden[:, None, :] * att_gates[:, :, None])
        .astype(jnp.bfloat16)
        .reshape(rows_dev * 2, features)
    )
    grad_slices = lax.all_to_all(
        send_slices(att_grad, att_table, group_size), "dp", split_axis=0, concat_axis=0, tiled=True
    )
    w_out_grad = jnp.einsum(
        "sch,scd->hd", out_rows, grad_slices, preferred_element_type=jnp.float32
    )
    d_attn_part = jnp.einsum(
        "scd,hd->sch", grad_slices, w_out[0], preferred_element_type=jnp.float32
    )
    d_attn = owners_summed(output_return(d_attn_part), att_where, group_size)
    d_attn = d_attn.astype(jnp.bfloat16).reshape(rows_dev, 2, head_count, HD)
    probability = jnp.exp(masked_scores(query_rot, keys, allowed) - log_total)
    d_prob = jnp.einsum("ikjd,mjd->kjim", d_attn, values, preferred_element_type=jnp.float32)
    d_values = jnp.einsum(
        "kjim,ikjd->mjd",
        probability.astype(jnp.bfloat16),
        d_attn,
        preferred_element_type=jnp.float32,
    )
    delta = jnp.sum(d_prob * probability, axis=-1, keepdims=True)
    d_scores = (probability * (d_prob - delta)).astype(jnp.bfloat16)
    root_hd = math.sqrt(HD)
    d_query = (
        jnp.einsum("kjim,mjd->ikjd", d_scores, keys, preferred_element_type=jnp.float32) / root_hd
    )
    d_keys = (
        jnp.einsum("kjim,ikjd->mjd", d_scores, query_rot, preferred_element_type=jnp.float32)
        / root_hd
    )
    dq_pre = (
        rotate(d_query, positions, -1.0).astype(jnp.bfloat16).reshape(rows_dev * 2, head_count * HD)
    )
    dk_pre = rotate(d_keys, positions, -1.0).reshape(rows_dev, head_count * HD)
    d_kv = jnp.stack([dk_pre, d_values.reshape(rows_dev, head_count * HD)], axis=1).astype(
        jnp.bfloat16
    )
    dq_rows = lax.all_to_all(
        send_copies(dq_pre, att_table, group_size), "dp", split_axis=0, concat_axis=0, tiled=True
    )
    w_query_grad = jnp.einsum(
        "scd,sch->dh", query_rows, dq_rows, preferred_element_type=jnp.float32
    )
    d_slice = jnp.einsum("sch,dh->scd", dq_rows, w_query[0], preferred_element_type=jnp.float32)
    d_norm_query = owners_joined(query_return(d_slice), att_where, group_size)
    d_norm_query = jnp.sum(d_norm_query.reshape(rows_dev, 2, features), axis=1)
    w_kv_grad = jnp.einsum("ld,lck->dck", normed, d_kv, preferred_element_type=jnp.float32)
    d_norm_kv = jnp.einsum("lck,dck->ld", d_kv, w_kv, preferred_element_type=jnp.float32)
    d_normed = tensor_total(d_norm_query + d_norm_kv)
    in_grad = d_hidden + norm_backward(residual, scale_attn, gain_attn, d_normed)
    gain_attn_grad = jnp.sum(d_normed * residual * scale_attn, axis=0)
    w_kv_grad, gain_attn_grad, gain_mlp_grad = (
        lax.psum(w_kv_grad.astype(jnp.bfloat16), "dp").astype(jnp.float32),
        lax.psum(gain_attn_grad.astype(jnp.bfloat16), "dp").astype(jnp.float32),
        lax.psum(gain_mlp_grad.astype(jnp.bfloat16), "dp").astype(jnp.float32),
    )
    send_mixed = mixed_rows.astype(jnp.bfloat16)[placed].reshape(device_count, per_peer, features)
    send_input = in_grad.astype(jnp.bfloat16)[placed].reshape(device_count, per_peer, features)
    back_mixed, back_input = (
        lax.all_to_all(send_mixed, "dp", split_axis=0, concat_axis=0, tiled=True),
        lax.all_to_all(send_input, "dp", split_axis=0, concat_axis=0, tiled=True),
    )
    mixed = back_mixed.reshape(rows_dev, features)[unorder]
    tokens_grad = back_input.reshape(rows_dev, features)[unorder]
    return (
        mixed,
        tokens_grad,
        gain_attn_grad,
        w_kv_grad,
        w_query_grad[None],
        w_out_grad[None],
        gain_mlp_grad,
        w_gate_grad,
        w_up_grad,
        w_down_grad,
    )


MESH = pl.DeviceIdType.MESH
VM = pltpu.VMEM
DMA = pltpu.SemaphoreType.DMA
BF = jnp.bfloat16
F32 = jnp.float32

def rcopy(src, dst, ss, rs, dp, tn):
    return pltpu.make_async_remote_copy(src_ref=src, dst_ref=dst, send_sem=ss, recv_sem=rs,
        device_id={"dp": dp, "tensor": tn}, device_id_type=MESH)

def greet(targets):
    b = pltpu.get_barrier_semaphore()
    for dp, tn in targets:
        pl.semaphore_signal(b, inc=1, device_id={"dp": dp, "tensor": tn}, device_id_type=MESH)
    pl.semaphore_wait(b, len(targets))

def ranks():
    g = lax.axis_index("dp"); t = lax.axis_index("tensor")
    return g, t, lax.rem(t + 2, 4), t + 1 - 2 * lax.rem(t, 2)

def params(cid):
    return pltpu.CompilerParams(collective_id=cid, has_side_effects=True, vmem_limit_bytes=56*2**20)

def gather_body(n, mode, src, out, ssem, rsem, xs, xr, cs, cr, c2s, c2r, lsem):
    g, t, tx, tc = ranks()
    w = src.shape[-1]
    greet([(lax.rem(g + o, n), t) for o in range(1, n)] + [(g, tx), (g, tc)])
    cols = pl.ds(pl.multiple_of(t * w, w), w)
    colsx = pl.ds(pl.multiple_of(tx * w, w), w)
    pick = (lambda d: src.at[d]) if mode == "rows" else (lambda d: src)
    at = (lambda b, cc: out.at[:, b, :, cc]) if mode == "deal" else (lambda b, cc: out.at[b, :, cc])
    sends = []
    for o in range(1, n):
        d = lax.rem(g + o, n)
        c = rcopy(pick(d), at(g, cols), ssem.at[o], rsem.at[o], d, t)
        c.start(); sends.append(c)
    loc = pltpu.make_async_copy(pick(g), at(g, cols), lsem)
    loc.start(); loc.wait()
    fx = []; fc = []; fc2 = []
    for o in range(n):
        b = lax.rem(g - o + n, n)
        if o > 0: sends[o - 1].wait_recv()
        c = rcopy(at(b, cols), at(b, cols), xs.at[o], xr.at[o], g, tx); c.start(); fx.append(c)
        c = rcopy(at(b, cols), at(b, cols), cs.at[o], cr.at[o], g, tc); c.start(); fc.append(c)
    for o in range(n):
        b = lax.rem(g - o + n, n)
        fx[o].wait_recv()
        c = rcopy(at(b, colsx), at(b, colsx), c2s.at[o], c2r.at[o], g, tc); c.start(); fc2.append(c)
    for c in fc + fc2: c.wait_recv()
    for c in sends + fx + fc + fc2: c.wait_send()

def gather(src, n, bcast=False, deal=False, cid=0, space=VM):
    r, w = src.shape[-2:]
    mode = "deal" if deal else "copy" if bcast else "rows"
    shape = (n, n, r, 4 * w) if deal else (n, r, 4 * w)
    return pl.pallas_call(functools.partial(gather_body, n, mode),
        out_shape=jax.ShapeDtypeStruct(shape, src.dtype),
        in_specs=[pl.BlockSpec(memory_space=VM)], out_specs=pl.BlockSpec(memory_space=space),
        scratch_shapes=[DMA((n,))]*8 + [DMA],
        name="gather_rows", compiler_params=params(cid))(src)

def reduce_body(n, nb, src, out, cbuf, cin, xbuf, xin, dbuf, cs, cr, xs, xr, ds_, dr):
    g, t, tx, tc = ranks()
    tcx = lax.rem(tc + 2, 4); w = out.shape[-1]
    greet([(lax.rem(g + o, n), t) for o in range(1, n)] + [(g, tx), (g, tc)])
    sl = lambda q: pl.ds(pl.multiple_of(q * w, w), w)
    order = list(range(1, n)) + [0] + list(range(n, nb))
    at = lambda o: lax.rem(g + o, n) if o < n else o
    C = {}; X = {}; Dd = {}
    for o in order:
        d = at(o)
        cbuf[o, 0] = src[d, :, sl(tc)].astype(BF)
        cbuf[o, 1] = src[d, :, sl(tcx)].astype(BF)
        C[o] = rcopy(cbuf.at[o], cin.at[o], cs.at[o], cr.at[o], g, tc); C[o].start()
    for o in order:
        C[o].wait_recv()
        xbuf[o] = (src[at(o), :, sl(tx)] + cin[o, 1].astype(F32)).astype(BF)
        X[o] = rcopy(xbuf.at[o], xin.at[o], xs.at[o], xr.at[o], g, tx); X[o].start()
    for o in order:
        d = at(o)
        X[o].wait_recv()
        total = (src[d, :, sl(t)] + cin[o, 0].astype(F32) + xin[o].astype(F32)).astype(BF)
        if 0 < o < n:
            dbuf[o] = total
            Dd[o] = rcopy(dbuf.at[o], out.at[g], ds_.at[o], dr.at[o], d, t); Dd[o].start()
        elif o == 0:
            out[g] = total
        else:
            out[o] = total
    for c in Dd.values(): c.wait_recv()
    for c in list(C.values()) + list(X.values()) + list(Dd.values()): c.wait_send()

def reduce(src, n, cid=1):
    nb, r, w = src.shape; w //= 4
    return pl.pallas_call(functools.partial(reduce_body, n, nb),
        out_shape=jax.ShapeDtypeStruct((nb, r, w), BF),
        in_specs=[pl.BlockSpec(memory_space=VM)], out_specs=pl.BlockSpec(memory_space=VM),
        scratch_shapes=[VM((nb,2,r,w),BF), VM((nb,2,r,w),BF), VM((nb,r,w),BF), VM((nb,r,w),BF), VM((n,r,w),BF)] + [DMA((nb,))]*4 + [DMA((n,))]*2,
        name="reduce_rows", compiler_params=params(cid))(src)

def a2a_body(n, src, out, ss, rs):
    g, t, tx, tc = ranks()
    greet([(lax.rem(g + o, n), t) for o in range(1, n)])
    cs = []
    for o in range(1, n):
        d = lax.rem(g + o, n)
        c = rcopy(src.at[d], out.at[g], ss.at[o], rs.at[o], d, t); c.start(); cs.append(c)
    out[g] = src[g]
    for c in cs: c.wait()

def a2a(src, n, cid=2):
    return pl.pallas_call(functools.partial(a2a_body, n),
        out_shape=jax.ShapeDtypeStruct(src.shape, src.dtype),
        in_specs=[pl.BlockSpec(memory_space=VM)], out_specs=pl.BlockSpec(memory_space=VM),
        scratch_shapes=[DMA((n,))]*2,
        name="a2a_rows", compiler_params=params(cid))(src)

def a2a_copy_body(n, src, out, ss, rs):
    g, t, tx, tc = ranks()
    greet([(lax.rem(g + o, n), t) for o in range(1, n)])
    cs = []
    for o in range(1, n):
        d = lax.rem(g + o, n)
        c = rcopy(src, out.at[g], ss.at[o], rs.at[o], d, t); c.start(); cs.append(c)
    out[g] = src[...]
    for c in cs: c.wait()

def a2a_copy(src, n, cid):
    return pl.pallas_call(functools.partial(a2a_copy_body, n),
        out_shape=jax.ShapeDtypeStruct((n,) + src.shape, src.dtype),
        in_specs=[pl.BlockSpec(memory_space=VM)], out_specs=pl.BlockSpec(memory_space=VM),
        scratch_shapes=[DMA((n,))]*2,
        name="copy_rows", compiler_params=params(cid))(src)

def dot(a, b, dims):
    return lax.dot_general(a, b, dims, preferred_element_type=F32)


def mm(a, b):
    return dot(a, b, (((a.ndim - 1,), (0,)), ((), ())))


def mm_t(a, b):
    return dot(a, b, (((1,), (1,)), ((), ())))


def mm_rows(a, b):
    return dot(a, b, (((0,), (0,)), ((), ())))


class Ring:
    def __init__(self, n):
        self.n = n
        self.g, self.t, self.tx, self.tc = ranks()
        self.tcx = lax.rem(self.tc + 2, 4)
        self.tail = []

    def to(self, o):
        return lax.rem(self.g + o, self.n)

    def greet_all(self):
        greet([(self.to(o), self.t) for o in range(1, self.n)] + [(self.g, self.tx), (self.g, self.tc)])

    def greet_everyone(self):
        greet([(self.to(o), self.t) for o in range(1, self.n)] + [(self.g, q) for q in (self.tx, self.tc, self.tcx)])

    def send(self, src, dst, ss, rs, dp, tn):
        c = rcopy(src, dst, ss, rs, dp, tn)
        c.start()
        self.tail.append(c)
        return c

    def finish(self):
        for c in self.tail:
            c.wait_send()
        self.tail = []


def cols_of(q, j, width, cw):
    return pl.ds(pl.multiple_of(q * width + j * cw, cw), cw)


REDUCE_SEMS = lambda nc, n: [DMA((nc,))] * 4 + [DMA((nc, n))] * 2
GATHER_SEMS = lambda nc, n: [DMA((nc, n))] * 2 + [DMA((nc,))] * 6
REDUCE_BUFS = lambda nc, n, r, cw: [
    VM((nc, 2, n, r, cw), BF), VM((nc, 2, n, r, cw), BF), VM((nc, 2, n, r, cw), F32),
    VM((nc, n, r, cw), BF), VM((nc, n, r, cw), BF), VM((nc, n, r, cw), BF), VM((nc, n, r, cw), BF)]


class Reduce:
    def __init__(self, ring, partial, bufs, sems):
        self.ring, self.partial = ring, partial
        self.cbuf, self.cin, self.pbuf, self.xbuf, self.xin, self.dbuf, self.rbuf = bufs
        self.cs, self.cr, self.xs, self.xr, self.ds, self.dr = sems
        self.c, self.x, self.d = {}, {}, {}

    def core(self):
        k = self.ring
        nc, _, n, r, cw = self.cbuf.shape
        for i, q in enumerate((k.tc, k.tcx)):
            v = self.partial(q).astype(BF)
            for j in range(nc):
                self.cbuf[j, i] = v[:, j * cw:(j + 1) * cw].reshape(n, r, cw)
        for j in range(nc):
            self.c[j] = k.send(self.cbuf.at[j], self.cin.at[j], self.cs.at[j], self.cr.at[j], k.g, k.tc)
        for i, q in ((1, k.tx), (0, k.t)):
            v = self.partial(q)
            for j in range(nc):
                self.pbuf[j, i] = v[:, j * cw:(j + 1) * cw].reshape(n, r, cw)
            if i:
                for j in range(nc):
                    self.cross(j)

    def cross(self, j):
        k = self.ring
        self.c[j].wait_recv()
        self.xbuf[j] = (self.pbuf[j, 1] + self.cin[j, 1].astype(F32)).astype(BF)
        self.x[j] = k.send(self.xbuf.at[j], self.xin.at[j], self.xs.at[j], self.xr.at[j], k.g, k.tx)

    def home(self, j):
        k = self.ring
        self.x[j].wait_recv()
        self.dbuf[j] = (self.pbuf[j, 0] + self.cin[j, 0].astype(F32) + self.xin[j].astype(F32)).astype(BF)
        for o in range(1, k.n):
            d = k.to(o)
            self.d[j, o] = k.send(
                self.dbuf.at[j, d], self.rbuf.at[j, k.g], self.ds.at[j, o], self.dr.at[j, o], d, k.t)
        self.rbuf[j, k.g] = self.dbuf[j, k.g]

    def rows(self, j):
        for o in range(1, self.ring.n):
            self.d[j, o].wait_recv()
        return self.rbuf[j].reshape(-1, self.rbuf.shape[-1])


class Gather:
    def __init__(self, ring, width, full, sbuf, sems):
        self.ring, self.width, self.full, self.sbuf = ring, width, full, sbuf
        self.ss, self.rs, self.xs, self.xr, self.cs, self.cr, self.c2s, self.c2r = sems
        self.d, self.x, self.c = {}, {}, []

    def at(self, q, j):
        return cols_of(q, j, self.width, self.sbuf.shape[-1])

    def out(self, j, rows):
        k, cc = self.ring, self.at(self.ring.t, j)
        self.sbuf[j] = rows.reshape(self.sbuf.shape[1:])
        for o in range(1, k.n):
            d = k.to(o)
            self.d[j, o] = k.send(
                self.sbuf.at[j, d], self.full.at[k.g, :, cc], self.ss.at[j, o], self.rs.at[j, o], d, k.t)
        self.full[k.g, :, cc] = self.sbuf[j, k.g]

    def cross(self, j):
        k, ref = self.ring, self.full.at[:, :, self.at(self.ring.t, j)]
        for o in range(1, k.n):
            self.d[j, o].wait_recv()
        self.x[j] = k.send(ref, ref, self.xs.at[j], self.xr.at[j], k.g, k.tx)
        self.c.append(k.send(ref, ref, self.cs.at[j], self.cr.at[j], k.g, k.tc))

    def core(self, j):
        k, ref = self.ring, self.full.at[:, :, self.at(self.ring.tx, j)]
        self.x[j].wait_recv()
        self.c.append(k.send(ref, ref, self.c2s.at[j], self.c2r.at[j], k.g, k.tc))

    def finish(self):
        for c in self.c:
            c.wait_recv()


def paired(reduce_one, gather_one, middle, nc):
    reduce_one.core()
    steps = []
    for j in range(nc):
        steps += [(2 * j, 0, lambda j=j: reduce_one.home(j)), (2 * j + 3, 1, lambda j=j: gather_one.out(j, middle(j, reduce_one.rows(j))))]
        steps += [(2 * j + 7, 2, lambda j=j: gather_one.cross(j)), (2 * j + 9, 3, lambda j=j: gather_one.core(j))]
    for _, _, step in sorted(steps, key=lambda s: s[:2]):
        step()
    gather_one.finish()


NC = 4


def split_bf(v):
    high = v.astype(BF)
    return high, (v - high.astype(F32)).astype(BF)


def hidden_body(n, attn, wo, x_own, comb, gates, pick, hidden, full, scale, *scratch):
    bufs, sbuf, sq, sq_in, qs, qr, sems = scratch[:7], *scratch[7:12], scratch[12:]
    ring = Ring(n)
    ring.greet_everyone()
    rows, width = x_own.shape
    shared = []
    cw = width // NC

    def partial(q):
        return mm(attn[...], wo[:, cols_of(q, 0, width, width)])

    def middle(j, rows):
        high, low = split_bf(rows.astype(F32) * gates[...])
        got = x_own[:, j * cw:(j + 1) * cw] + mm(comb[...], high) + mm(comb[...], low)
        hidden[:, j * cw:(j + 1) * cw] = got
        high, low = split_bf(got * got)
        ones = jnp.ones((8, cw), BF)
        squares = mm_t(ones, high) + mm_t(ones, low)
        sq[...] = squares if j == 0 else sq[...] + squares
        if j == NC - 1:
            for i, q in enumerate([ring.tc, ring.tx, ring.tcx]):
                shared.append(ring.send(sq, sq_in.at[i], qs.at[i], qr.at[i], ring.g, q))
        return mm(pick[...], got.astype(BF)).astype(BF)

    red = Reduce(ring, partial, bufs, sems[:6])
    gat = Gather(ring, width, full, sbuf, sems[6:])
    paired(red, gat, middle, NC)
    for c in shared:
        c.wait_recv()
    total = (sq[...] + sq_in[0] + sq_in[1] + sq_in[2])[:1]
    eye = lax.broadcasted_iota(jnp.int32, (rows, rows), 0) == lax.broadcasted_iota(jnp.int32, (rows, rows), 1)
    column = jnp.sum(jnp.where(eye, total, 0.0), axis=1, keepdims=True)
    scale[...] = lax.rsqrt(column / (4 * width) + EPSILON)
    ring.finish()


def hidden_rows(attn, wo, x_own, comb, gates, pick, n, cid):
    slots = attn.shape[0]
    r, (rows, width) = slots // n, x_own.shape
    return pl.pallas_call(
        functools.partial(hidden_body, n),
        out_shape=(
            jax.ShapeDtypeStruct((rows, width), F32), jax.ShapeDtypeStruct((n, r, 4 * width), BF),
            jax.ShapeDtypeStruct((rows, 1), F32)),
        in_specs=[pl.BlockSpec(memory_space=VM)] * 6,
        out_specs=[pl.BlockSpec(memory_space=VM)] * 3,
        scratch_shapes=REDUCE_BUFS(NC, n, r, width // NC) + [VM((NC, n, r, width // NC), BF)]
        + [VM((8, rows), F32), VM((3, 8, rows), F32), DMA((3,)), DMA((3,))]
        + REDUCE_SEMS(NC, n) + GATHER_SEMS(NC, n),
        name="hidden_rows", compiler_params=params(cid),
    )(attn, wo, x_own, comb, gates, pick)


def expert_body(
    n, hid_rows, d_mbr, gain, wg_hbm, wu_hbm, wd_hbm, hidden, dy_own, gain_t, scale, mlp_t, mlp_gates, mlp_rows, att_rows,
    full, d_hidden, mixed, gain_part, n2, inner, d_gate, d_up, *scratch,
):
    ring = Ring(n)
    bufs, bufs2 = scratch[:7], scratch[7:14]
    sbuf, wg, wu, wd, r_own, r_in, r_to, r_back = scratch[14:22]
    wsem, rss, rsr, rds, rdr = scratch[22:27]
    sems = scratch[27:]
    ff = wg.shape[1]
    rows, width = hidden.shape
    slots = n2.shape[0]
    features = 4 * width
    cw = width // NC
    loads = [pltpu.make_async_copy(a, b, wsem.at[i]) for i, (a, b) in enumerate([(wg_hbm, wg), (wu_hbm, wu), (wd_hbm, wd)])]
    for c in loads:
        c.start()
    ring.greet_everyone()

    def norm_rows(i, _):
        at = pl.ds(pl.multiple_of(i * 64, 64), 64)
        v = hid_rows[i].astype(F32)
        s = lax.rsqrt(jnp.mean(v * v, axis=-1, keepdims=True) + EPSILON)
        n2[at, :] = (v * s * gain[...]).astype(BF)
        return _

    lax.fori_loop(0, n, norm_rows, 0)
    for c in loads:
        c.wait()
    r_own[...] = jnp.zeros_like(r_own)

    def units(at, size):
        a = n2[...]
        gate = mm(a, wg[:, at])
        up = mm(a, wu[:, at])
        d_in = mm_t(d_mbr[...], wd[at, :])
        sig = jax.nn.sigmoid(gate)
        silu = gate * sig
        inner[:, at] = (silu * up).astype(BF)
        du = (d_in * silu).astype(BF)
        dg = (d_in * up * sig * (1.0 + gate * (1.0 - sig))).astype(BF)
        d_up[:, at] = du
        d_gate[:, at] = dg
        both = (gate * dg.astype(F32) + up * du.astype(F32)).astype(BF)
        r_own[...] += mm_t(jnp.ones((8, size), BF), both)

    tile = 256

    def unit_tile(i, _):
        units(pl.ds(pl.multiple_of(i * tile, tile), tile), tile)
        return _

    lax.fori_loop(0, ff // tile, unit_tile, 0)
    if ff % tile:
        units(pl.ds(ff // tile * tile, ff % tile), ff % tile)

    others = [ring.tc, ring.tx, ring.tcx]
    r_sends = [ring.send(r_own, r_in.at[i], rss.at[i], rsr.at[i], ring.g, q) for i, q in enumerate(others)]

    def partial(q):
        at = cols_of(q, 0, width, width)
        return mm_t(d_gate[...], wg[at, :]) + mm_t(d_up[...], wu[at, :])

    def partial_mixed(q):
        return mm(inner[...], wd[:, cols_of(q, 0, width, width)])

    pairs = {}

    def share_r():
        for c in r_sends:
            c.wait_recv()
        r_to[...] = r_own[...] + r_in[0] + r_in[1] + r_in[2]
        for o in range(1, n):
            d = ring.to(o)
            half = pl.ds(pl.multiple_of(d // 2 * 128, 128), 128)
            pairs[o] = ring.send(r_to.at[:, half], r_back.at[ring.g], rds.at[o], rdr.at[o], d, ring.t)
        r_back[ring.g] = r_to[:, pl.ds(pl.multiple_of(ring.g // 2 * 128, 128), 128)]

    total_r = {}

    def take_r():
        for o in range(1, n):
            pairs[o].wait_recv()
        odd = lax.rem(ring.g, 2) == 1
        got = jnp.concatenate(
            [jnp.where(odd, r_back[e][:, 64:], r_back[e][:, :64]) for e in range(n)], axis=1)
        high = got.astype(BF)
        low = (got - high.astype(F32)).astype(BF)
        total_r[0] = (mm_t(mlp_t[...], high) + mm_t(mlp_t[...], low))[:, :1] / features

    def middle(j, got):
        if j == 0:
            take_r()
        cc = slice(j * cw, (j + 1) * cw)
        s2, h = scale[...], hidden[:, cc]
        d_n = mm(mlp_t[...], got)
        d_h = dy_own[:, cc] + s2 * (gain_t[:, cc] * d_n) - h * (s2 * s2) * total_r[0]
        d_hidden[:, cc] = d_h
        gain_part[:, cc] = jnp.broadcast_to(jnp.sum(d_n * h * s2, axis=0, keepdims=True), (8, cw))
        return mm(att_rows[...], d_h.astype(BF)).astype(BF)

    red = Reduce(ring, partial, bufs, sems[:6])
    gat = Gather(ring, width, full, sbuf, sems[6:14])
    red2 = Reduce(ring, partial_mixed, bufs2, sems[14:20])

    def settle(j):
        got = red2.rows(j)
        scaled = got.astype(F32) * mlp_gates[...]
        high = scaled.astype(BF)
        low = (scaled - high.astype(F32)).astype(BF)
        cc = slice(j * cw, (j + 1) * cw)
        mixed[:, cc] = (hidden[:, cc] + mm(mlp_t[...], high) + mm(mlp_t[...], low)).astype(BF)

    red.core()
    share_r()
    steps = []
    for j in range(NC):
        steps += [(2 * j, 1, lambda j=j: red.home(j)), (2 * j + 3, 2, lambda j=j: gat.out(j, middle(j, red.rows(j))))]
        steps += [(2 * j + 7, 3, lambda j=j: gat.cross(j)), (2 * j + 9, 4, lambda j=j: gat.core(j))]
        steps += [(2 * j + 12, 7, lambda j=j: red2.home(j)), (2 * j + 16, 8, lambda j=j: settle(j))]
    steps += [(9.5, 5, red2.core)]
    steps.sort(key=lambda s: s[:2])
    for _, _, run in steps:
        run()
    gat.finish()
    ring.finish()


def expert_layer(hid_rows, d_mbr, gain, wg, wu, wd, hidden, dy_own, gain_t, scale, mlp_t, mlp_gates, mlp_rows, att_rows, n, cid):
    r, features = hid_rows.shape[1:]
    ff = wg.shape[1]
    rows, width = hidden.shape
    slots, cw = n * r, width // NC
    any_, vm = pl.BlockSpec(memory_space=pl.ANY), pl.BlockSpec(memory_space=VM)
    sds = jax.ShapeDtypeStruct
    return pl.pallas_call(
        functools.partial(expert_body, n),
        out_shape=(
            sds((n, r, features), BF), sds((rows, width), F32), sds((rows, width), BF), sds((8, width), F32),
            sds((slots, features), BF), sds((slots, ff), BF), sds((slots, ff), BF), sds((slots, ff), BF)),
        in_specs=[vm, vm, vm, any_, any_, any_] + [vm] * 8,
        out_specs=[vm] * 8,
        scratch_shapes=REDUCE_BUFS(NC, n, r, cw) + REDUCE_BUFS(NC, n, r, cw) + [
            VM((NC, n, r, cw), BF), VM((features, ff), BF), VM((features, ff), BF), VM((ff, features), BF),
            VM((8, slots), F32), VM((3, 8, slots), F32), VM((8, slots), F32), VM((n, 8, 128), F32),
            DMA((3,)), DMA((3,)), DMA((3,)), DMA((n,)), DMA((n,))]
        + REDUCE_SEMS(NC, n) + GATHER_SEMS(NC, n) + REDUCE_SEMS(NC, n),
        name="expert_layer", compiler_params=params(cid),
    )(hid_rows, d_mbr, gain, wg, wu, wd, hidden, dy_own, gain_t, scale, mlp_t, mlp_gates, mlp_rows, att_rows)


META = {name: i for i, name in enumerate(
    ("ar0", "ar1", "ag0", "ag1", "mr0", "mr1", "mg0", "mg1", "pos", "seg", "wpos"))}


def iota(shape, dim):
    return lax.broadcasted_iota(jnp.int32, shape, dim)


def slot_table(meta, first, name, cap):
    member = (meta[first:first + 1] == name) | (meta[first + 1:first + 2] == name)
    tokens = meta.shape[1]
    before = jnp.where(iota((tokens, tokens), 0) < iota((tokens, tokens), 1), 1.0, 0.0).astype(BF)
    rank = mm(jnp.broadcast_to(jnp.where(member, 1.0, 0.0), (8, tokens)).astype(BF), before)[:1]
    return jnp.where((rank == iota((cap, tokens), 0).astype(F32)) & member, 1.0, 0.0).astype(BF)


def allowed_pairs(meta, meta_t):
    seg, wpos = META["seg"], META["wpos"]
    same = meta_t[:, seg:seg + 1] == meta[seg:seg + 1]
    return jnp.where(same & (meta[wpos:wpos + 1] <= meta_t[:, wpos:wpos + 1]), 1.0, 0.0).astype(BF)


def position_rows(meta_t):
    pos = META["pos"]
    tokens = meta_t.shape[0]
    return jnp.where(meta_t[:, pos:pos + 1] == iota((tokens, tokens), 1).astype(F32), 1.0, 0.0).astype(BF)


def looked_up(rows, table):
    got = mm(rows, table)
    w = got.shape[1] // 3
    return got[:, :w] + got[:, w:2 * w] + got[:, 2 * w:]


def turned(v, cosine, sine):
    out = []
    for h in range(v.shape[1] // HD):
        u = v[:, h * HD:(h + 1) * HD]
        out.append(u * cosine + pltpu.roll(u, HD // 2, 1) * sine)
    return jnp.concatenate(out, axis=1)


def angle_tables(positions):
    half = HD // 2
    frequency = np.exp(-math.log(THETA) * np.arange(half) / half)
    turned_by = np.arange(positions)[:, None] * frequency[None, :]
    cosine = np.concatenate([np.cos(turned_by)] * 2, axis=1).astype(np.float32)
    sine = np.concatenate([-np.sin(turned_by), np.sin(turned_by)], axis=1).astype(np.float32)

    def parts(v):
        out, left = [], v
        for _ in range(3):
            p = left.astype(jnp.bfloat16)
            out.append(p)
            left = left - p.astype(np.float32)
        return np.concatenate(out, axis=1)

    return jnp.asarray(parts(cosine)), jnp.asarray(parts(sine))


def softmax_rows(scores):
    top = jnp.max(scores, axis=-1, keepdims=True)
    expo = jnp.exp(scores - top)
    return expo / jnp.sum(expo, axis=-1, keepdims=True)


def attend_body(
    x, gain, w_k, w_v, w_q, meta, meta_t, cos_t, sin_t,
    normed, picked, keys, values, query, attn, scale, bias, turn_slots, k_scr, v_scr, q_scr, n_scr,
):
    me = lax.axis_index("dp").astype(F32)
    pair, rows, features = x.shape
    cap = picked.shape[1]
    heads = w_q.shape[1] // HD
    flat = x[...].reshape(pair * rows, features).astype(F32)
    s = lax.rsqrt(jnp.mean(flat * flat, axis=-1, keepdims=True) + EPSILON)
    scale[...] = s.reshape(pair, rows, 1)
    low = (flat * s * gain[...]).astype(BF)
    n_scr[...] = low
    normed[...] = low.reshape(pair, rows, features)
    k_all, v_all = mm(n_scr[...], w_k[...]), mm(n_scr[...], w_v[...])
    slots = []
    for p in range(pair):
        m, m_t = meta[p], meta_t[p]
        table = slot_table(m, META["ar0"], me, cap)
        at_pos = position_rows(m_t)
        rr = slice(p * rows, (p + 1) * rows)
        kk = turned(k_all[rr], looked_up(at_pos, cos_t[...]), looked_up(at_pos, sin_t[...])).astype(BF)
        k_scr[p] = kk
        v_scr[p] = v_all[rr].astype(BF)
        picked[p] = mm(table, n_scr[rr, :]).astype(BF)
        slot_pos = mm(table, at_pos).astype(BF)
        turn_slots[p, :, :HD] = looked_up(slot_pos, cos_t[...])
        turn_slots[p, :, HD:] = looked_up(slot_pos, sin_t[...])
        bias[p] = (mm(table, allowed_pairs(m, m_t)) - 1.0) * 1e30
        slots.append(table)
    keys[...] = k_scr[...]
    values[...] = v_scr[...]
    q_all = mm(picked[...].reshape(pair * cap, features), w_q[...])
    for p in range(pair):
        qq = turned(q_all[p * cap:(p + 1) * cap], turn_slots[p, :, :HD], turn_slots[p, :, HD:]).astype(BF)
        q_scr[p] = qq
        query[p] = qq
    for p in range(pair):
        for h in range(heads):
            hh = slice(h * HD, (h + 1) * HD)
            scores = mm_t(q_scr[p, :, hh], k_scr[p, :, hh]) / math.sqrt(HD) + bias[p]
            probs = softmax_rows(scores).astype(BF)
            attn[p, :, hh] = mm(probs, v_scr[p, :, hh]).astype(BF)


def attend(x_all, gain, w_k, w_v, w_q, meta, meta_t, cos_t, sin_t):
    n, rows, features = x_all.shape
    hw, cap, pair = w_q.shape[1], CAP, 2
    sds = jax.ShapeDtypeStruct
    block = lambda *s: pl.BlockSpec((pair,) + s, lambda i: (i,) + (0,) * len(s))
    whole = lambda a: pl.BlockSpec(a.shape, lambda i: (0,) * a.ndim)
    return pl.pallas_call(
        attend_body, grid=(n // pair,),
        out_shape=(
            sds((n, rows, features), BF), sds((n, cap, features), BF), sds((n, rows, hw), BF), sds((n, rows, hw), BF),
            sds((n, cap, hw), BF), sds((n, cap, hw), BF), sds((n, rows, 1), F32), sds((n, cap, rows), F32),
            sds((n, cap, 2 * HD), F32)),
        in_specs=[block(rows, features), whole(gain), whole(w_k), whole(w_v), whole(w_q), block(16, rows), block(rows, 16),
                  whole(cos_t), whole(sin_t)],
        out_specs=(
            block(rows, features), block(cap, features), block(rows, hw), block(rows, hw), block(cap, hw), block(cap, hw),
            block(rows, 1), block(cap, rows), block(cap, 2 * HD)),
        scratch_shapes=[VM((pair, rows, hw), BF), VM((pair, rows, hw), BF), VM((pair, cap, hw), BF), VM((pair * rows, features), BF)],
        name="attend", compiler_params=pltpu.CompilerParams(vmem_limit_bytes=56 * 2**20),
    )(x_all, gain, w_k, w_v, w_q, meta, meta_t, cos_t, sin_t)


def attend_back_body(rows_in, gates, w_o, query, keys, values, bias, turn_slots, d_obr, d_attn, dq_pre, o_scr):
    pair, cap, features = rows_in.shape
    heads = w_o.shape[0] // HD
    for p in range(pair):
        o_scr[p * cap:(p + 1) * cap] = (rows_in[p].astype(F32) * gates[p]).astype(BF)
    d_obr[...] = o_scr[...].reshape(pair, cap, features)
    back = mm_t(o_scr[...], w_o[...]).astype(BF)
    root = math.sqrt(HD)
    for p in range(pair):
        d_o = back[p * cap:(p + 1) * cap]
        d_attn[p] = d_o
        dq = []
        for h in range(heads):
            hh = slice(h * HD, (h + 1) * HD)
            probs = softmax_rows(mm_t(query[p, :, hh], keys[p, :, hh]) / root + bias[p])
            d_probs = mm_t(d_o[:, hh], values[p, :, hh])
            delta = jnp.sum(d_probs * probs, axis=-1, keepdims=True)
            d_scores = (probs * (d_probs - delta)).astype(BF)
            dq.append(mm(d_scores, keys[p, :, hh]) / root)
        dq = jnp.concatenate(dq, axis=1)
        dq_pre[p] = turned(dq, turn_slots[p, :, :HD], -turn_slots[p, :, HD:]).astype(BF)


def attend_back(rows_in, gates, w_o, query, keys, values, bias, turn_slots):
    n, cap, features = rows_in.shape
    hw, rows, pair = w_o.shape[0], keys.shape[1], 2
    sds = jax.ShapeDtypeStruct
    block = lambda *s: pl.BlockSpec((pair,) + s, lambda i: (i,) + (0,) * len(s))
    return pl.pallas_call(
        attend_back_body, grid=(n // pair,),
        out_shape=(sds((n, cap, features), BF), sds((n, cap, hw), BF), sds((n, cap, hw), BF)),
        in_specs=[block(cap, features), block(cap, 1), pl.BlockSpec(w_o.shape, lambda i: (0, 0)), block(cap, hw), block(rows, hw),
                  block(rows, hw), block(cap, rows), block(cap, 2 * HD)],
        out_specs=(block(cap, features), block(cap, hw), block(cap, hw)),
        scratch_shapes=[VM((pair * cap, features), BF)],
        name="attend_back", compiler_params=pltpu.CompilerParams(vmem_limit_bytes=56 * 2**20),
    )(rows_in, gates, w_o, query, keys, values, bias, turn_slots)


def keys_back_body(query, d_attn, keys, values, meta, meta_t, cos_t, sin_t, d_kv, *, cap):
    n = query.shape[0]
    hw = keys.shape[1]
    m, m_t = meta[...], meta_t[...]
    tables = jnp.concatenate([slot_table(m, META["ar0"], float(e), cap) for e in range(n)], axis=0)
    bias = (mm(tables, allowed_pairs(m, m_t)) - 1.0) * 1e30
    at_pos = position_rows(m_t)
    cosine, sine = looked_up(at_pos, cos_t[...]), looked_up(at_pos, sin_t[...])
    root = math.sqrt(HD)
    for h in range(hw // HD):
        hh = slice(h * HD, (h + 1) * HD)
        q = query[:, :, hh].reshape(n * cap, HD)
        d_o = d_attn[:, :, hh].reshape(n * cap, HD)
        k, v = keys[:, hh], values[:, hh]
        probs = softmax_rows(mm_t(q, k) / root + bias)
        d_probs = mm_t(d_o, v)
        delta = jnp.sum(d_probs * probs, axis=-1, keepdims=True)
        d_scores = (probs * (d_probs - delta)).astype(BF)
        d_kv[:, hw + h * HD:hw + (h + 1) * HD] = mm_rows(probs.astype(BF), d_o).astype(BF)
        d_k = mm_rows(d_scores, q) / root
        d_kv[:, hh] = turned(d_k, cosine, -sine).astype(BF)


def keys_back(query, d_attn, keys, values, meta, meta_t, cos_t, sin_t):
    rows, hw = keys.shape
    args = (query, d_attn, keys, values, meta, meta_t, cos_t, sin_t)
    return pl.pallas_call(
        functools.partial(keys_back_body, cap=query.shape[1]),
        out_shape=jax.ShapeDtypeStruct((rows, 2 * hw), BF),
        in_specs=[pl.BlockSpec(memory_space=VM)] * len(args), out_specs=pl.BlockSpec(memory_space=VM),
        name="keys_back", compiler_params=pltpu.CompilerParams(vmem_limit_bytes=56 * 2**20),
    )(*args)


def slots_of(route_a, route_b, names, cap):
    tokens = route_a.shape[-1]
    member = (route_a == names) | (route_b == names)
    before = (jnp.arange(tokens)[:, None] < jnp.arange(tokens)[None, :]).astype(BF)
    rank = mm(member.astype(BF), before)
    slot = jnp.arange(cap, dtype=F32)[None, :, None]
    return ((rank[:, None, :] == slot) & member[:, None, :]).astype(BF)


def slot_gate(table, route_a, route_b, gate_a, gate_b, names):
    per_token = jnp.where(route_a == names, gate_a, 0.0) + jnp.where(route_b == names, gate_b, 0.0)
    return jnp.sum(table.astype(F32) * per_token[:, None, :], axis=-1)


def weigh(table, gates, rows):
    slots = table.reshape(-1, table.shape[-1])
    scaled = rows.reshape(slots.shape[0], -1).astype(F32) * gates.reshape(-1, 1)
    high = scaled.astype(BF)
    low = (scaled - high.astype(F32)).astype(BF)
    return mm_rows(slots, high) + mm_rows(slots, low)


def angles(positions):
    half = HD // 2
    frequency = jnp.exp(-math.log(THETA) * jnp.arange(half, dtype=F32) / half)
    turned = positions[..., None] * frequency
    return jnp.cos(turned)[..., None, :], jnp.sin(turned)[..., None, :]


def turn(vectors, cosine, sine):
    half = HD // 2
    a, b = vectors[..., :half], vectors[..., half:]
    return jnp.concatenate([a * cosine - b * sine, b * cosine + a * sine], axis=-1)


def fast_local(
    tokens, out_grad, row_place, seq_lengths, att_routes, att_gates, mlp_routes, mlp_gates,
    gain_attn, w_kv, w_query, w_out, gain_mlp, w_gate, w_up, w_down,
):
    rows, features = tokens.shape
    n = lax.axis_size("dp")
    g, t = lax.axis_index("dp"), lax.axis_index("tensor")
    width = features // 4
    per = rows // n
    hw = w_kv.shape[2]
    part = lambda a: lax.dynamic_slice_in_dim(a, t * width, width, a.ndim - 1)
    counting = jnp.arange(rows, dtype=jnp.int32)

    place = row_place.reshape(n, rows)
    group = place // rows
    earlier = (group[:, :, None] == group[:, None, :]) & (counting[None, :] < counting[:, None])
    arrival = jnp.sum(earlier.astype(jnp.int32), axis=-1)
    mine = lax.dynamic_index_in_dim(group * per + arrival, g, 0, keepdims=False)
    sorter = (mine[None, :] == counting[:, None]).astype(BF)
    x_sorted = mm(sorter, part(tokens)).astype(BF).reshape(n, per, width)
    x_all = gather(x_sorted, n, deal=True, cid=1).reshape(n, rows, features)

    here = (group == g) & True
    spot = (jnp.arange(n, dtype=jnp.int32)[:, None] * per + arrival)
    work_of = jnp.sum(
        jnp.where(here[None] & (spot[None] == counting[:, None, None]), place[None] % rows, 0), axis=(1, 2)
    )
    ends = jnp.cumsum(seq_lengths[0])
    segment = jnp.sum((counting[:, None] >= ends[None, :]).astype(jnp.int32), axis=1)
    begins = jnp.sum(
        jnp.where(segment[:, None] == jnp.arange(ends.shape[0])[None, :], (ends - seq_lengths[0])[None, :], 0), axis=1
    )
    carried = jnp.stack(
        [v.astype(F32) for v in (
            att_routes[:, 0], att_routes[:, 1], att_gates[:, 0], att_gates[:, 1],
            mlp_routes[:, 0], mlp_routes[:, 1], mlp_gates[:, 0], mlp_gates[:, 1],
            counting - begins, segment, counting)] + [jnp.zeros((rows,), F32)] * 5)
    moved = jnp.sum(
        jnp.where(work_of[None, :, None] == counting[None, None, :], carried[:, None, :], 0.0), axis=2
    )
    meta_all = a2a_copy(moved, n, cid=8)
    ar0, ar1, ag0, ag1, mr0, mr1, mg0, mg1, pos, seg, wpos = [meta_all[:, i] for i in range(11)]
    me = g.astype(F32)
    names = jnp.arange(n, dtype=F32)[:, None]
    own = lambda a: lax.dynamic_index_in_dim(a, g, 0, keepdims=False)

    att_in = slots_of(ar0, ar1, me, CAP)
    att_in_gate = slot_gate(att_in, ar0, ar1, ag0, ag1, me)
    mlp_in = slots_of(mr0, mr1, me, CAP)
    mlp_in_gate = slot_gate(mlp_in, mr0, mr1, mg0, mg1, me)
    o_ar0, o_ar1, o_ag0, o_ag1 = own(ar0)[None], own(ar1)[None], own(ag0)[None], own(ag1)[None]
    o_mr0, o_mr1, o_mg0, o_mg1 = own(mr0)[None], own(mr1)[None], own(mg0)[None], own(mg1)[None]
    att_out = slots_of(o_ar0, o_ar1, names, CAP)
    att_out_gate = slot_gate(att_out, o_ar0, o_ar1, o_ag0, o_ag1, names)
    mlp_out = slots_of(o_mr0, o_mr1, names, CAP)
    mlp_out_gate = slot_gate(mlp_out, o_mr0, o_mr1, o_mg0, o_mg1, names)

    meta_t = meta_all.transpose(0, 2, 1)
    cos_t, sin_t = angle_tables(rows)
    normed, picked, keys, values, query, attn, scale_attn, bias, turn_slots = attend(
        x_all, gain_attn[None], w_kv[:, 0], w_kv[:, 1], w_query[0], meta_all, meta_t, cos_t, sin_t)
    normed_flat, picked = normed.reshape(n * rows, features), picked.reshape(n * CAP, features)
    attn = attn.reshape(n * CAP, hw)
    query_back = lax.all_to_all(query, "dp", split_axis=0, concat_axis=0, tiled=True)
    x_own = part(own(x_all)).astype(F32)
    att_rows = att_out.reshape(n * CAP, rows)
    mlp_rows = mlp_out.reshape(n * CAP, rows)
    hidden, hid_rows, scale_mlp = hidden_rows(
        attn, w_out[0], x_own, att_rows.T, att_out_gate.reshape(-1, 1), mlp_rows, n, cid=9)
    dy_all = lax.all_gather(mm(sorter, out_grad).astype(BF), "dp", axis=0).reshape(n, n, per, features)
    dy_all = dy_all.transpose(1, 0, 2, 3).reshape(n, rows, features)
    d_mbr = jnp.einsum("gst,gtd->gsd", mlp_in, dy_all, preferred_element_type=F32) * mlp_in_gate[..., None]
    d_mbr = d_mbr.astype(BF).reshape(n * CAP, features)
    dy_own = part(own(dy_all)).astype(F32)
    gain_mlp_t, gain_attn_t = part(gain_mlp), part(gain_attn)
    d_obr, d_hidden, mixed_rows, gain_mlp_part, normed2, inner, d_gate, d_up = expert_layer(
        hid_rows, d_mbr, gain_mlp[None], w_gate[0], w_up[0], w_down[0], hidden, dy_own, gain_mlp_t[None], scale_mlp,
        mlp_rows.T, mlp_out_gate.reshape(-1, 1), mlp_rows, att_rows, n, cid=10)
    w_gate_grad = mm_rows(normed2, d_gate)[None]
    w_up_grad = mm_rows(normed2, d_up)[None]
    w_down_grad = mm_rows(inner, d_mbr)[None]

    d_obr, d_attn, dq_pre = attend_back(
        d_obr, att_in_gate[..., None], w_out[0], query, keys, values, bias, turn_slots)
    d_attn_back = a2a(d_attn, n, cid=4)
    d_obr, dq_pre = d_obr.reshape(n * CAP, features), dq_pre.reshape(n * CAP, hw)
    w_out_grad = mm_rows(attn, d_obr)[None]
    w_query_grad = mm_rows(picked, dq_pre)[None]
    d_norm_q = mm_t(dq_pre, w_query[0]).reshape(n, CAP, features)
    d_kv = keys_back(query_back, d_attn_back, own(keys), own(values), own(meta_all), own(meta_t), cos_t, sin_t)
    d_kv_all = a2a_copy(d_kv, n, cid=5)
    w_kv_grad = jnp.einsum(
        "ld,lck->dck", normed_flat, d_kv_all.reshape(n * rows, 2, hw), preferred_element_type=F32)
    d_norm_kv = mm_t(d_kv, w_kv.reshape(features, 2 * hw)).reshape(rows // CAP, CAP, features)

    d_norm = reduce(jnp.concatenate([d_norm_q, d_norm_kv], axis=0), n, cid=3)
    d_normed = mm_rows(att_rows, d_norm[:n].reshape(n * CAP, width))
    d_normed = d_normed + d_norm[n:].reshape(rows, width).astype(F32)
    scale_own = own(scale_attn)
    e1 = gain_attn_t * d_normed
    sum_1 = lax.psum(jnp.sum(x_own * e1, axis=1, keepdims=True), "tensor")
    in_grad = d_hidden + scale_own * e1 - x_own * (scale_own * scale_own * scale_own) * (sum_1 / features)
    gain_attn_part = jnp.sum(d_normed * x_own * scale_own, axis=0)

    gains = jnp.concatenate([gain_mlp_part[:1], gain_attn_part[None], jnp.zeros((6, width), F32)], axis=0)
    gains = jnp.sum(gather(gains, n, bcast=True, cid=7), axis=0)
    back = jnp.concatenate(
        [mixed_rows.reshape(n, per, width), in_grad.astype(BF).reshape(n, per, width)], axis=1
    )
    back = gather(back, n, cid=6)
    mixed = mm_rows(sorter, back[:, :per].reshape(rows, features)).astype(BF)
    tokens_grad = mm_rows(sorter, back[:, per:].reshape(rows, features)).astype(BF)
    return (
        mixed, tokens_grad, gains[1], w_kv_grad, w_query_grad, w_out_grad, gains[0],
        w_gate_grad, w_up_grad, w_down_grad,
    )


def solution(mesh):
    placed = (
        P("dp", None),
        P("dp", None),
        P(),
        P("dp", None),
        P("dp", None),
        P("dp", None),
        P("dp", None),
        P("dp", None),
        P(),
        P(None, None, "tensor"),
        P("dp", None, "tensor"),
        P("dp", "tensor", None),
        P(),
        P("dp", None, "tensor"),
        P("dp", None, "tensor"),
        P("dp", "tensor", None),
    )
    dealt = mesh.shape["dp"] == EXPERTS and mesh.shape["tensor"] == 4
    return jax.shard_map(
        fast_local if dealt else local,
        mesh=mesh,
        in_specs=placed,
        out_specs=(
            P("dp", None),
            P("dp", None),
            P(),
            P(None, None, "tensor"),
            P("dp", None, "tensor"),
            P("dp", "tensor", None),
            P(),
            P("dp", None, "tensor"),
            P("dp", None, "tensor"),
            P("dp", "tensor", None),
        ),
        check_vma=False,
    )
```

```python
import functools
import math

import jax
import jax.numpy as jnp
import numpy as np
from jax import lax
from jax.experimental import pallas as pl
from jax.experimental.pallas import tpu as pltpu
from jax.sharding import PartitionSpec as P

HD = 128
ATT_EXPERTS = 8
EXPERTS = 8
CAP = 64


EPSILON = 1e-05
THETA = 10000.0


def inverse_rms(values_in):
    return lax.rsqrt(jnp.mean(values_in * values_in, axis=-1, keepdims=True) + EPSILON)


def norm_backward(inputs, inv_root, gain, incoming):
    weighted = incoming * gain
    inner_mean = jnp.mean(inputs * weighted, axis=-1, keepdims=True)
    return inv_root * weighted - inputs * (inv_root * inv_root * inv_root) * inner_mean


def rotate(vectors, positions, direction):
    half_dim = vectors.shape[-1] // 2
    frequency = jnp.exp(-math.log(THETA) * jnp.arange(half_dim, dtype=jnp.float32) / half_dim)
    angles = positions.astype(jnp.float32)[:, None] * frequency[None, :]
    target = (vectors.shape[0],) + (1,) * (vectors.ndim - 2) + (half_dim,)
    cosine = jnp.cos(angles).reshape(target)
    sine = direction * jnp.sin(angles).reshape(target)
    former = vectors[..., :half_dim]
    latter = vectors[..., half_dim:]
    return jnp.concatenate(
        [former * cosine - latter * sine, latter * cosine + former * sine], axis=-1
    )


def expert_slots(routes, experts, capacity):
    flattened = routes.reshape(-1)
    pair_count = flattened.shape[0]
    one_hot = (flattened[:, None] == jnp.arange(experts, dtype=jnp.int32)[None, :]).astype(
        jnp.int32
    )
    earlier = jnp.cumsum(one_hot, axis=0) - one_hot
    position = jnp.sum(earlier * one_hot, axis=1)
    slot_table = jnp.full((experts, capacity), pair_count, jnp.int32)
    slot_table = slot_table.at[flattened, position].set(jnp.arange(pair_count, dtype=jnp.int32))
    return (flattened * capacity + position, slot_table)


def pick_rows(source_rows, slot_table):
    padded = jnp.concatenate(
        [source_rows, jnp.zeros((1, source_rows.shape[1]), source_rows.dtype)], axis=0
    )
    return padded[slot_table]


def send_slices(source_rows, slot_table, group_size):
    picked = pick_rows(source_rows, slot_table)
    experts, capacity, features = picked.shape
    divided = picked.reshape(experts, capacity, group_size, features // group_size)
    return divided.transpose(0, 2, 1, 3).reshape(
        experts * group_size, capacity, features // group_size
    )


def send_copies(source_rows, slot_table, group_size):
    picked = pick_rows(source_rows, slot_table)
    experts, capacity, features = picked.shape
    copies = jnp.broadcast_to(picked[:, None], (experts, group_size, capacity, features))
    return copies.reshape(experts * group_size, capacity, features)


def owners_summed(returned, pair_where, group_size):
    owners, capacity, features = returned.shape
    summed = returned.reshape(owners // group_size, group_size, capacity, features).sum(axis=1)
    return summed.reshape(-1, features)[pair_where]


def owners_joined(returned, pair_where, group_size):
    owners, capacity, features = returned.shape
    joined = returned.reshape(owners // group_size, group_size, capacity, features).transpose(
        0, 2, 1, 3
    )
    return joined.reshape(-1, group_size * features)[pair_where]


def query_return(pieces):
    return lax.all_to_all(pieces, "dp", split_axis=0, concat_axis=0, tiled=True)


def output_return(pieces):
    return lax.all_to_all(pieces, "dp", split_axis=0, concat_axis=0, tiled=True)


def expert_return(pieces):
    return lax.all_to_all(pieces, "dp", split_axis=0, concat_axis=0, tiled=True)


def tensor_total(pieces):
    return lax.psum(pieces, "tensor")


def deal_plan(row_place, rows_dev):
    device_count = lax.axis_size("dp")
    my_index = lax.axis_index("dp")
    per_peer = rows_dev // device_count
    every_place = row_place.reshape(device_count, rows_dev)
    my_places = lax.dynamic_index_in_dim(every_place, my_index, 0, keepdims=False)
    counting = jnp.arange(rows_dev, dtype=jnp.int32)
    ordering = jnp.argsort(my_places // rows_dev * rows_dev + counting)
    wanted = every_place // rows_dev == my_index
    chosen = jnp.argsort(
        jnp.where(wanted, counting[None, :], rows_dev + counting[None, :]), axis=1
    )[:, :per_peer]
    placed = jnp.take_along_axis(every_place, chosen, axis=1) % rows_dev
    return (ordering, placed.reshape(-1))


def masked_scores(query_b, keys_b, allowed):
    raw = jnp.einsum(
        "ikjd,mjd->kjim", query_b, keys_b, preferred_element_type=jnp.float32
    ) / math.sqrt(query_b.shape[-1])
    return jnp.where(allowed[None, None], raw, -1e30)


def local(
    tokens,
    out_grad,
    row_place,
    seq_lengths,
    att_routes,
    att_gates,
    mlp_routes,
    mlp_gates,
    gain_attn,
    w_kv,
    w_query,
    w_out,
    gain_mlp,
    w_gate,
    w_up,
    w_down,
):
    rows_dev, features = tokens.shape
    device_count = lax.axis_size("dp")
    group_size = device_count // EXPERTS
    per_peer = rows_dev // device_count
    counting = jnp.arange(rows_dev, dtype=jnp.int32)
    ordering, placed = deal_plan(row_place, rows_dev)
    unplace = jnp.zeros((rows_dev,), jnp.int32).at[placed].set(counting)
    unorder = jnp.zeros((rows_dev,), jnp.int32).at[ordering].set(counting)
    dealt_x, dealt_g = (
        lax.all_to_all(
            tokens[ordering].reshape(device_count, per_peer, features),
            "dp",
            split_axis=0,
            concat_axis=0,
            tiled=True,
        ),
        lax.all_to_all(
            out_grad[ordering].reshape(device_count, per_peer, features),
            "dp",
            split_axis=0,
            concat_axis=0,
            tiled=True,
        ),
    )
    residual = dealt_x.reshape(rows_dev, features)[unplace].astype(jnp.float32)
    top_grad = dealt_g.reshape(rows_dev, features)[unplace].astype(jnp.float32)
    lengths = seq_lengths[0]
    seq_ends = jnp.cumsum(lengths)
    segment = jnp.sum((counting[:, None] >= seq_ends[None, :]).astype(jnp.int32), axis=1)
    starts = seq_ends - lengths
    member = segment[:, None] == jnp.arange(lengths.shape[0], dtype=jnp.int32)[None, :]
    begins = jnp.sum(jnp.where(member, starts[None, :], 0), axis=1)
    positions = counting - begins
    allowed = (segment[:, None] == segment[None, :]) & (counting[None, :] <= counting[:, None])
    head_count = w_kv.shape[2] // HD
    scale_attn = inverse_rms(residual)
    normed = (residual * scale_attn * gain_attn).astype(jnp.bfloat16)
    kv_proj = jnp.einsum("ld,dck->lck", normed, w_kv, preferred_element_type=jnp.float32)
    keys = rotate(kv_proj[:, 0].reshape(rows_dev, head_count, HD), positions, 1.0).astype(
        jnp.bfloat16
    )
    values = kv_proj[:, 1].reshape(rows_dev, head_count, HD).astype(jnp.bfloat16)
    att_where, att_table = expert_slots(att_routes, ATT_EXPERTS, CAP)
    query_rows = lax.all_to_all(
        send_slices(normed, att_table // 2, group_size),
        "dp",
        split_axis=0,
        concat_axis=0,
        tiled=True,
    )
    query_part = jnp.einsum(
        "scd,dh->sch", query_rows, w_query[0], preferred_element_type=jnp.float32
    )
    query_pre = owners_summed(query_return(query_part), att_where, group_size)
    query_rot = rotate(query_pre.reshape(rows_dev, 2, head_count, HD), positions, 1.0).astype(
        jnp.bfloat16
    )
    scores = masked_scores(query_rot, keys, allowed)
    highest = jnp.max(scores, axis=-1, keepdims=True)
    expo = jnp.exp(scores - highest)
    row_total = jnp.sum(expo, axis=-1, keepdims=True)
    log_total = highest + jnp.log(row_total)
    probability = expo / row_total
    attn = jnp.einsum(
        "kjim,mjd->ikjd",
        probability.astype(jnp.bfloat16),
        values,
        preferred_element_type=jnp.float32,
    )
    attn_low = attn.astype(jnp.bfloat16).reshape(rows_dev * 2, head_count * HD)
    out_rows = lax.all_to_all(
        send_copies(attn_low, att_table, group_size), "dp", split_axis=0, concat_axis=0, tiled=True
    )
    out_part = jnp.einsum("sch,hd->scd", out_rows, w_out[0], preferred_element_type=jnp.float32)
    out_pairs = owners_joined(output_return(out_part), att_where, group_size).reshape(
        rows_dev, 2, features
    )
    hidden = residual + tensor_total(jnp.sum(out_pairs * att_gates[:, :, None], axis=1))
    gate_map, up_map, down_map = (w_gate[0], w_up[0], w_down[0])
    scale_mlp = inverse_rms(hidden)
    normed2 = (hidden * scale_mlp * gain_mlp).astype(jnp.bfloat16)
    mlp_where, mlp_table = expert_slots(mlp_routes, EXPERTS, CAP)
    expert_sent = send_copies(normed2, mlp_table // 2, group_size)
    expert_rows = lax.all_to_all(expert_sent, "dp", split_axis=0, concat_axis=0, tiled=True)
    flat_rows = expert_rows.reshape(-1, features)
    gate_act = jnp.dot(flat_rows, gate_map, preferred_element_type=jnp.float32)
    up_act = jnp.dot(flat_rows, up_map, preferred_element_type=jnp.float32)
    inner = (jax.nn.silu(gate_act) * up_act).astype(jnp.bfloat16)
    expert_part = jnp.dot(inner, down_map, preferred_element_type=jnp.float32).reshape(
        expert_rows.shape
    )
    expert_pairs = owners_summed(expert_return(expert_part), mlp_where, group_size).reshape(
        rows_dev, 2, features
    )
    mixed_rows = hidden + tensor_total(jnp.sum(expert_pairs * mlp_gates[:, :, None], axis=1))
    branch_grad = (
        (top_grad[:, None, :] * mlp_gates[:, :, None])
        .astype(jnp.bfloat16)
        .reshape(rows_dev * 2, features)
    )
    grad_sent = send_copies(branch_grad, mlp_table, group_size)
    grad_back, rows_back = (
        lax.all_to_all(grad_sent, "dp", split_axis=0, concat_axis=0, tiled=True),
        lax.all_to_all(expert_sent, "dp", split_axis=0, concat_axis=0, tiled=True),
    )
    grad_rows = grad_back.reshape(-1, features)
    rows_again = rows_back.reshape(-1, features)
    gate_again = jnp.dot(rows_again, gate_map, preferred_element_type=jnp.float32)
    up_again = jnp.dot(rows_again, up_map, preferred_element_type=jnp.float32)
    inner_again = (jax.nn.silu(gate_again) * up_again).astype(jnp.bfloat16)
    contract_rows = (((0,), (0,)), ((), ()))
    contract_cols = (((1,), (1,)), ((), ()))
    d_inner = lax.dot_general(
        grad_rows, down_map, contract_cols, preferred_element_type=jnp.float32
    )
    down_grad_all = lax.dot_general(
        inner_again, grad_rows, contract_rows, preferred_element_type=jnp.float32
    )
    sigmoid_g = jax.nn.sigmoid(gate_again)
    d_up = (d_inner * gate_again * sigmoid_g).astype(jnp.bfloat16)
    d_gate = (d_inner * up_again * sigmoid_g * (1.0 + gate_again * (1.0 - sigmoid_g))).astype(
        jnp.bfloat16
    )
    gate_grad_all = lax.dot_general(
        rows_again, d_gate, contract_rows, preferred_element_type=jnp.float32
    )
    up_grad_all = lax.dot_general(
        rows_again, d_up, contract_rows, preferred_element_type=jnp.float32
    )
    d_rows = lax.dot_general(d_gate, gate_map, contract_cols, preferred_element_type=jnp.float32)
    d_rows = d_rows + lax.dot_general(
        d_up, up_map, contract_cols, preferred_element_type=jnp.float32
    )
    d_pairs = owners_summed(expert_return(d_rows.reshape(expert_rows.shape)), mlp_where, group_size)
    w_gate_grad = gate_grad_all[None]
    w_up_grad = up_grad_all[None]
    w_down_grad = down_grad_all[None]
    d_normed2 = tensor_total(jnp.sum(d_pairs.reshape(rows_dev, 2, features), axis=1))
    d_hidden = top_grad + norm_backward(hidden, scale_mlp, gain_mlp, d_normed2)
    gain_mlp_grad = jnp.sum(d_normed2 * hidden * scale_mlp, axis=0)
    att_grad = (
        (d_hidden[:, None, :] * att_gates[:, :, None])
        .astype(jnp.bfloat16)
        .reshape(rows_dev * 2, features)
    )
    grad_slices = lax.all_to_all(
        send_slices(att_grad, att_table, group_size), "dp", split_axis=0, concat_axis=0, tiled=True
    )
    w_out_grad = jnp.einsum(
        "sch,scd->hd", out_rows, grad_slices, preferred_element_type=jnp.float32
    )
    d_attn_part = jnp.einsum(
        "scd,hd->sch", grad_slices, w_out[0], preferred_element_type=jnp.float32
    )
    d_attn = owners_summed(output_return(d_attn_part), att_where, group_size)
    d_attn = d_attn.astype(jnp.bfloat16).reshape(rows_dev, 2, head_count, HD)
    probability = jnp.exp(masked_scores(query_rot, keys, allowed) - log_total)
    d_prob = jnp.einsum("ikjd,mjd->kjim", d_attn, values, preferred_element_type=jnp.float32)
    d_values = jnp.einsum(
        "kjim,ikjd->mjd",
        probability.astype(jnp.bfloat16),
        d_attn,
        preferred_element_type=jnp.float32,
    )
    delta = jnp.sum(d_prob * probability, axis=-1, keepdims=True)
    d_scores = (probability * (d_prob - delta)).astype(jnp.bfloat16)
    root_hd = math.sqrt(HD)
    d_query = (
        jnp.einsum("kjim,mjd->ikjd", d_scores, keys, preferred_element_type=jnp.float32) / root_hd
    )
    d_keys = (
        jnp.einsum("kjim,ikjd->mjd", d_scores, query_rot, preferred_element_type=jnp.float32)
        / root_hd
    )
    dq_pre = (
        rotate(d_query, positions, -1.0).astype(jnp.bfloat16).reshape(rows_dev * 2, head_count * HD)
    )
    dk_pre = rotate(d_keys, positions, -1.0).reshape(rows_dev, head_count * HD)
    d_kv = jnp.stack([dk_pre, d_values.reshape(rows_dev, head_count * HD)], axis=1).astype(
        jnp.bfloat16
    )
    dq_rows = lax.all_to_all(
        send_copies(dq_pre, att_table, group_size), "dp", split_axis=0, concat_axis=0, tiled=True
    )
    w_query_grad = jnp.einsum(
        "scd,sch->dh", query_rows, dq_rows, preferred_element_type=jnp.float32
    )
    d_slice = jnp.einsum("sch,dh->scd", dq_rows, w_query[0], preferred_element_type=jnp.float32)
    d_norm_query = owners_joined(query_return(d_slice), att_where, group_size)
    d_norm_query = jnp.sum(d_norm_query.reshape(rows_dev, 2, features), axis=1)
    w_kv_grad = jnp.einsum("ld,lck->dck", normed, d_kv, preferred_element_type=jnp.float32)
    d_norm_kv = jnp.einsum("lck,dck->ld", d_kv, w_kv, preferred_element_type=jnp.float32)
    d_normed = tensor_total(d_norm_query + d_norm_kv)
    in_grad = d_hidden + norm_backward(residual, scale_attn, gain_attn, d_normed)
    gain_attn_grad = jnp.sum(d_normed * residual * scale_attn, axis=0)
    w_kv_grad, gain_attn_grad, gain_mlp_grad = (
        lax.psum(w_kv_grad.astype(jnp.bfloat16), "dp").astype(jnp.float32),
        lax.psum(gain_attn_grad.astype(jnp.bfloat16), "dp").astype(jnp.float32),
        lax.psum(gain_mlp_grad.astype(jnp.bfloat16), "dp").astype(jnp.float32),
    )
    send_mixed = mixed_rows.astype(jnp.bfloat16)[placed].reshape(device_count, per_peer, features)
    send_input = in_grad.astype(jnp.bfloat16)[placed].reshape(device_count, per_peer, features)
    back_mixed, back_input = (
        lax.all_to_all(send_mixed, "dp", split_axis=0, concat_axis=0, tiled=True),
        lax.all_to_all(send_input, "dp", split_axis=0, concat_axis=0, tiled=True),
    )
    mixed = back_mixed.reshape(rows_dev, features)[unorder]
    tokens_grad = back_input.reshape(rows_dev, features)[unorder]
    return (
        mixed,
        tokens_grad,
        gain_attn_grad,
        w_kv_grad,
        w_query_grad[None],
        w_out_grad[None],
        gain_mlp_grad,
        w_gate_grad,
        w_up_grad,
        w_down_grad,
    )


MESH = pl.DeviceIdType.MESH
VM = pltpu.VMEM
DMA = pltpu.SemaphoreType.DMA
BF = jnp.bfloat16
F32 = jnp.float32

def rcopy(src, dst, ss, rs, dp, tn):
    return pltpu.make_async_remote_copy(src_ref=src, dst_ref=dst, send_sem=ss, recv_sem=rs,
        device_id={"dp": dp, "tensor": tn}, device_id_type=MESH)

def greet(targets):
    b = pltpu.get_barrier_semaphore()
    for dp, tn in targets:
        pl.semaphore_signal(b, inc=1, device_id={"dp": dp, "tensor": tn}, device_id_type=MESH)
    pl.semaphore_wait(b, len(targets))

def ranks():
    g = lax.axis_index("dp"); t = lax.axis_index("tensor")
    return g, t, lax.rem(t + 2, 4), t + 1 - 2 * lax.rem(t, 2)

def params(cid):
    return pltpu.CompilerParams(collective_id=cid, has_side_effects=True, vmem_limit_bytes=56*2**20)

def gather_body(n, mode, src, out, ssem, rsem, xs, xr, cs, cr, c2s, c2r, lsem):
    g, t, tx, tc = ranks()
    w = src.shape[-1]
    greet([(lax.rem(g + o, n), t) for o in range(1, n)] + [(g, tx), (g, tc)])
    cols = pl.ds(pl.multiple_of(t * w, w), w)
    colsx = pl.ds(pl.multiple_of(tx * w, w), w)
    pick = (lambda d: src.at[d]) if mode == "rows" else (lambda d: src)
    at = (lambda b, cc: out.at[:, b, :, cc]) if mode == "deal" else (lambda b, cc: out.at[b, :, cc])
    sends = []
    for o in range(1, n):
        d = lax.rem(g + o, n)
        c = rcopy(pick(d), at(g, cols), ssem.at[o], rsem.at[o], d, t)
        c.start(); sends.append(c)
    loc = pltpu.make_async_copy(pick(g), at(g, cols), lsem)
    loc.start(); loc.wait()
    fx = []; fc = []; fc2 = []
    for o in range(n):
        b = lax.rem(g - o + n, n)
        if o > 0: sends[o - 1].wait_recv()
        c = rcopy(at(b, cols), at(b, cols), xs.at[o], xr.at[o], g, tx); c.start(); fx.append(c)
        c = rcopy(at(b, cols), at(b, cols), cs.at[o], cr.at[o], g, tc); c.start(); fc.append(c)
    for o in range(n):
        b = lax.rem(g - o + n, n)
        fx[o].wait_recv()
        c = rcopy(at(b, colsx), at(b, colsx), c2s.at[o], c2r.at[o], g, tc); c.start(); fc2.append(c)
    for c in fc + fc2: c.wait_recv()
    for c in sends + fx + fc + fc2: c.wait_send()

def gather(src, n, bcast=False, deal=False, cid=0, space=VM):
    r, w = src.shape[-2:]
    mode = "deal" if deal else "copy" if bcast else "rows"
    shape = (n, n, r, 4 * w) if deal else (n, r, 4 * w)
    return pl.pallas_call(functools.partial(gather_body, n, mode),
        out_shape=jax.ShapeDtypeStruct(shape, src.dtype),
        in_specs=[pl.BlockSpec(memory_space=VM)], out_specs=pl.BlockSpec(memory_space=space),
        scratch_shapes=[DMA((n,))]*8 + [DMA],
        name="gather_rows", compiler_params=params(cid))(src)

def reduce_body(n, nb, src, out, cbuf, cin, xbuf, xin, dbuf, cs, cr, xs, xr, ds_, dr):
    g, t, tx, tc = ranks()
    tcx = lax.rem(tc + 2, 4); w = out.shape[-1]
    greet([(lax.rem(g + o, n), t) for o in range(1, n)] + [(g, tx), (g, tc)])
    sl = lambda q: pl.ds(pl.multiple_of(q * w, w), w)
    order = list(range(1, n)) + [0] + list(range(n, nb))
    at = lambda o: lax.rem(g + o, n) if o < n else o
    C = {}; X = {}; Dd = {}
    for o in order:
        d = at(o)
        cbuf[o, 0] = src[d, :, sl(tc)].astype(BF)
        cbuf[o, 1] = src[d, :, sl(tcx)].astype(BF)
        C[o] = rcopy(cbuf.at[o], cin.at[o], cs.at[o], cr.at[o], g, tc); C[o].start()
    for o in order:
        C[o].wait_recv()
        xbuf[o] = (src[at(o), :, sl(tx)] + cin[o, 1].astype(F32)).astype(BF)
        X[o] = rcopy(xbuf.at[o], xin.at[o], xs.at[o], xr.at[o], g, tx); X[o].start()
    for o in order:
        d = at(o)
        X[o].wait_recv()
        total = (src[d, :, sl(t)] + cin[o, 0].astype(F32) + xin[o].astype(F32)).astype(BF)
        if 0 < o < n:
            dbuf[o] = total
            Dd[o] = rcopy(dbuf.at[o], out.at[g], ds_.at[o], dr.at[o], d, t); Dd[o].start()
        elif o == 0:
            out[g] = total
        else:
            out[o] = total
    for c in Dd.values(): c.wait_recv()
    for c in list(C.values()) + list(X.values()) + list(Dd.values()): c.wait_send()

def reduce(src, n, cid=1):
    nb, r, w = src.shape; w //= 4
    return pl.pallas_call(functools.partial(reduce_body, n, nb),
        out_shape=jax.ShapeDtypeStruct((nb, r, w), BF),
        in_specs=[pl.BlockSpec(memory_space=VM)], out_specs=pl.BlockSpec(memory_space=VM),
        scratch_shapes=[VM((nb,2,r,w),BF), VM((nb,2,r,w),BF), VM((nb,r,w),BF), VM((nb,r,w),BF), VM((n,r,w),BF)] + [DMA((nb,))]*4 + [DMA((n,))]*2,
        name="reduce_rows", compiler_params=params(cid))(src)

def a2a_body(n, src, out, ss, rs):
    g, t, tx, tc = ranks()
    greet([(lax.rem(g + o, n), t) for o in range(1, n)])
    cs = []
    for o in range(1, n):
        d = lax.rem(g + o, n)
        c = rcopy(src.at[d], out.at[g], ss.at[o], rs.at[o], d, t); c.start(); cs.append(c)
    out[g] = src[g]
    for c in cs: c.wait()

def a2a(src, n, cid=2):
    return pl.pallas_call(functools.partial(a2a_body, n),
        out_shape=jax.ShapeDtypeStruct(src.shape, src.dtype),
        in_specs=[pl.BlockSpec(memory_space=VM)], out_specs=pl.BlockSpec(memory_space=VM),
        scratch_shapes=[DMA((n,))]*2,
        name="a2a_rows", compiler_params=params(cid))(src)

def a2a_copy_body(n, src, out, ss, rs):
    g, t, tx, tc = ranks()
    greet([(lax.rem(g + o, n), t) for o in range(1, n)])
    cs = []
    for o in range(1, n):
        d = lax.rem(g + o, n)
        c = rcopy(src, out.at[g], ss.at[o], rs.at[o], d, t); c.start(); cs.append(c)
    out[g] = src[...]
    for c in cs: c.wait()

def a2a_copy(src, n, cid):
    return pl.pallas_call(functools.partial(a2a_copy_body, n),
        out_shape=jax.ShapeDtypeStruct((n,) + src.shape, src.dtype),
        in_specs=[pl.BlockSpec(memory_space=VM)], out_specs=pl.BlockSpec(memory_space=VM),
        scratch_shapes=[DMA((n,))]*2,
        name="copy_rows", compiler_params=params(cid))(src)

def dot(a, b, dims):
    return lax.dot_general(a, b, dims, preferred_element_type=F32)


def mm(a, b):
    return dot(a, b, (((a.ndim - 1,), (0,)), ((), ())))


def mm_t(a, b):
    return dot(a, b, (((1,), (1,)), ((), ())))


def mm_rows(a, b):
    return dot(a, b, (((0,), (0,)), ((), ())))


class Ring:
    def __init__(self, n):
        self.n = n
        self.g, self.t, self.tx, self.tc = ranks()
        self.tcx = lax.rem(self.tc + 2, 4)
        self.tail = []
        self.dest = [lax.rem(self.g + o, n) for o in range(n)]

    def to(self, o):
        return self.dest[o]

    def greet_all(self):
        greet([(self.to(o), self.t) for o in range(1, self.n)] + [(self.g, self.tx), (self.g, self.tc)])

    def greet_everyone(self):
        greet([(self.to(o), self.t) for o in range(1, self.n)] + [(self.g, q) for q in (self.tx, self.tc, self.tcx)])

    def send(self, src, dst, ss, rs, dp, tn):
        c = rcopy(src, dst, ss, rs, dp, tn)
        c.start()
        self.tail.append(c)
        return c

    def finish(self):
        for c in self.tail:
            c.wait_send()
        self.tail = []


def cols_of(q, j, width, cw):
    return pl.ds(pl.multiple_of(q * width + j * cw, cw), cw)


REDUCE_SEMS = lambda nc, n: [DMA((nc,))] * 4 + [DMA((nc, n))] * 2
GATHER_SEMS = lambda nc, n: [DMA((nc, n))] * 2 + [DMA((nc,))] * 6
REDUCE_BUFS = lambda nc, n, r, cw: [
    VM((nc, 2, n, r, cw), BF), VM((nc, 2, n, r, cw), BF), VM((nc, 2, n, r, cw), F32),
    VM((nc, n, r, cw), BF), VM((nc, n, r, cw), BF), VM((nc, n, r, cw), BF), VM((nc, n, r, cw), BF)]


class Reduce:
    def __init__(self, ring, partial, bufs, sems):
        self.ring, self.partial = ring, partial
        self.cbuf, self.cin, self.pbuf, self.xbuf, self.xin, self.dbuf, self.rbuf = bufs
        self.cs, self.cr, self.xs, self.xr, self.ds, self.dr = sems
        self.c, self.x, self.d = {}, {}, {}

    def core(self):
        k = self.ring
        nc, _, n, r, cw = self.cbuf.shape
        for i, q in enumerate((k.tc, k.tcx)):
            v = self.partial(q).astype(BF)
            for j in range(nc):
                self.cbuf[j, i] = v[:, j * cw:(j + 1) * cw].reshape(n, r, cw)
        for j in range(nc):
            self.c[j] = k.send(self.cbuf.at[j], self.cin.at[j], self.cs.at[j], self.cr.at[j], k.g, k.tc)
        for i, q in ((1, k.tx), (0, k.t)):
            v = self.partial(q)
            for j in range(nc):
                self.pbuf[j, i] = v[:, j * cw:(j + 1) * cw].reshape(n, r, cw)
            if i:
                for j in range(nc):
                    self.cross(j)

    def cross(self, j):
        k = self.ring
        self.c[j].wait_recv()
        self.xbuf[j] = (self.pbuf[j, 1] + self.cin[j, 1].astype(F32)).astype(BF)
        self.x[j] = k.send(self.xbuf.at[j], self.xin.at[j], self.xs.at[j], self.xr.at[j], k.g, k.tx)

    def home(self, j):
        k = self.ring
        self.x[j].wait_recv()
        self.dbuf[j] = (self.pbuf[j, 0] + self.cin[j, 0].astype(F32) + self.xin[j].astype(F32)).astype(BF)
        for o in range(1, k.n):
            d = k.to(o)
            self.d[j, o] = k.send(
                self.dbuf.at[j, d], self.rbuf.at[j, k.g], self.ds.at[j, o], self.dr.at[j, o], d, k.t)
        self.rbuf[j, k.g] = self.dbuf[j, k.g]

    def rows(self, j):
        for o in range(1, self.ring.n):
            self.d[j, o].wait_recv()
        return self.rbuf[j].reshape(-1, self.rbuf.shape[-1])


class Gather:
    def __init__(self, ring, width, full, sbuf, sems):
        self.ring, self.full, self.sbuf = ring, full, sbuf
        ss, rs, xs, xr, cs, cr, c2s, c2r = sems
        k, (nc, n, _, cw) = ring, sbuf.shape
        self.d, self.x, self.c, self.c2, self.own = {}, {}, {}, {}, {}
        for j in range(nc):
            cc, cx = cols_of(k.t, j, width, cw), cols_of(k.tx, j, width, cw)
            self.own[j] = cc
            for o in range(1, n):
                d = k.to(o)
                self.d[j, o] = rcopy(sbuf.at[j, d], full.at[k.g, :, cc], ss.at[j, o], rs.at[j, o], d, k.t)
            ref, ref2 = full.at[:, :, cc], full.at[:, :, cx]
            self.x[j] = rcopy(ref, ref, xs.at[j], xr.at[j], k.g, k.tx)
            self.c[j] = rcopy(ref, ref, cs.at[j], cr.at[j], k.g, k.tc)
            self.c2[j] = rcopy(ref2, ref2, c2s.at[j], c2r.at[j], k.g, k.tc)

    def out(self, j, rows):
        self.sbuf[j] = rows.reshape(self.sbuf.shape[1:])
        for o in range(1, self.ring.n):
            self.d[j, o].start()
        self.full[self.ring.g, :, self.own[j]] = self.sbuf[j, self.ring.g]

    def cross(self, j):
        for o in range(1, self.ring.n):
            self.d[j, o].wait_recv()
        self.x[j].start()
        self.c[j].start()

    def core(self, j):
        self.x[j].wait_recv()
        self.c2[j].start()

    def finish(self):
        for c in list(self.c.values()) + list(self.c2.values()):
            c.wait_recv()
        for c in [*self.d.values(), *self.x.values(), *self.c.values(), *self.c2.values()]:
            c.wait_send()


def paired(reduce_one, gather_one, middle, nc):
    reduce_one.core()
    steps = []
    for j in range(nc):
        steps += [(2 * j, 0, lambda j=j: reduce_one.home(j)), (2 * j + 3, 1, lambda j=j: gather_one.out(j, middle(j, reduce_one.rows(j))))]
        steps += [(2 * j + 7, 2, lambda j=j: gather_one.cross(j)), (2 * j + 9, 3, lambda j=j: gather_one.core(j))]
    for _, _, step in sorted(steps, key=lambda s: s[:2]):
        step()
    gather_one.finish()


NC = 4


def split_bf(v):
    high = v.astype(BF)
    return high, (v - high.astype(F32)).astype(BF)


def hidden_body(n, attn, wo, x_own, comb, gates, pick, hidden, full, scale, *scratch):
    bufs, sbuf, sq, sq_in, qs, qr, sems = scratch[:7], *scratch[7:12], scratch[12:]
    ring = Ring(n)
    ring.greet_everyone()
    rows, width = x_own.shape
    shared = []
    cw = width // NC

    def partial(q):
        return mm(attn[...], wo[:, cols_of(q, 0, width, width)])

    def middle(j, rows):
        high, low = split_bf(rows.astype(F32) * gates[...])
        got = x_own[:, j * cw:(j + 1) * cw] + mm(comb[...], high) + mm(comb[...], low)
        hidden[:, j * cw:(j + 1) * cw] = got
        high, low = split_bf(got * got)
        ones = jnp.ones((8, cw), BF)
        squares = mm_t(ones, high) + mm_t(ones, low)
        sq[...] = squares if j == 0 else sq[...] + squares
        if j == NC - 1:
            for i, q in enumerate([ring.tc, ring.tx, ring.tcx]):
                shared.append(ring.send(sq, sq_in.at[i], qs.at[i], qr.at[i], ring.g, q))
        return mm(pick[...], got.astype(BF)).astype(BF)

    red = Reduce(ring, partial, bufs, sems[:6])
    gat = Gather(ring, width, full, sbuf, sems[6:])
    paired(red, gat, middle, NC)
    for c in shared:
        c.wait_recv()
    total = (sq[...] + sq_in[0] + sq_in[1] + sq_in[2])[:1]
    eye = lax.broadcasted_iota(jnp.int32, (rows, rows), 0) == lax.broadcasted_iota(jnp.int32, (rows, rows), 1)
    column = jnp.sum(jnp.where(eye, total, 0.0), axis=1, keepdims=True)
    scale[...] = lax.rsqrt(column / (4 * width) + EPSILON)
    ring.finish()


def hidden_rows(attn, wo, x_own, comb, gates, pick, n, cid):
    slots = attn.shape[0]
    r, (rows, width) = slots // n, x_own.shape
    return pl.pallas_call(
        functools.partial(hidden_body, n),
        out_shape=(
            jax.ShapeDtypeStruct((rows, width), F32), jax.ShapeDtypeStruct((n, r, 4 * width), BF),
            jax.ShapeDtypeStruct((rows, 1), F32)),
        in_specs=[pl.BlockSpec(memory_space=VM)] * 6,
        out_specs=[pl.BlockSpec(memory_space=VM)] * 3,
        scratch_shapes=REDUCE_BUFS(NC, n, r, width // NC) + [VM((NC, n, r, width // NC), BF)]
        + [VM((8, rows), F32), VM((3, 8, rows), F32), DMA((3,)), DMA((3,))]
        + REDUCE_SEMS(NC, n) + GATHER_SEMS(NC, n),
        name="hidden_rows", compiler_params=params(cid),
    )(attn, wo, x_own, comb, gates, pick)


def expert_body(
    n, hid_rows, d_mbr, gain, wg_hbm, wu_hbm, wd_hbm, hidden, dy_own, gain_t, scale, mlp_t, mlp_gates, mlp_rows, att_rows,
    full, d_hidden, mixed, gain_part, n2, inner, d_gate, d_up, *scratch,
):
    ring = Ring(n)
    bufs, bufs2 = scratch[:7], scratch[7:14]
    sbuf, wg, wu, wd, r_own, r_in, r_to, r_back = scratch[14:22]
    wsem, rss, rsr, rds, rdr = scratch[22:27]
    sems = scratch[27:]
    ff = wg.shape[1]
    rows, width = hidden.shape
    slots = n2.shape[0]
    features = 4 * width
    cw = width // NC
    loads = [pltpu.make_async_copy(a, b, wsem.at[i]) for i, (a, b) in enumerate([(wg_hbm, wg), (wu_hbm, wu), (wd_hbm, wd)])]
    for c in loads:
        c.start()
    ring.greet_everyone()

    def norm_rows(i, _):
        at = pl.ds(pl.multiple_of(i * 64, 64), 64)
        v = hid_rows[i].astype(F32)
        s = lax.rsqrt(jnp.mean(v * v, axis=-1, keepdims=True) + EPSILON)
        n2[at, :] = (v * s * gain[...]).astype(BF)
        return _

    lax.fori_loop(0, n, norm_rows, 0)
    for c in loads:
        c.wait()
    r_own[...] = jnp.zeros_like(r_own)

    def units(at, size):
        a = n2[...]
        gate = mm(a, wg[:, at])
        up = mm(a, wu[:, at])
        d_in = mm_t(d_mbr[...], wd[at, :])
        sig = jax.nn.sigmoid(gate)
        silu = gate * sig
        inner[:, at] = (silu * up).astype(BF)
        du = (d_in * silu).astype(BF)
        dg = (d_in * up * sig * (1.0 + gate * (1.0 - sig))).astype(BF)
        d_up[:, at] = du
        d_gate[:, at] = dg
        both = (gate * dg.astype(F32) + up * du.astype(F32)).astype(BF)
        r_own[...] += mm_t(jnp.ones((8, size), BF), both)

    tile = 256

    def unit_tile(i, _):
        units(pl.ds(pl.multiple_of(i * tile, tile), tile), tile)
        return _

    lax.fori_loop(0, ff // tile, unit_tile, 0)
    if ff % tile:
        units(pl.ds(ff // tile * tile, ff % tile), ff % tile)

    others = [ring.tc, ring.tx, ring.tcx]
    r_sends = [ring.send(r_own, r_in.at[i], rss.at[i], rsr.at[i], ring.g, q) for i, q in enumerate(others)]

    def partial(q):
        at = cols_of(q, 0, width, width)
        return mm_t(d_gate[...], wg[at, :]) + mm_t(d_up[...], wu[at, :])

    def partial_mixed(q):
        return mm(inner[...], wd[:, cols_of(q, 0, width, width)])

    pairs = {}

    def share_r():
        for c in r_sends:
            c.wait_recv()
        r_to[...] = r_own[...] + r_in[0] + r_in[1] + r_in[2]
        for o in range(1, n):
            d = ring.to(o)
            half = pl.ds(pl.multiple_of(d // 2 * 128, 128), 128)
            pairs[o] = ring.send(r_to.at[:, half], r_back.at[ring.g], rds.at[o], rdr.at[o], d, ring.t)
        r_back[ring.g] = r_to[:, pl.ds(pl.multiple_of(ring.g // 2 * 128, 128), 128)]

    total_r = {}

    def take_r():
        for o in range(1, n):
            pairs[o].wait_recv()
        odd = lax.rem(ring.g, 2) == 1
        got = jnp.concatenate(
            [jnp.where(odd, r_back[e][:, 64:], r_back[e][:, :64]) for e in range(n)], axis=1)
        high = got.astype(BF)
        low = (got - high.astype(F32)).astype(BF)
        total_r[0] = (mm_t(mlp_t[...], high) + mm_t(mlp_t[...], low))[:, :1] / features

    def middle(j, got):
        if j == 0:
            take_r()
        cc = slice(j * cw, (j + 1) * cw)
        s2, h = scale[...], hidden[:, cc]
        d_n = mm(mlp_t[...], got)
        d_h = dy_own[:, cc] + s2 * (gain_t[:, cc] * d_n) - h * (s2 * s2) * total_r[0]
        d_hidden[:, cc] = d_h
        gain_part[:, cc] = jnp.broadcast_to(jnp.sum(d_n * h * s2, axis=0, keepdims=True), (8, cw))
        return mm(att_rows[...], d_h.astype(BF)).astype(BF)

    red = Reduce(ring, partial, bufs, sems[:6])
    gat = Gather(ring, width, full, sbuf, sems[6:14])
    red2 = Reduce(ring, partial_mixed, bufs2, sems[14:20])

    def settle(j):
        got = red2.rows(j)
        scaled = got.astype(F32) * mlp_gates[...]
        high = scaled.astype(BF)
        low = (scaled - high.astype(F32)).astype(BF)
        cc = slice(j * cw, (j + 1) * cw)
        mixed[:, cc] = (hidden[:, cc] + mm(mlp_t[...], high) + mm(mlp_t[...], low)).astype(BF)

    red.core()
    share_r()
    steps = []
    for j in range(NC):
        steps += [(2 * j, 1, lambda j=j: red.home(j)), (2 * j + 3, 2, lambda j=j: gat.out(j, middle(j, red.rows(j))))]
        steps += [(2 * j + 7, 3, lambda j=j: gat.cross(j)), (2 * j + 9, 4, lambda j=j: gat.core(j))]
        steps += [(2 * j + 12, 7, lambda j=j: red2.home(j)), (2 * j + 16, 8, lambda j=j: settle(j))]
    steps += [(9.5, 5, red2.core)]
    steps.sort(key=lambda s: s[:2])
    for _, _, run in steps:
        run()
    gat.finish()
    ring.finish()


def expert_layer(hid_rows, d_mbr, gain, wg, wu, wd, hidden, dy_own, gain_t, scale, mlp_t, mlp_gates, mlp_rows, att_rows, n, cid):
    r, features = hid_rows.shape[1:]
    ff = wg.shape[1]
    rows, width = hidden.shape
    slots, cw = n * r, width // NC
    any_, vm = pl.BlockSpec(memory_space=pl.ANY), pl.BlockSpec(memory_space=VM)
    sds = jax.ShapeDtypeStruct
    return pl.pallas_call(
        functools.partial(expert_body, n),
        out_shape=(
            sds((n, r, features), BF), sds((rows, width), F32), sds((rows, width), BF), sds((8, width), F32),
            sds((slots, features), BF), sds((slots, ff), BF), sds((slots, ff), BF), sds((slots, ff), BF)),
        in_specs=[vm, vm, vm, any_, any_, any_] + [vm] * 8,
        out_specs=[vm] * 8,
        scratch_shapes=REDUCE_BUFS(NC, n, r, cw) + REDUCE_BUFS(NC, n, r, cw) + [
            VM((NC, n, r, cw), BF), VM((features, ff), BF), VM((features, ff), BF), VM((ff, features), BF),
            VM((8, slots), F32), VM((3, 8, slots), F32), VM((8, slots), F32), VM((n, 8, 128), F32),
            DMA((3,)), DMA((3,)), DMA((3,)), DMA((n,)), DMA((n,))]
        + REDUCE_SEMS(NC, n) + GATHER_SEMS(NC, n) + REDUCE_SEMS(NC, n),
        name="expert_layer", compiler_params=params(cid),
    )(hid_rows, d_mbr, gain, wg, wu, wd, hidden, dy_own, gain_t, scale, mlp_t, mlp_gates, mlp_rows, att_rows)


META = {name: i for i, name in enumerate(
    ("ar0", "ar1", "ag0", "ag1", "mr0", "mr1", "mg0", "mg1", "pos", "seg", "wpos"))}


def iota(shape, dim):
    return lax.broadcasted_iota(jnp.int32, shape, dim)


def slot_table(meta, first, name, cap):
    member = (meta[first:first + 1] == name) | (meta[first + 1:first + 2] == name)
    tokens = meta.shape[1]
    before = jnp.where(iota((tokens, tokens), 0) < iota((tokens, tokens), 1), 1.0, 0.0).astype(BF)
    rank = mm(jnp.broadcast_to(jnp.where(member, 1.0, 0.0), (8, tokens)).astype(BF), before)[:1]
    return jnp.where((rank == iota((cap, tokens), 0).astype(F32)) & member, 1.0, 0.0).astype(BF)


def allowed_pairs(meta, meta_t):
    seg, wpos = META["seg"], META["wpos"]
    same = meta_t[:, seg:seg + 1] == meta[seg:seg + 1]
    return jnp.where(same & (meta[wpos:wpos + 1] <= meta_t[:, wpos:wpos + 1]), 1.0, 0.0).astype(BF)


def position_rows(meta_t):
    pos = META["pos"]
    tokens = meta_t.shape[0]
    return jnp.where(meta_t[:, pos:pos + 1] == iota((tokens, tokens), 1).astype(F32), 1.0, 0.0).astype(BF)


def looked_up(rows, table):
    got = mm(rows, table)
    w = got.shape[1] // 3
    return got[:, :w] + got[:, w:2 * w] + got[:, 2 * w:]


def turned(v, cosine, sine):
    out = []
    for h in range(v.shape[1] // HD):
        u = v[:, h * HD:(h + 1) * HD]
        out.append(u * cosine + pltpu.roll(u, HD // 2, 1) * sine)
    return jnp.concatenate(out, axis=1)


def angle_tables(positions):
    half = HD // 2
    frequency = np.exp(-math.log(THETA) * np.arange(half) / half)
    turned_by = np.arange(positions)[:, None] * frequency[None, :]
    cosine = np.concatenate([np.cos(turned_by)] * 2, axis=1).astype(np.float32)
    sine = np.concatenate([-np.sin(turned_by), np.sin(turned_by)], axis=1).astype(np.float32)

    def parts(v):
        out, left = [], v
        for _ in range(3):
            p = left.astype(jnp.bfloat16)
            out.append(p)
            left = left - p.astype(np.float32)
        return np.concatenate(out, axis=1)

    return jnp.asarray(parts(cosine)), jnp.asarray(parts(sine))


def softmax_rows(scores):
    top = jnp.max(scores, axis=-1, keepdims=True)
    expo = jnp.exp(scores - top)
    return expo / jnp.sum(expo, axis=-1, keepdims=True)


def attend_body(
    n, x, gain, w_k, w_v, w_q, meta, cos_t, sin_t, dy_part, dy_gate,
    normed, picked, keys, values, query, attn, scale, bias, turn_slots, d_mbr, k_scr, v_scr, q_scr, n_scr, dy_rows,
    xs, xr, cs, cr,
):
    step = pl.program_id(0)
    ring = Ring(n)
    width = dy_part.shape[2]

    near, far = [dy_rows.at[:, :, cols_of(q, 0, width, width)] for q in (ring.t, ring.tx)]
    over_x = rcopy(near, near, xs, xr, ring.g, ring.tx)
    to_core = [rcopy(ref, ref, cs.at[i], cr.at[i], ring.g, ring.tc) for i, ref in enumerate((near, far))]

    @pl.when(step == 0)
    def _():
        greet([(ring.g, ring.tx), (ring.g, ring.tc)])
        near[...] = dy_part[...]
        over_x.start()
        to_core[0].start()

    @pl.when(step == 2)
    def _():
        over_x.wait_recv()
        to_core[1].start()

    me = ring.g.astype(F32)
    pair, rows, features = x.shape
    cap = picked.shape[1]
    heads = w_q.shape[1] // HD
    flat = x[...].reshape(pair * rows, features).astype(F32)
    s = lax.rsqrt(jnp.mean(flat * flat, axis=-1, keepdims=True) + EPSILON)
    scale[...] = s.reshape(pair, rows, 1)
    low = (flat * s * gain[...]).astype(BF)
    n_scr[...] = low
    normed[...] = low.reshape(pair, rows, features)
    k_all, v_all = mm(n_scr[...], w_k[...]), mm(n_scr[...], w_v[...])
    slots = []
    for p in range(pair):
        m = meta[p]
        m_t = m.T
        table = slot_table(m, META["ar0"], me, cap)
        at_pos = position_rows(m_t)
        rr = slice(p * rows, (p + 1) * rows)
        kk = turned(k_all[rr], looked_up(at_pos, cos_t[...]), looked_up(at_pos, sin_t[...])).astype(BF)
        k_scr[p] = kk
        v_scr[p] = v_all[rr].astype(BF)
        picked[p] = mm(table, n_scr[rr, :]).astype(BF)
        slot_pos = mm(table, at_pos).astype(BF)
        turn_slots[p, :, :HD] = looked_up(slot_pos, cos_t[...])
        turn_slots[p, :, HD:] = looked_up(slot_pos, sin_t[...])
        bias[p] = (mm(table, allowed_pairs(m, m_t)) - 1.0) * 1e30
        slots.append(table)
    keys[...] = k_scr[...]
    values[...] = v_scr[...]
    q_all = mm(picked[...].reshape(pair * cap, features), w_q[...])
    for p in range(pair):
        qq = turned(q_all[p * cap:(p + 1) * cap], turn_slots[p, :, :HD], turn_slots[p, :, HD:]).astype(BF)
        q_scr[p] = qq
        query[p] = qq
    for p in range(pair):
        for h in range(heads):
            hh = slice(h * HD, (h + 1) * HD)
            scores = mm_t(q_scr[p, :, hh], k_scr[p, :, hh]) / math.sqrt(HD) + bias[p]
            probs = softmax_rows(scores).astype(BF)
            attn[p, :, hh] = mm(probs, v_scr[p, :, hh]).astype(BF)

    @pl.when(step == 3)
    def _():
        for c in to_core:
            c.wait()
        over_x.wait_send()
        for e in range(n):
            d_mbr[e] = (dy_rows[e].astype(F32) * dy_gate[e]).astype(BF)


def attend(x_all, gain, w_k, w_v, w_q, meta, cos_t, sin_t, dy_part, dy_gate, cid):
    n, rows, features = x_all.shape
    hw, cap, pair = w_q.shape[1], CAP, 2
    sds = jax.ShapeDtypeStruct
    block = lambda *s: pl.BlockSpec((pair,) + s, lambda i: (i,) + (0,) * len(s))
    whole = lambda a: pl.BlockSpec(a.shape, lambda i: (0,) * a.ndim)
    return pl.pallas_call(
        functools.partial(attend_body, n), grid=(n // pair,),
        out_shape=(
            sds((n, rows, features), BF), sds((n, cap, features), BF), sds((n, rows, hw), BF), sds((n, rows, hw), BF),
            sds((n, cap, hw), BF), sds((n, cap, hw), BF), sds((n, rows, 1), F32), sds((n, cap, rows), F32),
            sds((n, cap, 2 * HD), F32), sds((n, cap, features), BF)),
        in_specs=[block(rows, features), whole(gain), whole(w_k), whole(w_v), whole(w_q), block(16, rows),
                  whole(cos_t), whole(sin_t), whole(dy_part), whole(dy_gate)],
        out_specs=(
            block(rows, features), block(cap, features), block(rows, hw), block(rows, hw), block(cap, hw), block(cap, hw),
            block(rows, 1), block(cap, rows), block(cap, 2 * HD), pl.BlockSpec((n, cap, features), lambda i: (0, 0, 0))),
        scratch_shapes=[VM((pair, rows, hw), BF), VM((pair, rows, hw), BF), VM((pair, cap, hw), BF), VM((pair * rows, features), BF),
                        VM((n, cap, features), BF), DMA, DMA, DMA((2,)), DMA((2,))],
        name="attend", compiler_params=params(cid),
    )(x_all, gain, w_k, w_v, w_q, meta, cos_t, sin_t, dy_part, dy_gate)


def attend_back_body(rows_in, gates, w_o, query, keys, values, bias, turn_slots, d_obr, d_attn, dq_pre, o_scr):
    pair, cap, features = rows_in.shape
    heads = w_o.shape[0] // HD
    for p in range(pair):
        o_scr[p * cap:(p + 1) * cap] = (rows_in[p].astype(F32) * gates[p]).astype(BF)
    d_obr[...] = o_scr[...].reshape(pair, cap, features)
    back = mm_t(o_scr[...], w_o[...]).astype(BF)
    root = math.sqrt(HD)
    for p in range(pair):
        d_o = back[p * cap:(p + 1) * cap]
        d_attn[p] = d_o
        dq = []
        for h in range(heads):
            hh = slice(h * HD, (h + 1) * HD)
            probs = softmax_rows(mm_t(query[p, :, hh], keys[p, :, hh]) / root + bias[p])
            d_probs = mm_t(d_o[:, hh], values[p, :, hh])
            delta = jnp.sum(d_probs * probs, axis=-1, keepdims=True)
            d_scores = (probs * (d_probs - delta)).astype(BF)
            dq.append(mm(d_scores, keys[p, :, hh]) / root)
        dq = jnp.concatenate(dq, axis=1)
        dq_pre[p] = turned(dq, turn_slots[p, :, :HD], -turn_slots[p, :, HD:]).astype(BF)


def attend_back(rows_in, gates, w_o, query, keys, values, bias, turn_slots):
    n, cap, features = rows_in.shape
    hw, rows, pair = w_o.shape[0], keys.shape[1], 2
    sds = jax.ShapeDtypeStruct
    block = lambda *s: pl.BlockSpec((pair,) + s, lambda i: (i,) + (0,) * len(s))
    return pl.pallas_call(
        attend_back_body, grid=(n // pair,),
        out_shape=(sds((n, cap, features), BF), sds((n, cap, hw), BF), sds((n, cap, hw), BF)),
        in_specs=[block(cap, features), block(cap, 1), pl.BlockSpec(w_o.shape, lambda i: (0, 0)), block(cap, hw), block(rows, hw),
                  block(rows, hw), block(cap, rows), block(cap, 2 * HD)],
        out_specs=(block(cap, features), block(cap, hw), block(cap, hw)),
        scratch_shapes=[VM((pair * cap, features), BF)],
        name="attend_back", compiler_params=pltpu.CompilerParams(vmem_limit_bytes=56 * 2**20),
    )(rows_in, gates, w_o, query, keys, values, bias, turn_slots)


def keys_back_body(query, d_attn, keys, values, meta, cos_t, sin_t, d_kv, *, cap):
    n = query.shape[0]
    hw = keys.shape[1]
    m = meta[...]
    m_t = m.T
    tables = jnp.concatenate([slot_table(m, META["ar0"], float(e), cap) for e in range(n)], axis=0)
    bias = (mm(tables, allowed_pairs(m, m_t)) - 1.0) * 1e30
    at_pos = position_rows(m_t)
    cosine, sine = looked_up(at_pos, cos_t[...]), looked_up(at_pos, sin_t[...])
    root = math.sqrt(HD)
    for h in range(hw // HD):
        hh = slice(h * HD, (h + 1) * HD)
        q = query[:, :, hh].reshape(n * cap, HD)
        d_o = d_attn[:, :, hh].reshape(n * cap, HD)
        k, v = keys[:, hh], values[:, hh]
        probs = softmax_rows(mm_t(q, k) / root + bias)
        d_probs = mm_t(d_o, v)
        delta = jnp.sum(d_probs * probs, axis=-1, keepdims=True)
        d_scores = (probs * (d_probs - delta)).astype(BF)
        d_kv[:, hw + h * HD:hw + (h + 1) * HD] = mm_rows(probs.astype(BF), d_o).astype(BF)
        d_k = mm_rows(d_scores, q) / root
        d_kv[:, hh] = turned(d_k, cosine, -sine).astype(BF)


def map_grad_body(normed, d_kv, out, d_cols):
    hw = d_kv.shape[1] // 2

    @pl.when(pl.program_id(0) == 0)
    def _():
        for i in range(hw // 128):
            for c in range(2):
                d_cols[:, (2 * i + c) * 128:(2 * i + c + 1) * 128] = d_kv[:, c * hw + i * 128:c * hw + (i + 1) * 128]

    out[...] = mm_rows(normed[...], d_cols[...]).reshape(out.shape)


def map_grad(normed, d_kv):
    total, features = normed.shape
    both = d_kv.shape[1]
    size, tiles = 256, both // 128
    out = pl.pallas_call(
        map_grad_body, grid=(features // size,),
        out_shape=jax.ShapeDtypeStruct((features, tiles, 128), F32),
        in_specs=[pl.BlockSpec((total, size), lambda i: (0, i)), pl.BlockSpec((total, both), lambda i: (0, 0))],
        out_specs=pl.BlockSpec((size, tiles, 128), lambda i: (i, 0, 0)), scratch_shapes=[VM((total, both), BF)],
        name="map_grad", compiler_params=pltpu.CompilerParams(vmem_limit_bytes=56 * 2**20),
    )(normed, d_kv)
    return out.reshape(features, tiles // 2, 2, 128).transpose(0, 2, 1, 3).reshape(features, 2, both // 2)


def tail_body(
    n, dq_pre, w_q, d_attn, q_back, keys, values, meta, cos_t, sin_t, w_k, w_v,
    x_own, scale, gain_t, d_hidden, mixed, gain_mlp_part, comb, d_kv_all, back, gains, *scratch,
):
    ring = Ring(n)
    bufs = scratch[:7]
    at_in, d_kv, kc_out, kc_in, kv_keep, kx_out, kx_in, sbuf, sq, sq_in, g_out, g_in, g_sum, d_norm = scratch[7:21]
    (as_, ar, zs, zr, ws, wr, ys, yr, ks, kr, lxs, lxr, qs, qr, gs, gr, ts, tr) = scratch[21:39]
    sems, fsems = scratch[39:45], scratch[45:]
    rows, width = x_own.shape
    hw = keys.shape[2]
    features = 4 * width
    keys, values, meta, scale = keys.at[ring.g], values.at[ring.g], meta.at[ring.g], scale.at[ring.g]
    z, y = ring.g // 2, lax.rem(ring.g, 2)
    depth = n // 2
    ring.greet_everyone()

    arrive = []
    for o in range(1, n):
        d = ring.to(o)
        arrive.append(ring.send(d_attn.at[d], at_in.at[ring.g], as_.at[o], ar.at[o], d, ring.t))
    at_in[ring.g] = d_attn[ring.g]
    red = Reduce(
        ring, lambda q: mm_t(dq_pre[...], w_q[cols_of(q, 0, width, width), :]), bufs, sems)
    red.core()
    for c in arrive:
        c.wait_recv()
    red.home(0)
    keys_back_body(q_back, at_in, keys, values, meta, cos_t, sin_t, d_kv, cap=q_back.shape[1])
    red.home(1)

    halves = [(c, slice(c * hw, (c + 1) * hw)) for c in range(2)]
    mine = d_kv_all.at[ring.g]
    mine[...] = d_kv[...]
    pairs = lambda zz, yy: zz * 2 + yy
    across = []

    def unit(zz, c):
        return d_kv_all.at[pairs(zz, y), :, pl.ds(c * hw, hw)]

    def step(up, hop, c, first):
        zz = z - hop if up else z + hop
        here = zz >= 0 if up else zz < depth
        ss, rs = (zs, zr) if up else (ws, wr)
        on, back_to = (z + 1, z - 1) if up else (z - 1, z + 1)

        @pl.when(here)
        def _():
            ref = unit(zz, c)
            if not first:
                rcopy(ref, ref, ss.at[hop - 1, c], rs.at[hop - 1, c], pairs(back_to, y), ring.t).wait_recv()

            @pl.when((on < depth) if up else (on >= 0))
            def _():
                rcopy(ref, ref, ss.at[hop, c], rs.at[hop, c], pairs(on, y), ring.t).start()

            if up or not first:
                rcopy(ref, ref, ys.at[zz, c], yr.at[zz, c], pairs(z, 1 - y), ring.t).start()

    def drain(up, hop, c):
        zz = z - hop if up else z + hop
        here = zz >= 0 if up else zz < depth
        ss, rs = (zs, zr) if up else (ws, wr)
        on = z + 1 if up else z - 1

        @pl.when(here & ((on < depth) if up else (on >= 0)))
        def _():
            ref = unit(zz, c)
            rcopy(ref, ref, ss.at[hop, c], rs.at[hop, c], pairs(on, y), ring.t).wait_send()

    def spread(hop):
        for c, _ in halves:
            step(True, hop, c, hop == 0)
            step(False, hop, c, hop == 0)

    spread(0)

    def kv_part(q):
        at = cols_of(q, 0, width, width)
        return mm_t(d_kv[:, :hw], w_k[at, :]) + mm_t(d_kv[:, hw:], w_v[at, :])

    kc_out[0] = kv_part(ring.tc).astype(BF)
    kc_out[1] = kv_part(ring.tcx).astype(BF)
    kc = ring.send(kc_out, kc_in, ks, kr, ring.g, ring.tc)
    red.home(2)
    kv_keep[1] = kv_part(ring.tx)
    kc.wait_recv()
    kx_out[...] = (kv_keep[1] + kc_in[1].astype(F32)).astype(BF)
    kx = ring.send(kx_out, kx_in, lxs, lxr, ring.g, ring.tx)
    kv_keep[0] = kv_part(ring.t)
    red.home(3)
    spread(1)
    kx.wait_recv()
    local = kv_keep[0] + kc_in[0].astype(F32) + kx_in[...].astype(F32)
    cw = width // NC
    squares = jnp.zeros((8, rows), F32)
    for j in range(NC):
        cc = slice(j * cw, (j + 1) * cw)
        got = mm(comb[...], red.rows(j)) + local[:, cc]
        d_norm[:, cc] = got
        high, low = split_bf(x_own[:, cc] * gain_t[:, cc] * got)
        ones = jnp.ones((8, cw), BF)
        squares = squares + mm_t(ones, high) + mm_t(ones, low)
        g_out[:, cc] = jnp.concatenate([
            gain_mlp_part[:1, cc], jnp.sum(got * x_own[:, cc] * scale[...], axis=0, keepdims=True), jnp.zeros((6, cw), F32)], axis=0)
    sq[...] = squares
    shared = [ring.send(sq, sq_in.at[i], qs.at[i], qr.at[i], ring.g, q) for i, q in enumerate([ring.tc, ring.tx, ring.tcx])]
    sums = []
    for o in range(1, n):
        sums.append(ring.send(g_out, g_in.at[ring.g], gs.at[o], gr.at[o], ring.to(o), ring.t))
    g_in[ring.g] = g_out[...]
    for c in shared:
        c.wait_recv()
    total = (sq[...] + sq_in[0] + sq_in[1] + sq_in[2])[:1]
    eye = iota((rows, rows), 0) == iota((rows, rows), 1)
    mean = jnp.sum(jnp.where(eye, total, 0.0), axis=1, keepdims=True) / features
    s = scale[...]
    in_grad = d_hidden[...] + s * (gain_t[...] * d_norm[...]) - x_own[...] * (s * s * s * mean)
    per = rows // n
    fin = Gather(ring, width, back, sbuf, fsems)
    fin.out(0, jnp.concatenate(
        [mixed[...].reshape(n, per, width), in_grad.astype(BF).reshape(n, per, width)], axis=1))
    for c in sums:
        c.wait_recv()
    g_sum[...] = functools.reduce(lambda a, b: a + b, [g_in[e] for e in range(n)])
    at_t = cols_of(ring.t, 0, width, width)
    gains[:, at_t] = g_sum[...]
    told = [ring.send(g_sum, gains.at[:, at_t], ts.at[i], tr.at[i], ring.g, q) for i, q in enumerate([ring.tc, ring.tx, ring.tcx])]
    spread(2)
    fin.cross(0)
    spread(3)
    fin.core(0)
    fin.finish()
    for c in told:
        c.wait_recv()
    for c, _ in halves:
        for zz in range(depth):
            ref = d_kv_all.at[pairs(zz, 1 - y), :, pl.ds(c * hw, hw)]
            rcopy(ref, ref, ys.at[zz, c], yr.at[zz, c], pairs(z, 1 - y), ring.t).wait()
        for hop in range(depth - 1):
            drain(True, hop, c)
            drain(False, hop, c)
    ring.finish()


def layer_tail(args, n, cid):
    dq_pre, w_q, d_attn, q_back, keys = args[:5]
    x_own = args[11]
    rows, width = x_own.shape
    cap, hw = d_attn.shape[1:]
    cw, features, depth = width // NC, 4 * width, n // 2
    sds = jax.ShapeDtypeStruct
    per = 2 * rows // n
    return pl.pallas_call(
        functools.partial(tail_body, n),
        out_shape=(sds((n, rows, 2 * hw), BF), sds((n, per, features), BF), sds((8, features), F32)),
        in_specs=[pl.BlockSpec(memory_space=VM)] * len(args), out_specs=[pl.BlockSpec(memory_space=VM)] * 3,
        scratch_shapes=REDUCE_BUFS(NC, n, cap, cw) + [
            VM((n, cap, hw), BF), VM((rows, 2 * hw), BF), VM((2, rows, width), BF), VM((2, rows, width), BF),
            VM((2, rows, width), F32), VM((rows, width), BF), VM((rows, width), BF), VM((1, n, per, width), BF),
            VM((8, rows), F32), VM((3, 8, rows), F32), VM((8, width), F32), VM((n, 8, width), F32), VM((8, width), F32),
            VM((rows, width), F32),
            DMA((n,)), DMA((n,)), DMA((depth, 2)), DMA((depth, 2)), DMA((depth, 2)), DMA((depth, 2)), DMA((depth, 2)), DMA((depth, 2)),
            DMA, DMA, DMA, DMA, DMA((3,)), DMA((3,)), DMA((n,)), DMA((n,)), DMA((3,)), DMA((3,))]
        + REDUCE_SEMS(NC, n) + GATHER_SEMS(1, n),
        name="layer_tail", compiler_params=params(cid),
    )(*args)


def start_body(
    n, tokens, out_grad, place_r, place_c, meta_w, w_kv, x_all, dy_own, meta_all, sorter_out,
    att_rows, att_gate, mlp_rows, mlp_gate, in_gate, w_k, w_v, x_own, dy_part, dy_send, dy_slots, *sems,
):
    ms, mr, dys, dyr, dps, dpr, zs, zr, ws, wr, ys, yr, xs, xr, cs, cr = sems
    ring = Ring(n)
    g, t = ring.g, ring.t
    rows, features = tokens.shape
    width, per = features // 4, rows // n
    z, y, depth = g // 2, lax.rem(g, 2), n // 2
    pairs = lambda zz, yy: zz * 2 + yy
    ring.greet_all()

    def arrival(row, col):
        g_row, g_col = row // rows, col // rows
        before = (g_col == g_row) & (iota((rows, rows), 0) < iota((rows, rows), 1))
        return g_row, jnp.sum(jnp.where(before, 1.0, 0.0), axis=0, keepdims=True).astype(jnp.int32)

    col_g = jnp.sum(jnp.where(iota((rows, n), 1) == g, place_c[...], 0), axis=1, keepdims=True)
    g_row, rank = arrival(place_r[pl.ds(g, 1), :], col_g)
    sorter = jnp.where(g_row * per + rank == iota((rows, rows), 0), 1.0, 0.0).astype(BF)
    sorter_out[...] = sorter

    half = width // 2
    chunks = [("b", t, half), ("a", t, 0), ("c", ring.tx, 0)]
    cols = [pl.ds(pl.multiple_of(q * width + off, half), half) for _, q, off in chunks]
    for cc in cols:
        x_all[:, g, :, cc] = mm(sorter, tokens[:, cc]).astype(BF).reshape(n, per, half)

    def unit(zz, yy, c):
        return x_all.at[:, pairs(zz, yy), :, cols[c]]

    def cross(zz, yy, c):
        if chunks[c][0] == "b":
            ref = unit(zz, yy, c)
            rcopy(ref, ref, xs.at[pairs(zz, yy)], xr.at[pairs(zz, yy)], g, ring.tx).start()

    def hop_on(up, hop, c):
        zz = z - hop if up else z + hop
        here = zz >= 0 if up else zz < depth
        ss, rs = (zs, zr) if up else (ws, wr)
        on, source = (z + 1, z - 1) if up else (z - 1, z + 1)

        @pl.when(here)
        def _():
            ref = unit(zz, y, c)
            if hop:
                rcopy(ref, ref, ss.at[hop - 1, c], rs.at[hop - 1, c], pairs(source, y), t).wait_recv()

            @pl.when((on < depth) if up else (on >= 0))
            def _():
                rcopy(ref, ref, ss.at[hop, c], rs.at[hop, c], pairs(on, y), t).start()

            if up or hop:
                rcopy(ref, ref, ys.at[zz, c], yr.at[zz, c], pairs(z, 1 - y), t).start()
                cross(zz, y, c)

    def from_y(zz, c):
        ref = unit(zz, 1 - y, c)
        rcopy(ref, ref, ys.at[zz, c], yr.at[zz, c], pairs(z, 1 - y), t).wait_recv()
        cross(zz, 1 - y, c)

    count = range(len(chunks))
    for c in count:
        hop_on(True, 0, c)
        hop_on(False, 0, c)

    spot = jnp.zeros((rows, rows), F32)
    for s in range(n):
        row, col = place_r[s:s + 1, :], place_c[:, s:s + 1]
        s_row, s_rank = arrival(row, col)
        put = jnp.where((s_row == g) & (s_rank + s * per == iota((rows, rows), 0)), 1.0, 0.0).astype(BF)
        work = jnp.where(col - col // rows * rows == iota((rows, rows), 1), 1.0, 0.0).astype(BF)
        spot = spot + mm(put, work)
    spot = spot.astype(BF)
    left, moved = meta_w[...], 0.0
    for _ in range(3):
        piece = left.astype(BF)
        moved = moved + mm_t(piece, spot)
        left = left - piece.astype(F32)
    meta_all[g] = moved
    sent = [ring.send(meta_all.at[g], meta_all.at[g], ms.at[o], mr.at[o], ring.to(o), t) for o in range(1, n)]

    mine = pl.ds(pl.multiple_of(t * width, width), width)
    dy_send[...] = mm(sorter, out_grad[:, mine]).astype(BF).reshape(n, per, width)
    dealt = [ring.send(dy_send.at[ring.to(o)], dy_own.at[g], dys.at[o], dyr.at[o], ring.to(o), t) for o in range(1, n)]
    dy_own[g] = dy_send[g]

    def split(i):
        rr = slice(i * 256, (i + 1) * 256)
        w_k[rr] = w_kv[rr, 0, :]
        w_v[rr] = w_kv[rr, 1, :]

    def tables(first, gate, out_rows, out_gate):
        m = meta_all[g]
        for e in range(n):
            out_rows[e] = slot_table(m, first, float(e), CAP)
            out_gate[e] = slot_gates(m, first, gate, float(e), out_rows[e])

    def hops(k):
        for c in count:
            hop_on(True, k, c)
            hop_on(False, k, c)

    tables(META["mr0"], META["mg0"], mlp_rows, mlp_gate)
    split(0)
    hops(1)
    for c in dealt:
        c.wait_recv()
    slots = mm(mlp_rows[...].reshape(n * CAP, rows), dy_own[...].reshape(rows, width)).astype(BF)
    dy_slots[...] = slots.reshape(n, CAP, width)
    parts = [ring.send(dy_slots.at[ring.to(o)], dy_part.at[g], dps.at[o], dpr.at[o], ring.to(o), t) for o in range(1, n)]
    dy_part[g] = dy_slots[g]
    split(1)
    split(2)
    hops(2)
    split(3)
    tables(META["ar0"], META["ag0"], att_rows, att_gate)
    hops(3)
    split(4)
    for c in sent:
        c.wait_recv()
    from_y(0, 0)
    from_y(1, 0)
    me = g.astype(F32)
    for e in range(n):
        m = meta_all[e]
        in_gate[0, e] = slot_gates(m, META["ar0"], META["ag0"], me, slot_table(m, META["ar0"], me, CAP))
        in_gate[1, e] = slot_gates(m, META["mr0"], META["mg0"], me, slot_table(m, META["mr0"], me, CAP))
    from_y(2, 0)
    from_y(3, 0)
    split(5)

    def whole(q, off):
        return x_all.at[:, :, :, pl.ds(pl.multiple_of(q * width + off, half), half)]

    cores = [ring.send(whole(t, half), whole(t, half), cs.at[0], cr.at[0], g, ring.tc)]
    for c in (1, 2):
        split(5 + c)
        for zz in range(depth):
            from_y(zz, c)
        ref = whole(chunks[c][1], 0)
        cores.append(ring.send(ref, ref, cs.at[c], cr.at[c], g, ring.tc))
    for u in range(n):
        ref = x_all.at[:, u, :, pl.ds(pl.multiple_of(ring.tx * width + half, half), half)]
        rcopy(ref, ref, xs.at[u], xr.at[u], g, ring.tx).wait_recv()
    cores.append(ring.send(whole(ring.tx, half), whole(ring.tx, half), cs.at[3], cr.at[3], g, ring.tc))
    x_own[...] = x_all[g, :, :, mine].reshape(rows, width).astype(F32)
    for c in cores + parts:
        c.wait_recv()
    for u in range(n):
        ref = x_all.at[:, u, :, cols[0]]
        rcopy(ref, ref, xs.at[u], xr.at[u], g, ring.tx).wait_send()
    for c in count:
        for zz in range(depth):
            ref = unit(zz, y, c)
            rcopy(ref, ref, ys.at[zz, c], yr.at[zz, c], pairs(z, 1 - y), t).wait_send()
        for hop in range(depth - 1):
            for up in (True, False):
                zz = z - hop if up else z + hop
                on = z + 1 if up else z - 1
                ss, rs = (zs, zr) if up else (ws, wr)

                @pl.when((zz >= 0) & (on < depth) if up else (zz < depth) & (on >= 0))
                def _(zz=zz, on=on, ss=ss, rs=rs, hop=hop, c=c):
                    ref = unit(zz, y, c)
                    rcopy(ref, ref, ss.at[hop, c], rs.at[hop, c], pairs(on, y), t).wait_send()
    ring.finish()


def slot_gates(meta, first, gate, name, table):
    per_token = (jnp.where(meta[first:first + 1] == name, meta[gate:gate + 1], 0.0)
                 + jnp.where(meta[first + 1:first + 2] == name, meta[gate + 1:gate + 2], 0.0))
    return jnp.sum(table.astype(F32) * per_token, axis=1, keepdims=True)


def layer_start(tokens, out_grad, place_r, place_c, meta_w, w_kv, n, cid):
    rows, features = tokens.shape
    width, per, depth = features // 4, rows // n, n // 2
    hw = w_kv.shape[2]
    sds = jax.ShapeDtypeStruct
    vm = pl.BlockSpec(memory_space=VM)
    return pl.pallas_call(
        functools.partial(start_body, n),
        out_shape=(
            sds((n, n, per, features), BF), sds((n, per, width), BF), sds((n, 16, rows), F32), sds((rows, rows), BF),
            sds((n, CAP, rows), BF), sds((n, CAP, 1), F32), sds((n, CAP, rows), BF), sds((n, CAP, 1), F32),
            sds((2, n, CAP, 1), F32), sds((features, hw), BF), sds((features, hw), BF), sds((rows, width), F32),
            sds((n, CAP, width), BF)),
        in_specs=[vm] * 6, out_specs=[vm] * 13,
        scratch_shapes=[VM((n, per, width), BF), VM((n, CAP, width), BF)] + [DMA((n,))] * 6 + [DMA((depth, 3))] * 6 + [DMA((n,))] * 2 + [DMA((4,))] * 2,
        name="layer_start", compiler_params=params(cid),
    )(tokens, out_grad, place_r, place_c, meta_w, w_kv)


def fast_local(
    tokens, out_grad, row_place, seq_lengths, att_routes, att_gates, mlp_routes, mlp_gates,
    gain_attn, w_kv, w_query, w_out, gain_mlp, w_gate, w_up, w_down,
):
    rows, features = tokens.shape
    n = lax.axis_size("dp")
    g, t = lax.axis_index("dp"), lax.axis_index("tensor")
    width = features // 4
    per = rows // n
    hw = w_kv.shape[2]
    part = lambda a: lax.dynamic_slice_in_dim(a, t * width, width, a.ndim - 1)
    counting = jnp.arange(rows, dtype=jnp.int32)

    ends = jnp.cumsum(seq_lengths[0])
    segment = jnp.sum((counting[:, None] >= ends[None, :]).astype(jnp.int32), axis=1)
    begins = jnp.sum(
        jnp.where(segment[:, None] == jnp.arange(ends.shape[0])[None, :], (ends - seq_lengths[0])[None, :], 0), axis=1
    )
    carried = jnp.stack(
        [v.astype(F32) for v in (
            att_routes[:, 0], att_routes[:, 1], att_gates[:, 0], att_gates[:, 1],
            mlp_routes[:, 0], mlp_routes[:, 1], mlp_gates[:, 0], mlp_gates[:, 1],
            counting - begins, segment, counting)] + [jnp.zeros((rows,), F32)] * 5)
    place = row_place.reshape(n, rows)
    (x_all, dy_own, meta_all, sorter, att_out, att_gate, mlp_out, mlp_gate, in_gate, w_k, w_v, x_own,
     dy_part) = layer_start(tokens, out_grad, place, place.T, carried, w_kv, n, cid=12)
    x_all, dy_own = x_all.reshape(n, rows, features), dy_own.reshape(rows, width)
    att_rows, mlp_rows = att_out.reshape(n * CAP, rows), mlp_out.reshape(n * CAP, rows)

    cos_t, sin_t = angle_tables(rows)
    normed, picked, keys, values, query, attn, scale_attn, bias, turn_slots, d_mbr = attend(
        x_all, gain_attn[None], w_k, w_v, w_query[0], meta_all, cos_t, sin_t, dy_part, in_gate[1], cid=13)
    normed_flat, picked = normed.reshape(n * rows, features), picked.reshape(n * CAP, features)
    attn = attn.reshape(n * CAP, hw)
    query_back = lax.all_to_all(query, "dp", split_axis=0, concat_axis=0, tiled=True)
    hidden, hid_rows, scale_mlp = hidden_rows(
        attn, w_out[0], x_own, att_rows.T, att_gate.reshape(-1, 1), mlp_rows, n, cid=9)

    gain_mlp_t, gain_attn_t = part(gain_mlp), part(gain_attn)
    d_mbr = d_mbr.reshape(n * CAP, features)
    d_obr, d_hidden, mixed_rows, gain_mlp_part, normed2, inner, d_gate, d_up = expert_layer(
        hid_rows, d_mbr, gain_mlp[None], w_gate[0], w_up[0], w_down[0], hidden, dy_own.astype(F32), gain_mlp_t[None],
        scale_mlp, mlp_rows.T, mlp_gate.reshape(-1, 1), mlp_rows, att_rows, n, cid=10)
    w_gate_grad = mm_rows(normed2, d_gate)[None]
    w_up_grad = mm_rows(normed2, d_up)[None]
    w_down_grad = mm_rows(inner, d_mbr)[None]

    d_obr, d_attn, dq_pre = attend_back(
        d_obr, in_gate[0], w_out[0], query, keys, values, bias, turn_slots)
    d_obr, dq_flat = d_obr.reshape(n * CAP, features), dq_pre.reshape(n * CAP, hw)
    d_kv_all, back, gains = layer_tail(
        (dq_flat, w_query[0], d_attn, query_back, keys, values, meta_all, cos_t, sin_t,
         w_k, w_v, x_own, scale_attn, gain_attn_t[None], d_hidden, mixed_rows, gain_mlp_part, att_rows.T), n, cid=11)
    w_out_grad = mm_rows(attn, d_obr)[None]
    w_query_grad = mm_rows(picked, dq_flat)[None]
    w_kv_grad = map_grad(normed_flat, d_kv_all.reshape(n * rows, 2 * hw))
    mixed = mm_rows(sorter, back[:, :per].reshape(rows, features)).astype(BF)
    tokens_grad = mm_rows(sorter, back[:, per:].reshape(rows, features)).astype(BF)
    return (
        mixed, tokens_grad, gains[1], w_kv_grad, w_query_grad, w_out_grad, gains[0],
        w_gate_grad, w_up_grad, w_down_grad,
    )


def solution(mesh):
    placed = (
        P("dp", None),
        P("dp", None),
        P(),
        P("dp", None),
        P("dp", None),
        P("dp", None),
        P("dp", None),
        P("dp", None),
        P(),
        P(None, None, "tensor"),
        P("dp", None, "tensor"),
        P("dp", "tensor", None),
        P(),
        P("dp", None, "tensor"),
        P("dp", None, "tensor"),
        P("dp", "tensor", None),
    )
    dealt = mesh.shape["dp"] == EXPERTS and mesh.shape["tensor"] == 4
    return jax.shard_map(
        fast_local if dealt else local,
        mesh=mesh,
        in_specs=placed,
        out_specs=(
            P("dp", None),
            P("dp", None),
            P(),
            P(None, None, "tensor"),
            P("dp", None, "tensor"),
            P("dp", "tensor", None),
            P(),
            P("dp", None, "tensor"),
            P("dp", None, "tensor"),
            P("dp", "tensor", None),
        ),
        check_vma=False,
    )
```

```python
import functools
import math

import jax
import jax.numpy as jnp
import numpy as np
from jax import lax
from jax.experimental import pallas as pl
from jax.experimental.pallas import tpu as pltpu
from jax.sharding import PartitionSpec as P

HD = 128
ATT_EXPERTS = 8
EXPERTS = 8
CAP = 64


EPSILON = 1e-05
THETA = 10000.0


def inverse_rms(values_in):
    return lax.rsqrt(jnp.mean(values_in * values_in, axis=-1, keepdims=True) + EPSILON)


def norm_backward(inputs, inv_root, gain, incoming):
    weighted = incoming * gain
    inner_mean = jnp.mean(inputs * weighted, axis=-1, keepdims=True)
    return inv_root * weighted - inputs * (inv_root * inv_root * inv_root) * inner_mean


def rotate(vectors, positions, direction):
    half_dim = vectors.shape[-1] // 2
    frequency = jnp.exp(-math.log(THETA) * jnp.arange(half_dim, dtype=jnp.float32) / half_dim)
    angles = positions.astype(jnp.float32)[:, None] * frequency[None, :]
    target = (vectors.shape[0],) + (1,) * (vectors.ndim - 2) + (half_dim,)
    cosine = jnp.cos(angles).reshape(target)
    sine = direction * jnp.sin(angles).reshape(target)
    former = vectors[..., :half_dim]
    latter = vectors[..., half_dim:]
    return jnp.concatenate(
        [former * cosine - latter * sine, latter * cosine + former * sine], axis=-1
    )


def expert_slots(routes, experts, capacity):
    flattened = routes.reshape(-1)
    pair_count = flattened.shape[0]
    one_hot = (flattened[:, None] == jnp.arange(experts, dtype=jnp.int32)[None, :]).astype(
        jnp.int32
    )
    earlier = jnp.cumsum(one_hot, axis=0) - one_hot
    position = jnp.sum(earlier * one_hot, axis=1)
    slot_table = jnp.full((experts, capacity), pair_count, jnp.int32)
    slot_table = slot_table.at[flattened, position].set(jnp.arange(pair_count, dtype=jnp.int32))
    return (flattened * capacity + position, slot_table)


def pick_rows(source_rows, slot_table):
    padded = jnp.concatenate(
        [source_rows, jnp.zeros((1, source_rows.shape[1]), source_rows.dtype)], axis=0
    )
    return padded[slot_table]


def send_slices(source_rows, slot_table, group_size):
    picked = pick_rows(source_rows, slot_table)
    experts, capacity, features = picked.shape
    divided = picked.reshape(experts, capacity, group_size, features // group_size)
    return divided.transpose(0, 2, 1, 3).reshape(
        experts * group_size, capacity, features // group_size
    )


def send_copies(source_rows, slot_table, group_size):
    picked = pick_rows(source_rows, slot_table)
    experts, capacity, features = picked.shape
    copies = jnp.broadcast_to(picked[:, None], (experts, group_size, capacity, features))
    return copies.reshape(experts * group_size, capacity, features)


def owners_summed(returned, pair_where, group_size):
    owners, capacity, features = returned.shape
    summed = returned.reshape(owners // group_size, group_size, capacity, features).sum(axis=1)
    return summed.reshape(-1, features)[pair_where]


def owners_joined(returned, pair_where, group_size):
    owners, capacity, features = returned.shape
    joined = returned.reshape(owners // group_size, group_size, capacity, features).transpose(
        0, 2, 1, 3
    )
    return joined.reshape(-1, group_size * features)[pair_where]


def query_return(pieces):
    return lax.all_to_all(pieces, "dp", split_axis=0, concat_axis=0, tiled=True)


def output_return(pieces):
    return lax.all_to_all(pieces, "dp", split_axis=0, concat_axis=0, tiled=True)


def expert_return(pieces):
    return lax.all_to_all(pieces, "dp", split_axis=0, concat_axis=0, tiled=True)


def tensor_total(pieces):
    return lax.psum(pieces, "tensor")


def deal_plan(row_place, rows_dev):
    device_count = lax.axis_size("dp")
    my_index = lax.axis_index("dp")
    per_peer = rows_dev // device_count
    every_place = row_place.reshape(device_count, rows_dev)
    my_places = lax.dynamic_index_in_dim(every_place, my_index, 0, keepdims=False)
    counting = jnp.arange(rows_dev, dtype=jnp.int32)
    ordering = jnp.argsort(my_places // rows_dev * rows_dev + counting)
    wanted = every_place // rows_dev == my_index
    chosen = jnp.argsort(
        jnp.where(wanted, counting[None, :], rows_dev + counting[None, :]), axis=1
    )[:, :per_peer]
    placed = jnp.take_along_axis(every_place, chosen, axis=1) % rows_dev
    return (ordering, placed.reshape(-1))


def masked_scores(query_b, keys_b, allowed):
    raw = jnp.einsum(
        "ikjd,mjd->kjim", query_b, keys_b, preferred_element_type=jnp.float32
    ) / math.sqrt(query_b.shape[-1])
    return jnp.where(allowed[None, None], raw, -1e30)


def local(
    tokens,
    out_grad,
    row_place,
    seq_lengths,
    att_routes,
    att_gates,
    mlp_routes,
    mlp_gates,
    gain_attn,
    w_kv,
    w_query,
    w_out,
    gain_mlp,
    w_gate,
    w_up,
    w_down,
):
    rows_dev, features = tokens.shape
    device_count = lax.axis_size("dp")
    group_size = device_count // EXPERTS
    per_peer = rows_dev // device_count
    counting = jnp.arange(rows_dev, dtype=jnp.int32)
    ordering, placed = deal_plan(row_place, rows_dev)
    unplace = jnp.zeros((rows_dev,), jnp.int32).at[placed].set(counting)
    unorder = jnp.zeros((rows_dev,), jnp.int32).at[ordering].set(counting)
    dealt_x, dealt_g = (
        lax.all_to_all(
            tokens[ordering].reshape(device_count, per_peer, features),
            "dp",
            split_axis=0,
            concat_axis=0,
            tiled=True,
        ),
        lax.all_to_all(
            out_grad[ordering].reshape(device_count, per_peer, features),
            "dp",
            split_axis=0,
            concat_axis=0,
            tiled=True,
        ),
    )
    residual = dealt_x.reshape(rows_dev, features)[unplace].astype(jnp.float32)
    top_grad = dealt_g.reshape(rows_dev, features)[unplace].astype(jnp.float32)
    lengths = seq_lengths[0]
    seq_ends = jnp.cumsum(lengths)
    segment = jnp.sum((counting[:, None] >= seq_ends[None, :]).astype(jnp.int32), axis=1)
    starts = seq_ends - lengths
    member = segment[:, None] == jnp.arange(lengths.shape[0], dtype=jnp.int32)[None, :]
    begins = jnp.sum(jnp.where(member, starts[None, :], 0), axis=1)
    positions = counting - begins
    allowed = (segment[:, None] == segment[None, :]) & (counting[None, :] <= counting[:, None])
    head_count = w_kv.shape[2] // HD
    scale_attn = inverse_rms(residual)
    normed = (residual * scale_attn * gain_attn).astype(jnp.bfloat16)
    kv_proj = jnp.einsum("ld,dck->lck", normed, w_kv, preferred_element_type=jnp.float32)
    keys = rotate(kv_proj[:, 0].reshape(rows_dev, head_count, HD), positions, 1.0).astype(
        jnp.bfloat16
    )
    values = kv_proj[:, 1].reshape(rows_dev, head_count, HD).astype(jnp.bfloat16)
    att_where, att_table = expert_slots(att_routes, ATT_EXPERTS, CAP)
    query_rows = lax.all_to_all(
        send_slices(normed, att_table // 2, group_size),
        "dp",
        split_axis=0,
        concat_axis=0,
        tiled=True,
    )
    query_part = jnp.einsum(
        "scd,dh->sch", query_rows, w_query[0], preferred_element_type=jnp.float32
    )
    query_pre = owners_summed(query_return(query_part), att_where, group_size)
    query_rot = rotate(query_pre.reshape(rows_dev, 2, head_count, HD), positions, 1.0).astype(
        jnp.bfloat16
    )
    scores = masked_scores(query_rot, keys, allowed)
    highest = jnp.max(scores, axis=-1, keepdims=True)
    expo = jnp.exp(scores - highest)
    row_total = jnp.sum(expo, axis=-1, keepdims=True)
    log_total = highest + jnp.log(row_total)
    probability = expo / row_total
    attn = jnp.einsum(
        "kjim,mjd->ikjd",
        probability.astype(jnp.bfloat16),
        values,
        preferred_element_type=jnp.float32,
    )
    attn_low = attn.astype(jnp.bfloat16).reshape(rows_dev * 2, head_count * HD)
    out_rows = lax.all_to_all(
        send_copies(attn_low, att_table, group_size), "dp", split_axis=0, concat_axis=0, tiled=True
    )
    out_part = jnp.einsum("sch,hd->scd", out_rows, w_out[0], preferred_element_type=jnp.float32)
    out_pairs = owners_joined(output_return(out_part), att_where, group_size).reshape(
        rows_dev, 2, features
    )
    hidden = residual + tensor_total(jnp.sum(out_pairs * att_gates[:, :, None], axis=1))
    gate_map, up_map, down_map = (w_gate[0], w_up[0], w_down[0])
    scale_mlp = inverse_rms(hidden)
    normed2 = (hidden * scale_mlp * gain_mlp).astype(jnp.bfloat16)
    mlp_where, mlp_table = expert_slots(mlp_routes, EXPERTS, CAP)
    expert_sent = send_copies(normed2, mlp_table // 2, group_size)
    expert_rows = lax.all_to_all(expert_sent, "dp", split_axis=0, concat_axis=0, tiled=True)
    flat_rows = expert_rows.reshape(-1, features)
    gate_act = jnp.dot(flat_rows, gate_map, preferred_element_type=jnp.float32)
    up_act = jnp.dot(flat_rows, up_map, preferred_element_type=jnp.float32)
    inner = (jax.nn.silu(gate_act) * up_act).astype(jnp.bfloat16)
    expert_part = jnp.dot(inner, down_map, preferred_element_type=jnp.float32).reshape(
        expert_rows.shape
    )
    expert_pairs = owners_summed(expert_return(expert_part), mlp_where, group_size).reshape(
        rows_dev, 2, features
    )
    mixed_rows = hidden + tensor_total(jnp.sum(expert_pairs * mlp_gates[:, :, None], axis=1))
    branch_grad = (
        (top_grad[:, None, :] * mlp_gates[:, :, None])
        .astype(jnp.bfloat16)
        .reshape(rows_dev * 2, features)
    )
    grad_sent = send_copies(branch_grad, mlp_table, group_size)
    grad_back, rows_back = (
        lax.all_to_all(grad_sent, "dp", split_axis=0, concat_axis=0, tiled=True),
        lax.all_to_all(expert_sent, "dp", split_axis=0, concat_axis=0, tiled=True),
    )
    grad_rows = grad_back.reshape(-1, features)
    rows_again = rows_back.reshape(-1, features)
    gate_again = jnp.dot(rows_again, gate_map, preferred_element_type=jnp.float32)
    up_again = jnp.dot(rows_again, up_map, preferred_element_type=jnp.float32)
    inner_again = (jax.nn.silu(gate_again) * up_again).astype(jnp.bfloat16)
    contract_rows = (((0,), (0,)), ((), ()))
    contract_cols = (((1,), (1,)), ((), ()))
    d_inner = lax.dot_general(
        grad_rows, down_map, contract_cols, preferred_element_type=jnp.float32
    )
    down_grad_all = lax.dot_general(
        inner_again, grad_rows, contract_rows, preferred_element_type=jnp.float32
    )
    sigmoid_g = jax.nn.sigmoid(gate_again)
    d_up = (d_inner * gate_again * sigmoid_g).astype(jnp.bfloat16)
    d_gate = (d_inner * up_again * sigmoid_g * (1.0 + gate_again * (1.0 - sigmoid_g))).astype(
        jnp.bfloat16
    )
    gate_grad_all = lax.dot_general(
        rows_again, d_gate, contract_rows, preferred_element_type=jnp.float32
    )
    up_grad_all = lax.dot_general(
        rows_again, d_up, contract_rows, preferred_element_type=jnp.float32
    )
    d_rows = lax.dot_general(d_gate, gate_map, contract_cols, preferred_element_type=jnp.float32)
    d_rows = d_rows + lax.dot_general(
        d_up, up_map, contract_cols, preferred_element_type=jnp.float32
    )
    d_pairs = owners_summed(expert_return(d_rows.reshape(expert_rows.shape)), mlp_where, group_size)
    w_gate_grad = gate_grad_all[None]
    w_up_grad = up_grad_all[None]
    w_down_grad = down_grad_all[None]
    d_normed2 = tensor_total(jnp.sum(d_pairs.reshape(rows_dev, 2, features), axis=1))
    d_hidden = top_grad + norm_backward(hidden, scale_mlp, gain_mlp, d_normed2)
    gain_mlp_grad = jnp.sum(d_normed2 * hidden * scale_mlp, axis=0)
    att_grad = (
        (d_hidden[:, None, :] * att_gates[:, :, None])
        .astype(jnp.bfloat16)
        .reshape(rows_dev * 2, features)
    )
    grad_slices = lax.all_to_all(
        send_slices(att_grad, att_table, group_size), "dp", split_axis=0, concat_axis=0, tiled=True
    )
    w_out_grad = jnp.einsum(
        "sch,scd->hd", out_rows, grad_slices, preferred_element_type=jnp.float32
    )
    d_attn_part = jnp.einsum(
        "scd,hd->sch", grad_slices, w_out[0], preferred_element_type=jnp.float32
    )
    d_attn = owners_summed(output_return(d_attn_part), att_where, group_size)
    d_attn = d_attn.astype(jnp.bfloat16).reshape(rows_dev, 2, head_count, HD)
    probability = jnp.exp(masked_scores(query_rot, keys, allowed) - log_total)
    d_prob = jnp.einsum("ikjd,mjd->kjim", d_attn, values, preferred_element_type=jnp.float32)
    d_values = jnp.einsum(
        "kjim,ikjd->mjd",
        probability.astype(jnp.bfloat16),
        d_attn,
        preferred_element_type=jnp.float32,
    )
    delta = jnp.sum(d_prob * probability, axis=-1, keepdims=True)
    d_scores = (probability * (d_prob - delta)).astype(jnp.bfloat16)
    root_hd = math.sqrt(HD)
    d_query = (
        jnp.einsum("kjim,mjd->ikjd", d_scores, keys, preferred_element_type=jnp.float32) / root_hd
    )
    d_keys = (
        jnp.einsum("kjim,ikjd->mjd", d_scores, query_rot, preferred_element_type=jnp.float32)
        / root_hd
    )
    dq_pre = (
        rotate(d_query, positions, -1.0).astype(jnp.bfloat16).reshape(rows_dev * 2, head_count * HD)
    )
    dk_pre = rotate(d_keys, positions, -1.0).reshape(rows_dev, head_count * HD)
    d_kv = jnp.stack([dk_pre, d_values.reshape(rows_dev, head_count * HD)], axis=1).astype(
        jnp.bfloat16
    )
    dq_rows = lax.all_to_all(
        send_copies(dq_pre, att_table, group_size), "dp", split_axis=0, concat_axis=0, tiled=True
    )
    w_query_grad = jnp.einsum(
        "scd,sch->dh", query_rows, dq_rows, preferred_element_type=jnp.float32
    )
    d_slice = jnp.einsum("sch,dh->scd", dq_rows, w_query[0], preferred_element_type=jnp.float32)
    d_norm_query = owners_joined(query_return(d_slice), att_where, group_size)
    d_norm_query = jnp.sum(d_norm_query.reshape(rows_dev, 2, features), axis=1)
    w_kv_grad = jnp.einsum("ld,lck->dck", normed, d_kv, preferred_element_type=jnp.float32)
    d_norm_kv = jnp.einsum("lck,dck->ld", d_kv, w_kv, preferred_element_type=jnp.float32)
    d_normed = tensor_total(d_norm_query + d_norm_kv)
    in_grad = d_hidden + norm_backward(residual, scale_attn, gain_attn, d_normed)
    gain_attn_grad = jnp.sum(d_normed * residual * scale_attn, axis=0)
    w_kv_grad, gain_attn_grad, gain_mlp_grad = (
        lax.psum(w_kv_grad.astype(jnp.bfloat16), "dp").astype(jnp.float32),
        lax.psum(gain_attn_grad.astype(jnp.bfloat16), "dp").astype(jnp.float32),
        lax.psum(gain_mlp_grad.astype(jnp.bfloat16), "dp").astype(jnp.float32),
    )
    send_mixed = mixed_rows.astype(jnp.bfloat16)[placed].reshape(device_count, per_peer, features)
    send_input = in_grad.astype(jnp.bfloat16)[placed].reshape(device_count, per_peer, features)
    back_mixed, back_input = (
        lax.all_to_all(send_mixed, "dp", split_axis=0, concat_axis=0, tiled=True),
        lax.all_to_all(send_input, "dp", split_axis=0, concat_axis=0, tiled=True),
    )
    mixed = back_mixed.reshape(rows_dev, features)[unorder]
    tokens_grad = back_input.reshape(rows_dev, features)[unorder]
    return (
        mixed,
        tokens_grad,
        gain_attn_grad,
        w_kv_grad,
        w_query_grad[None],
        w_out_grad[None],
        gain_mlp_grad,
        w_gate_grad,
        w_up_grad,
        w_down_grad,
    )


MESH = pl.DeviceIdType.MESH
VM = pltpu.VMEM
DMA = pltpu.SemaphoreType.DMA
BF = jnp.bfloat16
F32 = jnp.float32

def rcopy(src, dst, ss, rs, dp, tn):
    return pltpu.make_async_remote_copy(src_ref=src, dst_ref=dst, send_sem=ss, recv_sem=rs,
        device_id={"dp": dp, "tensor": tn}, device_id_type=MESH)

def greet(targets):
    b = pltpu.get_barrier_semaphore()
    for dp, tn in targets:
        pl.semaphore_signal(b, inc=1, device_id={"dp": dp, "tensor": tn}, device_id_type=MESH)
    pl.semaphore_wait(b, len(targets))

def ranks():
    g = lax.axis_index("dp"); t = lax.axis_index("tensor")
    return g, t, lax.rem(t + 2, 4), t + 1 - 2 * lax.rem(t, 2)

def params(cid):
    return pltpu.CompilerParams(collective_id=cid, has_side_effects=True, vmem_limit_bytes=56*2**20)

def gather_body(n, mode, src, out, ssem, rsem, xs, xr, cs, cr, c2s, c2r, lsem):
    g, t, tx, tc = ranks()
    w = src.shape[-1]
    greet([(lax.rem(g + o, n), t) for o in range(1, n)] + [(g, tx), (g, tc)])
    cols = pl.ds(pl.multiple_of(t * w, w), w)
    colsx = pl.ds(pl.multiple_of(tx * w, w), w)
    pick = (lambda d: src.at[d]) if mode == "rows" else (lambda d: src)
    at = (lambda b, cc: out.at[:, b, :, cc]) if mode == "deal" else (lambda b, cc: out.at[b, :, cc])
    sends = []
    for o in range(1, n):
        d = lax.rem(g + o, n)
        c = rcopy(pick(d), at(g, cols), ssem.at[o], rsem.at[o], d, t)
        c.start(); sends.append(c)
    loc = pltpu.make_async_copy(pick(g), at(g, cols), lsem)
    loc.start(); loc.wait()
    fx = []; fc = []; fc2 = []
    for o in range(n):
        b = lax.rem(g - o + n, n)
        if o > 0: sends[o - 1].wait_recv()
        c = rcopy(at(b, cols), at(b, cols), xs.at[o], xr.at[o], g, tx); c.start(); fx.append(c)
        c = rcopy(at(b, cols), at(b, cols), cs.at[o], cr.at[o], g, tc); c.start(); fc.append(c)
    for o in range(n):
        b = lax.rem(g - o + n, n)
        fx[o].wait_recv()
        c = rcopy(at(b, colsx), at(b, colsx), c2s.at[o], c2r.at[o], g, tc); c.start(); fc2.append(c)
    for c in fc + fc2: c.wait_recv()
    for c in sends + fx + fc + fc2: c.wait_send()

def gather(src, n, bcast=False, deal=False, cid=0, space=VM):
    r, w = src.shape[-2:]
    mode = "deal" if deal else "copy" if bcast else "rows"
    shape = (n, n, r, 4 * w) if deal else (n, r, 4 * w)
    return pl.pallas_call(functools.partial(gather_body, n, mode),
        out_shape=jax.ShapeDtypeStruct(shape, src.dtype),
        in_specs=[pl.BlockSpec(memory_space=VM)], out_specs=pl.BlockSpec(memory_space=space),
        scratch_shapes=[DMA((n,))]*8 + [DMA],
        name="gather_rows", compiler_params=params(cid))(src)

def reduce_body(n, nb, src, out, cbuf, cin, xbuf, xin, dbuf, cs, cr, xs, xr, ds_, dr):
    g, t, tx, tc = ranks()
    tcx = lax.rem(tc + 2, 4); w = out.shape[-1]
    greet([(lax.rem(g + o, n), t) for o in range(1, n)] + [(g, tx), (g, tc)])
    sl = lambda q: pl.ds(pl.multiple_of(q * w, w), w)
    order = list(range(1, n)) + [0] + list(range(n, nb))
    at = lambda o: lax.rem(g + o, n) if o < n else o
    C = {}; X = {}; Dd = {}
    for o in order:
        d = at(o)
        cbuf[o, 0] = src[d, :, sl(tc)].astype(BF)
        cbuf[o, 1] = src[d, :, sl(tcx)].astype(BF)
        C[o] = rcopy(cbuf.at[o], cin.at[o], cs.at[o], cr.at[o], g, tc); C[o].start()
    for o in order:
        C[o].wait_recv()
        xbuf[o] = (src[at(o), :, sl(tx)] + cin[o, 1].astype(F32)).astype(BF)
        X[o] = rcopy(xbuf.at[o], xin.at[o], xs.at[o], xr.at[o], g, tx); X[o].start()
    for o in order:
        d = at(o)
        X[o].wait_recv()
        total = (src[d, :, sl(t)] + cin[o, 0].astype(F32) + xin[o].astype(F32)).astype(BF)
        if 0 < o < n:
            dbuf[o] = total
            Dd[o] = rcopy(dbuf.at[o], out.at[g], ds_.at[o], dr.at[o], d, t); Dd[o].start()
        elif o == 0:
            out[g] = total
        else:
            out[o] = total
    for c in Dd.values(): c.wait_recv()
    for c in list(C.values()) + list(X.values()) + list(Dd.values()): c.wait_send()

def reduce(src, n, cid=1):
    nb, r, w = src.shape; w //= 4
    return pl.pallas_call(functools.partial(reduce_body, n, nb),
        out_shape=jax.ShapeDtypeStruct((nb, r, w), BF),
        in_specs=[pl.BlockSpec(memory_space=VM)], out_specs=pl.BlockSpec(memory_space=VM),
        scratch_shapes=[VM((nb,2,r,w),BF), VM((nb,2,r,w),BF), VM((nb,r,w),BF), VM((nb,r,w),BF), VM((n,r,w),BF)] + [DMA((nb,))]*4 + [DMA((n,))]*2,
        name="reduce_rows", compiler_params=params(cid))(src)

def a2a_body(n, src, out, ss, rs):
    g, t, tx, tc = ranks()
    greet([(lax.rem(g + o, n), t) for o in range(1, n)])
    cs = []
    for o in range(1, n):
        d = lax.rem(g + o, n)
        c = rcopy(src.at[d], out.at[g], ss.at[o], rs.at[o], d, t); c.start(); cs.append(c)
    out[g] = src[g]
    for c in cs: c.wait()

def a2a(src, n, cid=2):
    return pl.pallas_call(functools.partial(a2a_body, n),
        out_shape=jax.ShapeDtypeStruct(src.shape, src.dtype),
        in_specs=[pl.BlockSpec(memory_space=VM)], out_specs=pl.BlockSpec(memory_space=VM),
        scratch_shapes=[DMA((n,))]*2,
        name="a2a_rows", compiler_params=params(cid))(src)

def a2a_copy_body(n, src, out, ss, rs):
    g, t, tx, tc = ranks()
    greet([(lax.rem(g + o, n), t) for o in range(1, n)])
    cs = []
    for o in range(1, n):
        d = lax.rem(g + o, n)
        c = rcopy(src, out.at[g], ss.at[o], rs.at[o], d, t); c.start(); cs.append(c)
    out[g] = src[...]
    for c in cs: c.wait()

def a2a_copy(src, n, cid):
    return pl.pallas_call(functools.partial(a2a_copy_body, n),
        out_shape=jax.ShapeDtypeStruct((n,) + src.shape, src.dtype),
        in_specs=[pl.BlockSpec(memory_space=VM)], out_specs=pl.BlockSpec(memory_space=VM),
        scratch_shapes=[DMA((n,))]*2,
        name="copy_rows", compiler_params=params(cid))(src)

def dot(a, b, dims):
    return lax.dot_general(a, b, dims, preferred_element_type=F32)


def mm(a, b):
    return dot(a, b, (((a.ndim - 1,), (0,)), ((), ())))


def mm_t(a, b):
    return dot(a, b, (((1,), (1,)), ((), ())))


def mm_rows(a, b):
    return dot(a, b, (((0,), (0,)), ((), ())))


class Ring:
    def __init__(self, n):
        self.n = n
        self.g, self.t, self.tx, self.tc = ranks()
        self.tcx = lax.rem(self.tc + 2, 4)
        self.tail = []
        self.dest = [lax.rem(self.g + o, n) for o in range(n)]

    def to(self, o):
        return self.dest[o]

    def greet_all(self):
        greet([(self.to(o), self.t) for o in range(1, self.n)] + [(self.g, self.tx), (self.g, self.tc)])

    def greet_everyone(self):
        greet([(self.to(o), self.t) for o in range(1, self.n)] + [(self.g, q) for q in (self.tx, self.tc, self.tcx)])

    def send(self, src, dst, ss, rs, dp, tn):
        c = rcopy(src, dst, ss, rs, dp, tn)
        c.start()
        self.tail.append(c)
        return c

    def finish(self):
        for c in self.tail:
            c.wait_send()
        self.tail = []


def cols_of(q, j, width, cw):
    return pl.ds(pl.multiple_of(q * width + j * cw, cw), cw)


REDUCE_SEMS = lambda nc, n: [DMA((nc,))] * 4 + [DMA((nc, n))] * 2
GATHER_SEMS = lambda nc, n: [DMA((nc, n))] * 2 + [DMA((nc,))] * 6
REDUCE_BUFS = lambda nc, n, r, cw: [
    VM((nc, 2, n, r, cw), BF), VM((nc, 2, n, r, cw), BF), VM((nc, 2, n, r, cw), F32),
    VM((nc, n, r, cw), BF), VM((nc, n, r, cw), BF), VM((nc, n, r, cw), BF), VM((nc, n, r, cw), BF)]


class Reduce:
    def __init__(self, ring, partial, bufs, sems):
        self.ring, self.partial = ring, partial
        self.cbuf, self.cin, self.pbuf, self.xbuf, self.xin, self.dbuf, self.rbuf = bufs
        self.cs, self.cr, self.xs, self.xr, self.ds, self.dr = sems
        self.c, self.x, self.d = {}, {}, {}

    def core(self):
        k = self.ring
        nc, _, n, r, cw = self.cbuf.shape
        for i, q in enumerate((k.tc, k.tcx)):
            v = self.partial(q).astype(BF)
            for j in range(nc):
                self.cbuf[j, i] = v[:, j * cw:(j + 1) * cw].reshape(n, r, cw)
        for j in range(nc):
            self.c[j] = k.send(self.cbuf.at[j], self.cin.at[j], self.cs.at[j], self.cr.at[j], k.g, k.tc)
        for i, q in ((1, k.tx), (0, k.t)):
            v = self.partial(q)
            for j in range(nc):
                self.pbuf[j, i] = v[:, j * cw:(j + 1) * cw].reshape(n, r, cw)
            if i:
                for j in range(nc):
                    self.cross(j)

    def cross(self, j):
        k = self.ring
        self.c[j].wait_recv()
        self.xbuf[j] = (self.pbuf[j, 1] + self.cin[j, 1].astype(F32)).astype(BF)
        self.x[j] = k.send(self.xbuf.at[j], self.xin.at[j], self.xs.at[j], self.xr.at[j], k.g, k.tx)

    def home(self, j):
        k = self.ring
        self.x[j].wait_recv()
        self.dbuf[j] = (self.pbuf[j, 0] + self.cin[j, 0].astype(F32) + self.xin[j].astype(F32)).astype(BF)
        for o in range(1, k.n):
            d = k.to(o)
            self.d[j, o] = k.send(
                self.dbuf.at[j, d], self.rbuf.at[j, k.g], self.ds.at[j, o], self.dr.at[j, o], d, k.t)
        self.rbuf[j, k.g] = self.dbuf[j, k.g]

    def rows(self, j):
        for o in range(1, self.ring.n):
            self.d[j, o].wait_recv()
        return self.rbuf[j].reshape(-1, self.rbuf.shape[-1])


class Gather:
    def __init__(self, ring, width, full, sbuf, sems):
        self.ring, self.full, self.sbuf = ring, full, sbuf
        ss, rs, xs, xr, cs, cr, c2s, c2r = sems
        k, (nc, n, _, cw) = ring, sbuf.shape
        self.d, self.x, self.c, self.c2, self.own = {}, {}, {}, {}, {}
        for j in range(nc):
            cc, cx = cols_of(k.t, j, width, cw), cols_of(k.tx, j, width, cw)
            self.own[j] = cc
            for o in range(1, n):
                d = k.to(o)
                self.d[j, o] = rcopy(sbuf.at[j, d], full.at[k.g, :, cc], ss.at[j, o], rs.at[j, o], d, k.t)
            ref, ref2 = full.at[:, :, cc], full.at[:, :, cx]
            self.x[j] = rcopy(ref, ref, xs.at[j], xr.at[j], k.g, k.tx)
            self.c[j] = rcopy(ref, ref, cs.at[j], cr.at[j], k.g, k.tc)
            self.c2[j] = rcopy(ref2, ref2, c2s.at[j], c2r.at[j], k.g, k.tc)

    def out(self, j, rows):
        self.sbuf[j] = rows.reshape(self.sbuf.shape[1:])
        for o in range(1, self.ring.n):
            self.d[j, o].start()
        self.full[self.ring.g, :, self.own[j]] = self.sbuf[j, self.ring.g]

    def cross(self, j):
        for o in range(1, self.ring.n):
            self.d[j, o].wait_recv()
        self.x[j].start()
        self.c[j].start()

    def core(self, j):
        self.x[j].wait_recv()
        self.c2[j].start()

    def finish(self):
        for c in list(self.c.values()) + list(self.c2.values()):
            c.wait_recv()
        for c in [*self.d.values(), *self.x.values(), *self.c.values(), *self.c2.values()]:
            c.wait_send()


def paired(reduce_one, gather_one, middle, nc):
    reduce_one.core()
    steps = []
    for j in range(nc):
        steps += [(2 * j, 0, lambda j=j: reduce_one.home(j)), (2 * j + 3, 1, lambda j=j: gather_one.out(j, middle(j, reduce_one.rows(j))))]
        steps += [(2 * j + 7, 2, lambda j=j: gather_one.cross(j)), (2 * j + 9, 3, lambda j=j: gather_one.core(j))]
    for _, _, step in sorted(steps, key=lambda s: s[:2]):
        step()
    gather_one.finish()


NC = 4


def split_bf(v):
    high = v.astype(BF)
    return high, (v - high.astype(F32)).astype(BF)


def hidden_body(n, attn, wo, x_own, comb, gates, pick, hidden, full, scale, *scratch):
    bufs, sbuf, sq, sq_in, qs, qr, sems = scratch[:7], *scratch[7:12], scratch[12:]
    ring = Ring(n)
    ring.greet_everyone()
    rows, width = x_own.shape
    shared = []
    cw = width // NC

    def partial(q):
        return mm(attn[...], wo[:, cols_of(q, 0, width, width)])

    def middle(j, rows):
        high, low = split_bf(rows.astype(F32) * gates[...])
        got = x_own[:, j * cw:(j + 1) * cw] + mm(comb[...], high) + mm(comb[...], low)
        hidden[:, j * cw:(j + 1) * cw] = got
        high, low = split_bf(got * got)
        ones = jnp.ones((8, cw), BF)
        squares = mm_t(ones, high) + mm_t(ones, low)
        sq[...] = squares if j == 0 else sq[...] + squares
        if j == NC - 1:
            for i, q in enumerate([ring.tc, ring.tx, ring.tcx]):
                shared.append(ring.send(sq, sq_in.at[i], qs.at[i], qr.at[i], ring.g, q))
        return mm(pick[...], got.astype(BF)).astype(BF)

    red = Reduce(ring, partial, bufs, sems[:6])
    gat = Gather(ring, width, full, sbuf, sems[6:])
    paired(red, gat, middle, NC)
    for c in shared:
        c.wait_recv()
    total = (sq[...] + sq_in[0] + sq_in[1] + sq_in[2])[:1]
    eye = lax.broadcasted_iota(jnp.int32, (rows, rows), 0) == lax.broadcasted_iota(jnp.int32, (rows, rows), 1)
    column = jnp.sum(jnp.where(eye, total, 0.0), axis=1, keepdims=True)
    scale[...] = lax.rsqrt(column / (4 * width) + EPSILON)
    ring.finish()


def hidden_rows(attn, wo, x_own, comb, gates, pick, n, cid):
    slots = attn.shape[0]
    r, (rows, width) = slots // n, x_own.shape
    return pl.pallas_call(
        functools.partial(hidden_body, n),
        out_shape=(
            jax.ShapeDtypeStruct((rows, width), F32), jax.ShapeDtypeStruct((n, r, 4 * width), BF),
            jax.ShapeDtypeStruct((rows, 1), F32)),
        in_specs=[pl.BlockSpec(memory_space=VM)] * 6,
        out_specs=[pl.BlockSpec(memory_space=VM)] * 3,
        scratch_shapes=REDUCE_BUFS(NC, n, r, width // NC) + [VM((NC, n, r, width // NC), BF)]
        + [VM((8, rows), F32), VM((3, 8, rows), F32), DMA((3,)), DMA((3,))]
        + REDUCE_SEMS(NC, n) + GATHER_SEMS(NC, n),
        name="hidden_rows", compiler_params=params(cid),
    )(attn, wo, x_own, comb, gates, pick)


def expert_body(
    n, hid_rows, d_mbr, gain, wg_hbm, wu_hbm, wd_hbm, hidden, dy_own, gain_t, scale, mlp_t, mlp_gates, mlp_rows, att_rows,
    full, d_hidden, mixed, gain_part, n2, inner, d_gate, d_up, *scratch,
):
    ring = Ring(n)
    bufs, bufs2 = scratch[:7], scratch[7:14]
    sbuf, wg, wu, wd, r_own, r_in, r_to, r_back = scratch[14:22]
    wsem, rss, rsr, rds, rdr = scratch[22:27]
    sems = scratch[27:]
    ff = wg.shape[1]
    rows, width = hidden.shape
    slots = n2.shape[0]
    features = 4 * width
    cw = width // NC
    loads = [pltpu.make_async_copy(a, b, wsem.at[i]) for i, (a, b) in enumerate([(wg_hbm, wg), (wu_hbm, wu), (wd_hbm, wd)])]
    for c in loads:
        c.start()
    ring.greet_everyone()

    def norm_rows(i, _):
        at = pl.ds(pl.multiple_of(i * 64, 64), 64)
        v = hid_rows[i].astype(F32)
        s = lax.rsqrt(jnp.mean(v * v, axis=-1, keepdims=True) + EPSILON)
        n2[at, :] = (v * s * gain[...]).astype(BF)
        return _

    lax.fori_loop(0, n, norm_rows, 0)
    for c in loads:
        c.wait()
    r_own[...] = jnp.zeros_like(r_own)

    def units(at, size):
        a = n2[...]
        gate = mm(a, wg[:, at])
        up = mm(a, wu[:, at])
        d_in = mm_t(d_mbr[...], wd[at, :])
        sig = jax.nn.sigmoid(gate)
        silu = gate * sig
        inner[:, at] = (silu * up).astype(BF)
        du = (d_in * silu).astype(BF)
        dg = (d_in * up * sig * (1.0 + gate * (1.0 - sig))).astype(BF)
        d_up[:, at] = du
        d_gate[:, at] = dg
        both = (gate * dg.astype(F32) + up * du.astype(F32)).astype(BF)
        r_own[...] += mm_t(jnp.ones((8, size), BF), both)

    tile = 256

    def unit_tile(i, _):
        units(pl.ds(pl.multiple_of(i * tile, tile), tile), tile)
        return _

    lax.fori_loop(0, ff // tile, unit_tile, 0)
    if ff % tile:
        units(pl.ds(ff // tile * tile, ff % tile), ff % tile)

    others = [ring.tc, ring.tx, ring.tcx]
    r_sends = [ring.send(r_own, r_in.at[i], rss.at[i], rsr.at[i], ring.g, q) for i, q in enumerate(others)]

    def partial(q):
        at = cols_of(q, 0, width, width)
        return mm_t(d_gate[...], wg[at, :]) + mm_t(d_up[...], wu[at, :])

    def partial_mixed(q):
        return mm(inner[...], wd[:, cols_of(q, 0, width, width)])

    pairs = {}

    def share_r():
        for c in r_sends:
            c.wait_recv()
        r_to[...] = r_own[...] + r_in[0] + r_in[1] + r_in[2]
        for o in range(1, n):
            d = ring.to(o)
            half = pl.ds(pl.multiple_of(d // 2 * 128, 128), 128)
            pairs[o] = ring.send(r_to.at[:, half], r_back.at[ring.g], rds.at[o], rdr.at[o], d, ring.t)
        r_back[ring.g] = r_to[:, pl.ds(pl.multiple_of(ring.g // 2 * 128, 128), 128)]

    total_r = {}

    def take_r():
        for o in range(1, n):
            pairs[o].wait_recv()
        odd = lax.rem(ring.g, 2) == 1
        got = jnp.concatenate(
            [jnp.where(odd, r_back[e][:, 64:], r_back[e][:, :64]) for e in range(n)], axis=1)
        high = got.astype(BF)
        low = (got - high.astype(F32)).astype(BF)
        total_r[0] = (mm_t(mlp_t[...], high) + mm_t(mlp_t[...], low))[:, :1] / features

    def middle(j, got):
        if j == 0:
            take_r()
        cc = slice(j * cw, (j + 1) * cw)
        s2, h = scale[...], hidden[:, cc]
        d_n = mm(mlp_t[...], got)
        d_h = dy_own[:, cc] + s2 * (gain_t[:, cc] * d_n) - h * (s2 * s2) * total_r[0]
        d_hidden[:, cc] = d_h
        gain_part[:, cc] = jnp.broadcast_to(jnp.sum(d_n * h * s2, axis=0, keepdims=True), (8, cw))
        return mm(att_rows[...], d_h.astype(BF)).astype(BF)

    red = Reduce(ring, partial, bufs, sems[:6])
    gat = Gather(ring, width, full, sbuf, sems[6:14])
    red2 = Reduce(ring, partial_mixed, bufs2, sems[14:20])

    def settle(j):
        got = red2.rows(j)
        scaled = got.astype(F32) * mlp_gates[...]
        high = scaled.astype(BF)
        low = (scaled - high.astype(F32)).astype(BF)
        cc = slice(j * cw, (j + 1) * cw)
        mixed[:, cc] = (hidden[:, cc] + mm(mlp_t[...], high) + mm(mlp_t[...], low)).astype(BF)

    red.core()
    share_r()
    steps = []
    for j in range(NC):
        steps += [(2 * j, 1, lambda j=j: red.home(j)), (2 * j + 3, 2, lambda j=j: gat.out(j, middle(j, red.rows(j))))]
        steps += [(2 * j + 7, 3, lambda j=j: gat.cross(j)), (2 * j + 9, 4, lambda j=j: gat.core(j))]
        steps += [(2 * j + 12, 7, lambda j=j: red2.home(j)), (2 * j + 16, 8, lambda j=j: settle(j))]
    steps += [(9.5, 5, red2.core)]
    steps.sort(key=lambda s: s[:2])
    for _, _, run in steps:
        run()
    gat.finish()
    ring.finish()


def expert_layer(hid_rows, d_mbr, gain, wg, wu, wd, hidden, dy_own, gain_t, scale, mlp_t, mlp_gates, mlp_rows, att_rows, n, cid):
    r, features = hid_rows.shape[1:]
    ff = wg.shape[1]
    rows, width = hidden.shape
    slots, cw = n * r, width // NC
    any_, vm = pl.BlockSpec(memory_space=pl.ANY), pl.BlockSpec(memory_space=VM)
    sds = jax.ShapeDtypeStruct
    return pl.pallas_call(
        functools.partial(expert_body, n),
        out_shape=(
            sds((n, r, features), BF), sds((rows, width), F32), sds((rows, width), BF), sds((8, width), F32),
            sds((slots, features), BF), sds((slots, ff), BF), sds((slots, ff), BF), sds((slots, ff), BF)),
        in_specs=[vm, vm, vm, any_, any_, any_] + [vm] * 8,
        out_specs=[vm] * 8,
        scratch_shapes=REDUCE_BUFS(NC, n, r, cw) + REDUCE_BUFS(NC, n, r, cw) + [
            VM((NC, n, r, cw), BF), VM((features, ff), BF), VM((features, ff), BF), VM((ff, features), BF),
            VM((8, slots), F32), VM((3, 8, slots), F32), VM((8, slots), F32), VM((n, 8, 128), F32),
            DMA((3,)), DMA((3,)), DMA((3,)), DMA((n,)), DMA((n,))]
        + REDUCE_SEMS(NC, n) + GATHER_SEMS(NC, n) + REDUCE_SEMS(NC, n),
        name="expert_layer", compiler_params=params(cid),
    )(hid_rows, d_mbr, gain, wg, wu, wd, hidden, dy_own, gain_t, scale, mlp_t, mlp_gates, mlp_rows, att_rows)


META = {name: i for i, name in enumerate(
    ("ar0", "ar1", "ag0", "ag1", "mr0", "mr1", "mg0", "mg1", "pos", "seg", "wpos"))}


def iota(shape, dim):
    return lax.broadcasted_iota(jnp.int32, shape, dim)


def slot_table(meta, first, name, cap):
    member = (meta[first:first + 1] == name) | (meta[first + 1:first + 2] == name)
    tokens = meta.shape[1]
    before = jnp.where(iota((tokens, tokens), 0) < iota((tokens, tokens), 1), 1.0, 0.0).astype(BF)
    rank = mm(jnp.broadcast_to(jnp.where(member, 1.0, 0.0), (8, tokens)).astype(BF), before)[:1]
    return jnp.where((rank == iota((cap, tokens), 0).astype(F32)) & member, 1.0, 0.0).astype(BF)


def allowed_pairs(meta, meta_t):
    seg, wpos = META["seg"], META["wpos"]
    same = meta_t[:, seg:seg + 1] == meta[seg:seg + 1]
    return jnp.where(same & (meta[wpos:wpos + 1] <= meta_t[:, wpos:wpos + 1]), 1.0, 0.0).astype(BF)


def position_rows(meta_t):
    pos = META["pos"]
    tokens = meta_t.shape[0]
    return jnp.where(meta_t[:, pos:pos + 1] == iota((tokens, tokens), 1).astype(F32), 1.0, 0.0).astype(BF)


def looked_up(rows, table):
    got = mm(rows, table)
    w = got.shape[1] // 3
    return got[:, :w] + got[:, w:2 * w] + got[:, 2 * w:]


def turned(v, cosine, sine):
    out = []
    for h in range(v.shape[1] // HD):
        u = v[:, h * HD:(h + 1) * HD]
        out.append(u * cosine + pltpu.roll(u, HD // 2, 1) * sine)
    return jnp.concatenate(out, axis=1)


def angle_tables(positions):
    half = HD // 2
    frequency = np.exp(-math.log(THETA) * np.arange(half) / half)
    turned_by = np.arange(positions)[:, None] * frequency[None, :]
    cosine = np.concatenate([np.cos(turned_by)] * 2, axis=1).astype(np.float32)
    sine = np.concatenate([-np.sin(turned_by), np.sin(turned_by)], axis=1).astype(np.float32)

    def parts(v):
        out, left = [], v
        for _ in range(3):
            p = left.astype(jnp.bfloat16)
            out.append(p)
            left = left - p.astype(np.float32)
        return np.concatenate(out, axis=1)

    return jnp.asarray(parts(cosine)), jnp.asarray(parts(sine))


def softmax_rows(scores):
    top = jnp.max(scores, axis=-1, keepdims=True)
    expo = jnp.exp(scores - top)
    return expo / jnp.sum(expo, axis=-1, keepdims=True)


def attend_body(
    n, x, gain, w_k, w_v, w_q, meta, cos_t, sin_t, dy_part, dy_gate,
    normed, picked, keys, values, query, attn, scale, bias, turn_slots, d_mbr, k_scr, v_scr, q_scr, n_scr, dy_rows,
    xs, xr, cs, cr,
):
    step = pl.program_id(0)
    ring = Ring(n)
    width = dy_part.shape[2]

    near, far = [dy_rows.at[:, :, cols_of(q, 0, width, width)] for q in (ring.t, ring.tx)]
    over_x = rcopy(near, near, xs, xr, ring.g, ring.tx)
    to_core = [rcopy(ref, ref, cs.at[i], cr.at[i], ring.g, ring.tc) for i, ref in enumerate((near, far))]

    @pl.when(step == 0)
    def _():
        greet([(ring.g, ring.tx), (ring.g, ring.tc)])
        near[...] = dy_part[...]
        over_x.start()
        to_core[0].start()

    @pl.when(step == 2)
    def _():
        over_x.wait_recv()
        to_core[1].start()

    me = ring.g.astype(F32)
    pair, rows, features = x.shape
    cap = picked.shape[1]
    heads = w_q.shape[1] // HD
    flat = x[...].reshape(pair * rows, features).astype(F32)
    s = lax.rsqrt(jnp.mean(flat * flat, axis=-1, keepdims=True) + EPSILON)
    scale[...] = s.reshape(pair, rows, 1)
    low = (flat * s * gain[...]).astype(BF)
    n_scr[...] = low
    normed[...] = low.reshape(pair, rows, features)
    k_all, v_all = mm(n_scr[...], w_k[...]), mm(n_scr[...], w_v[...])
    slots = []
    for p in range(pair):
        m = meta[p]
        m_t = m.T
        table = slot_table(m, META["ar0"], me, cap)
        at_pos = position_rows(m_t)
        rr = slice(p * rows, (p + 1) * rows)
        kk = turned(k_all[rr], looked_up(at_pos, cos_t[...]), looked_up(at_pos, sin_t[...])).astype(BF)
        k_scr[p] = kk
        v_scr[p] = v_all[rr].astype(BF)
        picked[p] = mm(table, n_scr[rr, :]).astype(BF)
        slot_pos = mm(table, at_pos).astype(BF)
        turn_slots[p, :, :HD] = looked_up(slot_pos, cos_t[...])
        turn_slots[p, :, HD:] = looked_up(slot_pos, sin_t[...])
        bias[p] = (mm(table, allowed_pairs(m, m_t)) - 1.0) * 1e30
        slots.append(table)
    keys[...] = k_scr[...]
    values[...] = v_scr[...]
    q_all = mm(picked[...].reshape(pair * cap, features), w_q[...])
    for p in range(pair):
        qq = turned(q_all[p * cap:(p + 1) * cap], turn_slots[p, :, :HD], turn_slots[p, :, HD:]).astype(BF)
        q_scr[p] = qq
        query[p] = qq
    for p in range(pair):
        for h in range(heads):
            hh = slice(h * HD, (h + 1) * HD)
            scores = mm_t(q_scr[p, :, hh], k_scr[p, :, hh]) / math.sqrt(HD) + bias[p]
            probs = softmax_rows(scores).astype(BF)
            attn[p, :, hh] = mm(probs, v_scr[p, :, hh]).astype(BF)

    @pl.when(step == 3)
    def _():
        for c in to_core:
            c.wait()
        over_x.wait_send()
        for e in range(n):
            d_mbr[e] = (dy_rows[e].astype(F32) * dy_gate[e]).astype(BF)


def attend(x_all, gain, w_k, w_v, w_q, meta, cos_t, sin_t, dy_part, dy_gate, cid):
    n, rows, features = x_all.shape
    hw, cap, pair = w_q.shape[1], CAP, 2
    sds = jax.ShapeDtypeStruct
    block = lambda *s: pl.BlockSpec((pair,) + s, lambda i: (i,) + (0,) * len(s))
    whole = lambda a: pl.BlockSpec(a.shape, lambda i: (0,) * a.ndim)
    return pl.pallas_call(
        functools.partial(attend_body, n), grid=(n // pair,),
        out_shape=(
            sds((n, rows, features), BF), sds((n, cap, features), BF), sds((n, rows, hw), BF), sds((n, rows, hw), BF),
            sds((n, cap, hw), BF), sds((n, cap, hw), BF), sds((n, rows, 1), F32), sds((n, cap, rows), F32),
            sds((n, cap, 2 * HD), F32), sds((n, cap, features), BF)),
        in_specs=[block(rows, features), whole(gain), whole(w_k), whole(w_v), whole(w_q), block(16, rows),
                  whole(cos_t), whole(sin_t), whole(dy_part), whole(dy_gate)],
        out_specs=(
            block(rows, features), block(cap, features), block(rows, hw), block(rows, hw), block(cap, hw), block(cap, hw),
            block(rows, 1), block(cap, rows), block(cap, 2 * HD), pl.BlockSpec((n, cap, features), lambda i: (0, 0, 0))),
        scratch_shapes=[VM((pair, rows, hw), BF), VM((pair, rows, hw), BF), VM((pair, cap, hw), BF), VM((pair * rows, features), BF),
                        VM((n, cap, features), BF), DMA, DMA, DMA((2,)), DMA((2,))],
        name="attend", compiler_params=params(cid),
    )(x_all, gain, w_k, w_v, w_q, meta, cos_t, sin_t, dy_part, dy_gate)


def keys_back_body(query, d_attn, keys, values, meta, cos_t, sin_t, d_kv, *, cap):
    n = query.shape[0]
    hw = keys.shape[1]
    m = meta[...]
    m_t = m.T
    tables = jnp.concatenate([slot_table(m, META["ar0"], float(e), cap) for e in range(n)], axis=0)
    bias = (mm(tables, allowed_pairs(m, m_t)) - 1.0) * 1e30
    at_pos = position_rows(m_t)
    cosine, sine = looked_up(at_pos, cos_t[...]), looked_up(at_pos, sin_t[...])
    root = math.sqrt(HD)
    for h in range(hw // HD):
        hh = slice(h * HD, (h + 1) * HD)
        q = query[:, :, hh].reshape(n * cap, HD)
        d_o = d_attn[:, :, hh].reshape(n * cap, HD)
        k, v = keys[:, hh], values[:, hh]
        probs = softmax_rows(mm_t(q, k) / root + bias)
        d_probs = mm_t(d_o, v)
        delta = jnp.sum(d_probs * probs, axis=-1, keepdims=True)
        d_scores = (probs * (d_probs - delta)).astype(BF)
        d_kv[:, hw + h * HD:hw + (h + 1) * HD] = mm_rows(probs.astype(BF), d_o).astype(BF)
        d_k = mm_rows(d_scores, q) / root
        d_kv[:, hh] = turned(d_k, cosine, -sine).astype(BF)


def map_grad_body(normed, d_kv, out, d_cols):
    hw = d_kv.shape[1] // 2

    @pl.when(pl.program_id(0) == 0)
    def _():
        for i in range(hw // 128):
            for c in range(2):
                d_cols[:, (2 * i + c) * 128:(2 * i + c + 1) * 128] = d_kv[:, c * hw + i * 128:c * hw + (i + 1) * 128]

    out[...] = mm_rows(normed[...], d_cols[...]).reshape(out.shape)


def map_grad(normed, d_kv):
    total, features = normed.shape
    both = d_kv.shape[1]
    size, tiles = 256, both // 128
    out = pl.pallas_call(
        map_grad_body, grid=(features // size,),
        out_shape=jax.ShapeDtypeStruct((features, tiles, 128), F32),
        in_specs=[pl.BlockSpec((total, size), lambda i: (0, i)), pl.BlockSpec((total, both), lambda i: (0, 0))],
        out_specs=pl.BlockSpec((size, tiles, 128), lambda i: (i, 0, 0)), scratch_shapes=[VM((total, both), BF)],
        name="map_grad", compiler_params=pltpu.CompilerParams(vmem_limit_bytes=56 * 2**20),
    )(normed, d_kv)
    return out.reshape(features, tiles // 2, 2, 128).transpose(0, 2, 1, 3).reshape(features, 2, both // 2)


def attention_back(i, d_attn, query, keys, values, bias, turn_slots, dq_pre):
    root = math.sqrt(HD)
    dq = []
    for h in range(query.shape[2] // HD):
        hh = slice(h * HD, (h + 1) * HD)
        k = keys[i, :, hh]
        probs = softmax_rows(mm_t(query[i, :, hh], k) / root + bias[i])
        d_probs = mm_t(d_attn[i, :, hh], values[i, :, hh])
        delta = jnp.sum(d_probs * probs, axis=-1, keepdims=True)
        dq.append(mm((probs * (d_probs - delta)).astype(BF), k) / root)
    dq_pre[i] = turned(jnp.concatenate(dq, axis=1), turn_slots[i, :, :HD], -turn_slots[i, :, HD:]).astype(BF)


def tail_body(
    n, d_rows, in_gate, query, bias, turn_slots, q_back, keys, values, meta, cos_t, sin_t,
    x_own, scale, gain_t, d_hidden, hidden, mbr, mlp_gate, mlp_rows, att_rows, gain_mlp_part, wo_hbm, wq_hbm, wk_hbm, wv_hbm,
    d_kv_all, back, gains, d_obr, dq_pre, *scratch,
):
    ring = Ring(n)
    (at_in, d_kv, kc_out, kc_in, kv_keep, kx_out, kx_in, sbuf, sq, sq_in, g_out, g_in, g_sum, d_norm, d_attn, mixed, comb, mlp_t,
     wo, w_q, w_k, w_v, whole, pbuf, pbuf3, cbuf, cbuf3, cin, cin3) = scratch[:29]
    xbuf, xin, dbuf, rbuf, xbuf3, xin3, dbuf3, rbuf3 = scratch[29:37]
    (as_, ar, zs, zr, ws, wr, ys, yr, ks, kr, lxs, lxr, qs, qr, gs, gr, ts, tr, wsem) = scratch[37:56]
    sems, sems3, fsems = scratch[56:62], scratch[62:68], scratch[68:]
    loads = [pltpu.make_async_copy(a, b, wsem.at[i]) for i, (a, b) in enumerate(
        [(wo_hbm, wo), (wq_hbm, w_q), (wk_hbm, w_k), (wv_hbm, w_v)])]
    for c in loads:
        c.start()
    rows, width = x_own.shape
    cw = width // NC
    slots, cap = query.shape[0] * query.shape[1], query.shape[1]
    all_keys, all_values = keys, values
    hw = keys.shape[2]
    features = 4 * width
    keys, values, meta, scale = keys.at[ring.g], values.at[ring.g], meta.at[ring.g], scale.at[ring.g]
    z, y = ring.g // 2, lax.rem(ring.g, 2)
    depth = n // 2
    ring.greet_everyone()

    red3 = ChunkReduce(ring, lambda j: mbr[j].astype(F32), whole, pbuf3, (cbuf3, xbuf3, dbuf3), (cin3, xin3, rbuf3), sems3)
    for j in range(NC):
        red3.core(j)
    for e in range(n):
        d_obr[e] = (d_rows[e].astype(F32) * in_gate[e]).astype(BF)
    loads[0].wait()
    d_attn[...] = mm_t(d_obr[...].reshape(slots, features), wo[...]).astype(BF).reshape(d_attn.shape)
    arrive = []
    for o in range(1, n):
        d = ring.to(o)
        arrive.append(ring.send(d_attn.at[d], at_in.at[ring.g], as_.at[o], ar.at[o], d, ring.t))
    at_in[ring.g] = d_attn[ring.g]

    def group_back(i, _):
        attention_back(i, d_attn, query, all_keys, all_values, bias, turn_slots, dq_pre)
        return _

    red3.cross(0)
    lax.fori_loop(0, n // 2, group_back, 0)
    for j in range(1, NC):
        red3.cross(j)
    lax.fori_loop(n // 2, n, group_back, 0)
    loads[1].wait()

    def back_cols(j):
        dq = dq_pre[...].reshape(slots, hw)
        return jnp.concatenate([mm_t(dq, w_q[q * width + j * cw:q * width + (j + 1) * cw, :]) for q in range(4)], axis=1)

    red = ChunkReduce(ring, back_cols, whole, pbuf, (cbuf, xbuf, dbuf), (cin, xin, rbuf), sems)
    for j in range(NC):
        red.core(j)
        if j:
            red.cross(j - 1)
    red.cross(NC - 1)
    for c in arrive:
        c.wait_recv()
    keys_back_body(q_back, at_in, keys, values, meta, cos_t, sin_t, d_kv, cap=cap)

    halves = [(c, slice(c * hw, (c + 1) * hw)) for c in range(2)]
    mine = d_kv_all.at[ring.g]
    mine[...] = d_kv[...]
    pairs = lambda zz, yy: zz * 2 + yy
    across = []

    def unit(zz, c):
        return d_kv_all.at[pairs(zz, y), :, pl.ds(c * hw, hw)]

    def step(up, hop, c, first):
        zz = z - hop if up else z + hop
        here = zz >= 0 if up else zz < depth
        ss, rs = (zs, zr) if up else (ws, wr)
        on, back_to = (z + 1, z - 1) if up else (z - 1, z + 1)

        @pl.when(here)
        def _():
            ref = unit(zz, c)
            if not first:
                rcopy(ref, ref, ss.at[hop - 1, c], rs.at[hop - 1, c], pairs(back_to, y), ring.t).wait_recv()

            @pl.when((on < depth) if up else (on >= 0))
            def _():
                rcopy(ref, ref, ss.at[hop, c], rs.at[hop, c], pairs(on, y), ring.t).start()

            if up or not first:
                rcopy(ref, ref, ys.at[zz, c], yr.at[zz, c], pairs(z, 1 - y), ring.t).start()

    def drain(up, hop, c):
        zz = z - hop if up else z + hop
        here = zz >= 0 if up else zz < depth
        ss, rs = (zs, zr) if up else (ws, wr)
        on = z + 1 if up else z - 1

        @pl.when(here & ((on < depth) if up else (on >= 0)))
        def _():
            ref = unit(zz, c)
            rcopy(ref, ref, ss.at[hop, c], rs.at[hop, c], pairs(on, y), ring.t).wait_send()

    def spread(hop):
        for c, _ in halves:
            step(True, hop, c, hop == 0)
            step(False, hop, c, hop == 0)

    spread(0)
    red.home(0)
    red.home(1)
    comb[...] = att_rows[...].T
    mlp_t[...] = mlp_rows[...].T
    loads[2].wait()
    loads[3].wait()

    def kv_part(q):
        at = cols_of(q, 0, width, width)
        return mm_t(d_kv[:, :hw], w_k[at, :]) + mm_t(d_kv[:, hw:], w_v[at, :])

    kc_out[0] = kv_part(ring.tc).astype(BF)
    kc_out[1] = kv_part(ring.tcx).astype(BF)
    kc = ring.send(kc_out, kc_in, ks, kr, ring.g, ring.tc)
    red.home(2)
    kv_keep[1] = kv_part(ring.tx)
    kc.wait_recv()
    kx_out[...] = (kv_keep[1] + kc_in[1].astype(F32)).astype(BF)
    kx = ring.send(kx_out, kx_in, lxs, lxr, ring.g, ring.tx)
    kv_keep[0] = kv_part(ring.t)
    red.home(3)
    spread(1)
    for j in range(NC):
        red3.home(j)
    kx.wait_recv()
    local = kv_keep[0] + kc_in[0].astype(F32) + kx_in[...].astype(F32)
    squares = jnp.zeros((8, rows), F32)
    for j in range(NC):
        cc = slice(j * cw, (j + 1) * cw)
        got = mm(comb[...], red.rows(j)) + local[:, cc]
        d_norm[:, cc] = got
        high, low = split_bf(x_own[:, cc] * gain_t[:, cc] * got)
        ones = jnp.ones((8, cw), BF)
        squares = squares + mm_t(ones, high) + mm_t(ones, low)
        g_out[:, cc] = jnp.concatenate([
            gain_mlp_part[:1, cc], jnp.sum(got * x_own[:, cc] * scale[...], axis=0, keepdims=True), jnp.zeros((6, cw), F32)], axis=0)
    sq[...] = squares
    spread(2)
    shared = [ring.send(sq, sq_in.at[i], qs.at[i], qr.at[i], ring.g, q) for i, q in enumerate([ring.tc, ring.tx, ring.tcx])]
    sums = []
    for o in range(1, n):
        sums.append(ring.send(g_out, g_in.at[ring.g], gs.at[o], gr.at[o], ring.to(o), ring.t))
    g_in[ring.g] = g_out[...]
    for j in range(NC):
        cc = slice(j * cw, (j + 1) * cw)
        high, low = split_bf(red3.rows(j).astype(F32) * mlp_gate[...])
        mixed[:, cc] = (hidden[:, cc] + mm(mlp_t[...], high) + mm(mlp_t[...], low)).astype(BF)
    for c in shared:
        c.wait_recv()
    total = (sq[...] + sq_in[0] + sq_in[1] + sq_in[2])[:1]
    eye = iota((rows, rows), 0) == iota((rows, rows), 1)
    mean = jnp.sum(jnp.where(eye, total, 0.0), axis=1, keepdims=True) / features
    s = scale[...]
    in_grad = d_hidden[...] + s * (gain_t[...] * d_norm[...]) - x_own[...] * (s * s * s * mean)
    per = rows // n
    fin = ChunkGather(
        ring, lambda j, q, e: back.at[slice(None) if e is None else e, :, cols_of(q, 0, width, width)], sbuf, fsems)
    fin.out(0, jnp.concatenate(
        [mixed[...].reshape(n, per, width), in_grad.astype(BF).reshape(n, per, width)], axis=1))
    for c in sums:
        c.wait_recv()
    g_sum[...] = functools.reduce(lambda a, b: a + b, [g_in[e] for e in range(n)])
    at_t = cols_of(ring.t, 0, width, width)
    gains[:, at_t] = g_sum[...]
    told = [ring.send(g_sum, gains.at[:, at_t], ts.at[i], tr.at[i], ring.g, q) for i, q in enumerate([ring.tc, ring.tx, ring.tcx])]
    fin.cross(0)
    spread(3)
    fin.core(0)
    fin.here(0)
    for c in told:
        c.wait_recv()
    for c, _ in halves:
        for zz in range(depth):
            ref = d_kv_all.at[pairs(zz, 1 - y), :, pl.ds(c * hw, hw)]
            rcopy(ref, ref, ys.at[zz, c], yr.at[zz, c], pairs(z, 1 - y), ring.t).wait()
        for hop in range(depth - 1):
            drain(True, hop, c)
            drain(False, hop, c)
    ring.finish()
    fin.sent()
    for r in (red, red3):
        r.sent_core()
        r.sent_rest()


def layer_tail(args, weights, n, cid):
    d_rows, query, keys, x_own = args[0], args[2], args[6], args[11]
    rows, width = x_own.shape
    cap, hw = query.shape[1:]
    cw, features, depth = width // NC, 4 * width, n // 2
    slots = n * cap
    sds = jax.ShapeDtypeStruct
    per = 2 * rows // n
    one, two = VM((NC, n, cap, cw), BF), VM((NC, 2, n, cap, cw), BF)
    part = VM((NC, 2, n, cap, cw), F32)
    any_, vm = pl.BlockSpec(memory_space=pl.ANY), pl.BlockSpec(memory_space=VM)
    return pl.pallas_call(
        functools.partial(tail_body, n),
        out_shape=(
            sds((n, rows, 2 * hw), BF), sds((n, per, features), BF), sds((8, features), F32),
            sds((n, cap, features), BF), sds((n, cap, hw), BF)),
        in_specs=[vm] * len(args) + [any_] * 4, out_specs=[vm] * 5,
        scratch_shapes=[
            VM((n, cap, hw), BF), VM((rows, 2 * hw), BF), VM((2, rows, width), BF), VM((2, rows, width), BF),
            VM((2, rows, width), F32), VM((rows, width), BF), VM((rows, width), BF), VM((1, n, per, width), BF),
            VM((8, rows), F32), VM((3, 8, rows), F32), VM((8, width), F32), VM((n, 8, width), F32), VM((8, width), F32),
            VM((rows, width), F32), VM((n, cap, hw), BF), VM((rows, width), BF), VM((rows, slots), BF), VM((rows, slots), BF),
            VM((hw, features), BF), VM((features, hw), BF), VM((features, hw), BF), VM((features, hw), BF),
            VM((slots, 4 * cw), F32), part, part, two, two, two, two] + [one] * 8 + [
            DMA((n,)), DMA((n,)), DMA((depth, 2)), DMA((depth, 2)), DMA((depth, 2)), DMA((depth, 2)), DMA((depth, 2)), DMA((depth, 2)),
            DMA, DMA, DMA, DMA, DMA((3,)), DMA((3,)), DMA((n,)), DMA((n,)), DMA((3,)), DMA((3,)), DMA((4,))]
        + REDUCE_SEMS(NC, n) * 2 + GATHER_SEMS(1, n),
        name="layer_tail", compiler_params=pltpu.CompilerParams(
            collective_id=cid, has_side_effects=True, vmem_limit_bytes=62 * 2**20),
    )(*args, *weights)


def start_body(
    n, tokens, out_grad, place_r, place_c, meta_w, w_kv, x_all, dy_own, meta_all, sorter_out,
    att_rows, att_gate, mlp_rows, mlp_gate, in_gate, w_k, w_v, x_own, dy_part, dy_send, dy_slots, *sems,
):
    ms, mr, dys, dyr, dps, dpr, zs, zr, ws, wr, ys, yr, xs, xr, cs, cr = sems
    ring = Ring(n)
    g, t = ring.g, ring.t
    rows, features = tokens.shape
    width, per = features // 4, rows // n
    z, y, depth = g // 2, lax.rem(g, 2), n // 2
    pairs = lambda zz, yy: zz * 2 + yy
    ring.greet_all()

    def arrival(row, col):
        g_row, g_col = row // rows, col // rows
        before = (g_col == g_row) & (iota((rows, rows), 0) < iota((rows, rows), 1))
        return g_row, jnp.sum(jnp.where(before, 1.0, 0.0), axis=0, keepdims=True).astype(jnp.int32)

    col_g = jnp.sum(jnp.where(iota((rows, n), 1) == g, place_c[...], 0), axis=1, keepdims=True)
    g_row, rank = arrival(place_r[pl.ds(g, 1), :], col_g)
    sorter = jnp.where(g_row * per + rank == iota((rows, rows), 0), 1.0, 0.0).astype(BF)
    sorter_out[...] = sorter

    half = width // 2
    chunks = [("b", t, half), ("a", t, 0), ("c", ring.tx, 0)]
    cols = [pl.ds(pl.multiple_of(q * width + off, half), half) for _, q, off in chunks]
    for cc in cols:
        x_all[:, g, :, cc] = mm(sorter, tokens[:, cc]).astype(BF).reshape(n, per, half)

    def unit(zz, yy, c):
        return x_all.at[:, pairs(zz, yy), :, cols[c]]

    def cross(zz, yy, c):
        if chunks[c][0] == "b":
            ref = unit(zz, yy, c)
            rcopy(ref, ref, xs.at[pairs(zz, yy)], xr.at[pairs(zz, yy)], g, ring.tx).start()

    def hop_on(up, hop, c):
        zz = z - hop if up else z + hop
        here = zz >= 0 if up else zz < depth
        ss, rs = (zs, zr) if up else (ws, wr)
        on, source = (z + 1, z - 1) if up else (z - 1, z + 1)

        @pl.when(here)
        def _():
            ref = unit(zz, y, c)
            if hop:
                rcopy(ref, ref, ss.at[hop - 1, c], rs.at[hop - 1, c], pairs(source, y), t).wait_recv()

            @pl.when((on < depth) if up else (on >= 0))
            def _():
                rcopy(ref, ref, ss.at[hop, c], rs.at[hop, c], pairs(on, y), t).start()

            if up or hop:
                rcopy(ref, ref, ys.at[zz, c], yr.at[zz, c], pairs(z, 1 - y), t).start()
                cross(zz, y, c)

    def from_y(zz, c):
        ref = unit(zz, 1 - y, c)
        rcopy(ref, ref, ys.at[zz, c], yr.at[zz, c], pairs(z, 1 - y), t).wait_recv()
        cross(zz, 1 - y, c)

    count = range(len(chunks))
    for c in count:
        hop_on(True, 0, c)
        hop_on(False, 0, c)

    spot = jnp.zeros((rows, rows), F32)
    for s in range(n):
        row, col = place_r[s:s + 1, :], place_c[:, s:s + 1]
        s_row, s_rank = arrival(row, col)
        put = jnp.where((s_row == g) & (s_rank + s * per == iota((rows, rows), 0)), 1.0, 0.0).astype(BF)
        work = jnp.where(col - col // rows * rows == iota((rows, rows), 1), 1.0, 0.0).astype(BF)
        spot = spot + mm(put, work)
    spot = spot.astype(BF)
    left, moved = meta_w[...], 0.0
    for _ in range(3):
        piece = left.astype(BF)
        moved = moved + mm_t(piece, spot)
        left = left - piece.astype(F32)
    meta_all[g] = moved
    sent = [ring.send(meta_all.at[g], meta_all.at[g], ms.at[o], mr.at[o], ring.to(o), t) for o in range(1, n)]

    mine = pl.ds(pl.multiple_of(t * width, width), width)
    dy_send[...] = mm(sorter, out_grad[:, mine]).astype(BF).reshape(n, per, width)
    dealt = [ring.send(dy_send.at[ring.to(o)], dy_own.at[g], dys.at[o], dyr.at[o], ring.to(o), t) for o in range(1, n)]
    dy_own[g] = dy_send[g]

    def split(i):
        rr = slice(i * 256, (i + 1) * 256)
        w_k[rr] = w_kv[rr, 0, :]
        w_v[rr] = w_kv[rr, 1, :]

    def tables(first, gate, out_rows, out_gate):
        m = meta_all[g]
        for e in range(n):
            out_rows[e] = slot_table(m, first, float(e), CAP)
            out_gate[e] = slot_gates(m, first, gate, float(e), out_rows[e])

    def hops(k):
        for c in count:
            hop_on(True, k, c)
            hop_on(False, k, c)

    tables(META["mr0"], META["mg0"], mlp_rows, mlp_gate)
    split(0)
    hops(1)
    for c in dealt:
        c.wait_recv()
    slots = mm(mlp_rows[...].reshape(n * CAP, rows), dy_own[...].reshape(rows, width)).astype(BF)
    dy_slots[...] = slots.reshape(n, CAP, width)
    parts = [ring.send(dy_slots.at[ring.to(o)], dy_part.at[g], dps.at[o], dpr.at[o], ring.to(o), t) for o in range(1, n)]
    dy_part[g] = dy_slots[g]
    split(1)
    split(2)
    hops(2)
    split(3)
    tables(META["ar0"], META["ag0"], att_rows, att_gate)
    hops(3)
    split(4)
    for c in sent:
        c.wait_recv()
    from_y(0, 0)
    from_y(1, 0)
    me = g.astype(F32)
    for e in range(n):
        m = meta_all[e]
        in_gate[0, e] = slot_gates(m, META["ar0"], META["ag0"], me, slot_table(m, META["ar0"], me, CAP))
        in_gate[1, e] = slot_gates(m, META["mr0"], META["mg0"], me, slot_table(m, META["mr0"], me, CAP))
    from_y(2, 0)
    from_y(3, 0)
    split(5)

    def whole(q, off):
        return x_all.at[:, :, :, pl.ds(pl.multiple_of(q * width + off, half), half)]

    cores = [ring.send(whole(t, half), whole(t, half), cs.at[0], cr.at[0], g, ring.tc)]
    for c in (1, 2):
        split(5 + c)
        for zz in range(depth):
            from_y(zz, c)
        ref = whole(chunks[c][1], 0)
        cores.append(ring.send(ref, ref, cs.at[c], cr.at[c], g, ring.tc))
    for u in range(n):
        ref = x_all.at[:, u, :, pl.ds(pl.multiple_of(ring.tx * width + half, half), half)]
        rcopy(ref, ref, xs.at[u], xr.at[u], g, ring.tx).wait_recv()
    cores.append(ring.send(whole(ring.tx, half), whole(ring.tx, half), cs.at[3], cr.at[3], g, ring.tc))
    x_own[...] = x_all[g, :, :, mine].reshape(rows, width).astype(F32)
    for c in cores + parts:
        c.wait_recv()
    for u in range(n):
        ref = x_all.at[:, u, :, cols[0]]
        rcopy(ref, ref, xs.at[u], xr.at[u], g, ring.tx).wait_send()
    for c in count:
        for zz in range(depth):
            ref = unit(zz, y, c)
            rcopy(ref, ref, ys.at[zz, c], yr.at[zz, c], pairs(z, 1 - y), t).wait_send()
        for hop in range(depth - 1):
            for up in (True, False):
                zz = z - hop if up else z + hop
                on = z + 1 if up else z - 1
                ss, rs = (zs, zr) if up else (ws, wr)

                @pl.when((zz >= 0) & (on < depth) if up else (zz < depth) & (on >= 0))
                def _(zz=zz, on=on, ss=ss, rs=rs, hop=hop, c=c):
                    ref = unit(zz, y, c)
                    rcopy(ref, ref, ss.at[hop, c], rs.at[hop, c], pairs(on, y), t).wait_send()
    ring.finish()


def slot_gates(meta, first, gate, name, table):
    per_token = (jnp.where(meta[first:first + 1] == name, meta[gate:gate + 1], 0.0)
                 + jnp.where(meta[first + 1:first + 2] == name, meta[gate + 1:gate + 2], 0.0))
    return jnp.sum(table.astype(F32) * per_token, axis=1, keepdims=True)


def layer_start(tokens, out_grad, place_r, place_c, meta_w, w_kv, n, cid):
    rows, features = tokens.shape
    width, per, depth = features // 4, rows // n, n // 2
    hw = w_kv.shape[2]
    sds = jax.ShapeDtypeStruct
    vm = pl.BlockSpec(memory_space=VM)
    return pl.pallas_call(
        functools.partial(start_body, n),
        out_shape=(
            sds((n, n, per, features), BF), sds((n, per, width), BF), sds((n, 16, rows), F32), sds((rows, rows), BF),
            sds((n, CAP, rows), BF), sds((n, CAP, 1), F32), sds((n, CAP, rows), BF), sds((n, CAP, 1), F32),
            sds((2, n, CAP, 1), F32), sds((features, hw), BF), sds((features, hw), BF), sds((rows, width), F32),
            sds((n, CAP, width), BF)),
        in_specs=[vm] * 6, out_specs=[vm] * 13,
        scratch_shapes=[VM((n, per, width), BF), VM((n, CAP, width), BF)] + [DMA((n,))] * 6 + [DMA((depth, 3))] * 6 + [DMA((n,))] * 2 + [DMA((4,))] * 2,
        name="layer_start", compiler_params=params(cid),
    )(tokens, out_grad, place_r, place_c, meta_w, w_kv)


def tile_list(size, step):
    return [(a, min(step, size - a)) for a in range(0, size, step)]


class ChunkReduce:
    def __init__(self, ring, partial, whole, pbuf, sent, got, sems):
        self.ring, self.partial, self.whole, self.pbuf = ring, partial, whole, pbuf
        self.cbuf, self.xbuf, self.dbuf = sent
        self.cin, self.xin, self.rbuf = got
        cs, cr, xs, xr, ds, dr = sems
        k, (nc, n, _, _) = ring, self.xbuf.shape
        self.c = [rcopy(self.cbuf.at[j], self.cin.at[j], cs.at[j], cr.at[j], k.g, k.tc) for j in range(nc)]
        self.x = [rcopy(self.xbuf.at[j], self.xin.at[j], xs.at[j], xr.at[j], k.g, k.tx) for j in range(nc)]
        self.d = [
            [rcopy(self.dbuf.at[j, k.to(o)], self.rbuf.at[j, k.g], ds.at[j, o], dr.at[j, o], k.to(o), k.t) for o in range(1, n)]
            for j in range(nc)]

    def core(self, j):
        k = self.ring
        n, r, cw = self.xbuf.shape[1:]
        self.whole[...] = self.partial(j)
        take = lambda q: self.whole[:, pl.ds(pl.multiple_of(q * cw, cw), cw)].reshape(n, r, cw)
        self.cbuf[j, 0] = take(k.tc).astype(BF)
        self.cbuf[j, 1] = take(k.tcx).astype(BF)
        self.c[j].start()
        self.pbuf[j, 0] = take(k.t)
        self.pbuf[j, 1] = take(k.tx)

    def cross(self, j):
        self.c[j].wait_recv()
        self.xbuf[j] = (self.pbuf[j, 1] + self.cin[j, 1].astype(F32)).astype(BF)
        self.x[j].start()

    def home(self, j):
        g = self.ring.g
        self.x[j].wait_recv()
        self.dbuf[j] = (self.pbuf[j, 0] + self.cin[j, 0].astype(F32) + self.xin[j].astype(F32)).astype(BF)
        for c in self.d[j]:
            c.start()
        self.rbuf[j, g] = self.dbuf[j, g]

    def rows(self, j):
        for c in self.d[j]:
            c.wait_recv()
        return self.rbuf[j].reshape(-1, self.rbuf.shape[-1])

    def sent_core(self):
        for c in self.c:
            c.wait_send()

    def sent_rest(self):
        for c in self.x + [c for row in self.d for c in row]:
            c.wait_send()


class ChunkGather:
    def __init__(self, ring, place, sbuf, sems):
        self.ring, self.place, self.sbuf = ring, place, sbuf
        ss, rs, xs, xr, cs, cr, c2s, c2r = sems
        k, (nc, n, _, cw) = ring, sbuf.shape
        self.d = [
            [rcopy(sbuf.at[j, k.to(o)], place(j, k.t, k.g), ss.at[j, o], rs.at[j, o], k.to(o), k.t) for o in range(1, n)]
            for j in range(nc)]
        pair = lambda j, q, a, b, to: rcopy(place(j, q, None), place(j, q, None), a.at[j], b.at[j], k.g, to)
        self.x = [pair(j, k.t, xs, xr, k.tx) for j in range(nc)]
        self.c = [pair(j, k.t, cs, cr, k.tc) for j in range(nc)]
        self.c2 = [pair(j, k.tx, c2s, c2r, k.tc) for j in range(nc)]

    def out(self, j, rows):
        self.sbuf[j] = rows.reshape(self.sbuf.shape[1:])
        for c in self.d[j]:
            c.start()
        self.place(j, self.ring.t, self.ring.g)[...] = self.sbuf[j, self.ring.g]

    def cross(self, j):
        for c in self.d[j]:
            c.wait_recv()
        self.x[j].start()
        self.c[j].start()

    def core(self, j):
        self.x[j].wait_recv()
        self.c2[j].start()

    def here(self, j):
        self.c[j].wait_recv()
        self.c2[j].wait_recv()

    def sent(self):
        for c in [c for row in self.d for c in row] + self.x + self.c + self.c2:
            c.wait_send()


def middle_body(
    n, attn, x_own, att_rows, att_gate, mlp_rows, dy_own, gain_p, gain_t, d_mbr, query, wo_hbm, wg_hbm, wu_hbm, wd_hbm,
    d_rows, d_hidden, hidden, mbr, gain_part, n2, inner, d_gate, d_up, q_back, *scratch,
):
    (wo, wg, wu, wd, hid, att_t, mlp_t, whole, gate_acc, up_acc, d_in, pbuf, cbuf, xbuf, dbuf,
     cin1, xin1, rb1, cin2, xin2, rb2, sb1, sb2, sq, sq_in, r_own, r_in, r_to, r_back, s_col) = scratch[:30]
    wsem, qs, qr, as_, ar, rss, rsr, rds, rdr = scratch[30:39]
    s1, s2s, g1, g2 = scratch[39:45], scratch[45:51], scratch[51:59], scratch[59:67]
    ring = Ring(n)
    g, t = ring.g, ring.t
    rows, width = x_own.shape
    cw = width // NC
    features, ff = 4 * width, wg.shape[1]
    slots = attn.shape[0]

    loads = {"wo": [], "wg": [], "wu": []}
    for j in range(NC):
        for q in range(4):
            to, at = pl.ds((j * 4 + q) * cw, cw), pl.ds(q * width + j * cw, cw)
            i = j * 4 + q
            loads["wo"].append(pltpu.make_async_copy(wo_hbm.at[:, at], wo.at[:, to], wsem.at[0, i]))
            loads["wg"].append(pltpu.make_async_copy(wg_hbm.at[at, :], wg.at[to, :], wsem.at[1, i]))
            loads["wu"].append(pltpu.make_async_copy(wu_hbm.at[at, :], wu.at[to, :], wsem.at[2, i]))
    loads["wd"] = [pltpu.make_async_copy(wd_hbm, wd, wsem.at[3, 0])]
    for name in ("wo", "wd", "wg", "wu"):
        for c in loads[name]:
            c.start()

    def loaded(name):
        for c in loads[name]:
            c.wait()

    chunk = lambda j: pl.ds(j * 4 * cw, 4 * cw)
    att_t[...] = att_rows[...].T
    mlp_t[...] = mlp_rows[...].T
    ring.greet_everyone()
    asked = [rcopy(query.at[ring.to(o)], q_back.at[g], as_.at[o], ar.at[o], ring.to(o), t) for o in range(1, n)]

    red1 = ChunkReduce(
        ring, lambda j: mm(attn[...], wo[:, chunk(j)]), whole, pbuf, (cbuf, xbuf, dbuf), (cin1, xin1, rb1), s1)
    gat1 = ChunkGather(
        ring, lambda j, q, e: hid.at[j, slice(None) if e is None else e, :, pl.ds(pl.multiple_of(q * cw, cw), cw)], sb1, g1)
    shared = [rcopy(sq, sq_in.at[i], qs.at[i], qr.at[i], g, q) for i, q in enumerate([ring.tc, ring.tx, ring.tcx])]
    ones = jnp.ones((8, cw), BF)

    def hidden_chunk(j):
        high, low = split_bf(red1.rows(j).astype(F32) * att_gate[...])
        got = x_own[:, j * cw:(j + 1) * cw] + mm(att_t[...], high) + mm(att_t[...], low)
        hidden[:, j * cw:(j + 1) * cw] = got
        gat1.out(j, mm(mlp_rows[...], got.astype(BF)).astype(BF))
        high, low = split_bf(got * got)
        squares = mm_t(ones, high) + mm_t(ones, low)
        sq[...] = squares if j == 0 else sq[...] + squares
        if j == NC - 1:
            for c in shared:
                c.start()

    pieces = tile_list(ff, 512)

    def d_inner(i):
        if i == 0:
            loaded("wd")
        a, w = pieces[i]
        d_in[:, a:a + w] = mm_t(d_mbr[...], wd[a:a + w, :])

    def absorb(j):
        gat1.here(j)
        v = hid[j].reshape(slots, 4 * cw).astype(F32)
        part = jnp.sum(v * v, axis=1, keepdims=True)
        s_col[...] = part if j == 0 else s_col[...] + part
        u = (v * gain_p[:, j * 4 * cw:(j + 1) * 4 * cw]).astype(BF)
        for a, w in pieces:
            cc = slice(a, a + w)
            gate, up = mm(u, wg[chunk(j), cc]), mm(u, wu[chunk(j), cc])
            gate_acc[:, cc] = gate if j == 0 else gate_acc[:, cc] + gate
            up_acc[:, cc] = up if j == 0 else up_acc[:, cc] + up

    loaded("wo")
    for j in range(NC):
        red1.core(j)
        if j:
            red1.cross(j - 1)
    red1.cross(NC - 1)
    plan = [(2 * j, 0, functools.partial(red1.home, j)) for j in range(NC)]
    plan += [(2 * j + 3, 1, functools.partial(hidden_chunk, j)) for j in range(NC)]
    plan += [(2 * j + 7, 2, functools.partial(gat1.cross, j)) for j in range(NC)]
    plan += [(2 * j + 9, 3, functools.partial(gat1.core, j)) for j in range(NC)]
    plan += [(2 * i + 1.5, 4, functools.partial(d_inner, i)) for i in range(len(pieces))]
    plan += [(2 * j + 10.5, 5, functools.partial(absorb, j)) for j in range(NC)]
    plan += [(10.2, 0, lambda: (loaded("wg"), loaded("wu")))]
    plan += [(9.5, 0, lambda: [c.start() for c in asked])]
    for _, _, run in sorted(plan, key=lambda s: s[:2]):
        run()

    s_col[...] = lax.rsqrt(s_col[...] / features + EPSILON)
    r_own[...] = jnp.zeros_like(r_own)

    def units(at, size):
        s = s_col[...]
        gate, up, d = gate_acc[:, at] * s, up_acc[:, at] * s, d_in[:, at]
        sig = jax.nn.sigmoid(gate)
        silu = gate * sig
        inner[:, at] = (silu * up).astype(BF)
        du = (d * silu).astype(BF)
        dg = (d * up * sig * (1.0 + gate * (1.0 - sig))).astype(BF)
        d_up[:, at] = du
        d_gate[:, at] = dg
        r_own[...] += mm_t(jnp.ones((8, size), BF), (gate * dg.astype(F32) + up * du.astype(F32)).astype(BF))

    def unit_tile(i, _):
        units(pl.ds(pl.multiple_of(i * 128, 128), 128), 128)
        return _

    lax.fori_loop(0, ff // 128, unit_tile, 0)
    red1.sent_core()
    red1.sent_rest()
    for c in shared:
        c.wait_recv()
    total = (sq[...] + sq_in[0] + sq_in[1] + sq_in[2])[:1]
    eye = iota((rows, rows), 0) == iota((rows, rows), 1)
    scale = lax.rsqrt(jnp.sum(jnp.where(eye, total, 0.0), axis=1, keepdims=True) / features + EPSILON)

    told = [rcopy(r_own, r_in.at[i], rss.at[i], rsr.at[i], g, q) for i, q in enumerate([ring.tc, ring.tx, ring.tcx])]
    for c in told:
        c.start()
    half = lambda d: pl.ds(pl.multiple_of(d // 2 * 128, 128), 128)
    pairs = [rcopy(r_to.at[:, half(ring.to(o))], r_back.at[g], rds.at[o], rdr.at[o], ring.to(o), t) for o in range(1, n)]

    def share_r():
        for c in told:
            c.wait_recv()
        r_to[...] = r_own[...] + r_in[0] + r_in[1] + r_in[2]
        for c in pairs:
            c.start()
        r_back[g] = r_to[:, half(g)]

    total_r = {}

    def take_r():
        for c in pairs:
            c.wait_recv()
        odd = lax.rem(g, 2) == 1
        got = jnp.concatenate([jnp.where(odd, r_back[e][:, 64:], r_back[e][:, :64]) for e in range(n)], axis=1)
        high, low = split_bf(got)
        total_r[0] = (mm_t(mlp_t[...], high) + mm_t(mlp_t[...], low))[:, :1] / features

    red2 = ChunkReduce(
        ring, lambda j: mm_t(d_gate[...], wg[chunk(j), :]) + mm_t(d_up[...], wu[chunk(j), :]), whole, pbuf,
        (cbuf, xbuf, dbuf), (cin2, xin2, rb2), s2s)
    gat2 = ChunkGather(
        ring, lambda j, q, e: d_rows.at[slice(None) if e is None else e, :, cols_of(q, j, width, cw)], sb2, g2)

    def mixed_cols(j):
        for q in range(4):
            mbr[j, :, q * cw:(q + 1) * cw] = mm(inner[...], wd[:, q * width + j * cw:q * width + (j + 1) * cw]).astype(BF)

    def d_hidden_chunk(j):
        got = red2.rows(j)
        if j == 0:
            take_r()
        cc = slice(j * cw, (j + 1) * cw)
        h = hidden[:, cc]
        d_n = mm(mlp_t[...], got)
        d_h = dy_own[:, cc].astype(F32) + scale * (gain_t[:, cc] * d_n) - h * (scale * scale) * total_r[0]
        d_hidden[:, cc] = d_h
        gain_part[:, cc] = jnp.broadcast_to(jnp.sum(d_n * h * scale, axis=0, keepdims=True), (8, cw))
        gat2.out(j, mm(att_rows[...], d_h.astype(BF)).astype(BF))

    def keep_normed(j):
        for q in range(4):
            at, to = slice((j * 4 + q) * cw, (j * 4 + q + 1) * cw), slice(q * width + j * cw, q * width + (j + 1) * cw)
            v = hid[j, :, :, q * cw:(q + 1) * cw].reshape(slots, cw).astype(F32)
            n2[:, to] = (v * s_col[...] * gain_p[:, at]).astype(BF)

    for j in range(NC):
        red2.core(j)
        if j == 0:
            share_r()
        else:
            red2.cross(j - 1)
    red2.cross(NC - 1)
    plan = [(2 * j, 0, functools.partial(red2.home, j)) for j in range(NC)]
    plan += [(2 * j + 3, 1, functools.partial(d_hidden_chunk, j)) for j in range(NC)]
    plan += [(2 * j + 7, 2, functools.partial(gat2.cross, j)) for j in range(NC)]
    plan += [(2 * j + 9, 3, functools.partial(gat2.core, j)) for j in range(NC)]
    plan += [(2 * j + 1.5, 4, functools.partial(keep_normed, j)) for j in range(NC)]
    plan += [(2 * j + 4.5, 5, functools.partial(mixed_cols, j)) for j in range(NC)]
    for _, _, run in sorted(plan, key=lambda s: s[:2]):
        run()
    for c in asked:
        c.wait_recv()
    q_back[g] = query[g]
    for j in range(NC):
        gat2.here(j)
    for c in asked + shared + told + pairs:
        c.wait_send()
    gat1.sent()
    gat2.sent()
    red2.sent_core()
    red2.sent_rest()


def middle(attn, x_own, att_rows, att_gate, mlp_rows, dy_own, gain, gain_t, d_mbr, query, wo, wg, wu, wd, n, cid):
    slots, (rows, width) = attn.shape[0], x_own.shape
    r, cw, features, ff, hw = slots // n, width // NC, 4 * width, wg.shape[1], attn.shape[1]
    gain_p = gain.reshape(4, NC, cw).transpose(1, 0, 2).reshape(1, features)
    any_, vm = pl.BlockSpec(memory_space=pl.ANY), pl.BlockSpec(memory_space=VM)
    sds = jax.ShapeDtypeStruct
    one, two = VM((NC, n, r, cw), BF), VM((NC, 2, n, r, cw), BF)
    return pl.pallas_call(
        functools.partial(middle_body, n),
        out_shape=(
            sds((n, r, features), BF), sds((rows, width), F32), sds((rows, width), F32), sds((NC, slots, 4 * cw), BF), sds((8, width), F32),
            sds((slots, features), BF), sds((slots, ff), BF), sds((slots, ff), BF), sds((slots, ff), BF), sds((n, r, hw), BF)),
        in_specs=[vm] * 10 + [any_] * 4, out_specs=[vm] * 10,
        scratch_shapes=[
            VM((hw, features), BF), VM((features, ff), BF), VM((features, ff), BF), VM((ff, features), BF),
            VM((NC, n, r, 4 * cw), BF), VM((rows, slots), BF), VM((rows, slots), BF),
            VM((slots, 4 * cw), F32), VM((slots, ff), F32), VM((slots, ff), F32), VM((slots, ff), F32),
            VM((NC, 2, n, r, cw), F32), two, one, one]
        + [two, one, one] * 2 + [one, one]
        + [VM((8, rows), F32), VM((3, 8, rows), F32), VM((8, slots), F32), VM((3, 8, slots), F32), VM((8, slots), F32),
           VM((n, 8, 128), F32), VM((slots, 1), F32)]
        + [DMA((4, 16)), DMA((3,)), DMA((3,)), DMA((n,)), DMA((n,)), DMA((3,)), DMA((3,)), DMA((n,)), DMA((n,))]
        + REDUCE_SEMS(NC, n) * 2 + GATHER_SEMS(NC, n) * 2,
        name="middle", compiler_params=pltpu.CompilerParams(
            collective_id=cid, has_side_effects=True, vmem_limit_bytes=63 * 2**20),
    )(attn, x_own, att_rows, att_gate, mlp_rows, dy_own, gain_p, gain_t, d_mbr, query, wo, wg, wu, wd)


def fast_local(
    tokens, out_grad, row_place, seq_lengths, att_routes, att_gates, mlp_routes, mlp_gates,
    gain_attn, w_kv, w_query, w_out, gain_mlp, w_gate, w_up, w_down,
):
    rows, features = tokens.shape
    n = lax.axis_size("dp")
    g, t = lax.axis_index("dp"), lax.axis_index("tensor")
    width = features // 4
    per = rows // n
    hw = w_kv.shape[2]
    part = lambda a: lax.dynamic_slice_in_dim(a, t * width, width, a.ndim - 1)
    counting = jnp.arange(rows, dtype=jnp.int32)

    ends = jnp.cumsum(seq_lengths[0])
    segment = jnp.sum((counting[:, None] >= ends[None, :]).astype(jnp.int32), axis=1)
    begins = jnp.sum(
        jnp.where(segment[:, None] == jnp.arange(ends.shape[0])[None, :], (ends - seq_lengths[0])[None, :], 0), axis=1
    )
    carried = jnp.stack(
        [v.astype(F32) for v in (
            att_routes[:, 0], att_routes[:, 1], att_gates[:, 0], att_gates[:, 1],
            mlp_routes[:, 0], mlp_routes[:, 1], mlp_gates[:, 0], mlp_gates[:, 1],
            counting - begins, segment, counting)] + [jnp.zeros((rows,), F32)] * 5)
    place = row_place.reshape(n, rows)
    (x_all, dy_own, meta_all, sorter, att_out, att_gate, mlp_out, mlp_gate, in_gate, w_k, w_v, x_own,
     dy_part) = layer_start(tokens, out_grad, place, place.T, carried, w_kv, n, cid=12)
    x_all, dy_own = x_all.reshape(n, rows, features), dy_own.reshape(rows, width)
    att_rows, mlp_rows = att_out.reshape(n * CAP, rows), mlp_out.reshape(n * CAP, rows)

    cos_t, sin_t = angle_tables(rows)
    normed, picked, keys, values, query, attn, scale_attn, bias, turn_slots, d_mbr = attend(
        x_all, gain_attn[None], w_k, w_v, w_query[0], meta_all, cos_t, sin_t, dy_part, in_gate[1], cid=13)
    normed_flat, picked = normed.reshape(n * rows, features), picked.reshape(n * CAP, features)
    attn = attn.reshape(n * CAP, hw)
    d_mbr = d_mbr.reshape(n * CAP, features)

    gain_mlp_t, gain_attn_t = part(gain_mlp), part(gain_attn)
    d_rows, d_hidden, hidden, mbr, gain_mlp_part, normed2, inner, d_gate, d_up, query_back = middle(
        attn, x_own, att_rows, att_gate.reshape(-1, 1), mlp_rows, dy_own, gain_mlp, gain_mlp_t[None],
        d_mbr, query, w_out[0], w_gate[0], w_up[0], w_down[0], n, cid=9)
    w_gate_grad = mm_rows(normed2, d_gate)[None]
    w_up_grad = mm_rows(normed2, d_up)[None]
    w_down_grad = mm_rows(inner, d_mbr)[None]

    d_kv_all, back, gains, d_obr, dq_pre = layer_tail(
        (d_rows, in_gate[0], query, bias, turn_slots, query_back, keys, values, meta_all, cos_t, sin_t, x_own, scale_attn,
         gain_attn_t[None], d_hidden, hidden, mbr, mlp_gate.reshape(-1, 1), mlp_rows, att_rows, gain_mlp_part),
        (w_out[0], w_query[0], w_k, w_v), n, cid=11)
    d_obr, dq_flat = d_obr.reshape(n * CAP, features), dq_pre.reshape(n * CAP, hw)
    w_out_grad = mm_rows(attn, d_obr)[None]
    w_query_grad = mm_rows(picked, dq_flat)[None]
    w_kv_grad = map_grad(normed_flat, d_kv_all.reshape(n * rows, 2 * hw))
    mixed = mm_rows(sorter, back[:, :per].reshape(rows, features)).astype(BF)
    tokens_grad = mm_rows(sorter, back[:, per:].reshape(rows, features)).astype(BF)
    return (
        mixed, tokens_grad, gains[1], w_kv_grad, w_query_grad, w_out_grad, gains[0],
        w_gate_grad, w_up_grad, w_down_grad,
    )


def solution(mesh):
    placed = (
        P("dp", None),
        P("dp", None),
        P(),
        P("dp", None),
        P("dp", None),
        P("dp", None),
        P("dp", None),
        P("dp", None),
        P(),
        P(None, None, "tensor"),
        P("dp", None, "tensor"),
        P("dp", "tensor", None),
        P(),
        P("dp", None, "tensor"),
        P("dp", None, "tensor"),
        P("dp", "tensor", None),
    )
    dealt = mesh.shape["dp"] == EXPERTS and mesh.shape["tensor"] == 4
    return jax.shard_map(
        fast_local if dealt else local,
        mesh=mesh,
        in_specs=placed,
        out_specs=(
            P("dp", None),
            P("dp", None),
            P(),
            P(None, None, "tensor"),
            P("dp", None, "tensor"),
            P("dp", "tensor", None),
            P(),
            P("dp", None, "tensor"),
            P("dp", None, "tensor"),
            P("dp", "tensor", None),
        ),
        check_vma=False,
    )
```

```python
import functools
import math

import jax
import jax.numpy as jnp
import numpy as np
from jax import lax
from jax.experimental import pallas as pl
from jax.experimental.pallas import tpu as pltpu
from jax.sharding import PartitionSpec as P

HD = 128
ATT_EXPERTS = 8
EXPERTS = 8
CAP = 64


EPSILON = 1e-05
THETA = 10000.0


def inverse_rms(values_in):
    return lax.rsqrt(jnp.mean(values_in * values_in, axis=-1, keepdims=True) + EPSILON)


def norm_backward(inputs, inv_root, gain, incoming):
    weighted = incoming * gain
    inner_mean = jnp.mean(inputs * weighted, axis=-1, keepdims=True)
    return inv_root * weighted - inputs * (inv_root * inv_root * inv_root) * inner_mean


def rotate(vectors, positions, direction):
    half_dim = vectors.shape[-1] // 2
    frequency = jnp.exp(-math.log(THETA) * jnp.arange(half_dim, dtype=jnp.float32) / half_dim)
    angles = positions.astype(jnp.float32)[:, None] * frequency[None, :]
    target = (vectors.shape[0],) + (1,) * (vectors.ndim - 2) + (half_dim,)
    cosine = jnp.cos(angles).reshape(target)
    sine = direction * jnp.sin(angles).reshape(target)
    former = vectors[..., :half_dim]
    latter = vectors[..., half_dim:]
    return jnp.concatenate(
        [former * cosine - latter * sine, latter * cosine + former * sine], axis=-1
    )


def expert_slots(routes, experts, capacity):
    flattened = routes.reshape(-1)
    pair_count = flattened.shape[0]
    one_hot = (flattened[:, None] == jnp.arange(experts, dtype=jnp.int32)[None, :]).astype(
        jnp.int32
    )
    earlier = jnp.cumsum(one_hot, axis=0) - one_hot
    position = jnp.sum(earlier * one_hot, axis=1)
    slot_table = jnp.full((experts, capacity), pair_count, jnp.int32)
    slot_table = slot_table.at[flattened, position].set(jnp.arange(pair_count, dtype=jnp.int32))
    return (flattened * capacity + position, slot_table)


def pick_rows(source_rows, slot_table):
    padded = jnp.concatenate(
        [source_rows, jnp.zeros((1, source_rows.shape[1]), source_rows.dtype)], axis=0
    )
    return padded[slot_table]


def send_slices(source_rows, slot_table, group_size):
    picked = pick_rows(source_rows, slot_table)
    experts, capacity, features = picked.shape
    divided = picked.reshape(experts, capacity, group_size, features // group_size)
    return divided.transpose(0, 2, 1, 3).reshape(
        experts * group_size, capacity, features // group_size
    )


def send_copies(source_rows, slot_table, group_size):
    picked = pick_rows(source_rows, slot_table)
    experts, capacity, features = picked.shape
    copies = jnp.broadcast_to(picked[:, None], (experts, group_size, capacity, features))
    return copies.reshape(experts * group_size, capacity, features)


def owners_summed(returned, pair_where, group_size):
    owners, capacity, features = returned.shape
    summed = returned.reshape(owners // group_size, group_size, capacity, features).sum(axis=1)
    return summed.reshape(-1, features)[pair_where]


def owners_joined(returned, pair_where, group_size):
    owners, capacity, features = returned.shape
    joined = returned.reshape(owners // group_size, group_size, capacity, features).transpose(
        0, 2, 1, 3
    )
    return joined.reshape(-1, group_size * features)[pair_where]


def query_return(pieces):
    return lax.all_to_all(pieces, "dp", split_axis=0, concat_axis=0, tiled=True)


def output_return(pieces):
    return lax.all_to_all(pieces, "dp", split_axis=0, concat_axis=0, tiled=True)


def expert_return(pieces):
    return lax.all_to_all(pieces, "dp", split_axis=0, concat_axis=0, tiled=True)


def tensor_total(pieces):
    return lax.psum(pieces, "tensor")


def deal_plan(row_place, rows_dev):
    device_count = lax.axis_size("dp")
    my_index = lax.axis_index("dp")
    per_peer = rows_dev // device_count
    every_place = row_place.reshape(device_count, rows_dev)
    my_places = lax.dynamic_index_in_dim(every_place, my_index, 0, keepdims=False)
    counting = jnp.arange(rows_dev, dtype=jnp.int32)
    ordering = jnp.argsort(my_places // rows_dev * rows_dev + counting)
    wanted = every_place // rows_dev == my_index
    chosen = jnp.argsort(
        jnp.where(wanted, counting[None, :], rows_dev + counting[None, :]), axis=1
    )[:, :per_peer]
    placed = jnp.take_along_axis(every_place, chosen, axis=1) % rows_dev
    return (ordering, placed.reshape(-1))


def masked_scores(query_b, keys_b, allowed):
    raw = jnp.einsum(
        "ikjd,mjd->kjim", query_b, keys_b, preferred_element_type=jnp.float32
    ) / math.sqrt(query_b.shape[-1])
    return jnp.where(allowed[None, None], raw, -1e30)


def local(
    tokens,
    out_grad,
    row_place,
    seq_lengths,
    att_routes,
    att_gates,
    mlp_routes,
    mlp_gates,
    gain_attn,
    w_kv,
    w_query,
    w_out,
    gain_mlp,
    w_gate,
    w_up,
    w_down,
):
    rows_dev, features = tokens.shape
    device_count = lax.axis_size("dp")
    group_size = device_count // EXPERTS
    per_peer = rows_dev // device_count
    counting = jnp.arange(rows_dev, dtype=jnp.int32)
    ordering, placed = deal_plan(row_place, rows_dev)
    unplace = jnp.zeros((rows_dev,), jnp.int32).at[placed].set(counting)
    unorder = jnp.zeros((rows_dev,), jnp.int32).at[ordering].set(counting)
    dealt_x, dealt_g = (
        lax.all_to_all(
            tokens[ordering].reshape(device_count, per_peer, features),
            "dp",
            split_axis=0,
            concat_axis=0,
            tiled=True,
        ),
        lax.all_to_all(
            out_grad[ordering].reshape(device_count, per_peer, features),
            "dp",
            split_axis=0,
            concat_axis=0,
            tiled=True,
        ),
    )
    residual = dealt_x.reshape(rows_dev, features)[unplace].astype(jnp.float32)
    top_grad = dealt_g.reshape(rows_dev, features)[unplace].astype(jnp.float32)
    lengths = seq_lengths[0]
    seq_ends = jnp.cumsum(lengths)
    segment = jnp.sum((counting[:, None] >= seq_ends[None, :]).astype(jnp.int32), axis=1)
    starts = seq_ends - lengths
    member = segment[:, None] == jnp.arange(lengths.shape[0], dtype=jnp.int32)[None, :]
    begins = jnp.sum(jnp.where(member, starts[None, :], 0), axis=1)
    positions = counting - begins
    allowed = (segment[:, None] == segment[None, :]) & (counting[None, :] <= counting[:, None])
    head_count = w_kv.shape[2] // HD
    scale_attn = inverse_rms(residual)
    normed = (residual * scale_attn * gain_attn).astype(jnp.bfloat16)
    kv_proj = jnp.einsum("ld,dck->lck", normed, w_kv, preferred_element_type=jnp.float32)
    keys = rotate(kv_proj[:, 0].reshape(rows_dev, head_count, HD), positions, 1.0).astype(
        jnp.bfloat16
    )
    values = kv_proj[:, 1].reshape(rows_dev, head_count, HD).astype(jnp.bfloat16)
    att_where, att_table = expert_slots(att_routes, ATT_EXPERTS, CAP)
    query_rows = lax.all_to_all(
        send_slices(normed, att_table // 2, group_size),
        "dp",
        split_axis=0,
        concat_axis=0,
        tiled=True,
    )
    query_part = jnp.einsum(
        "scd,dh->sch", query_rows, w_query[0], preferred_element_type=jnp.float32
    )
    query_pre = owners_summed(query_return(query_part), att_where, group_size)
    query_rot = rotate(query_pre.reshape(rows_dev, 2, head_count, HD), positions, 1.0).astype(
        jnp.bfloat16
    )
    scores = masked_scores(query_rot, keys, allowed)
    highest = jnp.max(scores, axis=-1, keepdims=True)
    expo = jnp.exp(scores - highest)
    row_total = jnp.sum(expo, axis=-1, keepdims=True)
    log_total = highest + jnp.log(row_total)
    probability = expo / row_total
    attn = jnp.einsum(
        "kjim,mjd->ikjd",
        probability.astype(jnp.bfloat16),
        values,
        preferred_element_type=jnp.float32,
    )
    attn_low = attn.astype(jnp.bfloat16).reshape(rows_dev * 2, head_count * HD)
    out_rows = lax.all_to_all(
        send_copies(attn_low, att_table, group_size), "dp", split_axis=0, concat_axis=0, tiled=True
    )
    out_part = jnp.einsum("sch,hd->scd", out_rows, w_out[0], preferred_element_type=jnp.float32)
    out_pairs = owners_joined(output_return(out_part), att_where, group_size).reshape(
        rows_dev, 2, features
    )
    hidden = residual + tensor_total(jnp.sum(out_pairs * att_gates[:, :, None], axis=1))
    gate_map, up_map, down_map = (w_gate[0], w_up[0], w_down[0])
    scale_mlp = inverse_rms(hidden)
    normed2 = (hidden * scale_mlp * gain_mlp).astype(jnp.bfloat16)
    mlp_where, mlp_table = expert_slots(mlp_routes, EXPERTS, CAP)
    expert_sent = send_copies(normed2, mlp_table // 2, group_size)
    expert_rows = lax.all_to_all(expert_sent, "dp", split_axis=0, concat_axis=0, tiled=True)
    flat_rows = expert_rows.reshape(-1, features)
    gate_act = jnp.dot(flat_rows, gate_map, preferred_element_type=jnp.float32)
    up_act = jnp.dot(flat_rows, up_map, preferred_element_type=jnp.float32)
    inner = (jax.nn.silu(gate_act) * up_act).astype(jnp.bfloat16)
    expert_part = jnp.dot(inner, down_map, preferred_element_type=jnp.float32).reshape(
        expert_rows.shape
    )
    expert_pairs = owners_summed(expert_return(expert_part), mlp_where, group_size).reshape(
        rows_dev, 2, features
    )
    mixed_rows = hidden + tensor_total(jnp.sum(expert_pairs * mlp_gates[:, :, None], axis=1))
    branch_grad = (
        (top_grad[:, None, :] * mlp_gates[:, :, None])
        .astype(jnp.bfloat16)
        .reshape(rows_dev * 2, features)
    )
    grad_sent = send_copies(branch_grad, mlp_table, group_size)
    grad_back, rows_back = (
        lax.all_to_all(grad_sent, "dp", split_axis=0, concat_axis=0, tiled=True),
        lax.all_to_all(expert_sent, "dp", split_axis=0, concat_axis=0, tiled=True),
    )
    grad_rows = grad_back.reshape(-1, features)
    rows_again = rows_back.reshape(-1, features)
    gate_again = jnp.dot(rows_again, gate_map, preferred_element_type=jnp.float32)
    up_again = jnp.dot(rows_again, up_map, preferred_element_type=jnp.float32)
    inner_again = (jax.nn.silu(gate_again) * up_again).astype(jnp.bfloat16)
    contract_rows = (((0,), (0,)), ((), ()))
    contract_cols = (((1,), (1,)), ((), ()))
    d_inner = lax.dot_general(
        grad_rows, down_map, contract_cols, preferred_element_type=jnp.float32
    )
    down_grad_all = lax.dot_general(
        inner_again, grad_rows, contract_rows, preferred_element_type=jnp.float32
    )
    sigmoid_g = jax.nn.sigmoid(gate_again)
    d_up = (d_inner * gate_again * sigmoid_g).astype(jnp.bfloat16)
    d_gate = (d_inner * up_again * sigmoid_g * (1.0 + gate_again * (1.0 - sigmoid_g))).astype(
        jnp.bfloat16
    )
    gate_grad_all = lax.dot_general(
        rows_again, d_gate, contract_rows, preferred_element_type=jnp.float32
    )
    up_grad_all = lax.dot_general(
        rows_again, d_up, contract_rows, preferred_element_type=jnp.float32
    )
    d_rows = lax.dot_general(d_gate, gate_map, contract_cols, preferred_element_type=jnp.float32)
    d_rows = d_rows + lax.dot_general(
        d_up, up_map, contract_cols, preferred_element_type=jnp.float32
    )
    d_pairs = owners_summed(expert_return(d_rows.reshape(expert_rows.shape)), mlp_where, group_size)
    w_gate_grad = gate_grad_all[None]
    w_up_grad = up_grad_all[None]
    w_down_grad = down_grad_all[None]
    d_normed2 = tensor_total(jnp.sum(d_pairs.reshape(rows_dev, 2, features), axis=1))
    d_hidden = top_grad + norm_backward(hidden, scale_mlp, gain_mlp, d_normed2)
    gain_mlp_grad = jnp.sum(d_normed2 * hidden * scale_mlp, axis=0)
    att_grad = (
        (d_hidden[:, None, :] * att_gates[:, :, None])
        .astype(jnp.bfloat16)
        .reshape(rows_dev * 2, features)
    )
    grad_slices = lax.all_to_all(
        send_slices(att_grad, att_table, group_size), "dp", split_axis=0, concat_axis=0, tiled=True
    )
    w_out_grad = jnp.einsum(
        "sch,scd->hd", out_rows, grad_slices, preferred_element_type=jnp.float32
    )
    d_attn_part = jnp.einsum(
        "scd,hd->sch", grad_slices, w_out[0], preferred_element_type=jnp.float32
    )
    d_attn = owners_summed(output_return(d_attn_part), att_where, group_size)
    d_attn = d_attn.astype(jnp.bfloat16).reshape(rows_dev, 2, head_count, HD)
    probability = jnp.exp(masked_scores(query_rot, keys, allowed) - log_total)
    d_prob = jnp.einsum("ikjd,mjd->kjim", d_attn, values, preferred_element_type=jnp.float32)
    d_values = jnp.einsum(
        "kjim,ikjd->mjd",
        probability.astype(jnp.bfloat16),
        d_attn,
        preferred_element_type=jnp.float32,
    )
    delta = jnp.sum(d_prob * probability, axis=-1, keepdims=True)
    d_scores = (probability * (d_prob - delta)).astype(jnp.bfloat16)
    root_hd = math.sqrt(HD)
    d_query = (
        jnp.einsum("kjim,mjd->ikjd", d_scores, keys, preferred_element_type=jnp.float32) / root_hd
    )
    d_keys = (
        jnp.einsum("kjim,ikjd->mjd", d_scores, query_rot, preferred_element_type=jnp.float32)
        / root_hd
    )
    dq_pre = (
        rotate(d_query, positions, -1.0).astype(jnp.bfloat16).reshape(rows_dev * 2, head_count * HD)
    )
    dk_pre = rotate(d_keys, positions, -1.0).reshape(rows_dev, head_count * HD)
    d_kv = jnp.stack([dk_pre, d_values.reshape(rows_dev, head_count * HD)], axis=1).astype(
        jnp.bfloat16
    )
    dq_rows = lax.all_to_all(
        send_copies(dq_pre, att_table, group_size), "dp", split_axis=0, concat_axis=0, tiled=True
    )
    w_query_grad = jnp.einsum(
        "scd,sch->dh", query_rows, dq_rows, preferred_element_type=jnp.float32
    )
    d_slice = jnp.einsum("sch,dh->scd", dq_rows, w_query[0], preferred_element_type=jnp.float32)
    d_norm_query = owners_joined(query_return(d_slice), att_where, group_size)
    d_norm_query = jnp.sum(d_norm_query.reshape(rows_dev, 2, features), axis=1)
    w_kv_grad = jnp.einsum("ld,lck->dck", normed, d_kv, preferred_element_type=jnp.float32)
    d_norm_kv = jnp.einsum("lck,dck->ld", d_kv, w_kv, preferred_element_type=jnp.float32)
    d_normed = tensor_total(d_norm_query + d_norm_kv)
    in_grad = d_hidden + norm_backward(residual, scale_attn, gain_attn, d_normed)
    gain_attn_grad = jnp.sum(d_normed * residual * scale_attn, axis=0)
    w_kv_grad, gain_attn_grad, gain_mlp_grad = (
        lax.psum(w_kv_grad.astype(jnp.bfloat16), "dp").astype(jnp.float32),
        lax.psum(gain_attn_grad.astype(jnp.bfloat16), "dp").astype(jnp.float32),
        lax.psum(gain_mlp_grad.astype(jnp.bfloat16), "dp").astype(jnp.float32),
    )
    send_mixed = mixed_rows.astype(jnp.bfloat16)[placed].reshape(device_count, per_peer, features)
    send_input = in_grad.astype(jnp.bfloat16)[placed].reshape(device_count, per_peer, features)
    back_mixed, back_input = (
        lax.all_to_all(send_mixed, "dp", split_axis=0, concat_axis=0, tiled=True),
        lax.all_to_all(send_input, "dp", split_axis=0, concat_axis=0, tiled=True),
    )
    mixed = back_mixed.reshape(rows_dev, features)[unorder]
    tokens_grad = back_input.reshape(rows_dev, features)[unorder]
    return (
        mixed,
        tokens_grad,
        gain_attn_grad,
        w_kv_grad,
        w_query_grad[None],
        w_out_grad[None],
        gain_mlp_grad,
        w_gate_grad,
        w_up_grad,
        w_down_grad,
    )


MESH = pl.DeviceIdType.MESH
VM = pltpu.VMEM
DMA = pltpu.SemaphoreType.DMA
BF = jnp.bfloat16
F32 = jnp.float32

def rcopy(src, dst, ss, rs, dp, tn):
    return pltpu.make_async_remote_copy(src_ref=src, dst_ref=dst, send_sem=ss, recv_sem=rs,
        device_id={"dp": dp, "tensor": tn}, device_id_type=MESH)

def greet(targets):
    b = pltpu.get_barrier_semaphore()
    for dp, tn in targets:
        pl.semaphore_signal(b, inc=1, device_id={"dp": dp, "tensor": tn}, device_id_type=MESH)
    pl.semaphore_wait(b, len(targets))

def ranks():
    g = lax.axis_index("dp"); t = lax.axis_index("tensor")
    return g, t, lax.rem(t + 2, 4), t + 1 - 2 * lax.rem(t, 2)

def params(cid):
    return pltpu.CompilerParams(collective_id=cid, has_side_effects=True, vmem_limit_bytes=56*2**20)

def gather_body(n, mode, src, out, ssem, rsem, xs, xr, cs, cr, c2s, c2r, lsem):
    g, t, tx, tc = ranks()
    w = src.shape[-1]
    greet([(lax.rem(g + o, n), t) for o in range(1, n)] + [(g, tx), (g, tc)])
    cols = pl.ds(pl.multiple_of(t * w, w), w)
    colsx = pl.ds(pl.multiple_of(tx * w, w), w)
    pick = (lambda d: src.at[d]) if mode == "rows" else (lambda d: src)
    at = (lambda b, cc: out.at[:, b, :, cc]) if mode == "deal" else (lambda b, cc: out.at[b, :, cc])
    sends = []
    for o in range(1, n):
        d = lax.rem(g + o, n)
        c = rcopy(pick(d), at(g, cols), ssem.at[o], rsem.at[o], d, t)
        c.start(); sends.append(c)
    loc = pltpu.make_async_copy(pick(g), at(g, cols), lsem)
    loc.start(); loc.wait()
    fx = []; fc = []; fc2 = []
    for o in range(n):
        b = lax.rem(g - o + n, n)
        if o > 0: sends[o - 1].wait_recv()
        c = rcopy(at(b, cols), at(b, cols), xs.at[o], xr.at[o], g, tx); c.start(); fx.append(c)
        c = rcopy(at(b, cols), at(b, cols), cs.at[o], cr.at[o], g, tc); c.start(); fc.append(c)
    for o in range(n):
        b = lax.rem(g - o + n, n)
        fx[o].wait_recv()
        c = rcopy(at(b, colsx), at(b, colsx), c2s.at[o], c2r.at[o], g, tc); c.start(); fc2.append(c)
    for c in fc + fc2: c.wait_recv()
    for c in sends + fx + fc + fc2: c.wait_send()

def gather(src, n, bcast=False, deal=False, cid=0, space=VM):
    r, w = src.shape[-2:]
    mode = "deal" if deal else "copy" if bcast else "rows"
    shape = (n, n, r, 4 * w) if deal else (n, r, 4 * w)
    return pl.pallas_call(functools.partial(gather_body, n, mode),
        out_shape=jax.ShapeDtypeStruct(shape, src.dtype),
        in_specs=[pl.BlockSpec(memory_space=VM)], out_specs=pl.BlockSpec(memory_space=space),
        scratch_shapes=[DMA((n,))]*8 + [DMA],
        name="gather_rows", compiler_params=params(cid))(src)

def reduce_body(n, nb, src, out, cbuf, cin, xbuf, xin, dbuf, cs, cr, xs, xr, ds_, dr):
    g, t, tx, tc = ranks()
    tcx = lax.rem(tc + 2, 4); w = out.shape[-1]
    greet([(lax.rem(g + o, n), t) for o in range(1, n)] + [(g, tx), (g, tc)])
    sl = lambda q: pl.ds(pl.multiple_of(q * w, w), w)
    order = list(range(1, n)) + [0] + list(range(n, nb))
    at = lambda o: lax.rem(g + o, n) if o < n else o
    C = {}; X = {}; Dd = {}
    for o in order:
        d = at(o)
        cbuf[o, 0] = src[d, :, sl(tc)].astype(BF)
        cbuf[o, 1] = src[d, :, sl(tcx)].astype(BF)
        C[o] = rcopy(cbuf.at[o], cin.at[o], cs.at[o], cr.at[o], g, tc); C[o].start()
    for o in order:
        C[o].wait_recv()
        xbuf[o] = (src[at(o), :, sl(tx)] + cin[o, 1].astype(F32)).astype(BF)
        X[o] = rcopy(xbuf.at[o], xin.at[o], xs.at[o], xr.at[o], g, tx); X[o].start()
    for o in order:
        d = at(o)
        X[o].wait_recv()
        total = (src[d, :, sl(t)] + cin[o, 0].astype(F32) + xin[o].astype(F32)).astype(BF)
        if 0 < o < n:
            dbuf[o] = total
            Dd[o] = rcopy(dbuf.at[o], out.at[g], ds_.at[o], dr.at[o], d, t); Dd[o].start()
        elif o == 0:
            out[g] = total
        else:
            out[o] = total
    for c in Dd.values(): c.wait_recv()
    for c in list(C.values()) + list(X.values()) + list(Dd.values()): c.wait_send()

def reduce(src, n, cid=1):
    nb, r, w = src.shape; w //= 4
    return pl.pallas_call(functools.partial(reduce_body, n, nb),
        out_shape=jax.ShapeDtypeStruct((nb, r, w), BF),
        in_specs=[pl.BlockSpec(memory_space=VM)], out_specs=pl.BlockSpec(memory_space=VM),
        scratch_shapes=[VM((nb,2,r,w),BF), VM((nb,2,r,w),BF), VM((nb,r,w),BF), VM((nb,r,w),BF), VM((n,r,w),BF)] + [DMA((nb,))]*4 + [DMA((n,))]*2,
        name="reduce_rows", compiler_params=params(cid))(src)

def a2a_body(n, src, out, ss, rs):
    g, t, tx, tc = ranks()
    greet([(lax.rem(g + o, n), t) for o in range(1, n)])
    cs = []
    for o in range(1, n):
        d = lax.rem(g + o, n)
        c = rcopy(src.at[d], out.at[g], ss.at[o], rs.at[o], d, t); c.start(); cs.append(c)
    out[g] = src[g]
    for c in cs: c.wait()

def a2a(src, n, cid=2):
    return pl.pallas_call(functools.partial(a2a_body, n),
        out_shape=jax.ShapeDtypeStruct(src.shape, src.dtype),
        in_specs=[pl.BlockSpec(memory_space=VM)], out_specs=pl.BlockSpec(memory_space=VM),
        scratch_shapes=[DMA((n,))]*2,
        name="a2a_rows", compiler_params=params(cid))(src)

def a2a_copy_body(n, src, out, ss, rs):
    g, t, tx, tc = ranks()
    greet([(lax.rem(g + o, n), t) for o in range(1, n)])
    cs = []
    for o in range(1, n):
        d = lax.rem(g + o, n)
        c = rcopy(src, out.at[g], ss.at[o], rs.at[o], d, t); c.start(); cs.append(c)
    out[g] = src[...]
    for c in cs: c.wait()

def a2a_copy(src, n, cid):
    return pl.pallas_call(functools.partial(a2a_copy_body, n),
        out_shape=jax.ShapeDtypeStruct((n,) + src.shape, src.dtype),
        in_specs=[pl.BlockSpec(memory_space=VM)], out_specs=pl.BlockSpec(memory_space=VM),
        scratch_shapes=[DMA((n,))]*2,
        name="copy_rows", compiler_params=params(cid))(src)

def dot(a, b, dims):
    return lax.dot_general(a, b, dims, preferred_element_type=F32)


def mm(a, b):
    return dot(a, b, (((a.ndim - 1,), (0,)), ((), ())))


def mm_t(a, b):
    return dot(a, b, (((1,), (1,)), ((), ())))


def mm_rows(a, b):
    return dot(a, b, (((0,), (0,)), ((), ())))


class Ring:
    def __init__(self, n):
        self.n = n
        self.g, self.t, self.tx, self.tc = ranks()
        self.tcx = lax.rem(self.tc + 2, 4)
        self.tail = []
        self.dest = [lax.rem(self.g + o, n) for o in range(n)]

    def to(self, o):
        return self.dest[o]

    def greet_all(self):
        greet([(self.to(o), self.t) for o in range(1, self.n)] + [(self.g, self.tx), (self.g, self.tc)])

    def greet_everyone(self):
        greet([(self.to(o), self.t) for o in range(1, self.n)] + [(self.g, q) for q in (self.tx, self.tc, self.tcx)])

    def send(self, src, dst, ss, rs, dp, tn):
        c = rcopy(src, dst, ss, rs, dp, tn)
        c.start()
        self.tail.append(c)
        return c

    def finish(self):
        for c in self.tail:
            c.wait_send()
        self.tail = []


def cols_of(q, j, width, cw):
    return pl.ds(pl.multiple_of(q * width + j * cw, cw), cw)


REDUCE_SEMS = lambda nc, n: [DMA((nc,))] * 4 + [DMA((nc, n))] * 2
GATHER_SEMS = lambda nc, n: [DMA((nc, n))] * 2 + [DMA((nc,))] * 6
REDUCE_BUFS = lambda nc, n, r, cw: [
    VM((nc, 2, n, r, cw), BF), VM((nc, 2, n, r, cw), BF), VM((nc, 2, n, r, cw), F32),
    VM((nc, n, r, cw), BF), VM((nc, n, r, cw), BF), VM((nc, n, r, cw), BF), VM((nc, n, r, cw), BF)]


class Reduce:
    def __init__(self, ring, partial, bufs, sems):
        self.ring, self.partial = ring, partial
        self.cbuf, self.cin, self.pbuf, self.xbuf, self.xin, self.dbuf, self.rbuf = bufs
        self.cs, self.cr, self.xs, self.xr, self.ds, self.dr = sems
        self.c, self.x, self.d = {}, {}, {}

    def core(self):
        k = self.ring
        nc, _, n, r, cw = self.cbuf.shape
        for i, q in enumerate((k.tc, k.tcx)):
            v = self.partial(q).astype(BF)
            for j in range(nc):
                self.cbuf[j, i] = v[:, j * cw:(j + 1) * cw].reshape(n, r, cw)
        for j in range(nc):
            self.c[j] = k.send(self.cbuf.at[j], self.cin.at[j], self.cs.at[j], self.cr.at[j], k.g, k.tc)
        for i, q in ((1, k.tx), (0, k.t)):
            v = self.partial(q)
            for j in range(nc):
                self.pbuf[j, i] = v[:, j * cw:(j + 1) * cw].reshape(n, r, cw)
            if i:
                for j in range(nc):
                    self.cross(j)

    def cross(self, j):
        k = self.ring
        self.c[j].wait_recv()
        self.xbuf[j] = (self.pbuf[j, 1] + self.cin[j, 1].astype(F32)).astype(BF)
        self.x[j] = k.send(self.xbuf.at[j], self.xin.at[j], self.xs.at[j], self.xr.at[j], k.g, k.tx)

    def home(self, j):
        k = self.ring
        self.x[j].wait_recv()
        self.dbuf[j] = (self.pbuf[j, 0] + self.cin[j, 0].astype(F32) + self.xin[j].astype(F32)).astype(BF)
        for o in range(1, k.n):
            d = k.to(o)
            self.d[j, o] = k.send(
                self.dbuf.at[j, d], self.rbuf.at[j, k.g], self.ds.at[j, o], self.dr.at[j, o], d, k.t)
        self.rbuf[j, k.g] = self.dbuf[j, k.g]

    def rows(self, j):
        for o in range(1, self.ring.n):
            self.d[j, o].wait_recv()
        return self.rbuf[j].reshape(-1, self.rbuf.shape[-1])


class Gather:
    def __init__(self, ring, width, full, sbuf, sems):
        self.ring, self.full, self.sbuf = ring, full, sbuf
        ss, rs, xs, xr, cs, cr, c2s, c2r = sems
        k, (nc, n, _, cw) = ring, sbuf.shape
        self.d, self.x, self.c, self.c2, self.own = {}, {}, {}, {}, {}
        for j in range(nc):
            cc, cx = cols_of(k.t, j, width, cw), cols_of(k.tx, j, width, cw)
            self.own[j] = cc
            for o in range(1, n):
                d = k.to(o)
                self.d[j, o] = rcopy(sbuf.at[j, d], full.at[k.g, :, cc], ss.at[j, o], rs.at[j, o], d, k.t)
            ref, ref2 = full.at[:, :, cc], full.at[:, :, cx]
            self.x[j] = rcopy(ref, ref, xs.at[j], xr.at[j], k.g, k.tx)
            self.c[j] = rcopy(ref, ref, cs.at[j], cr.at[j], k.g, k.tc)
            self.c2[j] = rcopy(ref2, ref2, c2s.at[j], c2r.at[j], k.g, k.tc)

    def out(self, j, rows):
        self.sbuf[j] = rows.reshape(self.sbuf.shape[1:])
        for o in range(1, self.ring.n):
            self.d[j, o].start()
        self.full[self.ring.g, :, self.own[j]] = self.sbuf[j, self.ring.g]

    def cross(self, j):
        for o in range(1, self.ring.n):
            self.d[j, o].wait_recv()
        self.x[j].start()
        self.c[j].start()

    def core(self, j):
        self.x[j].wait_recv()
        self.c2[j].start()

    def finish(self):
        for c in list(self.c.values()) + list(self.c2.values()):
            c.wait_recv()
        for c in [*self.d.values(), *self.x.values(), *self.c.values(), *self.c2.values()]:
            c.wait_send()


def paired(reduce_one, gather_one, middle, nc):
    reduce_one.core()
    steps = []
    for j in range(nc):
        steps += [(2 * j, 0, lambda j=j: reduce_one.home(j)), (2 * j + 3, 1, lambda j=j: gather_one.out(j, middle(j, reduce_one.rows(j))))]
        steps += [(2 * j + 7, 2, lambda j=j: gather_one.cross(j)), (2 * j + 9, 3, lambda j=j: gather_one.core(j))]
    for _, _, step in sorted(steps, key=lambda s: s[:2]):
        step()
    gather_one.finish()


NC = 4


def split_bf(v):
    high = v.astype(BF)
    return high, (v - high.astype(F32)).astype(BF)


def hidden_body(n, attn, wo, x_own, comb, gates, pick, hidden, full, scale, *scratch):
    bufs, sbuf, sq, sq_in, qs, qr, sems = scratch[:7], *scratch[7:12], scratch[12:]
    ring = Ring(n)
    ring.greet_everyone()
    rows, width = x_own.shape
    shared = []
    cw = width // NC

    def partial(q):
        return mm(attn[...], wo[:, cols_of(q, 0, width, width)])

    def middle(j, rows):
        high, low = split_bf(rows.astype(F32) * gates[...])
        got = x_own[:, j * cw:(j + 1) * cw] + mm(comb[...], high) + mm(comb[...], low)
        hidden[:, j * cw:(j + 1) * cw] = got
        high, low = split_bf(got * got)
        ones = jnp.ones((8, cw), BF)
        squares = mm_t(ones, high) + mm_t(ones, low)
        sq[...] = squares if j == 0 else sq[...] + squares
        if j == NC - 1:
            for i, q in enumerate([ring.tc, ring.tx, ring.tcx]):
                shared.append(ring.send(sq, sq_in.at[i], qs.at[i], qr.at[i], ring.g, q))
        return mm(pick[...], got.astype(BF)).astype(BF)

    red = Reduce(ring, partial, bufs, sems[:6])
    gat = Gather(ring, width, full, sbuf, sems[6:])
    paired(red, gat, middle, NC)
    for c in shared:
        c.wait_recv()
    total = (sq[...] + sq_in[0] + sq_in[1] + sq_in[2])[:1]
    eye = lax.broadcasted_iota(jnp.int32, (rows, rows), 0) == lax.broadcasted_iota(jnp.int32, (rows, rows), 1)
    column = jnp.sum(jnp.where(eye, total, 0.0), axis=1, keepdims=True)
    scale[...] = lax.rsqrt(column / (4 * width) + EPSILON)
    ring.finish()


def hidden_rows(attn, wo, x_own, comb, gates, pick, n, cid):
    slots = attn.shape[0]
    r, (rows, width) = slots // n, x_own.shape
    return pl.pallas_call(
        functools.partial(hidden_body, n),
        out_shape=(
            jax.ShapeDtypeStruct((rows, width), F32), jax.ShapeDtypeStruct((n, r, 4 * width), BF),
            jax.ShapeDtypeStruct((rows, 1), F32)),
        in_specs=[pl.BlockSpec(memory_space=VM)] * 6,
        out_specs=[pl.BlockSpec(memory_space=VM)] * 3,
        scratch_shapes=REDUCE_BUFS(NC, n, r, width // NC) + [VM((NC, n, r, width // NC), BF)]
        + [VM((8, rows), F32), VM((3, 8, rows), F32), DMA((3,)), DMA((3,))]
        + REDUCE_SEMS(NC, n) + GATHER_SEMS(NC, n),
        name="hidden_rows", compiler_params=params(cid),
    )(attn, wo, x_own, comb, gates, pick)


def expert_body(
    n, hid_rows, d_mbr, gain, wg_hbm, wu_hbm, wd_hbm, hidden, dy_own, gain_t, scale, mlp_t, mlp_gates, mlp_rows, att_rows,
    full, d_hidden, mixed, gain_part, n2, inner, d_gate, d_up, *scratch,
):
    ring = Ring(n)
    bufs, bufs2 = scratch[:7], scratch[7:14]
    sbuf, wg, wu, wd, r_own, r_in, r_to, r_back = scratch[14:22]
    wsem, rss, rsr, rds, rdr = scratch[22:27]
    sems = scratch[27:]
    ff = wg.shape[1]
    rows, width = hidden.shape
    slots = n2.shape[0]
    features = 4 * width
    cw = width // NC
    loads = [pltpu.make_async_copy(a, b, wsem.at[i]) for i, (a, b) in enumerate([(wg_hbm, wg), (wu_hbm, wu), (wd_hbm, wd)])]
    for c in loads:
        c.start()
    ring.greet_everyone()

    def norm_rows(i, _):
        at = pl.ds(pl.multiple_of(i * 64, 64), 64)
        v = hid_rows[i].astype(F32)
        s = lax.rsqrt(jnp.mean(v * v, axis=-1, keepdims=True) + EPSILON)
        n2[at, :] = (v * s * gain[...]).astype(BF)
        return _

    lax.fori_loop(0, n, norm_rows, 0)
    for c in loads:
        c.wait()
    r_own[...] = jnp.zeros_like(r_own)

    def units(at, size):
        a = n2[...]
        gate = mm(a, wg[:, at])
        up = mm(a, wu[:, at])
        d_in = mm_t(d_mbr[...], wd[at, :])
        sig = jax.nn.sigmoid(gate)
        silu = gate * sig
        inner[:, at] = (silu * up).astype(BF)
        du = (d_in * silu).astype(BF)
        dg = (d_in * up * sig * (1.0 + gate * (1.0 - sig))).astype(BF)
        d_up[:, at] = du
        d_gate[:, at] = dg
        both = (gate * dg.astype(F32) + up * du.astype(F32)).astype(BF)
        r_own[...] += mm_t(jnp.ones((8, size), BF), both)

    tile = 256

    def unit_tile(i, _):
        units(pl.ds(pl.multiple_of(i * tile, tile), tile), tile)
        return _

    lax.fori_loop(0, ff // tile, unit_tile, 0)
    if ff % tile:
        units(pl.ds(ff // tile * tile, ff % tile), ff % tile)

    others = [ring.tc, ring.tx, ring.tcx]
    r_sends = [ring.send(r_own, r_in.at[i], rss.at[i], rsr.at[i], ring.g, q) for i, q in enumerate(others)]

    def partial(q):
        at = cols_of(q, 0, width, width)
        return mm_t(d_gate[...], wg[at, :]) + mm_t(d_up[...], wu[at, :])

    def partial_mixed(q):
        return mm(inner[...], wd[:, cols_of(q, 0, width, width)])

    pairs = {}

    def share_r():
        for c in r_sends:
            c.wait_recv()
        r_to[...] = r_own[...] + r_in[0] + r_in[1] + r_in[2]
        for o in range(1, n):
            d = ring.to(o)
            half = pl.ds(pl.multiple_of(d // 2 * 128, 128), 128)
            pairs[o] = ring.send(r_to.at[:, half], r_back.at[ring.g], rds.at[o], rdr.at[o], d, ring.t)
        r_back[ring.g] = r_to[:, pl.ds(pl.multiple_of(ring.g // 2 * 128, 128), 128)]

    total_r = {}

    def take_r():
        for o in range(1, n):
            pairs[o].wait_recv()
        odd = lax.rem(ring.g, 2) == 1
        got = jnp.concatenate(
            [jnp.where(odd, r_back[e][:, 64:], r_back[e][:, :64]) for e in range(n)], axis=1)
        high = got.astype(BF)
        low = (got - high.astype(F32)).astype(BF)
        total_r[0] = (mm_t(mlp_t[...], high) + mm_t(mlp_t[...], low))[:, :1] / features

    def middle(j, got):
        if j == 0:
            take_r()
        cc = slice(j * cw, (j + 1) * cw)
        s2, h = scale[...], hidden[:, cc]
        d_n = mm(mlp_t[...], got)
        d_h = dy_own[:, cc] + s2 * (gain_t[:, cc] * d_n) - h * (s2 * s2) * total_r[0]
        d_hidden[:, cc] = d_h
        gain_part[:, cc] = jnp.broadcast_to(jnp.sum(d_n * h * s2, axis=0, keepdims=True), (8, cw))
        return mm(att_rows[...], d_h.astype(BF)).astype(BF)

    red = Reduce(ring, partial, bufs, sems[:6])
    gat = Gather(ring, width, full, sbuf, sems[6:14])
    red2 = Reduce(ring, partial_mixed, bufs2, sems[14:20])

    def settle(j):
        got = red2.rows(j)
        scaled = got.astype(F32) * mlp_gates[...]
        high = scaled.astype(BF)
        low = (scaled - high.astype(F32)).astype(BF)
        cc = slice(j * cw, (j + 1) * cw)
        mixed[:, cc] = (hidden[:, cc] + mm(mlp_t[...], high) + mm(mlp_t[...], low)).astype(BF)

    red.core()
    share_r()
    steps = []
    for j in range(NC):
        steps += [(2 * j, 1, lambda j=j: red.home(j)), (2 * j + 3, 2, lambda j=j: gat.out(j, middle(j, red.rows(j))))]
        steps += [(2 * j + 7, 3, lambda j=j: gat.cross(j)), (2 * j + 9, 4, lambda j=j: gat.core(j))]
        steps += [(2 * j + 12, 7, lambda j=j: red2.home(j)), (2 * j + 16, 8, lambda j=j: settle(j))]
    steps += [(9.5, 5, red2.core)]
    steps.sort(key=lambda s: s[:2])
    for _, _, run in steps:
        run()
    gat.finish()
    ring.finish()


def expert_layer(hid_rows, d_mbr, gain, wg, wu, wd, hidden, dy_own, gain_t, scale, mlp_t, mlp_gates, mlp_rows, att_rows, n, cid):
    r, features = hid_rows.shape[1:]
    ff = wg.shape[1]
    rows, width = hidden.shape
    slots, cw = n * r, width // NC
    any_, vm = pl.BlockSpec(memory_space=pl.ANY), pl.BlockSpec(memory_space=VM)
    sds = jax.ShapeDtypeStruct
    return pl.pallas_call(
        functools.partial(expert_body, n),
        out_shape=(
            sds((n, r, features), BF), sds((rows, width), F32), sds((rows, width), BF), sds((8, width), F32),
            sds((slots, features), BF), sds((slots, ff), BF), sds((slots, ff), BF), sds((slots, ff), BF)),
        in_specs=[vm, vm, vm, any_, any_, any_] + [vm] * 8,
        out_specs=[vm] * 8,
        scratch_shapes=REDUCE_BUFS(NC, n, r, cw) + REDUCE_BUFS(NC, n, r, cw) + [
            VM((NC, n, r, cw), BF), VM((features, ff), BF), VM((features, ff), BF), VM((ff, features), BF),
            VM((8, slots), F32), VM((3, 8, slots), F32), VM((8, slots), F32), VM((n, 8, 128), F32),
            DMA((3,)), DMA((3,)), DMA((3,)), DMA((n,)), DMA((n,))]
        + REDUCE_SEMS(NC, n) + GATHER_SEMS(NC, n) + REDUCE_SEMS(NC, n),
        name="expert_layer", compiler_params=params(cid),
    )(hid_rows, d_mbr, gain, wg, wu, wd, hidden, dy_own, gain_t, scale, mlp_t, mlp_gates, mlp_rows, att_rows)


META = {name: i for i, name in enumerate(
    ("ar0", "ar1", "ag0", "ag1", "mr0", "mr1", "mg0", "mg1", "pos", "seg", "wpos"))}


def iota(shape, dim):
    return lax.broadcasted_iota(jnp.int32, shape, dim)


def slot_table(meta, first, name, cap):
    member = (meta[first:first + 1] == name) | (meta[first + 1:first + 2] == name)
    tokens = meta.shape[1]
    before = jnp.where(iota((tokens, tokens), 0) < iota((tokens, tokens), 1), 1.0, 0.0).astype(BF)
    rank = mm(jnp.broadcast_to(jnp.where(member, 1.0, 0.0), (8, tokens)).astype(BF), before)[:1]
    return jnp.where((rank == iota((cap, tokens), 0).astype(F32)) & member, 1.0, 0.0).astype(BF)


def allowed_pairs(meta, meta_t):
    seg, wpos = META["seg"], META["wpos"]
    same = meta_t[:, seg:seg + 1] == meta[seg:seg + 1]
    return jnp.where(same & (meta[wpos:wpos + 1] <= meta_t[:, wpos:wpos + 1]), 1.0, 0.0).astype(BF)


def position_rows(meta_t):
    pos = META["pos"]
    tokens = meta_t.shape[0]
    return jnp.where(meta_t[:, pos:pos + 1] == iota((tokens, tokens), 1).astype(F32), 1.0, 0.0).astype(BF)


def looked_up(rows, table):
    got = mm(rows, table)
    w = got.shape[1] // 3
    return got[:, :w] + got[:, w:2 * w] + got[:, 2 * w:]


def turned(v, cosine, sine):
    out = []
    for h in range(v.shape[1] // HD):
        u = v[:, h * HD:(h + 1) * HD]
        out.append(u * cosine + pltpu.roll(u, HD // 2, 1) * sine)
    return jnp.concatenate(out, axis=1)


def angle_tables(positions):
    half = HD // 2
    frequency = np.exp(-math.log(THETA) * np.arange(half) / half)
    turned_by = np.arange(positions)[:, None] * frequency[None, :]
    cosine = np.concatenate([np.cos(turned_by)] * 2, axis=1).astype(np.float32)
    sine = np.concatenate([-np.sin(turned_by), np.sin(turned_by)], axis=1).astype(np.float32)

    def parts(v):
        out, left = [], v
        for _ in range(3):
            p = left.astype(jnp.bfloat16)
            out.append(p)
            left = left - p.astype(np.float32)
        return np.concatenate(out, axis=1)

    return jnp.asarray(parts(cosine)), jnp.asarray(parts(sine))


def softmax_rows(scores):
    top = jnp.max(scores, axis=-1, keepdims=True)
    expo = jnp.exp(scores - top)
    return expo / jnp.sum(expo, axis=-1, keepdims=True)


def keys_back_tables(meta, cos_t, sin_t, n, cap):
    m = meta[...]
    m_t = m.T
    tables = jnp.concatenate([slot_table(m, META["ar0"], float(e), cap) for e in range(n)], axis=0)
    at_pos = position_rows(m_t)
    return (mm(tables, allowed_pairs(m, m_t)) - 1.0) * 1e30, looked_up(at_pos, cos_t[...]), looked_up(at_pos, sin_t[...])


def keys_back_heads(part, query, d_attn, keys, values, bias, cosine, sine, d_kv):
    n, cap, hw = query.shape
    heads = hw // HD // 2
    root = math.sqrt(HD)
    for i in range(heads):
        h = part * heads + i
        hh = slice(h * HD, (h + 1) * HD)
        q = query[:, :, hh].reshape(n * cap, HD)
        d_o = d_attn[:, :, hh].reshape(n * cap, HD)
        k, v = keys[:, hh], values[:, hh]
        probs = softmax_rows(mm_t(q, k) / root + bias)
        d_probs = mm_t(d_o, v)
        delta = jnp.sum(d_probs * probs, axis=-1, keepdims=True)
        d_scores = (probs * (d_probs - delta)).astype(BF)
        at = part * hw + i * HD
        d_kv[:, at + hw // 2:at + hw // 2 + HD] = mm_rows(probs.astype(BF), d_o).astype(BF)
        d_k = mm_rows(d_scores, q) / root
        d_kv[:, at:at + HD] = turned(d_k, cosine, -sine).astype(BF)


def map_grad_body(normed, d_kv, out, d_cols):
    hw = d_kv.shape[1] // 2
    tiles = d_kv.shape[1] // 128
    half = tiles // 4

    @pl.when(pl.program_id(0) == 0)
    def _():
        for i in range(hw // 128):
            for c in range(2):
                at = i // half * hw + c * (hw // 2) + i % half * 128
                d_cols[:, (2 * i + c) * 128:(2 * i + c + 1) * 128] = d_kv[:, at:at + 128]

    got = mm_rows(normed[...], d_cols[...])
    for b in range(tiles):
        out[pl.ds(b, got.shape[0], stride=tiles), :] = got[:, b * 128:(b + 1) * 128]


def map_grad(normed, d_kv):
    total, features = normed.shape
    both = d_kv.shape[1]
    size, tiles = 512, both // 128
    out = pl.pallas_call(
        map_grad_body, grid=(features // size,),
        out_shape=jax.ShapeDtypeStruct((features * tiles, 128), F32),
        in_specs=[pl.BlockSpec((total, size), lambda i: (0, i)), pl.BlockSpec((total, both), lambda i: (0, 0))],
        out_specs=pl.BlockSpec((size * tiles, 128), lambda i: (i, 0)), scratch_shapes=[VM((total, both), BF)],
        name="map_grad", compiler_params=pltpu.CompilerParams(vmem_limit_bytes=56 * 2**20),
    )(normed, d_kv)
    return out.reshape(features, tiles // 2, 2, 128).transpose(0, 2, 1, 3).reshape(features, 2, both // 2)


def attention_back(i, d_attn, query, keys, values, bias, turn_slots, dq_pre):
    root = math.sqrt(HD)
    dq = []
    for h in range(query.shape[2] // HD):
        hh = slice(h * HD, (h + 1) * HD)
        k = keys[i, :, hh]
        probs = softmax_rows(mm_t(query[i, :, hh], k) / root + bias[i])
        d_probs = mm_t(d_attn[i, :, hh], values[i, :, hh])
        delta = jnp.sum(d_probs * probs, axis=-1, keepdims=True)
        dq.append(mm((probs * (d_probs - delta)).astype(BF), k) / root)
    dq_pre[i] = turned(jnp.concatenate(dq, axis=1), turn_slots[i, :, :HD], -turn_slots[i, :, HD:]).astype(BF)


def tail_body(
    n, d_attn, mb_rows, meta, cos_t, sin_t, x_own, scale, gain, d_hidden, hidden, mlp_gate, mlp_rows, att_rows, gain_mlp_part, sorter,
    query_hbm, keys_hbm, values_hbm, bias_hbm, turn_hbm, q_back_hbm, wq_hbm, wk_hbm, wv_hbm,
    d_kv_all, mixed_out, grad_out, gain_att_out, gain_mlp_out, dq_pre, *scratch,
):
    ring = Ring(n)
    (at_in, d_kv, kc_out, kc_in, kv_keep, kx_out, kx_in, sbuf, sq, sq_in, g_out, g_in, g_sum, d_norm, mixed, comb, mlp_t,
     query, keys, values, bias, turn_slots, q_back, w_q, w_k, w_v, whole, pbuf, cbuf, cin, back, gains) = scratch[:32]
    xbuf, xin, dbuf, rbuf = scratch[32:36]
    (as_, ar, zs, zr, ws, wr, ys, yr, ks, kr, lxs, lxr, qs, qr, gs, gr, ts, tr, wsem) = scratch[36:55]
    sems, fsems = scratch[55:61], scratch[61:]
    wanted = [(query_hbm, query), (keys_hbm, keys), (values_hbm, values), (bias_hbm, bias), (turn_hbm, turn_slots), (wq_hbm, w_q),
              (q_back_hbm, q_back), (wk_hbm, w_k), (wv_hbm, w_v)]
    loads = [pltpu.make_async_copy(a, b, wsem.at[i]) for i, (a, b) in enumerate(wanted)]
    for c in loads:
        c.start()
    rows, width = x_own.shape
    cw = width // NC
    cap = query.shape[1]
    slots = n * cap
    all_keys, all_values = keys, values
    hw = keys.shape[2]
    features = 4 * width
    keys, values, meta, scale = keys.at[ring.g], values.at[ring.g], meta.at[ring.g], scale.at[ring.g]
    z, y = ring.g // 2, lax.rem(ring.g, 2)
    depth = n // 2
    ring.greet_everyone()

    half = hw // 2
    arrive = []
    for c in range(2):
        cc = pl.ds(c * half, half)
        arrive.append([
            ring.send(d_attn.at[ring.to(o), :, cc], at_in.at[ring.g, :, cc], as_.at[c, o], ar.at[c, o], ring.to(o), ring.t)
            for o in range(1, n)])
    at_in[ring.g] = d_attn[ring.g]
    comb[...] = att_rows[...].T
    mlp_t[...] = mlp_rows[...].T
    own_bias, cosine, sine = keys_back_tables(meta, cos_t, sin_t, n, cap)
    for c in loads[:5]:
        c.wait()

    def group_back(i, _):
        attention_back(i, d_attn, query, all_keys, all_values, bias, turn_slots, dq_pre)
        return _

    halves = [(c, slice(c * hw, (c + 1) * hw)) for c in range(2)]
    pairs = lambda zz, yy: zz * 2 + yy
    across = []

    def unit(zz, c):
        return d_kv_all.at[pairs(zz, y), :, pl.ds(c * hw, hw)]

    def step(up, hop, c, first):
        zz = z - hop if up else z + hop
        here = zz >= 0 if up else zz < depth
        ss, rs = (zs, zr) if up else (ws, wr)
        on, back_to = (z + 1, z - 1) if up else (z - 1, z + 1)

        @pl.when(here)
        def _():
            ref = unit(zz, c)
            if not first:
                rcopy(ref, ref, ss.at[hop - 1, c], rs.at[hop - 1, c], pairs(back_to, y), ring.t).wait_recv()

            @pl.when((on < depth) if up else (on >= 0))
            def _():
                rcopy(ref, ref, ss.at[hop, c], rs.at[hop, c], pairs(on, y), ring.t).start()

            if up or not first:
                rcopy(ref, ref, ys.at[zz, c], yr.at[zz, c], pairs(z, 1 - y), ring.t).start()

    def drain(up, hop, c):
        zz = z - hop if up else z + hop
        here = zz >= 0 if up else zz < depth
        ss, rs = (zs, zr) if up else (ws, wr)
        on = z + 1 if up else z - 1

        @pl.when(here & ((on < depth) if up else (on >= 0)))
        def _():
            ref = unit(zz, c)
            rcopy(ref, ref, ss.at[hop, c], rs.at[hop, c], pairs(on, y), ring.t).wait_send()

    def spread(hop, c):
        step(True, hop, c, hop == 0)
        step(False, hop, c, hop == 0)

    def keys_values(c):
        for r in arrive[c]:
            r.wait_recv()
        keys_back_heads(c, q_back, at_in, keys, values, own_bias, cosine, sine, d_kv)
        cc = slice(c * hw, (c + 1) * hw)
        d_kv_all[ring.g, :, cc] = d_kv[:, cc]
        spread(0, c)

    lax.fori_loop(0, n // 2, group_back, 0)
    loads[6].wait()
    keys_values(0)
    lax.fori_loop(n // 2, n, group_back, 0)
    keys_values(1)
    loads[5].wait()

    def back_cols(j):
        dq = dq_pre[...].reshape(slots, hw)
        return jnp.concatenate([mm_t(dq, w_q[q * width + j * cw:q * width + (j + 1) * cw, :]) for q in range(4)], axis=1)

    red = ChunkReduce(ring, back_cols, whole, pbuf, (cbuf, xbuf, dbuf), (cin, xin, rbuf), sems)
    red.core(0)
    spread(1, 0)
    for j in range(1, NC):
        red.core(j)
        red.cross(j - 1)
    spread(1, 1)
    red.cross(NC - 1)
    red.home(0)
    red.home(1)
    loads[7].wait()
    loads[8].wait()

    def kv_part(q):
        at = cols_of(q, 0, width, width)
        return sum(
            mm_t(d_kv[:, c * hw:c * hw + half], w_k[at, c * half:(c + 1) * half])
            + mm_t(d_kv[:, c * hw + half:(c + 1) * hw], w_v[at, c * half:(c + 1) * half]) for c in range(2))

    kc_out[0] = kv_part(ring.tc).astype(BF)
    kc_out[1] = kv_part(ring.tcx).astype(BF)
    kc = ring.send(kc_out, kc_in, ks, kr, ring.g, ring.tc)
    red.home(2)
    kv_keep[1] = kv_part(ring.tx)
    kc.wait_recv()
    kx_out[...] = (kv_keep[1] + kc_in[1].astype(F32)).astype(BF)
    kx = ring.send(kx_out, kx_in, lxs, lxr, ring.g, ring.tx)
    kv_keep[0] = kv_part(ring.t)
    red.home(3)
    spread(2, 0)
    kx.wait_recv()
    local = kv_keep[0] + kc_in[0].astype(F32) + kx_in[...].astype(F32)
    spread(2, 1)
    spread(3, 0)
    squares = jnp.zeros((8, rows), F32)
    for j in range(NC):
        cc = slice(j * cw, (j + 1) * cw)
        got = mm(comb[...], red.rows(j)) + local[:, cc]
        d_norm[:, cc] = got
        high, low = split_bf(x_own[:, cc] * gain[:, cols_of(ring.t, j, width, cw)] * got)
        ones = jnp.ones((8, cw), BF)
        squares = squares + mm_t(ones, high) + mm_t(ones, low)
        g_out[:, cc] = jnp.concatenate([
            gain_mlp_part[:1, cc], jnp.sum(got * x_own[:, cc] * scale[...], axis=0, keepdims=True), jnp.zeros((6, cw), F32)], axis=0)
    sq[...] = squares
    shared = [ring.send(sq, sq_in.at[i], qs.at[i], qr.at[i], ring.g, q) for i, q in enumerate([ring.tc, ring.tx, ring.tcx])]
    spread(3, 1)
    sums = []
    for o in range(1, n):
        sums.append(ring.send(g_out, g_in.at[ring.g], gs.at[o], gr.at[o], ring.to(o), ring.t))
    g_in[ring.g] = g_out[...]
    for j in range(NC):
        cc = slice(j * cw, (j + 1) * cw)
        high, low = split_bf(mb_rows[j].reshape(slots, cw).astype(F32) * mlp_gate[...])
        mixed[:, cc] = (hidden[:, cc] + mm(mlp_t[...], high) + mm(mlp_t[...], low)).astype(BF)
    for c in shared:
        c.wait_recv()
    total = (sq[...] + sq_in[0] + sq_in[1] + sq_in[2])[:1]
    eye = iota((rows, rows), 0) == iota((rows, rows), 1)
    mean = jnp.sum(jnp.where(eye, total, 0.0), axis=1, keepdims=True) / features
    s = scale[...]
    in_grad = d_hidden[...] + s * (gain[:, cols_of(ring.t, 0, width, width)] * d_norm[...]) - x_own[...] * (s * s * s * mean)
    per = rows // n
    fin = ChunkGather(
        ring, lambda j, q, e: back.at[slice(None) if e is None else e, :, cols_of(q, 0, width, width)], sbuf, fsems)
    fin.out(0, jnp.concatenate(
        [mixed[...].reshape(n, per, width), in_grad.astype(BF).reshape(n, per, width)], axis=1))
    for c in sums:
        c.wait_recv()
    g_sum[...] = functools.reduce(lambda a, b: a + b, [g_in[e] for e in range(n)])
    at_t = cols_of(ring.t, 0, width, width)
    gains[:, at_t] = g_sum[...]
    told = [ring.send(g_sum, gains.at[:, at_t], ts.at[i], tr.at[i], ring.g, q) for i, q in enumerate([ring.tc, ring.tx, ring.tcx])]
    fin.cross(0)
    fin.core(0)
    fin.here(0)
    for ref, at in ((mixed_out, slice(0, per)), (grad_out, slice(per, 2 * per))):
        ref[...] = mm_rows(sorter[...], back[:, at].reshape(rows, features)).astype(BF)
    for c in told:
        c.wait_recv()
    gain_mlp_out[...] = gains[0:1]
    gain_att_out[...] = gains[1:2]
    for c, _ in halves:
        for zz in range(depth):
            ref = d_kv_all.at[pairs(zz, 1 - y), :, pl.ds(c * hw, hw)]
            rcopy(ref, ref, ys.at[zz, c], yr.at[zz, c], pairs(z, 1 - y), ring.t).wait()
        for hop in range(depth - 1):
            drain(True, hop, c)
            drain(False, hop, c)
    ring.finish()
    fin.sent()
    red.sent_core()
    red.sent_rest()


def layer_tail(args, later, n, cid):
    d_attn, x_own = args[0], args[5]
    rows, width = x_own.shape
    cap, hw = d_attn.shape[1:]
    cw, features, depth = width // NC, 4 * width, n // 2
    slots = n * cap
    sds = jax.ShapeDtypeStruct
    per = 2 * rows // n
    one, two = VM((NC, n, cap, cw), BF), VM((NC, 2, n, cap, cw), BF)
    any_, vm = pl.BlockSpec(memory_space=pl.ANY), pl.BlockSpec(memory_space=VM)
    return pl.pallas_call(
        functools.partial(tail_body, n),
        out_shape=(
            sds((n, rows, 2 * hw), BF), sds((rows, features), BF), sds((rows, features), BF), sds((1, features), F32),
            sds((1, features), F32), sds((n, cap, hw), BF)),
        in_specs=[vm] * len(args) + [any_] * len(later), out_specs=[vm] * 6,
        scratch_shapes=[
            VM((n, cap, hw), BF), VM((rows, 2 * hw), BF), VM((2, rows, width), BF), VM((2, rows, width), BF),
            VM((2, rows, width), F32), VM((rows, width), BF), VM((rows, width), BF), VM((1, n, per, width), BF),
            VM((8, rows), F32), VM((3, 8, rows), F32), VM((8, width), F32), VM((n, 8, width), F32), VM((8, width), F32),
            VM((rows, width), F32), VM((rows, width), BF), VM((rows, slots), BF), VM((rows, slots), BF)]
        + [VM(a.shape, a.dtype) for a in later]
        + [VM((slots, 4 * cw), F32), VM((NC, 2, n, cap, cw), F32), two, two, VM((n, per, features), BF), VM((8, features), F32)]
        + [one] * 4 + [
            DMA((2, n)), DMA((2, n)), DMA((depth, 2)), DMA((depth, 2)), DMA((depth, 2)), DMA((depth, 2)), DMA((depth, 2)), DMA((depth, 2)),
            DMA, DMA, DMA, DMA, DMA((3,)), DMA((3,)), DMA((n,)), DMA((n,)), DMA((3,)), DMA((3,)), DMA((len(later),))]
        + REDUCE_SEMS(NC, n) + GATHER_SEMS(1, n),
        name="layer_tail", compiler_params=pltpu.CompilerParams(
            collective_id=cid, has_side_effects=True, vmem_limit_bytes=63 * 2**20),
    )(*args, *later)


def front_body(
    n, tokens, out_grad, place_r, att_routes, att_gates, mlp_routes, mlp_gates, seq_lengths, gain, cos_t, sin_t, wkv_hbm, wq_hbm,
    dy_own, meta_all, sorter_out, att_rows, att_gate, mlp_rows, mlp_gate, att_in, wk_hbm, wv_hbm, x_own,
    normed_hbm, picked_hbm, keys, values, query, attn, scale, bias, turn_slots, d_mbr,
    x_all, dy_send, w_kv, w_k, w_v, w_q, meta_w, mlp_in, normed, picked, dy_rows, sbuf, ksem, osem, nsem, *sems,
):
    gsems, sems = sems[:8], sems[8:]
    ms, mr, dys, dyr, zs, zr, ws, wr, ys, yr, xs, xr, cs, cr = sems
    ring = Ring(n)
    g, t = ring.g, ring.t
    rows, features = tokens.shape
    width, per = features // 4, rows // n
    z, y, depth = g // 2, lax.rem(g, 2), n // 2
    pairs = lambda zz, yy: zz * 2 + yy
    fetch = pltpu.make_async_copy(wkv_hbm, w_kv, ksem.at[0])
    fetch.start()
    fetch_q = pltpu.make_async_copy(wq_hbm, w_q, ksem.at[1])
    fetch_q.start()
    gw = sbuf.shape[-1]
    gat = ChunkGather(
        ring, lambda j, q, e: dy_rows.at[slice(None) if e is None else e, :, cols_of(q, j, width, gw)], sbuf, gsems)
    ring.greet_all()
    place_c = place_r[...].astype(F32).T.astype(jnp.int32)

    def arrival(row, col):
        g_row, g_col = row // rows, col // rows
        before = (g_col == g_row) & (iota((rows, rows), 0) < iota((rows, rows), 1))
        return g_row, jnp.sum(jnp.where(before, 1.0, 0.0), axis=0, keepdims=True).astype(jnp.int32)

    col_g = jnp.sum(jnp.where(iota((rows, n), 1) == g, place_c, 0), axis=1, keepdims=True)
    g_row, rank = arrival(place_r[pl.ds(g, 1), :], col_g)
    sorter = jnp.where(g_row * per + rank == iota((rows, rows), 0), 1.0, 0.0).astype(BF)
    sorter_out[...] = sorter

    half = width // 2
    chunks = [("b", t, half), ("a", t, 0), ("c", ring.tx, 0)]
    cols = [pl.ds(pl.multiple_of(q * width + off, half), half) for _, q, off in chunks]
    for cc in cols:
        x_all[:, g, :, cc] = mm(sorter, tokens[:, cc]).astype(BF).reshape(n, per, half)

    def unit(zz, yy, c):
        return x_all.at[:, pairs(zz, yy), :, cols[c]]

    def cross(zz, yy, c):
        if chunks[c][0] == "b":
            ref = unit(zz, yy, c)
            rcopy(ref, ref, xs.at[pairs(zz, yy)], xr.at[pairs(zz, yy)], g, ring.tx).start()

    def hop_on(up, hop, c):
        zz = z - hop if up else z + hop
        here = zz >= 0 if up else zz < depth
        ss, rs = (zs, zr) if up else (ws, wr)
        on, source = (z + 1, z - 1) if up else (z - 1, z + 1)

        @pl.when(here)
        def _():
            ref = unit(zz, y, c)
            if hop:
                rcopy(ref, ref, ss.at[hop - 1, c], rs.at[hop - 1, c], pairs(source, y), t).wait_recv()

            @pl.when((on < depth) if up else (on >= 0))
            def _():
                rcopy(ref, ref, ss.at[hop, c], rs.at[hop, c], pairs(on, y), t).start()

            if up or hop:
                rcopy(ref, ref, ys.at[zz, c], yr.at[zz, c], pairs(z, 1 - y), t).start()
                cross(zz, y, c)

    def from_y(zz, c):
        ref = unit(zz, 1 - y, c)
        rcopy(ref, ref, ys.at[zz, c], yr.at[zz, c], pairs(z, 1 - y), t).wait_recv()
        cross(zz, 1 - y, c)

    count = range(len(chunks))
    for c in count:
        hop_on(True, 0, c)
        hop_on(False, 0, c)

    meta_w[...] = jnp.zeros_like(meta_w)
    for name, ref in (("ar0", att_routes), ("ag0", att_gates), ("mr0", mlp_routes), ("mg0", mlp_gates)):
        meta_w[META[name]:META[name] + 2] = ref[...].astype(F32)
    at = iota((1, rows), 1)
    end, segment, begin = jnp.zeros((1, 1), jnp.int32), jnp.zeros((1, rows), jnp.int32), jnp.zeros((1, rows), jnp.int32)
    for k in range(seq_lengths.shape[1]):
        end = end + seq_lengths[:, k:k + 1]
        segment = segment + jnp.where(at >= end, 1, 0)
        begin = jnp.where(at >= end, end, begin)
    for name, v in (("pos", at - begin), ("seg", segment), ("wpos", at)):
        meta_w[META[name]:META[name] + 1] = v.astype(F32)
    spot = jnp.zeros((rows, rows), F32)
    for s in range(n):
        row, col = place_r[s:s + 1, :], place_c[:, s:s + 1]
        s_row, s_rank = arrival(row, col)
        put = jnp.where((s_row == g) & (s_rank + s * per == iota((rows, rows), 0)), 1.0, 0.0).astype(BF)
        work = jnp.where(col - col // rows * rows == iota((rows, rows), 1), 1.0, 0.0).astype(BF)
        spot = spot + mm(put, work)
    spot = spot.astype(BF)
    left, moved = meta_w[...], 0.0
    for _ in range(3):
        piece = left.astype(BF)
        moved = moved + mm_t(piece, spot)
        left = left - piece.astype(F32)
    meta_all[g] = moved
    sent = [ring.send(meta_all.at[g], meta_all.at[g], ms.at[o], mr.at[o], ring.to(o), t) for o in range(1, n)]

    mine = pl.ds(pl.multiple_of(t * width, width), width)
    dy_send[...] = mm(sorter, out_grad[:, mine]).astype(BF).reshape(n, per, width)
    dealt = [ring.send(dy_send.at[ring.to(o)], dy_own.at[g], dys.at[o], dyr.at[o], ring.to(o), t) for o in range(1, n)]
    dy_own[g] = dy_send[g]

    stored = []

    def split(i):
        if i == 0:
            fetch.wait()
        at = pl.ds(i * 256, 256)
        for c, (v, hbm) in enumerate(((w_k, wk_hbm), (w_v, wv_hbm))):
            v[at, :] = w_kv[at, c, :]
            stored.append(pltpu.make_async_copy(v.at[at, :], hbm.at[at, :], osem.at[c, i]))
            stored[-1].start()

    def tables(first, gate, out_rows, out_gate):
        m = meta_all[g]
        for e in range(n):
            out_rows[e] = slot_table(m, first, float(e), CAP)
            out_gate[e] = slot_gates(m, first, gate, float(e), out_rows[e])

    def hops(k):
        for c in count:
            hop_on(True, k, c)
            hop_on(False, k, c)

    tables(META["mr0"], META["mg0"], mlp_rows, mlp_gate)
    hops(1)
    tables(META["ar0"], META["ag0"], att_rows, att_gate)
    hops(2)
    hops(3)
    for zz in range(depth):
        from_y(zz, 0)
    for c in dealt:
        c.wait_recv()
    slots = mm(mlp_rows[...].reshape(n * CAP, rows), dy_own[...].reshape(rows, width)).astype(BF)
    for j in range(2):
        gat.out(j, slots[:, j * gw:(j + 1) * gw])
    for i in range(4):
        split(i)

    def whole(q, off):
        return x_all.at[:, :, :, pl.ds(pl.multiple_of(q * width + off, half), half)]

    cores = [ring.send(whole(t, half), whole(t, half), cs.at[0], cr.at[0], g, ring.tc)]
    for c in (1, 2):
        split(3 + c)
        for zz in range(depth):
            from_y(zz, c)
        ref = whole(chunks[c][1], 0)
        cores.append(ring.send(ref, ref, cs.at[c], cr.at[c], g, ring.tc))
    for c in sent:
        c.wait_recv()
    me = g.astype(F32)
    for e in range(n):
        m = meta_all[e]
        att_in[e] = slot_gates(m, META["ar0"], META["ag0"], me, slot_table(m, META["ar0"], me, CAP))
        mlp_in[e] = slot_gates(m, META["mr0"], META["mg0"], me, slot_table(m, META["mr0"], me, CAP))
    split(6)
    split(7)
    for u in range(n):
        ref = x_all.at[:, u, :, pl.ds(pl.multiple_of(ring.tx * width + half, half), half)]
        rcopy(ref, ref, xs.at[u], xr.at[u], g, ring.tx).wait_recv()
    cores.append(ring.send(whole(ring.tx, half), whole(ring.tx, half), cs.at[3], cr.at[3], g, ring.tc))
    x_own[...] = x_all[g, :, :, mine].reshape(rows, width).astype(F32)
    for c in cores:
        c.wait_recv()
    for u in range(n):
        ref = x_all.at[:, u, :, cols[0]]
        rcopy(ref, ref, xs.at[u], xr.at[u], g, ring.tx).wait_send()
    for c in count:
        for zz in range(depth):
            ref = unit(zz, y, c)
            rcopy(ref, ref, ys.at[zz, c], yr.at[zz, c], pairs(z, 1 - y), t).wait_send()
        for hop in range(depth - 1):
            for up in (True, False):
                zz = z - hop if up else z + hop
                on = z + 1 if up else z - 1
                ss, rs = (zs, zr) if up else (ws, wr)

                @pl.when((zz >= 0) & (on < depth) if up else (zz < depth) & (on >= 0))
                def _(zz=zz, on=on, ss=ss, rs=rs, hop=hop, c=c):
                    ref = unit(zz, y, c)
                    rcopy(ref, ref, ss.at[hop, c], rs.at[hop, c], pairs(on, y), t).wait_send()
    fetch_q.wait()

    pair, steps = 2, n // 2
    heads = w_q.shape[1] // HD
    hw = w_q.shape[1]

    def out_copies(i):
        at = pl.ds(pair * i, pair)
        return (pltpu.make_async_copy(normed.at[at], normed_hbm.at[at], nsem.at[0, i]),
                pltpu.make_async_copy(picked.at[at], picked_hbm.at[at], nsem.at[1, i]))

    def two_groups(i, carry):
        @pl.when(i == 0)
        def _():
            gat.cross(0)

        @pl.when(i == 1)
        def _():
            gat.cross(1)

        @pl.when(i == 2)
        def _():
            gat.core(0)

        two = pl.ds(pair * i, pair)
        flat = x_all[two].reshape(pair * rows, features).astype(F32)
        s = lax.rsqrt(jnp.mean(flat * flat, axis=-1, keepdims=True) + EPSILON)
        scale[two] = s.reshape(pair, rows, 1)
        normed[two] = (flat * s * gain[...]).astype(BF).reshape(pair, rows, features)
        low = normed[two].reshape(pair * rows, features)
        k_all, v_all = mm(low, w_k[...]), mm(low, w_v[...])
        for p in range(pair):
            at = pair * i + p
            m = meta_all[at]
            m_t = m.T
            table = slot_table(m, META["ar0"], me, CAP)
            at_pos = position_rows(m_t)
            rr = slice(p * rows, (p + 1) * rows)
            keys[at] = turned(k_all[rr], looked_up(at_pos, cos_t[...]), looked_up(at_pos, sin_t[...])).astype(BF)
            values[at] = v_all[rr].astype(BF)
            picked[at] = mm(table, normed[at]).astype(BF)
            slot_pos = mm(table, at_pos).astype(BF)
            turn_slots[at, :, :HD] = looked_up(slot_pos, cos_t[...])
            turn_slots[at, :, HD:] = looked_up(slot_pos, sin_t[...])
            bias[at] = (mm(table, allowed_pairs(m, m_t)) - 1.0) * 1e30
        for c in out_copies(i):
            c.start()
        q_all = mm(picked[two].reshape(pair * CAP, features), w_q[...])
        for p in range(pair):
            at = pair * i + p
            query[at] = turned(q_all[p * CAP:(p + 1) * CAP], turn_slots[at, :, :HD], turn_slots[at, :, HD:]).astype(BF)
        for p in range(pair):
            at = pair * i + p
            for h in range(heads):
                hh = slice(h * HD, (h + 1) * HD)
                scores = mm_t(query[at, :, hh], keys[at, :, hh]) / math.sqrt(HD) + bias[at]
                attn[at, :, hh] = mm(softmax_rows(scores).astype(BF), values[at, :, hh]).astype(BF)
        return carry

    lax.fori_loop(0, steps, two_groups, 0)
    gat.core(1)
    for j in range(2):
        gat.here(j)
    for e in range(n):
        d_mbr[e] = (dy_rows[e].astype(F32) * mlp_in[e]).astype(BF)
    gat.sent()
    for i in range(steps):
        for c in out_copies(i):
            c.wait()
    for c in stored:
        c.wait()
    ring.finish()


def slot_gates(meta, first, gate, name, table):
    per_token = (jnp.where(meta[first:first + 1] == name, meta[gate:gate + 1], 0.0)
                 + jnp.where(meta[first + 1:first + 2] == name, meta[gate + 1:gate + 2], 0.0))
    return jnp.sum(table.astype(F32) * per_token, axis=1, keepdims=True)


def front(tokens, out_grad, place, att_routes, att_gates, mlp_routes, mlp_gates, seq_lengths, gain, cos_t, sin_t, w_kv, w_q, n, cid):
    rows, features = tokens.shape
    width, per, depth = features // 4, rows // n, n // 2
    hw = w_kv.shape[2]
    sds = jax.ShapeDtypeStruct
    vm, any_ = pl.BlockSpec(memory_space=VM), pl.BlockSpec(memory_space=pl.ANY)
    table, gate, plain = sds((n, CAP, rows), BF), sds((n, CAP, 1), F32), sds((features, hw), BF)
    group, slot = sds((n, rows, hw), BF), sds((n, CAP, hw), BF)
    return pl.pallas_call(
        functools.partial(front_body, n),
        out_shape=(
            sds((n, per, width), BF), sds((n, 16, rows), F32), sds((rows, rows), BF), table, gate, table, gate, gate,
            plain, plain, sds((rows, width), F32), sds((n, rows, features), BF), sds((n, CAP, features), BF),
            group, group, slot, slot, sds((n, rows, 1), F32), sds((n, CAP, rows), F32), sds((n, CAP, 2 * HD), F32),
            sds((n, CAP, features), BF)),
        in_specs=[vm] * 11 + [any_] * 2, out_specs=[vm] * 8 + [any_] * 2 + [vm] + [any_] * 2 + [vm] * 8,
        scratch_shapes=[
            VM((n, n, per, features), BF), VM((n, per, width), BF), VM(w_kv.shape, BF), VM((features, hw), BF),
            VM((features, hw), BF), VM((features, hw), BF), VM((16, rows), F32), VM((n, CAP, 1), F32), VM((n, rows, features), BF),
            VM((n, CAP, features), BF), VM((n, CAP, features), BF), VM((2, n, CAP, width // 2), BF),
            DMA((2,)), DMA((2, features // 256)), DMA((2, n // 2))] + GATHER_SEMS(2, n)
        + [DMA((n,))] * 4 + [DMA((depth, 3))] * 6 + [DMA((n,))] * 2 + [DMA((4,))] * 2,
        name="front", compiler_params=pltpu.CompilerParams(
            collective_id=cid, has_side_effects=True, vmem_limit_bytes=63 * 2**20),
    )(tokens, out_grad, place, att_routes, att_gates, mlp_routes, mlp_gates, seq_lengths, gain, cos_t, sin_t, w_kv, w_q)


def tile_list(size, step):
    return [(a, min(step, size - a)) for a in range(0, size, step)]


class ChunkReduce:
    def __init__(self, ring, partial, whole, pbuf, sent, got, sems):
        self.ring, self.partial, self.whole, self.pbuf = ring, partial, whole, pbuf
        self.cbuf, self.xbuf, self.dbuf = sent
        self.cin, self.xin, self.rbuf = got
        cs, cr, xs, xr, ds, dr = sems
        k, (nc, n, _, _) = ring, self.xbuf.shape
        self.c = [rcopy(self.cbuf.at[j], self.cin.at[j], cs.at[j], cr.at[j], k.g, k.tc) for j in range(nc)]
        self.x = [rcopy(self.xbuf.at[j], self.xin.at[j], xs.at[j], xr.at[j], k.g, k.tx) for j in range(nc)]
        self.d = [
            [rcopy(self.dbuf.at[j, k.to(o)], self.rbuf.at[j, k.g], ds.at[j, o], dr.at[j, o], k.to(o), k.t) for o in range(1, n)]
            for j in range(nc)]

    def core(self, j):
        k = self.ring
        n, r, cw = self.xbuf.shape[1:]
        self.whole[...] = self.partial(j)
        take = lambda q: self.whole[:, pl.ds(pl.multiple_of(q * cw, cw), cw)].reshape(n, r, cw)
        self.cbuf[j, 0] = take(k.tc).astype(BF)
        self.cbuf[j, 1] = take(k.tcx).astype(BF)
        self.c[j].start()
        self.pbuf[j, 0] = take(k.t)
        self.pbuf[j, 1] = take(k.tx)

    def cross(self, j):
        self.c[j].wait_recv()
        self.xbuf[j] = (self.pbuf[j, 1] + self.cin[j, 1].astype(F32)).astype(BF)
        self.x[j].start()

    def home(self, j):
        g = self.ring.g
        self.x[j].wait_recv()
        self.dbuf[j] = (self.pbuf[j, 0] + self.cin[j, 0].astype(F32) + self.xin[j].astype(F32)).astype(BF)
        for c in self.d[j]:
            c.start()
        self.rbuf[j, g] = self.dbuf[j, g]

    def rows(self, j):
        for c in self.d[j]:
            c.wait_recv()
        return self.rbuf[j].reshape(-1, self.rbuf.shape[-1])

    def sent_core(self):
        for c in self.c:
            c.wait_send()

    def sent_rest(self):
        for c in self.x + [c for row in self.d for c in row]:
            c.wait_send()


class ChunkGather:
    def __init__(self, ring, place, sbuf, sems):
        self.ring, self.place, self.sbuf = ring, place, sbuf
        ss, rs, xs, xr, cs, cr, c2s, c2r = sems
        k, (nc, n, _, cw) = ring, sbuf.shape
        self.d = [
            [rcopy(sbuf.at[j, k.to(o)], place(j, k.t, k.g), ss.at[j, o], rs.at[j, o], k.to(o), k.t) for o in range(1, n)]
            for j in range(nc)]
        pair = lambda j, q, a, b, to: rcopy(place(j, q, None), place(j, q, None), a.at[j], b.at[j], k.g, to)
        self.x = [pair(j, k.t, xs, xr, k.tx) for j in range(nc)]
        self.c = [pair(j, k.t, cs, cr, k.tc) for j in range(nc)]
        self.c2 = [pair(j, k.tx, c2s, c2r, k.tc) for j in range(nc)]

    def out(self, j, rows):
        self.sbuf[j] = rows.reshape(self.sbuf.shape[1:])
        for c in self.d[j]:
            c.start()
        self.place(j, self.ring.t, self.ring.g)[...] = self.sbuf[j, self.ring.g]

    def cross(self, j):
        for c in self.d[j]:
            c.wait_recv()
        self.x[j].start()
        self.c[j].start()

    def core(self, j):
        self.x[j].wait_recv()
        self.c2[j].start()

    def here(self, j):
        self.c[j].wait_recv()
        self.c2[j].wait_recv()

    def sent(self):
        for c in [c for row in self.d for c in row] + self.x + self.c + self.c2:
            c.wait_send()


def middle_body(
    n, attn, x_own, att_rows, att_gate, att_in, mlp_rows, dy_own, gain, query, dm_hbm, wo_hbm, wg_hbm, wu_hbm, wd_hbm,
    d_attn, d_hidden, hidden, mb_rows, gain_part, n2_hbm, inner_hbm, dg_hbm, du_hbm, obr_hbm, q_back, *scratch,
):
    (d_mbr, wo, wg, wu, wd, inner, d_gate, d_up, d_rows, n2_st, obr_st, xbuf3, mb_sum, cin3, xin3, hid, att_t, mlp_t, whole, gate_acc, up_acc, d_in, pbuf, cbuf, xbuf, dbuf,
     cin1, xin1, rb1, cin2, xin2, rb2, sb1, sb2, sq, sq_in, r_own, r_in, r_to, r_back, s_col) = scratch[:41]
    wsem, qs, qr, as_, ar, rss, rsr, rds, rdr, osem, nsem, bsem = scratch[41:53]
    s1, s2s, s3, g1, g2 = scratch[53:59], scratch[59:65], scratch[65:71], scratch[71:79], scratch[79:87]
    ring = Ring(n)
    g, t = ring.g, ring.t
    rows, width = x_own.shape
    cw = width // NC
    features, ff = 4 * width, wg.shape[1]
    slots = attn.shape[0]

    loads = {"wo": [], "wg": [], "wu": []}
    for j in range(NC):
        for q in range(4):
            to, at = pl.ds((j * 4 + q) * cw, cw), pl.ds(q * width + j * cw, cw)
            i = j * 4 + q
            loads["wo"].append(pltpu.make_async_copy(wo_hbm.at[:, at], wo.at[:, to], wsem.at[0, i]))
            loads["wg"].append(pltpu.make_async_copy(wg_hbm.at[at, :], wg.at[to, :], wsem.at[1, i]))
            loads["wu"].append(pltpu.make_async_copy(wu_hbm.at[at, :], wu.at[to, :], wsem.at[2, i]))
    loads["wd"] = [pltpu.make_async_copy(wd_hbm, wd, wsem.at[3, 0])]
    loads["dm"] = [pltpu.make_async_copy(dm_hbm, d_mbr, wsem.at[3, 1])]

    def fetch(*names):
        for name in names:
            for c in loads[name]:
                c.start()

    fetch("wo")

    def loaded(name):
        for c in loads[name]:
            c.wait()

    chunk = lambda j: pl.ds(j * 4 * cw, 4 * cw)
    att_t[...] = att_rows[...].T
    mlp_t[...] = mlp_rows[...].T
    ring.greet_everyone()
    asked = [rcopy(query.at[ring.to(o)], q_back.at[g], as_.at[o], ar.at[o], ring.to(o), t) for o in range(1, n)]

    red1 = ChunkReduce(
        ring, lambda j: mm(attn[...], wo[:, chunk(j)]), whole, pbuf, (cbuf, xbuf, dbuf), (cin1, xin1, rb1), s1)
    gat1 = ChunkGather(
        ring, lambda j, q, e: hid.at[j, slice(None) if e is None else e, :, pl.ds(pl.multiple_of(q * cw, cw), cw)], sb1, g1)
    shared = [rcopy(sq, sq_in.at[i], qs.at[i], qr.at[i], g, q) for i, q in enumerate([ring.tc, ring.tx, ring.tcx])]
    ones = jnp.ones((8, cw), BF)

    def hidden_chunk(j):
        high, low = split_bf(red1.rows(j).astype(F32) * att_gate[...])
        got = x_own[:, j * cw:(j + 1) * cw] + mm(att_t[...], high) + mm(att_t[...], low)
        hidden[:, j * cw:(j + 1) * cw] = got
        gat1.out(j, mm(mlp_rows[...], got.astype(BF)).astype(BF))
        high, low = split_bf(got * got)
        squares = mm_t(ones, high) + mm_t(ones, low)
        sq[...] = squares if j == 0 else sq[...] + squares
        if j == NC - 1:
            for c in shared:
                c.start()

    def gain_cols(j):
        return jnp.concatenate([gain[:, q * width + j * cw:q * width + (j + 1) * cw] for q in range(4)], axis=1)

    pieces = tile_list(ff, 512)

    def d_inner(i):
        if i == 0:
            loaded("wd")
            loaded("dm")
        a, w = pieces[i]
        d_in[:, a:a + w] = mm_t(d_mbr[...], wd[a:a + w, :])

    def absorb(j):
        gat1.here(j)
        v = hid[j].reshape(slots, 4 * cw).astype(F32)
        part = jnp.sum(v * v, axis=1, keepdims=True)
        s_col[...] = part if j == 0 else s_col[...] + part
        u = (v * gain_cols(j)).astype(BF)
        for a, w in pieces:
            cc = slice(a, a + w)
            gate, up = mm(u, wg[chunk(j), cc]), mm(u, wu[chunk(j), cc])
            gate_acc[:, cc] = gate if j == 0 else gate_acc[:, cc] + gate
            up_acc[:, cc] = up if j == 0 else up_acc[:, cc] + up

    loaded("wo")
    for j in range(NC):
        red1.core(j)
        if j:
            red1.cross(j - 1)
    red1.cross(NC - 1)
    fetch("wd", "dm", "wg", "wu")
    plan = [(2 * j, 0, functools.partial(red1.home, j)) for j in range(NC)]
    plan += [(2 * j + 3, 1, functools.partial(hidden_chunk, j)) for j in range(NC)]
    plan += [(2 * j + 7, 2, functools.partial(gat1.cross, j)) for j in range(NC)]
    plan += [(2 * j + 9, 3, functools.partial(gat1.core, j)) for j in range(NC)]
    plan += [(2 * i + 1.5, 4, functools.partial(d_inner, i)) for i in range(len(pieces))]
    plan += [(2 * j + 10.5, 5, functools.partial(absorb, j)) for j in range(NC)]
    plan += [(10.2, 0, lambda: (loaded("wg"), loaded("wu")))]
    plan += [(9.5, 0, lambda: [c.start() for c in asked])]
    for _, _, run in sorted(plan, key=lambda s: s[:2]):
        run()

    s_col[...] = lax.rsqrt(s_col[...] / features + EPSILON)
    r_own[...] = jnp.zeros_like(r_own)

    def units(at, size):
        s = s_col[...]
        gate, up, d = gate_acc[:, at] * s, up_acc[:, at] * s, d_in[:, at]
        sig = jax.nn.sigmoid(gate)
        silu = gate * sig
        inner[:, at] = (silu * up).astype(BF)
        du = (d * silu).astype(BF)
        dg = (d * up * sig * (1.0 + gate * (1.0 - sig))).astype(BF)
        d_up[:, at] = du
        d_gate[:, at] = dg
        r_own[...] += mm_t(jnp.ones((8, size), BF), (gate * dg.astype(F32) + up * du.astype(F32)).astype(BF))

    def unit_tile(i, _):
        units(pl.ds(pl.multiple_of(i * 128, 128), 128), 128)
        return _

    lax.fori_loop(0, ff // 128, unit_tile, 0)
    stored = [pltpu.make_async_copy(a, b, osem.at[i]) for i, (a, b) in enumerate(
        [(inner, inner_hbm), (d_gate, dg_hbm), (d_up, du_hbm)])]
    for c in stored:
        c.start()
    red1.sent_core()
    red1.sent_rest()
    for c in shared:
        c.wait_recv()
    total = (sq[...] + sq_in[0] + sq_in[1] + sq_in[2])[:1]
    eye = iota((rows, rows), 0) == iota((rows, rows), 1)
    scale = lax.rsqrt(jnp.sum(jnp.where(eye, total, 0.0), axis=1, keepdims=True) / features + EPSILON)

    told = [rcopy(r_own, r_in.at[i], rss.at[i], rsr.at[i], g, q) for i, q in enumerate([ring.tc, ring.tx, ring.tcx])]
    for c in told:
        c.start()
    half = lambda d: pl.ds(pl.multiple_of(d // 2 * 128, 128), 128)
    pairs = [rcopy(r_to.at[:, half(ring.to(o))], r_back.at[g], rds.at[o], rdr.at[o], ring.to(o), t) for o in range(1, n)]

    def share_r():
        for c in told:
            c.wait_recv()
        r_to[...] = r_own[...] + r_in[0] + r_in[1] + r_in[2]
        for c in pairs:
            c.start()
        r_back[g] = r_to[:, half(g)]

    total_r = {}

    def take_r():
        for c in pairs:
            c.wait_recv()
        odd = lax.rem(g, 2) == 1
        got = jnp.concatenate([jnp.where(odd, r_back[e][:, 64:], r_back[e][:, :64]) for e in range(n)], axis=1)
        high, low = split_bf(got)
        total_r[0] = (mm_t(mlp_t[...], high) + mm_t(mlp_t[...], low))[:, :1] / features

    red2 = ChunkReduce(
        ring, lambda j: mm_t(d_gate[...], wg[chunk(j), :]) + mm_t(d_up[...], wu[chunk(j), :]), whole, pbuf,
        (cbuf, xbuf, dbuf), (cin2, xin2, rb2), s2s)
    gat2 = ChunkGather(
        ring, lambda j, q, e: d_rows.at[slice(None) if e is None else e, :, cols_of(q, j, width, cw)], sb2, g2)

    def mixed_cols(j):
        return jnp.concatenate([mm(inner[...], wd[:, q * width + j * cw:q * width + (j + 1) * cw]) for q in range(4)], axis=1)

    red3 = ChunkReduce(ring, mixed_cols, whole, pbuf, (cbuf, xbuf3, mb_sum), (cin3, xin3, mb_rows), s3)

    def mixed_core(j):
        red2.c[j].wait_send()
        red3.core(j)

    def d_hidden_chunk(j):
        got = red2.rows(j)
        if j == 0:
            take_r()
        cc = slice(j * cw, (j + 1) * cw)
        h = hidden[:, cc]
        d_n = mm(mlp_t[...], got)
        d_h = dy_own[:, cc].astype(F32) + scale * (gain[:, cols_of(t, j, width, cw)] * d_n) - h * (scale * scale) * total_r[0]
        d_hidden[:, cc] = d_h
        gain_part[:, cc] = jnp.broadcast_to(jnp.sum(d_n * h * scale, axis=0, keepdims=True), (8, cw))
        gat2.out(j, mm(att_rows[...], d_h.astype(BF)).astype(BF))

    kept, given = [], []

    def keep_normed(j):
        st = n2_st.at[j % 2]
        if j > 1:
            for c in kept[4 * (j - 2):4 * (j - 1)]:
                c.wait()
        st[...] = (hid[j].reshape(slots, 4 * cw).astype(F32) * s_col[...] * gain_cols(j)).astype(BF)
        for q in range(4):
            kept.append(pltpu.make_async_copy(
                st.at[:, pl.ds(q * cw, cw)], n2_hbm.at[:, pl.ds(q * width + j * cw, cw)], nsem.at[j, q]))
            kept[-1].start()

    def attend_rows(j):
        gat2.here(j)
        st = obr_st.at[j % 2]
        if j > 1:
            for c in given[4 * (j - 2):4 * (j - 1)]:
                c.wait()
        for q in range(4):
            v = d_rows[:, :, q * width + j * cw:q * width + (j + 1) * cw].reshape(slots, cw)
            st[:, q * cw:(q + 1) * cw] = (v.astype(F32) * att_in[...]).astype(BF)
        for q in range(4):
            given.append(pltpu.make_async_copy(
                st.at[:, pl.ds(q * cw, cw)], obr_hbm.at[:, pl.ds(q * width + j * cw, cw)], bsem.at[j, q]))
            given[-1].start()
        got = mm_t(st[...], wo[:, chunk(j)])
        hw = wo.shape[0]
        d_in[:, :hw] = got if j == 0 else d_in[:, :hw] + got

    for j in range(NC):
        red2.core(j)
        if j == 0:
            share_r()
        else:
            red2.cross(j - 1)
    red2.cross(NC - 1)
    plan = [(2 * j, 0, functools.partial(red2.home, j)) for j in range(NC)]
    plan += [(2 * j + 3, 1, functools.partial(d_hidden_chunk, j)) for j in range(NC)]
    plan += [(2 * j + 7, 2, functools.partial(gat2.cross, j)) for j in range(NC)]
    plan += [(2 * j + 9, 3, functools.partial(gat2.core, j)) for j in range(NC)]
    plan += [(2 * j + 1.5, 4, functools.partial(keep_normed, j)) for j in range(NC)]
    plan += [(2 * j + 0.7, 5, functools.partial(mixed_core, j)) for j in range(NC)]
    plan += [(2 * j + 2.7, 6, functools.partial(red3.cross, j)) for j in range(NC)]
    plan += [(2 * j + 9.7, 7, functools.partial(red3.home, j)) for j in range(NC)]
    plan += [(2 * j + 11, 8, functools.partial(attend_rows, j)) for j in range(NC)]
    for _, _, run in sorted(plan, key=lambda s: s[:2]):
        run()
    d_attn[...] = d_in[:, :wo.shape[0]].astype(BF).reshape(d_attn.shape)
    for c in asked + [c for row in red3.d for c in row]:
        c.wait_recv()
    q_back[g] = query[g]
    for c in stored + kept[8:] + given[8:]:
        c.wait()
    for c in asked + shared + told + pairs:
        c.wait_send()
    gat1.sent()
    gat2.sent()
    red2.sent_rest()
    red3.sent_core()
    red3.sent_rest()


def middle(attn, x_own, att_rows, att_gate, att_in, mlp_rows, dy_own, gain, d_mbr, query, wo, wg, wu, wd, n, cid):
    slots, (rows, width) = attn.shape[0], x_own.shape
    r, cw, features, ff, hw = slots // n, width // NC, 4 * width, wg.shape[1], attn.shape[1]
    any_, vm = pl.BlockSpec(memory_space=pl.ANY), pl.BlockSpec(memory_space=VM)
    sds = jax.ShapeDtypeStruct
    one, two = VM((NC, n, r, cw), BF), VM((NC, 2, n, r, cw), BF)
    units = sds((slots, ff), BF)
    return pl.pallas_call(
        functools.partial(middle_body, n),
        out_shape=(
            sds((n, r, hw), BF), sds((rows, width), F32), sds((rows, width), F32), sds((NC, n, r, cw), BF), sds((8, width), F32),
            sds((slots, features), BF), units, units, units, sds((slots, features), BF), sds((n, r, hw), BF)),
        in_specs=[vm] * 9 + [any_] * 5, out_specs=[vm] * 5 + [any_] * 5 + [vm],
        scratch_shapes=[
            VM((slots, features), BF), VM((hw, features), BF), VM((features, ff), BF), VM((features, ff), BF), VM((ff, features), BF),
            VM((slots, ff), BF), VM((slots, ff), BF), VM((slots, ff), BF), VM((n, r, features), BF),
            VM((2, slots, 4 * cw), BF), VM((2, slots, 4 * cw), BF), one, one, two, one,
            VM((NC, n, r, 4 * cw), BF), VM((rows, slots), BF), VM((rows, slots), BF),
            VM((slots, 4 * cw), F32), VM((slots, ff), F32), VM((slots, ff), F32), VM((slots, ff), F32),
            VM((NC, 2, n, r, cw), F32), two, one, one]
        + [two, one, one] * 2 + [one, one]
        + [VM((8, rows), F32), VM((3, 8, rows), F32), VM((8, slots), F32), VM((3, 8, slots), F32), VM((8, slots), F32),
           VM((n, 8, 128), F32), VM((slots, 1), F32)]
        + [DMA((4, 16)), DMA((3,)), DMA((3,)), DMA((n,)), DMA((n,)), DMA((3,)), DMA((3,)), DMA((n,)), DMA((n,)), DMA((3,)),
           DMA((NC, 4)), DMA((NC, 4))]
        + REDUCE_SEMS(NC, n) * 3 + GATHER_SEMS(NC, n) * 2,
        name="middle", compiler_params=pltpu.CompilerParams(
            collective_id=cid, has_side_effects=True, vmem_limit_bytes=63 * 2**20),
    )(attn, x_own, att_rows, att_gate, att_in, mlp_rows, dy_own, gain, query, d_mbr, wo, wg, wu, wd)


def fast_local(
    tokens, out_grad, row_place, seq_lengths, att_routes, att_gates, mlp_routes, mlp_gates,
    gain_attn, w_kv, w_query, w_out, gain_mlp, w_gate, w_up, w_down,
):
    rows, features = tokens.shape
    n = lax.axis_size("dp")
    width = features // 4
    hw = w_kv.shape[2]

    cos_t, sin_t = angle_tables(rows)
    (dy_own, meta_all, sorter, att_out, att_gate, mlp_out, mlp_gate, att_in, w_k, w_v, x_own, normed, picked, keys, values,
     query, attn, scale_attn, bias, turn_slots, d_mbr) = front(
        tokens, out_grad, row_place.reshape(n, rows), att_routes.T, att_gates.T, mlp_routes.T, mlp_gates.T, seq_lengths,
        gain_attn[None], cos_t, sin_t, w_kv, w_query[0], n, cid=12)
    dy_own = dy_own.reshape(rows, width)
    att_rows, mlp_rows = att_out.reshape(n * CAP, rows), mlp_out.reshape(n * CAP, rows)
    normed_flat, picked = normed.reshape(n * rows, features), picked.reshape(n * CAP, features)
    attn = attn.reshape(n * CAP, hw)
    d_mbr = d_mbr.reshape(n * CAP, features)

    d_attn, d_hidden, hidden, mb_rows, gain_mlp_part, normed2, inner, d_gate, d_up, d_obr, query_back = middle(
        attn, x_own, att_rows, att_gate.reshape(-1, 1), att_in.reshape(-1, 1), mlp_rows, dy_own, gain_mlp[None],
        d_mbr, query, w_out[0], w_gate[0], w_up[0], w_down[0], n, cid=9)
    w_gate_grad = mm_rows(normed2, d_gate)[None]
    w_up_grad = mm_rows(normed2, d_up)[None]
    w_down_grad = mm_rows(inner, d_mbr)[None]

    d_kv_all, mixed, tokens_grad, gain_attn_grad, gain_mlp_grad, dq_pre = layer_tail(
        (d_attn, mb_rows, meta_all, cos_t, sin_t, x_own, scale_attn, gain_attn[None], d_hidden, hidden,
         mlp_gate.reshape(-1, 1), mlp_rows, att_rows, gain_mlp_part, sorter),
        (query, keys, values, bias, turn_slots, query_back, w_query[0], w_k, w_v), n, cid=11)
    w_out_grad = mm_rows(attn, d_obr)[None]
    w_query_grad = mm_rows(picked, dq_pre.reshape(n * CAP, hw))[None]
    w_kv_grad = map_grad(normed_flat, d_kv_all.reshape(n * rows, 2 * hw))
    return (
        mixed, tokens_grad, gain_attn_grad[0], w_kv_grad, w_query_grad, w_out_grad, gain_mlp_grad[0],
        w_gate_grad, w_up_grad, w_down_grad,
    )


def solution(mesh):
    placed = (
        P("dp", None),
        P("dp", None),
        P(),
        P("dp", None),
        P("dp", None),
        P("dp", None),
        P("dp", None),
        P("dp", None),
        P(),
        P(None, None, "tensor"),
        P("dp", None, "tensor"),
        P("dp", "tensor", None),
        P(),
        P("dp", None, "tensor"),
        P("dp", None, "tensor"),
        P("dp", "tensor", None),
    )
    dealt = mesh.shape["dp"] == EXPERTS and mesh.shape["tensor"] == 4
    return jax.shard_map(
        fast_local if dealt else local,
        mesh=mesh,
        in_specs=placed,
        out_specs=(
            P("dp", None),
            P("dp", None),
            P(),
            P(None, None, "tensor"),
            P("dp", None, "tensor"),
            P("dp", "tensor", None),
            P(),
            P("dp", None, "tensor"),
            P("dp", None, "tensor"),
            P("dp", "tensor", None),
        ),
        check_vma=False,
    )
```

```python
import functools
import math

import jax
import jax.numpy as jnp
import numpy as np
from jax import lax
from jax.experimental import pallas as pl
from jax.experimental.pallas import tpu as pltpu
from jax.sharding import PartitionSpec as P

HD = 128
ATT_EXPERTS = 8
EXPERTS = 8
CAP = 64


EPSILON = 1e-05
THETA = 10000.0


def inverse_rms(values_in):
    return lax.rsqrt(jnp.mean(values_in * values_in, axis=-1, keepdims=True) + EPSILON)


def norm_backward(inputs, inv_root, gain, incoming):
    weighted = incoming * gain
    inner_mean = jnp.mean(inputs * weighted, axis=-1, keepdims=True)
    return inv_root * weighted - inputs * (inv_root * inv_root * inv_root) * inner_mean


def rotate(vectors, positions, direction):
    half_dim = vectors.shape[-1] // 2
    frequency = jnp.exp(-math.log(THETA) * jnp.arange(half_dim, dtype=jnp.float32) / half_dim)
    angles = positions.astype(jnp.float32)[:, None] * frequency[None, :]
    target = (vectors.shape[0],) + (1,) * (vectors.ndim - 2) + (half_dim,)
    cosine = jnp.cos(angles).reshape(target)
    sine = direction * jnp.sin(angles).reshape(target)
    former = vectors[..., :half_dim]
    latter = vectors[..., half_dim:]
    return jnp.concatenate(
        [former * cosine - latter * sine, latter * cosine + former * sine], axis=-1
    )


def expert_slots(routes, experts, capacity):
    flattened = routes.reshape(-1)
    pair_count = flattened.shape[0]
    one_hot = (flattened[:, None] == jnp.arange(experts, dtype=jnp.int32)[None, :]).astype(
        jnp.int32
    )
    earlier = jnp.cumsum(one_hot, axis=0) - one_hot
    position = jnp.sum(earlier * one_hot, axis=1)
    slot_table = jnp.full((experts, capacity), pair_count, jnp.int32)
    slot_table = slot_table.at[flattened, position].set(jnp.arange(pair_count, dtype=jnp.int32))
    return (flattened * capacity + position, slot_table)


def pick_rows(source_rows, slot_table):
    padded = jnp.concatenate(
        [source_rows, jnp.zeros((1, source_rows.shape[1]), source_rows.dtype)], axis=0
    )
    return padded[slot_table]


def send_slices(source_rows, slot_table, group_size):
    picked = pick_rows(source_rows, slot_table)
    experts, capacity, features = picked.shape
    divided = picked.reshape(experts, capacity, group_size, features // group_size)
    return divided.transpose(0, 2, 1, 3).reshape(
        experts * group_size, capacity, features // group_size
    )


def send_copies(source_rows, slot_table, group_size):
    picked = pick_rows(source_rows, slot_table)
    experts, capacity, features = picked.shape
    copies = jnp.broadcast_to(picked[:, None], (experts, group_size, capacity, features))
    return copies.reshape(experts * group_size, capacity, features)


def owners_summed(returned, pair_where, group_size):
    owners, capacity, features = returned.shape
    summed = returned.reshape(owners // group_size, group_size, capacity, features).sum(axis=1)
    return summed.reshape(-1, features)[pair_where]


def owners_joined(returned, pair_where, group_size):
    owners, capacity, features = returned.shape
    joined = returned.reshape(owners // group_size, group_size, capacity, features).transpose(
        0, 2, 1, 3
    )
    return joined.reshape(-1, group_size * features)[pair_where]


def query_return(pieces):
    return lax.all_to_all(pieces, "dp", split_axis=0, concat_axis=0, tiled=True)


def output_return(pieces):
    return lax.all_to_all(pieces, "dp", split_axis=0, concat_axis=0, tiled=True)


def expert_return(pieces):
    return lax.all_to_all(pieces, "dp", split_axis=0, concat_axis=0, tiled=True)


def tensor_total(pieces):
    return lax.psum(pieces, "tensor")


def deal_plan(row_place, rows_dev):
    device_count = lax.axis_size("dp")
    my_index = lax.axis_index("dp")
    per_peer = rows_dev // device_count
    every_place = row_place.reshape(device_count, rows_dev)
    my_places = lax.dynamic_index_in_dim(every_place, my_index, 0, keepdims=False)
    counting = jnp.arange(rows_dev, dtype=jnp.int32)
    ordering = jnp.argsort(my_places // rows_dev * rows_dev + counting)
    wanted = every_place // rows_dev == my_index
    chosen = jnp.argsort(
        jnp.where(wanted, counting[None, :], rows_dev + counting[None, :]), axis=1
    )[:, :per_peer]
    placed = jnp.take_along_axis(every_place, chosen, axis=1) % rows_dev
    return (ordering, placed.reshape(-1))


def masked_scores(query_b, keys_b, allowed):
    raw = jnp.einsum(
        "ikjd,mjd->kjim", query_b, keys_b, preferred_element_type=jnp.float32
    ) / math.sqrt(query_b.shape[-1])
    return jnp.where(allowed[None, None], raw, -1e30)


def local(
    tokens,
    out_grad,
    row_place,
    seq_lengths,
    att_routes,
    att_gates,
    mlp_routes,
    mlp_gates,
    gain_attn,
    w_kv,
    w_query,
    w_out,
    gain_mlp,
    w_gate,
    w_up,
    w_down,
):
    rows_dev, features = tokens.shape
    device_count = lax.axis_size("dp")
    group_size = device_count // EXPERTS
    per_peer = rows_dev // device_count
    counting = jnp.arange(rows_dev, dtype=jnp.int32)
    ordering, placed = deal_plan(row_place, rows_dev)
    unplace = jnp.zeros((rows_dev,), jnp.int32).at[placed].set(counting)
    unorder = jnp.zeros((rows_dev,), jnp.int32).at[ordering].set(counting)
    dealt_x, dealt_g = (
        lax.all_to_all(
            tokens[ordering].reshape(device_count, per_peer, features),
            "dp",
            split_axis=0,
            concat_axis=0,
            tiled=True,
        ),
        lax.all_to_all(
            out_grad[ordering].reshape(device_count, per_peer, features),
            "dp",
            split_axis=0,
            concat_axis=0,
            tiled=True,
        ),
    )
    residual = dealt_x.reshape(rows_dev, features)[unplace].astype(jnp.float32)
    top_grad = dealt_g.reshape(rows_dev, features)[unplace].astype(jnp.float32)
    lengths = seq_lengths[0]
    seq_ends = jnp.cumsum(lengths)
    segment = jnp.sum((counting[:, None] >= seq_ends[None, :]).astype(jnp.int32), axis=1)
    starts = seq_ends - lengths
    member = segment[:, None] == jnp.arange(lengths.shape[0], dtype=jnp.int32)[None, :]
    begins = jnp.sum(jnp.where(member, starts[None, :], 0), axis=1)
    positions = counting - begins
    allowed = (segment[:, None] == segment[None, :]) & (counting[None, :] <= counting[:, None])
    head_count = w_kv.shape[2] // HD
    scale_attn = inverse_rms(residual)
    normed = (residual * scale_attn * gain_attn).astype(jnp.bfloat16)
    kv_proj = jnp.einsum("ld,dck->lck", normed, w_kv, preferred_element_type=jnp.float32)
    keys = rotate(kv_proj[:, 0].reshape(rows_dev, head_count, HD), positions, 1.0).astype(
        jnp.bfloat16
    )
    values = kv_proj[:, 1].reshape(rows_dev, head_count, HD).astype(jnp.bfloat16)
    att_where, att_table = expert_slots(att_routes, ATT_EXPERTS, CAP)
    query_rows = lax.all_to_all(
        send_slices(normed, att_table // 2, group_size),
        "dp",
        split_axis=0,
        concat_axis=0,
        tiled=True,
    )
    query_part = jnp.einsum(
        "scd,dh->sch", query_rows, w_query[0], preferred_element_type=jnp.float32
    )
    query_pre = owners_summed(query_return(query_part), att_where, group_size)
    query_rot = rotate(query_pre.reshape(rows_dev, 2, head_count, HD), positions, 1.0).astype(
        jnp.bfloat16
    )
    scores = masked_scores(query_rot, keys, allowed)
    highest = jnp.max(scores, axis=-1, keepdims=True)
    expo = jnp.exp(scores - highest)
    row_total = jnp.sum(expo, axis=-1, keepdims=True)
    log_total = highest + jnp.log(row_total)
    probability = expo / row_total
    attn = jnp.einsum(
        "kjim,mjd->ikjd",
        probability.astype(jnp.bfloat16),
        values,
        preferred_element_type=jnp.float32,
    )
    attn_low = attn.astype(jnp.bfloat16).reshape(rows_dev * 2, head_count * HD)
    out_rows = lax.all_to_all(
        send_copies(attn_low, att_table, group_size), "dp", split_axis=0, concat_axis=0, tiled=True
    )
    out_part = jnp.einsum("sch,hd->scd", out_rows, w_out[0], preferred_element_type=jnp.float32)
    out_pairs = owners_joined(output_return(out_part), att_where, group_size).reshape(
        rows_dev, 2, features
    )
    hidden = residual + tensor_total(jnp.sum(out_pairs * att_gates[:, :, None], axis=1))
    gate_map, up_map, down_map = (w_gate[0], w_up[0], w_down[0])
    scale_mlp = inverse_rms(hidden)
    normed2 = (hidden * scale_mlp * gain_mlp).astype(jnp.bfloat16)
    mlp_where, mlp_table = expert_slots(mlp_routes, EXPERTS, CAP)
    expert_sent = send_copies(normed2, mlp_table // 2, group_size)
    expert_rows = lax.all_to_all(expert_sent, "dp", split_axis=0, concat_axis=0, tiled=True)
    flat_rows = expert_rows.reshape(-1, features)
    gate_act = jnp.dot(flat_rows, gate_map, preferred_element_type=jnp.float32)
    up_act = jnp.dot(flat_rows, up_map, preferred_element_type=jnp.float32)
    inner = (jax.nn.silu(gate_act) * up_act).astype(jnp.bfloat16)
    expert_part = jnp.dot(inner, down_map, preferred_element_type=jnp.float32).reshape(
        expert_rows.shape
    )
    expert_pairs = owners_summed(expert_return(expert_part), mlp_where, group_size).reshape(
        rows_dev, 2, features
    )
    mixed_rows = hidden + tensor_total(jnp.sum(expert_pairs * mlp_gates[:, :, None], axis=1))
    branch_grad = (
        (top_grad[:, None, :] * mlp_gates[:, :, None])
        .astype(jnp.bfloat16)
        .reshape(rows_dev * 2, features)
    )
    grad_sent = send_copies(branch_grad, mlp_table, group_size)
    grad_back, rows_back = (
        lax.all_to_all(grad_sent, "dp", split_axis=0, concat_axis=0, tiled=True),
        lax.all_to_all(expert_sent, "dp", split_axis=0, concat_axis=0, tiled=True),
    )
    grad_rows = grad_back.reshape(-1, features)
    rows_again = rows_back.reshape(-1, features)
    gate_again = jnp.dot(rows_again, gate_map, preferred_element_type=jnp.float32)
    up_again = jnp.dot(rows_again, up_map, preferred_element_type=jnp.float32)
    inner_again = (jax.nn.silu(gate_again) * up_again).astype(jnp.bfloat16)
    contract_rows = (((0,), (0,)), ((), ()))
    contract_cols = (((1,), (1,)), ((), ()))
    d_inner = lax.dot_general(
        grad_rows, down_map, contract_cols, preferred_element_type=jnp.float32
    )
    down_grad_all = lax.dot_general(
        inner_again, grad_rows, contract_rows, preferred_element_type=jnp.float32
    )
    sigmoid_g = jax.nn.sigmoid(gate_again)
    d_up = (d_inner * gate_again * sigmoid_g).astype(jnp.bfloat16)
    d_gate = (d_inner * up_again * sigmoid_g * (1.0 + gate_again * (1.0 - sigmoid_g))).astype(
        jnp.bfloat16
    )
    gate_grad_all = lax.dot_general(
        rows_again, d_gate, contract_rows, preferred_element_type=jnp.float32
    )
    up_grad_all = lax.dot_general(
        rows_again, d_up, contract_rows, preferred_element_type=jnp.float32
    )
    d_rows = lax.dot_general(d_gate, gate_map, contract_cols, preferred_element_type=jnp.float32)
    d_rows = d_rows + lax.dot_general(
        d_up, up_map, contract_cols, preferred_element_type=jnp.float32
    )
    d_pairs = owners_summed(expert_return(d_rows.reshape(expert_rows.shape)), mlp_where, group_size)
    w_gate_grad = gate_grad_all[None]
    w_up_grad = up_grad_all[None]
    w_down_grad = down_grad_all[None]
    d_normed2 = tensor_total(jnp.sum(d_pairs.reshape(rows_dev, 2, features), axis=1))
    d_hidden = top_grad + norm_backward(hidden, scale_mlp, gain_mlp, d_normed2)
    gain_mlp_grad = jnp.sum(d_normed2 * hidden * scale_mlp, axis=0)
    att_grad = (
        (d_hidden[:, None, :] * att_gates[:, :, None])
        .astype(jnp.bfloat16)
        .reshape(rows_dev * 2, features)
    )
    grad_slices = lax.all_to_all(
        send_slices(att_grad, att_table, group_size), "dp", split_axis=0, concat_axis=0, tiled=True
    )
    w_out_grad = jnp.einsum(
        "sch,scd->hd", out_rows, grad_slices, preferred_element_type=jnp.float32
    )
    d_attn_part = jnp.einsum(
        "scd,hd->sch", grad_slices, w_out[0], preferred_element_type=jnp.float32
    )
    d_attn = owners_summed(output_return(d_attn_part), att_where, group_size)
    d_attn = d_attn.astype(jnp.bfloat16).reshape(rows_dev, 2, head_count, HD)
    probability = jnp.exp(masked_scores(query_rot, keys, allowed) - log_total)
    d_prob = jnp.einsum("ikjd,mjd->kjim", d_attn, values, preferred_element_type=jnp.float32)
    d_values = jnp.einsum(
        "kjim,ikjd->mjd",
        probability.astype(jnp.bfloat16),
        d_attn,
        preferred_element_type=jnp.float32,
    )
    delta = jnp.sum(d_prob * probability, axis=-1, keepdims=True)
    d_scores = (probability * (d_prob - delta)).astype(jnp.bfloat16)
    root_hd = math.sqrt(HD)
    d_query = (
        jnp.einsum("kjim,mjd->ikjd", d_scores, keys, preferred_element_type=jnp.float32) / root_hd
    )
    d_keys = (
        jnp.einsum("kjim,ikjd->mjd", d_scores, query_rot, preferred_element_type=jnp.float32)
        / root_hd
    )
    dq_pre = (
        rotate(d_query, positions, -1.0).astype(jnp.bfloat16).reshape(rows_dev * 2, head_count * HD)
    )
    dk_pre = rotate(d_keys, positions, -1.0).reshape(rows_dev, head_count * HD)
    d_kv = jnp.stack([dk_pre, d_values.reshape(rows_dev, head_count * HD)], axis=1).astype(
        jnp.bfloat16
    )
    dq_rows = lax.all_to_all(
        send_copies(dq_pre, att_table, group_size), "dp", split_axis=0, concat_axis=0, tiled=True
    )
    w_query_grad = jnp.einsum(
        "scd,sch->dh", query_rows, dq_rows, preferred_element_type=jnp.float32
    )
    d_slice = jnp.einsum("sch,dh->scd", dq_rows, w_query[0], preferred_element_type=jnp.float32)
    d_norm_query = owners_joined(query_return(d_slice), att_where, group_size)
    d_norm_query = jnp.sum(d_norm_query.reshape(rows_dev, 2, features), axis=1)
    w_kv_grad = jnp.einsum("ld,lck->dck", normed, d_kv, preferred_element_type=jnp.float32)
    d_norm_kv = jnp.einsum("lck,dck->ld", d_kv, w_kv, preferred_element_type=jnp.float32)
    d_normed = tensor_total(d_norm_query + d_norm_kv)
    in_grad = d_hidden + norm_backward(residual, scale_attn, gain_attn, d_normed)
    gain_attn_grad = jnp.sum(d_normed * residual * scale_attn, axis=0)
    w_kv_grad, gain_attn_grad, gain_mlp_grad = (
        lax.psum(w_kv_grad.astype(jnp.bfloat16), "dp").astype(jnp.float32),
        lax.psum(gain_attn_grad.astype(jnp.bfloat16), "dp").astype(jnp.float32),
        lax.psum(gain_mlp_grad.astype(jnp.bfloat16), "dp").astype(jnp.float32),
    )
    send_mixed = mixed_rows.astype(jnp.bfloat16)[placed].reshape(device_count, per_peer, features)
    send_input = in_grad.astype(jnp.bfloat16)[placed].reshape(device_count, per_peer, features)
    back_mixed, back_input = (
        lax.all_to_all(send_mixed, "dp", split_axis=0, concat_axis=0, tiled=True),
        lax.all_to_all(send_input, "dp", split_axis=0, concat_axis=0, tiled=True),
    )
    mixed = back_mixed.reshape(rows_dev, features)[unorder]
    tokens_grad = back_input.reshape(rows_dev, features)[unorder]
    return (
        mixed,
        tokens_grad,
        gain_attn_grad,
        w_kv_grad,
        w_query_grad[None],
        w_out_grad[None],
        gain_mlp_grad,
        w_gate_grad,
        w_up_grad,
        w_down_grad,
    )


MESH = pl.DeviceIdType.MESH
VM = pltpu.VMEM
DMA = pltpu.SemaphoreType.DMA
BF = jnp.bfloat16
F32 = jnp.float32

def rcopy(src, dst, ss, rs, dp, tn):
    return pltpu.make_async_remote_copy(src_ref=src, dst_ref=dst, send_sem=ss, recv_sem=rs,
        device_id={"dp": dp, "tensor": tn}, device_id_type=MESH)

def greet(targets):
    b = pltpu.get_barrier_semaphore()
    for dp, tn in targets:
        pl.semaphore_signal(b, inc=1, device_id={"dp": dp, "tensor": tn}, device_id_type=MESH)
    pl.semaphore_wait(b, len(targets))

def ranks():
    g = lax.axis_index("dp"); t = lax.axis_index("tensor")
    return g, t, lax.rem(t + 2, 4), t + 1 - 2 * lax.rem(t, 2)

def params(cid):
    return pltpu.CompilerParams(collective_id=cid, has_side_effects=True, vmem_limit_bytes=56*2**20)

def gather_body(n, mode, src, out, ssem, rsem, xs, xr, cs, cr, c2s, c2r, lsem):
    g, t, tx, tc = ranks()
    w = src.shape[-1]
    greet([(lax.rem(g + o, n), t) for o in range(1, n)] + [(g, tx), (g, tc)])
    cols = pl.ds(pl.multiple_of(t * w, w), w)
    colsx = pl.ds(pl.multiple_of(tx * w, w), w)
    pick = (lambda d: src.at[d]) if mode == "rows" else (lambda d: src)
    at = (lambda b, cc: out.at[:, b, :, cc]) if mode == "deal" else (lambda b, cc: out.at[b, :, cc])
    sends = []
    for o in range(1, n):
        d = lax.rem(g + o, n)
        c = rcopy(pick(d), at(g, cols), ssem.at[o], rsem.at[o], d, t)
        c.start(); sends.append(c)
    loc = pltpu.make_async_copy(pick(g), at(g, cols), lsem)
    loc.start(); loc.wait()
    fx = []; fc = []; fc2 = []
    for o in range(n):
        b = lax.rem(g - o + n, n)
        if o > 0: sends[o - 1].wait_recv()
        c = rcopy(at(b, cols), at(b, cols), xs.at[o], xr.at[o], g, tx); c.start(); fx.append(c)
        c = rcopy(at(b, cols), at(b, cols), cs.at[o], cr.at[o], g, tc); c.start(); fc.append(c)
    for o in range(n):
        b = lax.rem(g - o + n, n)
        fx[o].wait_recv()
        c = rcopy(at(b, colsx), at(b, colsx), c2s.at[o], c2r.at[o], g, tc); c.start(); fc2.append(c)
    for c in fc + fc2: c.wait_recv()
    for c in sends + fx + fc + fc2: c.wait_send()

def gather(src, n, bcast=False, deal=False, cid=0, space=VM):
    r, w = src.shape[-2:]
    mode = "deal" if deal else "copy" if bcast else "rows"
    shape = (n, n, r, 4 * w) if deal else (n, r, 4 * w)
    return pl.pallas_call(functools.partial(gather_body, n, mode),
        out_shape=jax.ShapeDtypeStruct(shape, src.dtype),
        in_specs=[pl.BlockSpec(memory_space=VM)], out_specs=pl.BlockSpec(memory_space=space),
        scratch_shapes=[DMA((n,))]*8 + [DMA],
        name="gather_rows", compiler_params=params(cid))(src)

def reduce_body(n, nb, src, out, cbuf, cin, xbuf, xin, dbuf, cs, cr, xs, xr, ds_, dr):
    g, t, tx, tc = ranks()
    tcx = lax.rem(tc + 2, 4); w = out.shape[-1]
    greet([(lax.rem(g + o, n), t) for o in range(1, n)] + [(g, tx), (g, tc)])
    sl = lambda q: pl.ds(pl.multiple_of(q * w, w), w)
    order = list(range(1, n)) + [0] + list(range(n, nb))
    at = lambda o: lax.rem(g + o, n) if o < n else o
    C = {}; X = {}; Dd = {}
    for o in order:
        d = at(o)
        cbuf[o, 0] = src[d, :, sl(tc)].astype(BF)
        cbuf[o, 1] = src[d, :, sl(tcx)].astype(BF)
        C[o] = rcopy(cbuf.at[o], cin.at[o], cs.at[o], cr.at[o], g, tc); C[o].start()
    for o in order:
        C[o].wait_recv()
        xbuf[o] = (src[at(o), :, sl(tx)] + cin[o, 1].astype(F32)).astype(BF)
        X[o] = rcopy(xbuf.at[o], xin.at[o], xs.at[o], xr.at[o], g, tx); X[o].start()
    for o in order:
        d = at(o)
        X[o].wait_recv()
        total = (src[d, :, sl(t)] + cin[o, 0].astype(F32) + xin[o].astype(F32)).astype(BF)
        if 0 < o < n:
            dbuf[o] = total
            Dd[o] = rcopy(dbuf.at[o], out.at[g], ds_.at[o], dr.at[o], d, t); Dd[o].start()
        elif o == 0:
            out[g] = total
        else:
            out[o] = total
    for c in Dd.values(): c.wait_recv()
    for c in list(C.values()) + list(X.values()) + list(Dd.values()): c.wait_send()

def reduce(src, n, cid=1):
    nb, r, w = src.shape; w //= 4
    return pl.pallas_call(functools.partial(reduce_body, n, nb),
        out_shape=jax.ShapeDtypeStruct((nb, r, w), BF),
        in_specs=[pl.BlockSpec(memory_space=VM)], out_specs=pl.BlockSpec(memory_space=VM),
        scratch_shapes=[VM((nb,2,r,w),BF), VM((nb,2,r,w),BF), VM((nb,r,w),BF), VM((nb,r,w),BF), VM((n,r,w),BF)] + [DMA((nb,))]*4 + [DMA((n,))]*2,
        name="reduce_rows", compiler_params=params(cid))(src)

def a2a_body(n, src, out, ss, rs):
    g, t, tx, tc = ranks()
    greet([(lax.rem(g + o, n), t) for o in range(1, n)])
    cs = []
    for o in range(1, n):
        d = lax.rem(g + o, n)
        c = rcopy(src.at[d], out.at[g], ss.at[o], rs.at[o], d, t); c.start(); cs.append(c)
    out[g] = src[g]
    for c in cs: c.wait()

def a2a(src, n, cid=2):
    return pl.pallas_call(functools.partial(a2a_body, n),
        out_shape=jax.ShapeDtypeStruct(src.shape, src.dtype),
        in_specs=[pl.BlockSpec(memory_space=VM)], out_specs=pl.BlockSpec(memory_space=VM),
        scratch_shapes=[DMA((n,))]*2,
        name="a2a_rows", compiler_params=params(cid))(src)

def a2a_copy_body(n, src, out, ss, rs):
    g, t, tx, tc = ranks()
    greet([(lax.rem(g + o, n), t) for o in range(1, n)])
    cs = []
    for o in range(1, n):
        d = lax.rem(g + o, n)
        c = rcopy(src, out.at[g], ss.at[o], rs.at[o], d, t); c.start(); cs.append(c)
    out[g] = src[...]
    for c in cs: c.wait()

def a2a_copy(src, n, cid):
    return pl.pallas_call(functools.partial(a2a_copy_body, n),
        out_shape=jax.ShapeDtypeStruct((n,) + src.shape, src.dtype),
        in_specs=[pl.BlockSpec(memory_space=VM)], out_specs=pl.BlockSpec(memory_space=VM),
        scratch_shapes=[DMA((n,))]*2,
        name="copy_rows", compiler_params=params(cid))(src)

def dot(a, b, dims):
    return lax.dot_general(a, b, dims, preferred_element_type=F32)


def mm(a, b):
    return dot(a, b, (((a.ndim - 1,), (0,)), ((), ())))


def mm_t(a, b):
    return dot(a, b, (((1,), (1,)), ((), ())))


def mm_rows(a, b):
    return dot(a, b, (((0,), (0,)), ((), ())))


class Ring:
    def __init__(self, n):
        self.n = n
        self.g, self.t, self.tx, self.tc = ranks()
        self.tcx = lax.rem(self.tc + 2, 4)
        self.tail = []
        self.dest = [lax.rem(self.g + o, n) for o in range(n)]

    def to(self, o):
        return self.dest[o]

    def greet_all(self):
        greet([(self.to(o), self.t) for o in range(1, self.n)] + [(self.g, self.tx), (self.g, self.tc)])

    def greet_everyone(self):
        greet([(self.to(o), self.t) for o in range(1, self.n)] + [(self.g, q) for q in (self.tx, self.tc, self.tcx)])

    def send(self, src, dst, ss, rs, dp, tn):
        c = rcopy(src, dst, ss, rs, dp, tn)
        c.start()
        self.tail.append(c)
        return c

    def finish(self):
        for c in self.tail:
            c.wait_send()
        self.tail = []


def cols_of(q, j, width, cw):
    return pl.ds(pl.multiple_of(q * width + j * cw, cw), cw)


REDUCE_SEMS = lambda nc, n: [DMA((nc,))] * 4 + [DMA((nc, n))] * 2
GATHER_SEMS = lambda nc, n: [DMA((nc, n))] * 2 + [DMA((nc,))] * 6
REDUCE_BUFS = lambda nc, n, r, cw: [
    VM((nc, 2, n, r, cw), BF), VM((nc, 2, n, r, cw), BF), VM((nc, 2, n, r, cw), F32),
    VM((nc, n, r, cw), BF), VM((nc, n, r, cw), BF), VM((nc, n, r, cw), BF), VM((nc, n, r, cw), BF)]


class Reduce:
    def __init__(self, ring, partial, bufs, sems):
        self.ring, self.partial = ring, partial
        self.cbuf, self.cin, self.pbuf, self.xbuf, self.xin, self.dbuf, self.rbuf = bufs
        self.cs, self.cr, self.xs, self.xr, self.ds, self.dr = sems
        self.c, self.x, self.d = {}, {}, {}

    def core(self):
        k = self.ring
        nc, _, n, r, cw = self.cbuf.shape
        for i, q in enumerate((k.tc, k.tcx)):
            v = self.partial(q).astype(BF)
            for j in range(nc):
                self.cbuf[j, i] = v[:, j * cw:(j + 1) * cw].reshape(n, r, cw)
        for j in range(nc):
            self.c[j] = k.send(self.cbuf.at[j], self.cin.at[j], self.cs.at[j], self.cr.at[j], k.g, k.tc)
        for i, q in ((1, k.tx), (0, k.t)):
            v = self.partial(q)
            for j in range(nc):
                self.pbuf[j, i] = v[:, j * cw:(j + 1) * cw].reshape(n, r, cw)
            if i:
                for j in range(nc):
                    self.cross(j)

    def cross(self, j):
        k = self.ring
        self.c[j].wait_recv()
        self.xbuf[j] = (self.pbuf[j, 1] + self.cin[j, 1].astype(F32)).astype(BF)
        self.x[j] = k.send(self.xbuf.at[j], self.xin.at[j], self.xs.at[j], self.xr.at[j], k.g, k.tx)

    def home(self, j):
        k = self.ring
        self.x[j].wait_recv()
        self.dbuf[j] = (self.pbuf[j, 0] + self.cin[j, 0].astype(F32) + self.xin[j].astype(F32)).astype(BF)
        for o in range(1, k.n):
            d = k.to(o)
            self.d[j, o] = k.send(
                self.dbuf.at[j, d], self.rbuf.at[j, k.g], self.ds.at[j, o], self.dr.at[j, o], d, k.t)
        self.rbuf[j, k.g] = self.dbuf[j, k.g]

    def rows(self, j):
        for o in range(1, self.ring.n):
            self.d[j, o].wait_recv()
        return self.rbuf[j].reshape(-1, self.rbuf.shape[-1])


class Gather:
    def __init__(self, ring, width, full, sbuf, sems):
        self.ring, self.full, self.sbuf = ring, full, sbuf
        ss, rs, xs, xr, cs, cr, c2s, c2r = sems
        k, (nc, n, _, cw) = ring, sbuf.shape
        self.d, self.x, self.c, self.c2, self.own = {}, {}, {}, {}, {}
        for j in range(nc):
            cc, cx = cols_of(k.t, j, width, cw), cols_of(k.tx, j, width, cw)
            self.own[j] = cc
            for o in range(1, n):
                d = k.to(o)
                self.d[j, o] = rcopy(sbuf.at[j, d], full.at[k.g, :, cc], ss.at[j, o], rs.at[j, o], d, k.t)
            ref, ref2 = full.at[:, :, cc], full.at[:, :, cx]
            self.x[j] = rcopy(ref, ref, xs.at[j], xr.at[j], k.g, k.tx)
            self.c[j] = rcopy(ref, ref, cs.at[j], cr.at[j], k.g, k.tc)
            self.c2[j] = rcopy(ref2, ref2, c2s.at[j], c2r.at[j], k.g, k.tc)

    def out(self, j, rows):
        self.sbuf[j] = rows.reshape(self.sbuf.shape[1:])
        for o in range(1, self.ring.n):
            self.d[j, o].start()
        self.full[self.ring.g, :, self.own[j]] = self.sbuf[j, self.ring.g]

    def cross(self, j):
        for o in range(1, self.ring.n):
            self.d[j, o].wait_recv()
        self.x[j].start()
        self.c[j].start()

    def core(self, j):
        self.x[j].wait_recv()
        self.c2[j].start()

    def finish(self):
        for c in list(self.c.values()) + list(self.c2.values()):
            c.wait_recv()
        for c in [*self.d.values(), *self.x.values(), *self.c.values(), *self.c2.values()]:
            c.wait_send()


def paired(reduce_one, gather_one, middle, nc):
    reduce_one.core()
    steps = []
    for j in range(nc):
        steps += [(2 * j, 0, lambda j=j: reduce_one.home(j)), (2 * j + 3, 1, lambda j=j: gather_one.out(j, middle(j, reduce_one.rows(j))))]
        steps += [(2 * j + 7, 2, lambda j=j: gather_one.cross(j)), (2 * j + 9, 3, lambda j=j: gather_one.core(j))]
    for _, _, step in sorted(steps, key=lambda s: s[:2]):
        step()
    gather_one.finish()


NC = 4


def split_bf(v):
    high = v.astype(BF)
    return high, (v - high.astype(F32)).astype(BF)


def hidden_body(n, attn, wo, x_own, comb, gates, pick, hidden, full, scale, *scratch):
    bufs, sbuf, sq, sq_in, qs, qr, sems = scratch[:7], *scratch[7:12], scratch[12:]
    ring = Ring(n)
    ring.greet_everyone()
    rows, width = x_own.shape
    shared = []
    cw = width // NC

    def partial(q):
        return mm(attn[...], wo[:, cols_of(q, 0, width, width)])

    def middle(j, rows):
        high, low = split_bf(rows.astype(F32) * gates[...])
        got = x_own[:, j * cw:(j + 1) * cw] + mm(comb[...], high) + mm(comb[...], low)
        hidden[:, j * cw:(j + 1) * cw] = got
        high, low = split_bf(got * got)
        ones = jnp.ones((8, cw), BF)
        squares = mm_t(ones, high) + mm_t(ones, low)
        sq[...] = squares if j == 0 else sq[...] + squares
        if j == NC - 1:
            for i, q in enumerate([ring.tc, ring.tx, ring.tcx]):
                shared.append(ring.send(sq, sq_in.at[i], qs.at[i], qr.at[i], ring.g, q))
        return mm(pick[...], got.astype(BF)).astype(BF)

    red = Reduce(ring, partial, bufs, sems[:6])
    gat = Gather(ring, width, full, sbuf, sems[6:])
    paired(red, gat, middle, NC)
    for c in shared:
        c.wait_recv()
    total = (sq[...] + sq_in[0] + sq_in[1] + sq_in[2])[:1]
    eye = lax.broadcasted_iota(jnp.int32, (rows, rows), 0) == lax.broadcasted_iota(jnp.int32, (rows, rows), 1)
    column = jnp.sum(jnp.where(eye, total, 0.0), axis=1, keepdims=True)
    scale[...] = lax.rsqrt(column / (4 * width) + EPSILON)
    ring.finish()


def hidden_rows(attn, wo, x_own, comb, gates, pick, n, cid):
    slots = attn.shape[0]
    r, (rows, width) = slots // n, x_own.shape
    return pl.pallas_call(
        functools.partial(hidden_body, n),
        out_shape=(
            jax.ShapeDtypeStruct((rows, width), F32), jax.ShapeDtypeStruct((n, r, 4 * width), BF),
            jax.ShapeDtypeStruct((rows, 1), F32)),
        in_specs=[pl.BlockSpec(memory_space=VM)] * 6,
        out_specs=[pl.BlockSpec(memory_space=VM)] * 3,
        scratch_shapes=REDUCE_BUFS(NC, n, r, width // NC) + [VM((NC, n, r, width // NC), BF)]
        + [VM((8, rows), F32), VM((3, 8, rows), F32), DMA((3,)), DMA((3,))]
        + REDUCE_SEMS(NC, n) + GATHER_SEMS(NC, n),
        name="hidden_rows", compiler_params=params(cid),
    )(attn, wo, x_own, comb, gates, pick)


def expert_body(
    n, hid_rows, d_mbr, gain, wg_hbm, wu_hbm, wd_hbm, hidden, dy_own, gain_t, scale, mlp_t, mlp_gates, mlp_rows, att_rows,
    full, d_hidden, mixed, gain_part, n2, inner, d_gate, d_up, *scratch,
):
    ring = Ring(n)
    bufs, bufs2 = scratch[:7], scratch[7:14]
    sbuf, wg, wu, wd, r_own, r_in, r_to, r_back = scratch[14:22]
    wsem, rss, rsr, rds, rdr = scratch[22:27]
    sems = scratch[27:]
    ff = wg.shape[1]
    rows, width = hidden.shape
    slots = n2.shape[0]
    features = 4 * width
    cw = width // NC
    loads = [pltpu.make_async_copy(a, b, wsem.at[i]) for i, (a, b) in enumerate([(wg_hbm, wg), (wu_hbm, wu), (wd_hbm, wd)])]
    for c in loads:
        c.start()
    ring.greet_everyone()

    def norm_rows(i, _):
        at = pl.ds(pl.multiple_of(i * 64, 64), 64)
        v = hid_rows[i].astype(F32)
        s = lax.rsqrt(jnp.mean(v * v, axis=-1, keepdims=True) + EPSILON)
        n2[at, :] = (v * s * gain[...]).astype(BF)
        return _

    lax.fori_loop(0, n, norm_rows, 0)
    for c in loads:
        c.wait()
    r_own[...] = jnp.zeros_like(r_own)

    def units(at, size):
        a = n2[...]
        gate = mm(a, wg[:, at])
        up = mm(a, wu[:, at])
        d_in = mm_t(d_mbr[...], wd[at, :])
        sig = jax.nn.sigmoid(gate)
        silu = gate * sig
        inner[:, at] = (silu * up).astype(BF)
        du = (d_in * silu).astype(BF)
        dg = (d_in * up * sig * (1.0 + gate * (1.0 - sig))).astype(BF)
        d_up[:, at] = du
        d_gate[:, at] = dg
        both = (gate * dg.astype(F32) + up * du.astype(F32)).astype(BF)
        r_own[...] += mm_t(jnp.ones((8, size), BF), both)

    tile = 256

    def unit_tile(i, _):
        units(pl.ds(pl.multiple_of(i * tile, tile), tile), tile)
        return _

    lax.fori_loop(0, ff // tile, unit_tile, 0)
    if ff % tile:
        units(pl.ds(ff // tile * tile, ff % tile), ff % tile)

    others = [ring.tc, ring.tx, ring.tcx]
    r_sends = [ring.send(r_own, r_in.at[i], rss.at[i], rsr.at[i], ring.g, q) for i, q in enumerate(others)]

    def partial(q):
        at = cols_of(q, 0, width, width)
        return mm_t(d_gate[...], wg[at, :]) + mm_t(d_up[...], wu[at, :])

    def partial_mixed(q):
        return mm(inner[...], wd[:, cols_of(q, 0, width, width)])

    pairs = {}

    def share_r():
        for c in r_sends:
            c.wait_recv()
        r_to[...] = r_own[...] + r_in[0] + r_in[1] + r_in[2]
        for o in range(1, n):
            d = ring.to(o)
            half = pl.ds(pl.multiple_of(d // 2 * 128, 128), 128)
            pairs[o] = ring.send(r_to.at[:, half], r_back.at[ring.g], rds.at[o], rdr.at[o], d, ring.t)
        r_back[ring.g] = r_to[:, pl.ds(pl.multiple_of(ring.g // 2 * 128, 128), 128)]

    total_r = {}

    def take_r():
        for o in range(1, n):
            pairs[o].wait_recv()
        odd = lax.rem(ring.g, 2) == 1
        got = jnp.concatenate(
            [jnp.where(odd, r_back[e][:, 64:], r_back[e][:, :64]) for e in range(n)], axis=1)
        high = got.astype(BF)
        low = (got - high.astype(F32)).astype(BF)
        total_r[0] = (mm_t(mlp_t[...], high) + mm_t(mlp_t[...], low))[:, :1] / features

    def middle(j, got):
        if j == 0:
            take_r()
        cc = slice(j * cw, (j + 1) * cw)
        s2, h = scale[...], hidden[:, cc]
        d_n = mm(mlp_t[...], got)
        d_h = dy_own[:, cc] + s2 * (gain_t[:, cc] * d_n) - h * (s2 * s2) * total_r[0]
        d_hidden[:, cc] = d_h
        gain_part[:, cc] = jnp.broadcast_to(jnp.sum(d_n * h * s2, axis=0, keepdims=True), (8, cw))
        return mm(att_rows[...], d_h.astype(BF)).astype(BF)

    red = Reduce(ring, partial, bufs, sems[:6])
    gat = Gather(ring, width, full, sbuf, sems[6:14])
    red2 = Reduce(ring, partial_mixed, bufs2, sems[14:20])

    def settle(j):
        got = red2.rows(j)
        scaled = got.astype(F32) * mlp_gates[...]
        high = scaled.astype(BF)
        low = (scaled - high.astype(F32)).astype(BF)
        cc = slice(j * cw, (j + 1) * cw)
        mixed[:, cc] = (hidden[:, cc] + mm(mlp_t[...], high) + mm(mlp_t[...], low)).astype(BF)

    red.core()
    share_r()
    steps = []
    for j in range(NC):
        steps += [(2 * j, 1, lambda j=j: red.home(j)), (2 * j + 3, 2, lambda j=j: gat.out(j, middle(j, red.rows(j))))]
        steps += [(2 * j + 7, 3, lambda j=j: gat.cross(j)), (2 * j + 9, 4, lambda j=j: gat.core(j))]
        steps += [(2 * j + 12, 7, lambda j=j: red2.home(j)), (2 * j + 16, 8, lambda j=j: settle(j))]
    steps += [(9.5, 5, red2.core)]
    steps.sort(key=lambda s: s[:2])
    for _, _, run in steps:
        run()
    gat.finish()
    ring.finish()


def expert_layer(hid_rows, d_mbr, gain, wg, wu, wd, hidden, dy_own, gain_t, scale, mlp_t, mlp_gates, mlp_rows, att_rows, n, cid):
    r, features = hid_rows.shape[1:]
    ff = wg.shape[1]
    rows, width = hidden.shape
    slots, cw = n * r, width // NC
    any_, vm = pl.BlockSpec(memory_space=pl.ANY), pl.BlockSpec(memory_space=VM)
    sds = jax.ShapeDtypeStruct
    return pl.pallas_call(
        functools.partial(expert_body, n),
        out_shape=(
            sds((n, r, features), BF), sds((rows, width), F32), sds((rows, width), BF), sds((8, width), F32),
            sds((slots, features), BF), sds((slots, ff), BF), sds((slots, ff), BF), sds((slots, ff), BF)),
        in_specs=[vm, vm, vm, any_, any_, any_] + [vm] * 8,
        out_specs=[vm] * 8,
        scratch_shapes=REDUCE_BUFS(NC, n, r, cw) + REDUCE_BUFS(NC, n, r, cw) + [
            VM((NC, n, r, cw), BF), VM((features, ff), BF), VM((features, ff), BF), VM((ff, features), BF),
            VM((8, slots), F32), VM((3, 8, slots), F32), VM((8, slots), F32), VM((n, 8, 128), F32),
            DMA((3,)), DMA((3,)), DMA((3,)), DMA((n,)), DMA((n,))]
        + REDUCE_SEMS(NC, n) + GATHER_SEMS(NC, n) + REDUCE_SEMS(NC, n),
        name="expert_layer", compiler_params=params(cid),
    )(hid_rows, d_mbr, gain, wg, wu, wd, hidden, dy_own, gain_t, scale, mlp_t, mlp_gates, mlp_rows, att_rows)


META = {name: i for i, name in enumerate(
    ("ar0", "ar1", "ag0", "ag1", "mr0", "mr1", "mg0", "mg1", "pos", "seg", "wpos"))}


def iota(shape, dim):
    return lax.broadcasted_iota(jnp.int32, shape, dim)


def slot_table(meta, first, name, cap):
    member = (meta[first:first + 1] == name) | (meta[first + 1:first + 2] == name)
    tokens = meta.shape[1]
    before = jnp.where(iota((tokens, tokens), 0) < iota((tokens, tokens), 1), 1.0, 0.0).astype(BF)
    rank = mm(jnp.broadcast_to(jnp.where(member, 1.0, 0.0), (8, tokens)).astype(BF), before)[:1]
    return jnp.where((rank == iota((cap, tokens), 0).astype(F32)) & member, 1.0, 0.0).astype(BF)


def allowed_pairs(meta, meta_t):
    seg, wpos = META["seg"], META["wpos"]
    same = meta_t[:, seg:seg + 1] == meta[seg:seg + 1]
    return jnp.where(same & (meta[wpos:wpos + 1] <= meta_t[:, wpos:wpos + 1]), 1.0, 0.0).astype(BF)


def position_rows(meta_t):
    pos = META["pos"]
    tokens = meta_t.shape[0]
    return jnp.where(meta_t[:, pos:pos + 1] == iota((tokens, tokens), 1).astype(F32), 1.0, 0.0).astype(BF)


def looked_up(rows, table):
    got = mm(rows, table)
    w = got.shape[1] // 3
    return got[:, :w] + got[:, w:2 * w] + got[:, 2 * w:]


def turned(v, cosine, sine):
    out = []
    for h in range(v.shape[1] // HD):
        u = v[:, h * HD:(h + 1) * HD]
        out.append(u * cosine + pltpu.roll(u, HD // 2, 1) * sine)
    return jnp.concatenate(out, axis=1)


def angle_tables(positions):
    half = HD // 2
    frequency = np.exp(-math.log(THETA) * np.arange(half) / half)
    turned_by = np.arange(positions)[:, None] * frequency[None, :]
    cosine = np.concatenate([np.cos(turned_by)] * 2, axis=1).astype(np.float32)
    sine = np.concatenate([-np.sin(turned_by), np.sin(turned_by)], axis=1).astype(np.float32)

    def parts(v):
        out, left = [], v
        for _ in range(3):
            p = left.astype(jnp.bfloat16)
            out.append(p)
            left = left - p.astype(np.float32)
        return np.concatenate(out, axis=1)

    return jnp.asarray(parts(cosine)), jnp.asarray(parts(sine))


def softmax_rows(scores):
    top = jnp.max(scores, axis=-1, keepdims=True)
    expo = jnp.exp(scores - top)
    return expo / jnp.sum(expo, axis=-1, keepdims=True)


def keys_back_tables(meta, cos_t, sin_t, n, cap):
    m = meta[...]
    m_t = m.T
    tables = jnp.concatenate([slot_table(m, META["ar0"], float(e), cap) for e in range(n)], axis=0)
    at_pos = position_rows(m_t)
    return (mm(tables, allowed_pairs(m, m_t)) - 1.0) * 1e30, looked_up(at_pos, cos_t[...]), looked_up(at_pos, sin_t[...])


def keys_back_heads(part, query, d_attn, keys, values, bias, cosine, sine, d_kv):
    n, cap, hw = query.shape
    heads = hw // HD // 2
    root = math.sqrt(HD)
    for i in range(heads):
        h = part * heads + i
        hh = slice(h * HD, (h + 1) * HD)
        q = query[:, :, hh].reshape(n * cap, HD)
        d_o = d_attn[:, :, hh].reshape(n * cap, HD)
        k, v = keys[:, hh], values[:, hh]
        probs = softmax_rows(mm_t(q, k) / root + bias)
        d_probs = mm_t(d_o, v)
        delta = jnp.sum(d_probs * probs, axis=-1, keepdims=True)
        d_scores = (probs * (d_probs - delta)).astype(BF)
        at = part * hw + i * HD
        d_kv[:, at + hw // 2:at + hw // 2 + HD] = mm_rows(probs.astype(BF), d_o).astype(BF)
        d_k = mm_rows(d_scores, q) / root
        d_kv[:, at:at + HD] = turned(d_k, cosine, -sine).astype(BF)


def map_grad_body(normed, d_kv, out, d_cols):
    hw = d_kv.shape[1] // 2
    tiles = d_kv.shape[1] // 128
    half = tiles // 4

    @pl.when(pl.program_id(0) == 0)
    def _():
        for i in range(hw // 128):
            for c in range(2):
                at = i // half * hw + c * (hw // 2) + i % half * 128
                d_cols[:, (2 * i + c) * 128:(2 * i + c + 1) * 128] = d_kv[:, at:at + 128]

    got = mm_rows(normed[...], d_cols[...])
    for b in range(tiles):
        out[pl.ds(b, got.shape[0], stride=tiles), :] = got[:, b * 128:(b + 1) * 128]


def map_grad(normed, d_kv):
    total, features = normed.shape
    both = d_kv.shape[1]
    size, tiles = 512, both // 128
    out = pl.pallas_call(
        map_grad_body, grid=(features // size,),
        out_shape=jax.ShapeDtypeStruct((features * tiles, 128), F32),
        in_specs=[pl.BlockSpec((total, size), lambda i: (0, i)), pl.BlockSpec((total, both), lambda i: (0, 0))],
        out_specs=pl.BlockSpec((size * tiles, 128), lambda i: (i, 0)), scratch_shapes=[VM((total, both), BF)],
        name="map_grad", compiler_params=pltpu.CompilerParams(vmem_limit_bytes=56 * 2**20),
    )(normed, d_kv)
    return out.reshape(features, tiles // 2, 2, 128).transpose(0, 2, 1, 3).reshape(features, 2, both // 2)


def attention_back(i, d_attn, query, keys, values, bias, turn_slots, dq_pre):
    root = math.sqrt(HD)
    dq = []
    for h in range(query.shape[2] // HD):
        hh = slice(h * HD, (h + 1) * HD)
        k = keys[i, :, hh]
        probs = softmax_rows(mm_t(query[i, :, hh], k) / root + bias[i])
        d_probs = mm_t(d_attn[i, :, hh], values[i, :, hh])
        delta = jnp.sum(d_probs * probs, axis=-1, keepdims=True)
        dq.append(mm((probs * (d_probs - delta)).astype(BF), k) / root)
    dq_pre[i] = turned(jnp.concatenate(dq, axis=1), turn_slots[i, :, :HD], -turn_slots[i, :, HD:]).astype(BF)


def tail_body(
    n, d_attn, mb_rows, meta, cos_t, sin_t, x_own, scale, gain, d_hidden, hidden, mlp_gate, mlp_rows, att_rows, gain_mlp_part, sorter,
    query_hbm, keys_hbm, values_hbm, bias_hbm, turn_hbm, q_back_hbm, wq_hbm, wk_hbm, wv_hbm,
    d_kv_all, mixed_out, grad_out, gain_att_out, gain_mlp_out, dq_pre, *scratch,
):
    ring = Ring(n)
    (at_in, d_kv, kc_out, kc_in, kv_keep, kx_out, kx_in, sbuf, sq, sq_in, g_out, g_in, g_sum, d_norm, mixed, comb, mlp_t,
     query, keys, values, bias, turn_slots, q_back, w_q, w_k, w_v, whole, pbuf, cbuf, cin, back, gains) = scratch[:32]
    xbuf, xin, dbuf, rbuf = scratch[32:36]
    (as_, ar, zs, zr, ws, wr, ys, yr, ks, kr, lxs, lxr, qs, qr, gs, gr, ts, tr, wsem, qsem) = scratch[36:56]
    sems, fsems = scratch[56:62], scratch[62:]
    wanted = [(query_hbm, query), (keys_hbm, keys), (values_hbm, values), (bias_hbm, bias), (turn_hbm, turn_slots), (wq_hbm, w_q),
              (q_back_hbm, q_back), (wk_hbm, w_k), (wv_hbm, w_v)]
    loads = [pltpu.make_async_copy(a, b, wsem.at[i]) for i, (a, b) in enumerate(wanted)]
    cw = x_own.shape[1] // NC
    q_loads = [
        pltpu.make_async_copy(
            wq_hbm.at[pl.ds(q * NC * cw + j * cw, cw), :], w_q.at[pl.ds((j * 4 + q) * cw, cw), :], qsem.at[j * 4 + q])
        for j in range(NC) for q in range(4)]
    for c in loads[:5] + q_loads + loads[6:]:
        c.start()
    rows, width = x_own.shape
    cw = width // NC
    cap = query.shape[1]
    slots = n * cap
    all_keys, all_values = keys, values
    hw = keys.shape[2]
    features = 4 * width
    keys, values, meta, scale = keys.at[ring.g], values.at[ring.g], meta.at[ring.g], scale.at[ring.g]
    z, y = ring.g // 2, lax.rem(ring.g, 2)
    depth = n // 2
    ring.greet_everyone()

    half = hw // 2
    arrive = []
    for c in range(2):
        cc = pl.ds(c * half, half)
        arrive.append([
            ring.send(d_attn.at[ring.to(o), :, cc], at_in.at[ring.g, :, cc], as_.at[c, o], ar.at[c, o], ring.to(o), ring.t)
            for o in range(1, n)])
    at_in[ring.g] = d_attn[ring.g]
    comb[...] = att_rows[...].T
    mlp_t[...] = mlp_rows[...].T
    own_bias, cosine, sine = keys_back_tables(meta, cos_t, sin_t, n, cap)
    for c in loads[:5]:
        c.wait()

    def group_back(i, _):
        attention_back(i, d_attn, query, all_keys, all_values, bias, turn_slots, dq_pre)
        return _

    halves = [(c, slice(c * hw, (c + 1) * hw)) for c in range(2)]
    pairs = lambda zz, yy: zz * 2 + yy
    across = []

    def unit(zz, c):
        return d_kv_all.at[pairs(zz, y), :, pl.ds(c * hw, hw)]

    def step(up, hop, c, first):
        zz = z - hop if up else z + hop
        here = zz >= 0 if up else zz < depth
        ss, rs = (zs, zr) if up else (ws, wr)
        on, back_to = (z + 1, z - 1) if up else (z - 1, z + 1)

        @pl.when(here)
        def _():
            ref = unit(zz, c)
            if not first:
                rcopy(ref, ref, ss.at[hop - 1, c], rs.at[hop - 1, c], pairs(back_to, y), ring.t).wait_recv()

            @pl.when((on < depth) if up else (on >= 0))
            def _():
                rcopy(ref, ref, ss.at[hop, c], rs.at[hop, c], pairs(on, y), ring.t).start()

            if up or not first:
                rcopy(ref, ref, ys.at[zz, c], yr.at[zz, c], pairs(z, 1 - y), ring.t).start()

    def drain(up, hop, c):
        zz = z - hop if up else z + hop
        here = zz >= 0 if up else zz < depth
        ss, rs = (zs, zr) if up else (ws, wr)
        on = z + 1 if up else z - 1

        @pl.when(here & ((on < depth) if up else (on >= 0)))
        def _():
            ref = unit(zz, c)
            rcopy(ref, ref, ss.at[hop, c], rs.at[hop, c], pairs(on, y), ring.t).wait_send()

    def spread(hop, c):
        step(True, hop, c, hop == 0)
        step(False, hop, c, hop == 0)

    def keys_values(c):
        for r in arrive[c]:
            r.wait_recv()
        keys_back_heads(c, q_back, at_in, keys, values, own_bias, cosine, sine, d_kv)
        cc = slice(c * hw, (c + 1) * hw)
        d_kv_all[ring.g, :, cc] = d_kv[:, cc]
        spread(0, c)

    lax.fori_loop(0, n // 2, group_back, 0)
    loads[6].wait()
    keys_values(0)
    lax.fori_loop(n // 2, n, group_back, 0)
    keys_values(1)
    for c in q_loads:
        c.wait()

    def back_cols(j):
        dq = dq_pre[...].reshape(slots, hw)
        return mm_t(dq, w_q[j * 4 * cw:(j + 1) * 4 * cw, :])

    red = ChunkReduce(ring, back_cols, whole, pbuf, (cbuf, xbuf, dbuf), (cin, xin, rbuf), sems)
    red.core(0)
    spread(1, 0)
    for j in range(1, NC):
        red.core(j)
        red.cross(j - 1)
    spread(1, 1)
    red.cross(NC - 1)
    red.home(0)
    red.home(1)
    loads[7].wait()
    loads[8].wait()

    def kv_part(q):
        at = cols_of(q, 0, width, width)
        return sum(
            mm_t(d_kv[:, c * hw:c * hw + half], w_k[at, c * half:(c + 1) * half])
            + mm_t(d_kv[:, c * hw + half:(c + 1) * hw], w_v[at, c * half:(c + 1) * half]) for c in range(2))

    kc_out[0] = kv_part(ring.tc).astype(BF)
    kc_out[1] = kv_part(ring.tcx).astype(BF)
    kc = ring.send(kc_out, kc_in, ks, kr, ring.g, ring.tc)
    red.home(2)
    kv_keep[1] = kv_part(ring.tx)
    kc.wait_recv()
    kx_out[...] = (kv_keep[1] + kc_in[1].astype(F32)).astype(BF)
    kx = ring.send(kx_out, kx_in, lxs, lxr, ring.g, ring.tx)
    kv_keep[0] = kv_part(ring.t)
    red.home(3)
    spread(2, 0)
    kx.wait_recv()
    local = kv_keep[0] + kc_in[0].astype(F32) + kx_in[...].astype(F32)
    spread(2, 1)
    spread(3, 0)
    squares = jnp.zeros((8, rows), F32)
    for j in range(NC):
        cc = slice(j * cw, (j + 1) * cw)
        got = mm(comb[...], red.rows(j)) + local[:, cc]
        d_norm[:, cc] = got
        high, low = split_bf(x_own[:, cc] * gain[:, cols_of(ring.t, j, width, cw)] * got)
        ones = jnp.ones((8, cw), BF)
        squares = squares + mm_t(ones, high) + mm_t(ones, low)
        g_out[:, cc] = jnp.concatenate([
            gain_mlp_part[:1, cc], jnp.sum(got * x_own[:, cc] * scale[...], axis=0, keepdims=True), jnp.zeros((6, cw), F32)], axis=0)
    sq[...] = squares
    shared = [ring.send(sq, sq_in.at[i], qs.at[i], qr.at[i], ring.g, q) for i, q in enumerate([ring.tc, ring.tx, ring.tcx])]
    spread(3, 1)
    sums = []
    for o in range(1, n):
        sums.append(ring.send(g_out, g_in.at[ring.g], gs.at[o], gr.at[o], ring.to(o), ring.t))
    g_in[ring.g] = g_out[...]
    for j in range(NC):
        cc = slice(j * cw, (j + 1) * cw)
        high, low = split_bf(mb_rows[j].reshape(slots, cw).astype(F32) * mlp_gate[...])
        mixed[:, cc] = (hidden[:, cc] + mm(mlp_t[...], high) + mm(mlp_t[...], low)).astype(BF)
    for c in shared:
        c.wait_recv()
    total = (sq[...] + sq_in[0] + sq_in[1] + sq_in[2])[:1]
    eye = iota((rows, rows), 0) == iota((rows, rows), 1)
    mean = jnp.sum(jnp.where(eye, total, 0.0), axis=1, keepdims=True) / features
    s = scale[...]
    in_grad = d_hidden[...] + s * (gain[:, cols_of(ring.t, 0, width, width)] * d_norm[...]) - x_own[...] * (s * s * s * mean)
    per = rows // n
    fin = ChunkGather(
        ring, lambda j, q, e: back.at[slice(None) if e is None else e, :, cols_of(q, 0, width, width)], sbuf, fsems)
    fin.out(0, jnp.concatenate(
        [mixed[...].reshape(n, per, width), in_grad.astype(BF).reshape(n, per, width)], axis=1))
    for c in sums:
        c.wait_recv()
    g_sum[...] = functools.reduce(lambda a, b: a + b, [g_in[e] for e in range(n)])
    at_t = cols_of(ring.t, 0, width, width)
    gains[:, at_t] = g_sum[...]
    told = [ring.send(g_sum, gains.at[:, at_t], ts.at[i], tr.at[i], ring.g, q) for i, q in enumerate([ring.tc, ring.tx, ring.tcx])]
    fin.cross(0)
    fin.core(0)
    fin.here(0)
    for ref, at in ((mixed_out, slice(0, per)), (grad_out, slice(per, 2 * per))):
        ref[...] = mm_rows(sorter[...], back[:, at].reshape(rows, features)).astype(BF)
    for c in told:
        c.wait_recv()
    gain_mlp_out[...] = gains[0:1]
    gain_att_out[...] = gains[1:2]
    for c, _ in halves:
        for zz in range(depth):
            ref = d_kv_all.at[pairs(zz, 1 - y), :, pl.ds(c * hw, hw)]
            rcopy(ref, ref, ys.at[zz, c], yr.at[zz, c], pairs(z, 1 - y), ring.t).wait()
        for hop in range(depth - 1):
            drain(True, hop, c)
            drain(False, hop, c)
    ring.finish()
    fin.sent()
    red.sent_core()
    red.sent_rest()


def layer_tail(args, later, n, cid):
    d_attn, x_own = args[0], args[5]
    rows, width = x_own.shape
    cap, hw = d_attn.shape[1:]
    cw, features, depth = width // NC, 4 * width, n // 2
    slots = n * cap
    sds = jax.ShapeDtypeStruct
    per = 2 * rows // n
    one, two = VM((NC, n, cap, cw), BF), VM((NC, 2, n, cap, cw), BF)
    any_, vm = pl.BlockSpec(memory_space=pl.ANY), pl.BlockSpec(memory_space=VM)
    return pl.pallas_call(
        functools.partial(tail_body, n),
        out_shape=(
            sds((n, rows, 2 * hw), BF), sds((rows, features), BF), sds((rows, features), BF), sds((1, features), F32),
            sds((1, features), F32), sds((n, cap, hw), BF)),
        in_specs=[vm] * len(args) + [any_] * len(later), out_specs=[vm] * 6,
        scratch_shapes=[
            VM((n, cap, hw), BF), VM((rows, 2 * hw), BF), VM((2, rows, width), BF), VM((2, rows, width), BF),
            VM((2, rows, width), F32), VM((rows, width), BF), VM((rows, width), BF), VM((1, n, per, width), BF),
            VM((8, rows), F32), VM((3, 8, rows), F32), VM((8, width), F32), VM((n, 8, width), F32), VM((8, width), F32),
            VM((rows, width), F32), VM((rows, width), BF), VM((rows, slots), BF), VM((rows, slots), BF)]
        + [VM(a.shape, a.dtype) for a in later]
        + [VM((slots, 4 * cw), F32), VM((NC, 2, n, cap, cw), F32), two, two, VM((n, per, features), BF), VM((8, features), F32)]
        + [one] * 4 + [
            DMA((2, n)), DMA((2, n)), DMA((depth, 2)), DMA((depth, 2)), DMA((depth, 2)), DMA((depth, 2)), DMA((depth, 2)), DMA((depth, 2)),
            DMA, DMA, DMA, DMA, DMA((3,)), DMA((3,)), DMA((n,)), DMA((n,)), DMA((3,)), DMA((3,)), DMA((len(later),)), DMA((4 * NC,))]
        + REDUCE_SEMS(NC, n) + GATHER_SEMS(1, n),
        name="layer_tail", compiler_params=pltpu.CompilerParams(
            collective_id=cid, has_side_effects=True, vmem_limit_bytes=63 * 2**20),
    )(*args, *later)


def front_body(
    n, tokens, out_grad, place_r, att_routes, att_gates, mlp_routes, mlp_gates, seq_lengths, gain, cos_t, sin_t, wkv_hbm, wq_hbm,
    dy_own, meta_all, sorter_out, att_rows, att_gate, mlp_rows, mlp_gate, att_in, wk_hbm, wv_hbm, x_own,
    normed_hbm, picked_hbm, keys, values, query, attn, scale, bias, turn_slots, d_mbr,
    x_all, dy_send, w_kv, w_k, w_v, w_q, meta_w, mlp_in, normed, picked, dy_rows, sbuf, ksem, osem, nsem, *sems,
):
    gsems, sems = sems[:8], sems[8:]
    ms, mr, dys, dyr, zs, zr, ws, wr, ys, yr, xs, xr, cs, cr = sems
    ring = Ring(n)
    g, t = ring.g, ring.t
    rows, features = tokens.shape
    width, per = features // 4, rows // n
    z, y, depth = g // 2, lax.rem(g, 2), n // 2
    pairs = lambda zz, yy: zz * 2 + yy
    fetch = pltpu.make_async_copy(wkv_hbm, w_kv, ksem.at[0])
    fetch.start()
    fetch_q = pltpu.make_async_copy(wq_hbm, w_q, ksem.at[1])
    fetch_q.start()
    gw = sbuf.shape[-1]
    gat = ChunkGather(
        ring, lambda j, q, e: dy_rows.at[slice(None) if e is None else e, :, cols_of(q, j, width, gw)], sbuf, gsems)
    ring.greet_all()
    place_c = place_r[...].astype(F32).T.astype(jnp.int32)

    def arrival(row, col):
        g_row, g_col = row // rows, col // rows
        before = (g_col == g_row) & (iota((rows, rows), 0) < iota((rows, rows), 1))
        return g_row, jnp.sum(jnp.where(before, 1.0, 0.0), axis=0, keepdims=True).astype(jnp.int32)

    col_g = jnp.sum(jnp.where(iota((rows, n), 1) == g, place_c, 0), axis=1, keepdims=True)
    g_row, rank = arrival(place_r[pl.ds(g, 1), :], col_g)
    sorter = jnp.where(g_row * per + rank == iota((rows, rows), 0), 1.0, 0.0).astype(BF)
    sorter_out[...] = sorter

    half = width // 2
    chunks = [("b", t, half), ("a", t, 0), ("c", ring.tx, 0)]
    cols = [pl.ds(pl.multiple_of(q * width + off, half), half) for _, q, off in chunks]
    for cc in cols:
        x_all[:, g, :, cc] = mm(sorter, tokens[:, cc]).astype(BF).reshape(n, per, half)

    def unit(zz, yy, c):
        return x_all.at[:, pairs(zz, yy), :, cols[c]]

    def cross(zz, yy, c):
        if chunks[c][0] == "b":
            ref = unit(zz, yy, c)
            rcopy(ref, ref, xs.at[pairs(zz, yy)], xr.at[pairs(zz, yy)], g, ring.tx).start()

    def hop_on(up, hop, c):
        zz = z - hop if up else z + hop
        here = zz >= 0 if up else zz < depth
        ss, rs = (zs, zr) if up else (ws, wr)
        on, source = (z + 1, z - 1) if up else (z - 1, z + 1)

        @pl.when(here)
        def _():
            ref = unit(zz, y, c)
            if hop:
                rcopy(ref, ref, ss.at[hop - 1, c], rs.at[hop - 1, c], pairs(source, y), t).wait_recv()

            @pl.when((on < depth) if up else (on >= 0))
            def _():
                rcopy(ref, ref, ss.at[hop, c], rs.at[hop, c], pairs(on, y), t).start()

            if up or hop:
                rcopy(ref, ref, ys.at[zz, c], yr.at[zz, c], pairs(z, 1 - y), t).start()
                cross(zz, y, c)

    def from_y(zz, c):
        ref = unit(zz, 1 - y, c)
        rcopy(ref, ref, ys.at[zz, c], yr.at[zz, c], pairs(z, 1 - y), t).wait_recv()
        cross(zz, 1 - y, c)

    count = range(len(chunks))
    for c in count:
        hop_on(True, 0, c)
        hop_on(False, 0, c)

    meta_w[...] = jnp.zeros_like(meta_w)
    for name, ref in (("ar0", att_routes), ("ag0", att_gates), ("mr0", mlp_routes), ("mg0", mlp_gates)):
        meta_w[META[name]:META[name] + 2] = ref[...].astype(F32)
    at = iota((1, rows), 1)
    end, segment, begin = jnp.zeros((1, 1), jnp.int32), jnp.zeros((1, rows), jnp.int32), jnp.zeros((1, rows), jnp.int32)
    for k in range(seq_lengths.shape[1]):
        end = end + seq_lengths[:, k:k + 1]
        segment = segment + jnp.where(at >= end, 1, 0)
        begin = jnp.where(at >= end, end, begin)
    for name, v in (("pos", at - begin), ("seg", segment), ("wpos", at)):
        meta_w[META[name]:META[name] + 1] = v.astype(F32)
    spot = jnp.zeros((rows, rows), F32)
    for s in range(n):
        row, col = place_r[s:s + 1, :], place_c[:, s:s + 1]
        s_row, s_rank = arrival(row, col)
        put = jnp.where((s_row == g) & (s_rank + s * per == iota((rows, rows), 0)), 1.0, 0.0).astype(BF)
        work = jnp.where(col - col // rows * rows == iota((rows, rows), 1), 1.0, 0.0).astype(BF)
        spot = spot + mm(put, work)
    spot = spot.astype(BF)
    left, moved = meta_w[...], 0.0
    for _ in range(3):
        piece = left.astype(BF)
        moved = moved + mm_t(piece, spot)
        left = left - piece.astype(F32)
    meta_all[g] = moved
    sent = [ring.send(meta_all.at[g], meta_all.at[g], ms.at[o], mr.at[o], ring.to(o), t) for o in range(1, n)]

    mine = pl.ds(pl.multiple_of(t * width, width), width)
    dy_send[...] = mm(sorter, out_grad[:, mine]).astype(BF).reshape(n, per, width)
    dealt = [ring.send(dy_send.at[ring.to(o)], dy_own.at[g], dys.at[o], dyr.at[o], ring.to(o), t) for o in range(1, n)]
    dy_own[g] = dy_send[g]

    stored = []

    def split(i):
        if i == 0:
            fetch.wait()
        at = pl.ds(i * 256, 256)
        for c, (v, hbm) in enumerate(((w_k, wk_hbm), (w_v, wv_hbm))):
            v[at, :] = w_kv[at, c, :]
            stored.append(pltpu.make_async_copy(v.at[at, :], hbm.at[at, :], osem.at[c, i]))
            stored[-1].start()

    def tables(first, gate, out_rows, out_gate):
        m = meta_all[g]
        for e in range(n):
            out_rows[e] = slot_table(m, first, float(e), CAP)
            out_gate[e] = slot_gates(m, first, gate, float(e), out_rows[e])

    def hops(k):
        for c in count:
            hop_on(True, k, c)
            hop_on(False, k, c)

    tables(META["mr0"], META["mg0"], mlp_rows, mlp_gate)
    hops(1)
    hops(2)
    hops(3)
    for zz in range(depth):
        from_y(zz, 0)
    for c in dealt:
        c.wait_recv()
    slots = mm(mlp_rows[...].reshape(n * CAP, rows), dy_own[...].reshape(rows, width)).astype(BF)
    for j in range(2):
        gat.out(j, slots[:, j * gw:(j + 1) * gw])
    for i in range(4):
        split(i)

    def whole(q, off):
        return x_all.at[:, :, :, pl.ds(pl.multiple_of(q * width + off, half), half)]

    cores = [ring.send(whole(t, half), whole(t, half), cs.at[0], cr.at[0], g, ring.tc)]
    for c in (1, 2):
        split(3 + c)
        for zz in range(depth):
            from_y(zz, c)
        ref = whole(chunks[c][1], 0)
        cores.append(ring.send(ref, ref, cs.at[c], cr.at[c], g, ring.tc))
    for c in sent:
        c.wait_recv()
    me = g.astype(F32)
    split(6)
    split(7)
    for u in range(n):
        ref = x_all.at[:, u, :, pl.ds(pl.multiple_of(ring.tx * width + half, half), half)]
        rcopy(ref, ref, xs.at[u], xr.at[u], g, ring.tx).wait_recv()
    cores.append(ring.send(whole(ring.tx, half), whole(ring.tx, half), cs.at[3], cr.at[3], g, ring.tc))
    x_own[...] = x_all[g, :, :, mine].reshape(rows, width).astype(F32)
    for c in cores:
        c.wait_recv()
    for u in range(n):
        ref = x_all.at[:, u, :, cols[0]]
        rcopy(ref, ref, xs.at[u], xr.at[u], g, ring.tx).wait_send()
    for c in count:
        for zz in range(depth):
            ref = unit(zz, y, c)
            rcopy(ref, ref, ys.at[zz, c], yr.at[zz, c], pairs(z, 1 - y), t).wait_send()
        for hop in range(depth - 1):
            for up in (True, False):
                zz = z - hop if up else z + hop
                on = z + 1 if up else z - 1
                ss, rs = (zs, zr) if up else (ws, wr)

                @pl.when((zz >= 0) & (on < depth) if up else (zz < depth) & (on >= 0))
                def _(zz=zz, on=on, ss=ss, rs=rs, hop=hop, c=c):
                    ref = unit(zz, y, c)
                    rcopy(ref, ref, ss.at[hop, c], rs.at[hop, c], pairs(on, y), t).wait_send()
    fetch_q.wait()

    pair, steps = 2, n // 2
    heads = w_q.shape[1] // HD
    hw = w_q.shape[1]

    def out_copies(i):
        at = pl.ds(pair * i, pair)
        return (pltpu.make_async_copy(normed.at[at], normed_hbm.at[at], nsem.at[0, i]),
                pltpu.make_async_copy(picked.at[at], picked_hbm.at[at], nsem.at[1, i]))

    def two_groups(i, carry):
        @pl.when(i == 0)
        def _():
            gat.cross(0)

        @pl.when(i == 1)
        def _():
            gat.cross(1)

        @pl.when(i == 2)
        def _():
            gat.core(0)

        two = pl.ds(pair * i, pair)
        flat = x_all[two].reshape(pair * rows, features).astype(F32)
        s = lax.rsqrt(jnp.mean(flat * flat, axis=-1, keepdims=True) + EPSILON)
        scale[two] = s.reshape(pair, rows, 1)
        normed[two] = (flat * s * gain[...]).astype(BF).reshape(pair, rows, features)
        low = normed[two].reshape(pair * rows, features)
        k_all, v_all = mm(low, w_k[...]), mm(low, w_v[...])
        for p in range(pair):
            at = pair * i + p
            m = meta_all[at]
            m_t = m.T
            table = slot_table(m, META["ar0"], me, CAP)
            at_pos = position_rows(m_t)
            rr = slice(p * rows, (p + 1) * rows)
            keys[at] = turned(k_all[rr], looked_up(at_pos, cos_t[...]), looked_up(at_pos, sin_t[...])).astype(BF)
            values[at] = v_all[rr].astype(BF)
            picked[at] = mm(table, normed[at]).astype(BF)
            att_in[at] = slot_gates(m, META["ar0"], META["ag0"], me, table)
            mlp_in[at] = slot_gates(m, META["mr0"], META["mg0"], me, slot_table(m, META["mr0"], me, CAP))
            name, mine_m = at.astype(F32), meta_all[g]
            att_rows[at] = slot_table(mine_m, META["ar0"], name, CAP)
            att_gate[at] = slot_gates(mine_m, META["ar0"], META["ag0"], name, att_rows[at])
            slot_pos = mm(table, at_pos).astype(BF)
            turn_slots[at, :, :HD] = looked_up(slot_pos, cos_t[...])
            turn_slots[at, :, HD:] = looked_up(slot_pos, sin_t[...])
            bias[at] = (mm(table, allowed_pairs(m, m_t)) - 1.0) * 1e30
        for c in out_copies(i):
            c.start()
        q_all = mm(picked[two].reshape(pair * CAP, features), w_q[...])
        for p in range(pair):
            at = pair * i + p
            query[at] = turned(q_all[p * CAP:(p + 1) * CAP], turn_slots[at, :, :HD], turn_slots[at, :, HD:]).astype(BF)
        for p in range(pair):
            at = pair * i + p
            for h in range(heads):
                hh = slice(h * HD, (h + 1) * HD)
                scores = mm_t(query[at, :, hh], keys[at, :, hh]) / math.sqrt(HD) + bias[at]
                attn[at, :, hh] = mm(softmax_rows(scores).astype(BF), values[at, :, hh]).astype(BF)
        return carry

    lax.fori_loop(0, steps, two_groups, 0)
    gat.core(1)
    for j in range(2):
        gat.here(j)
    for e in range(n):
        d_mbr[e] = (dy_rows[e].astype(F32) * mlp_in[e]).astype(BF)
    gat.sent()
    for i in range(steps):
        for c in out_copies(i):
            c.wait()
    for c in stored:
        c.wait()
    ring.finish()


def slot_gates(meta, first, gate, name, table):
    per_token = (jnp.where(meta[first:first + 1] == name, meta[gate:gate + 1], 0.0)
                 + jnp.where(meta[first + 1:first + 2] == name, meta[gate + 1:gate + 2], 0.0))
    return jnp.sum(table.astype(F32) * per_token, axis=1, keepdims=True)


def front(tokens, out_grad, place, att_routes, att_gates, mlp_routes, mlp_gates, seq_lengths, gain, cos_t, sin_t, w_kv, w_q, n, cid):
    rows, features = tokens.shape
    width, per, depth = features // 4, rows // n, n // 2
    hw = w_kv.shape[2]
    sds = jax.ShapeDtypeStruct
    vm, any_ = pl.BlockSpec(memory_space=VM), pl.BlockSpec(memory_space=pl.ANY)
    table, gate, plain = sds((n, CAP, rows), BF), sds((n, CAP, 1), F32), sds((features, hw), BF)
    group, slot = sds((n, rows, hw), BF), sds((n, CAP, hw), BF)
    return pl.pallas_call(
        functools.partial(front_body, n),
        out_shape=(
            sds((n, per, width), BF), sds((n, 16, rows), F32), sds((rows, rows), BF), table, gate, table, gate, gate,
            plain, plain, sds((rows, width), F32), sds((n, rows, features), BF), sds((n, CAP, features), BF),
            group, group, slot, slot, sds((n, rows, 1), F32), sds((n, CAP, rows), F32), sds((n, CAP, 2 * HD), F32),
            sds((n, CAP, features), BF)),
        in_specs=[vm] * 11 + [any_] * 2, out_specs=[vm] * 8 + [any_] * 2 + [vm] + [any_] * 2 + [vm] * 8,
        scratch_shapes=[
            VM((n, n, per, features), BF), VM((n, per, width), BF), VM(w_kv.shape, BF), VM((features, hw), BF),
            VM((features, hw), BF), VM((features, hw), BF), VM((16, rows), F32), VM((n, CAP, 1), F32), VM((n, rows, features), BF),
            VM((n, CAP, features), BF), VM((n, CAP, features), BF), VM((2, n, CAP, width // 2), BF),
            DMA((2,)), DMA((2, features // 256)), DMA((2, n // 2))] + GATHER_SEMS(2, n)
        + [DMA((n,))] * 4 + [DMA((depth, 3))] * 6 + [DMA((n,))] * 2 + [DMA((4,))] * 2,
        name="front", compiler_params=pltpu.CompilerParams(
            collective_id=cid, has_side_effects=True, vmem_limit_bytes=63 * 2**20),
    )(tokens, out_grad, place, att_routes, att_gates, mlp_routes, mlp_gates, seq_lengths, gain, cos_t, sin_t, w_kv, w_q)


def tile_list(size, step):
    return [(a, min(step, size - a)) for a in range(0, size, step)]


class ChunkReduce:
    def __init__(self, ring, partial, whole, pbuf, sent, got, sems):
        self.ring, self.partial, self.whole, self.pbuf = ring, partial, whole, pbuf
        self.cbuf, self.xbuf, self.dbuf = sent
        self.cin, self.xin, self.rbuf = got
        cs, cr, xs, xr, ds, dr = sems
        k, (nc, n, _, _) = ring, self.xbuf.shape
        self.c = [rcopy(self.cbuf.at[j], self.cin.at[j], cs.at[j], cr.at[j], k.g, k.tc) for j in range(nc)]
        self.x = [rcopy(self.xbuf.at[j], self.xin.at[j], xs.at[j], xr.at[j], k.g, k.tx) for j in range(nc)]
        self.d = [
            [rcopy(self.dbuf.at[j, k.to(o)], self.rbuf.at[j, k.g], ds.at[j, o], dr.at[j, o], k.to(o), k.t) for o in range(1, n)]
            for j in range(nc)]

    def core(self, j):
        k = self.ring
        n, r, cw = self.xbuf.shape[1:]
        self.whole[...] = self.partial(j)
        take = lambda q: self.whole[:, pl.ds(pl.multiple_of(q * cw, cw), cw)].reshape(n, r, cw)
        self.cbuf[j, 0] = take(k.tc).astype(BF)
        self.cbuf[j, 1] = take(k.tcx).astype(BF)
        self.c[j].start()
        self.pbuf[j, 0] = take(k.t)
        self.pbuf[j, 1] = take(k.tx)

    def cross(self, j):
        self.c[j].wait_recv()
        self.xbuf[j] = (self.pbuf[j, 1] + self.cin[j, 1].astype(F32)).astype(BF)
        self.x[j].start()

    def home(self, j):
        g = self.ring.g
        self.x[j].wait_recv()
        self.dbuf[j] = (self.pbuf[j, 0] + self.cin[j, 0].astype(F32) + self.xin[j].astype(F32)).astype(BF)
        for c in self.d[j]:
            c.start()
        self.rbuf[j, g] = self.dbuf[j, g]

    def rows(self, j):
        for c in self.d[j]:
            c.wait_recv()
        return self.rbuf[j].reshape(-1, self.rbuf.shape[-1])

    def sent_core(self):
        for c in self.c:
            c.wait_send()

    def sent_rest(self):
        for c in self.x + [c for row in self.d for c in row]:
            c.wait_send()


class ChunkGather:
    def __init__(self, ring, place, sbuf, sems):
        self.ring, self.place, self.sbuf = ring, place, sbuf
        ss, rs, xs, xr, cs, cr, c2s, c2r = sems
        k, (nc, n, _, cw) = ring, sbuf.shape
        self.d = [
            [rcopy(sbuf.at[j, k.to(o)], place(j, k.t, k.g), ss.at[j, o], rs.at[j, o], k.to(o), k.t) for o in range(1, n)]
            for j in range(nc)]
        pair = lambda j, q, a, b, to: rcopy(place(j, q, None), place(j, q, None), a.at[j], b.at[j], k.g, to)
        self.x = [pair(j, k.t, xs, xr, k.tx) for j in range(nc)]
        self.c = [pair(j, k.t, cs, cr, k.tc) for j in range(nc)]
        self.c2 = [pair(j, k.tx, c2s, c2r, k.tc) for j in range(nc)]

    def out(self, j, rows):
        self.sbuf[j] = rows.reshape(self.sbuf.shape[1:])
        for c in self.d[j]:
            c.start()
        self.place(j, self.ring.t, self.ring.g)[...] = self.sbuf[j, self.ring.g]

    def cross(self, j):
        for c in self.d[j]:
            c.wait_recv()
        self.x[j].start()
        self.c[j].start()

    def core(self, j):
        self.x[j].wait_recv()
        self.c2[j].start()

    def here(self, j):
        self.c[j].wait_recv()
        self.c2[j].wait_recv()

    def sent(self):
        for c in [c for row in self.d for c in row] + self.x + self.c + self.c2:
            c.wait_send()


def middle_body(
    n, attn, x_own, att_rows, att_gate, att_in, mlp_rows, dy_own, gain, query, dm_hbm, wo_hbm, wg_hbm, wu_hbm, wd_hbm,
    d_attn, d_hidden, hidden, mb_rows, gain_part, n2_hbm, inner_hbm, dg_hbm, du_hbm, obr_hbm, q_back, *scratch,
):
    (d_mbr, wo, wg, wu, wd, inner, d_gate, d_up, d_rows, n2_st, obr_st, xbuf3, mb_sum, cin3, xin3, hid, att_t, mlp_t, whole, gate_acc, up_acc, d_in, pbuf, cbuf, xbuf, dbuf,
     cin1, xin1, rb1, cin2, xin2, rb2, sb1, sb2, sq, sq_in, r_own, r_in, r_to, r_back, s_col) = scratch[:41]
    wsem, qs, qr, as_, ar, rss, rsr, rds, rdr, osem, nsem, bsem = scratch[41:53]
    s1, s2s, s3, g1, g2 = scratch[53:59], scratch[59:65], scratch[65:71], scratch[71:79], scratch[79:87]
    ring = Ring(n)
    g, t = ring.g, ring.t
    rows, width = x_own.shape
    cw = width // NC
    features, ff = 4 * width, wg.shape[1]
    slots = attn.shape[0]

    loads = {"wo": [], "wg": [], "wu": [], "wd": [], "dm": []}
    for j in range(NC):
        for q in range(4):
            to, at = pl.ds((j * 4 + q) * cw, cw), pl.ds(q * width + j * cw, cw)
            i = j * 4 + q
            loads["wo"].append(pltpu.make_async_copy(wo_hbm.at[:, at], wo.at[:, to], wsem.at[0, i]))
            loads["wg"].append(pltpu.make_async_copy(wg_hbm.at[at, :], wg.at[to, :], wsem.at[1, i]))
            loads["wu"].append(pltpu.make_async_copy(wu_hbm.at[at, :], wu.at[to, :], wsem.at[2, i]))
            loads["wd"].append(pltpu.make_async_copy(wd_hbm.at[:, at], wd.at[:, to], wsem.at[3, i]))
            loads["dm"].append(pltpu.make_async_copy(dm_hbm.at[:, at], d_mbr.at[:, to], wsem.at[4, i]))

    def fetch(*names):
        for name in names:
            for c in loads[name]:
                c.start()

    fetch("wo")

    def loaded(name):
        for c in loads[name]:
            c.wait()

    chunk = lambda j: pl.ds(j * 4 * cw, 4 * cw)
    att_t[...] = att_rows[...].T
    mlp_t[...] = mlp_rows[...].T
    ring.greet_everyone()
    asked = [rcopy(query.at[ring.to(o)], q_back.at[g], as_.at[o], ar.at[o], ring.to(o), t) for o in range(1, n)]

    red1 = ChunkReduce(
        ring, lambda j: mm(attn[...], wo[:, chunk(j)]), whole, pbuf, (cbuf, xbuf, dbuf), (cin1, xin1, rb1), s1)
    gat1 = ChunkGather(
        ring, lambda j, q, e: hid.at[j, slice(None) if e is None else e, :, pl.ds(pl.multiple_of(q * cw, cw), cw)], sb1, g1)
    shared = [rcopy(sq, sq_in.at[i], qs.at[i], qr.at[i], g, q) for i, q in enumerate([ring.tc, ring.tx, ring.tcx])]
    ones = jnp.ones((8, cw), BF)

    def hidden_chunk(j):
        high, low = split_bf(red1.rows(j).astype(F32) * att_gate[...])
        got = x_own[:, j * cw:(j + 1) * cw] + mm(att_t[...], high) + mm(att_t[...], low)
        hidden[:, j * cw:(j + 1) * cw] = got
        gat1.out(j, mm(mlp_rows[...], got.astype(BF)).astype(BF))
        high, low = split_bf(got * got)
        squares = mm_t(ones, high) + mm_t(ones, low)
        sq[...] = squares if j == 0 else sq[...] + squares
        if j == NC - 1:
            for c in shared:
                c.start()

    def gain_cols(j):
        return jnp.concatenate([gain[:, q * width + j * cw:q * width + (j + 1) * cw] for q in range(4)], axis=1)

    pieces = tile_list(ff, 512)

    def d_inner(i):
        if i == 0:
            loaded("wd")
            loaded("dm")
        a, w = pieces[i]
        d_in[:, a:a + w] = mm_t(d_mbr[...], wd[a:a + w, :])

    def absorb(j):
        gat1.here(j)
        v = hid[j].reshape(slots, 4 * cw).astype(F32)
        part = jnp.sum(v * v, axis=1, keepdims=True)
        s_col[...] = part if j == 0 else s_col[...] + part
        u = (v * gain_cols(j)).astype(BF)
        for a, w in pieces:
            cc = slice(a, a + w)
            gate, up = mm(u, wg[chunk(j), cc]), mm(u, wu[chunk(j), cc])
            gate_acc[:, cc] = gate if j == 0 else gate_acc[:, cc] + gate
            up_acc[:, cc] = up if j == 0 else up_acc[:, cc] + up

    loaded("wo")
    for j in range(NC):
        red1.core(j)
        if j:
            red1.cross(j - 1)
    red1.cross(NC - 1)
    fetch("wd", "dm", "wg", "wu")
    plan = [(2 * j, 0, functools.partial(red1.home, j)) for j in range(NC)]
    plan += [(2 * j + 3, 1, functools.partial(hidden_chunk, j)) for j in range(NC)]
    plan += [(2 * j + 7, 2, functools.partial(gat1.cross, j)) for j in range(NC)]
    plan += [(2 * j + 9, 3, functools.partial(gat1.core, j)) for j in range(NC)]
    plan += [(2 * i + 1.5, 4, functools.partial(d_inner, i)) for i in range(len(pieces))]
    plan += [(2 * j + 10.5, 5, functools.partial(absorb, j)) for j in range(NC)]
    plan += [(10.2, 0, lambda: (loaded("wg"), loaded("wu")))]
    plan += [(13.2, 0, lambda: [c.start() for c in asked])]
    for _, _, run in sorted(plan, key=lambda s: s[:2]):
        run()

    s_col[...] = lax.rsqrt(s_col[...] / features + EPSILON)
    r_own[...] = jnp.zeros_like(r_own)

    def units(at, size):
        s = s_col[...]
        gate, up, d = gate_acc[:, at] * s, up_acc[:, at] * s, d_in[:, at]
        sig = jax.nn.sigmoid(gate)
        silu = gate * sig
        inner[:, at] = (silu * up).astype(BF)
        du = (d * silu).astype(BF)
        dg = (d * up * sig * (1.0 + gate * (1.0 - sig))).astype(BF)
        d_up[:, at] = du
        d_gate[:, at] = dg
        r_own[...] += mm_t(jnp.ones((8, size), BF), (gate * dg.astype(F32) + up * du.astype(F32)).astype(BF))

    def unit_tile(i, _):
        units(pl.ds(pl.multiple_of(i * 128, 128), 128), 128)
        return _

    lax.fori_loop(0, ff // 128, unit_tile, 0)
    stored = [pltpu.make_async_copy(a, b, osem.at[i]) for i, (a, b) in enumerate(
        [(inner, inner_hbm), (d_gate, dg_hbm), (d_up, du_hbm)])]
    for c in stored:
        c.start()
    red1.sent_core()
    red1.sent_rest()
    for c in shared:
        c.wait_recv()
    total = (sq[...] + sq_in[0] + sq_in[1] + sq_in[2])[:1]
    eye = iota((rows, rows), 0) == iota((rows, rows), 1)
    scale = lax.rsqrt(jnp.sum(jnp.where(eye, total, 0.0), axis=1, keepdims=True) / features + EPSILON)

    told = [rcopy(r_own, r_in.at[i], rss.at[i], rsr.at[i], g, q) for i, q in enumerate([ring.tc, ring.tx, ring.tcx])]
    for c in told:
        c.start()
    half = lambda d: pl.ds(pl.multiple_of(d // 2 * 128, 128), 128)
    pairs = [rcopy(r_to.at[:, half(ring.to(o))], r_back.at[g], rds.at[o], rdr.at[o], ring.to(o), t) for o in range(1, n)]

    def share_r():
        for c in told:
            c.wait_recv()
        r_to[...] = r_own[...] + r_in[0] + r_in[1] + r_in[2]
        for c in pairs:
            c.start()
        r_back[g] = r_to[:, half(g)]

    total_r = {}

    def take_r():
        for c in pairs:
            c.wait_recv()
        odd = lax.rem(g, 2) == 1
        got = jnp.concatenate([jnp.where(odd, r_back[e][:, 64:], r_back[e][:, :64]) for e in range(n)], axis=1)
        high, low = split_bf(got)
        total_r[0] = (mm_t(mlp_t[...], high) + mm_t(mlp_t[...], low))[:, :1] / features

    red2 = ChunkReduce(
        ring, lambda j: mm_t(d_gate[...], wg[chunk(j), :]) + mm_t(d_up[...], wu[chunk(j), :]), whole, pbuf,
        (cbuf, xbuf, dbuf), (cin2, xin2, rb2), s2s)
    gat2 = ChunkGather(
        ring, lambda j, q, e: d_rows.at[slice(None) if e is None else e, :, cols_of(q, j, width, cw)], sb2, g2)

    def mixed_cols(j):
        return mm(inner[...], wd[:, chunk(j)])

    red3 = ChunkReduce(ring, mixed_cols, whole, pbuf, (cbuf, xbuf3, mb_sum), (cin3, xin3, mb_rows), s3)

    def mixed_core(j):
        red2.c[j].wait_send()
        red3.core(j)

    def d_hidden_chunk(j):
        got = red2.rows(j)
        if j == 0:
            take_r()
        cc = slice(j * cw, (j + 1) * cw)
        h = hidden[:, cc]
        d_n = mm(mlp_t[...], got)
        d_h = dy_own[:, cc].astype(F32) + scale * (gain[:, cols_of(t, j, width, cw)] * d_n) - h * (scale * scale) * total_r[0]
        d_hidden[:, cc] = d_h
        gain_part[:, cc] = jnp.broadcast_to(jnp.sum(d_n * h * scale, axis=0, keepdims=True), (8, cw))
        gat2.out(j, mm(att_rows[...], d_h.astype(BF)).astype(BF))

    kept, given = [], []

    def keep_normed(j):
        st = n2_st.at[j % 2]
        if j > 1:
            for c in kept[4 * (j - 2):4 * (j - 1)]:
                c.wait()
        st[...] = (hid[j].reshape(slots, 4 * cw).astype(F32) * s_col[...] * gain_cols(j)).astype(BF)
        for q in range(4):
            kept.append(pltpu.make_async_copy(
                st.at[:, pl.ds(q * cw, cw)], n2_hbm.at[:, pl.ds(q * width + j * cw, cw)], nsem.at[j, q]))
            kept[-1].start()

    def attend_rows(j):
        gat2.here(j)
        st = obr_st.at[j % 2]
        if j > 1:
            for c in given[4 * (j - 2):4 * (j - 1)]:
                c.wait()
        for q in range(4):
            v = d_rows[:, :, q * width + j * cw:q * width + (j + 1) * cw].reshape(slots, cw)
            st[:, q * cw:(q + 1) * cw] = (v.astype(F32) * att_in[...]).astype(BF)
        for q in range(4):
            given.append(pltpu.make_async_copy(
                st.at[:, pl.ds(q * cw, cw)], obr_hbm.at[:, pl.ds(q * width + j * cw, cw)], bsem.at[j, q]))
            given[-1].start()
        got = mm_t(st[...], wo[:, chunk(j)])
        hw = wo.shape[0]
        d_in[:, :hw] = got if j == 0 else d_in[:, :hw] + got

    for j in range(NC):
        red2.core(j)
        if j == 0:
            share_r()
        else:
            red2.cross(j - 1)
    red2.cross(NC - 1)
    plan = [(2 * j, 0, functools.partial(red2.home, j)) for j in range(NC)]
    plan += [(2 * j + 3, 1, functools.partial(d_hidden_chunk, j)) for j in range(NC)]
    plan += [(2 * j + 7, 2, functools.partial(gat2.cross, j)) for j in range(NC)]
    plan += [(2 * j + 9, 3, functools.partial(gat2.core, j)) for j in range(NC)]
    plan += [(2 * j + 1.5, 4, functools.partial(keep_normed, j)) for j in range(NC)]
    plan += [(2 * j + 0.7, 5, functools.partial(mixed_core, j)) for j in range(NC)]
    plan += [(2 * j + 2.7, 6, functools.partial(red3.cross, j)) for j in range(NC)]
    plan += [(2 * j + 8.2, 7, functools.partial(red3.home, j)) for j in range(NC)]
    plan += [(2 * j + 11, 8, functools.partial(attend_rows, j)) for j in range(NC)]
    for _, _, run in sorted(plan, key=lambda s: s[:2]):
        run()
    d_attn[...] = d_in[:, :wo.shape[0]].astype(BF).reshape(d_attn.shape)
    for c in asked + [c for row in red3.d for c in row]:
        c.wait_recv()
    q_back[g] = query[g]
    for c in stored + kept[8:] + given[8:]:
        c.wait()
    for c in asked + shared + told + pairs:
        c.wait_send()
    gat1.sent()
    gat2.sent()
    red2.sent_rest()
    red3.sent_core()
    red3.sent_rest()


def middle(attn, x_own, att_rows, att_gate, att_in, mlp_rows, dy_own, gain, d_mbr, query, wo, wg, wu, wd, n, cid):
    slots, (rows, width) = attn.shape[0], x_own.shape
    r, cw, features, ff, hw = slots // n, width // NC, 4 * width, wg.shape[1], attn.shape[1]
    any_, vm = pl.BlockSpec(memory_space=pl.ANY), pl.BlockSpec(memory_space=VM)
    sds = jax.ShapeDtypeStruct
    one, two = VM((NC, n, r, cw), BF), VM((NC, 2, n, r, cw), BF)
    units = sds((slots, ff), BF)
    return pl.pallas_call(
        functools.partial(middle_body, n),
        out_shape=(
            sds((n, r, hw), BF), sds((rows, width), F32), sds((rows, width), F32), sds((NC, n, r, cw), BF), sds((8, width), F32),
            sds((slots, features), BF), units, units, units, sds((slots, features), BF), sds((n, r, hw), BF)),
        in_specs=[vm] * 9 + [any_] * 5, out_specs=[vm] * 5 + [any_] * 5 + [vm],
        scratch_shapes=[
            VM((slots, features), BF), VM((hw, features), BF), VM((features, ff), BF), VM((features, ff), BF), VM((ff, features), BF),
            VM((slots, ff), BF), VM((slots, ff), BF), VM((slots, ff), BF), VM((n, r, features), BF),
            VM((2, slots, 4 * cw), BF), VM((2, slots, 4 * cw), BF), one, one, two, one,
            VM((NC, n, r, 4 * cw), BF), VM((rows, slots), BF), VM((rows, slots), BF),
            VM((slots, 4 * cw), F32), VM((slots, ff), F32), VM((slots, ff), F32), VM((slots, ff), F32),
            VM((NC, 2, n, r, cw), F32), two, one, one]
        + [two, one, one] * 2 + [one, one]
        + [VM((8, rows), F32), VM((3, 8, rows), F32), VM((8, slots), F32), VM((3, 8, slots), F32), VM((8, slots), F32),
           VM((n, 8, 128), F32), VM((slots, 1), F32)]
        + [DMA((5, 16)), DMA((3,)), DMA((3,)), DMA((n,)), DMA((n,)), DMA((3,)), DMA((3,)), DMA((n,)), DMA((n,)), DMA((3,)),
           DMA((NC, 4)), DMA((NC, 4))]
        + REDUCE_SEMS(NC, n) * 3 + GATHER_SEMS(NC, n) * 2,
        name="middle", compiler_params=pltpu.CompilerParams(
            collective_id=cid, has_side_effects=True, vmem_limit_bytes=63 * 2**20),
    )(attn, x_own, att_rows, att_gate, att_in, mlp_rows, dy_own, gain, query, d_mbr, wo, wg, wu, wd)


def fast_local(
    tokens, out_grad, row_place, seq_lengths, att_routes, att_gates, mlp_routes, mlp_gates,
    gain_attn, w_kv, w_query, w_out, gain_mlp, w_gate, w_up, w_down,
):
    rows, features = tokens.shape
    n = lax.axis_size("dp")
    width = features // 4
    hw = w_kv.shape[2]

    cos_t, sin_t = angle_tables(rows)
    (dy_own, meta_all, sorter, att_out, att_gate, mlp_out, mlp_gate, att_in, w_k, w_v, x_own, normed, picked, keys, values,
     query, attn, scale_attn, bias, turn_slots, d_mbr) = front(
        tokens, out_grad, row_place.reshape(n, rows), att_routes.T, att_gates.T, mlp_routes.T, mlp_gates.T, seq_lengths,
        gain_attn[None], cos_t, sin_t, w_kv, w_query[0], n, cid=12)
    dy_own = dy_own.reshape(rows, width)
    att_rows, mlp_rows = att_out.reshape(n * CAP, rows), mlp_out.reshape(n * CAP, rows)
    normed_flat, picked = normed.reshape(n * rows, features), picked.reshape(n * CAP, features)
    attn = attn.reshape(n * CAP, hw)
    d_mbr = d_mbr.reshape(n * CAP, features)

    d_attn, d_hidden, hidden, mb_rows, gain_mlp_part, normed2, inner, d_gate, d_up, d_obr, query_back = middle(
        attn, x_own, att_rows, att_gate.reshape(-1, 1), att_in.reshape(-1, 1), mlp_rows, dy_own, gain_mlp[None],
        d_mbr, query, w_out[0], w_gate[0], w_up[0], w_down[0], n, cid=9)
    w_gate_grad = mm_rows(normed2, d_gate)[None]
    w_up_grad = mm_rows(normed2, d_up)[None]
    w_down_grad = mm_rows(inner, d_mbr)[None]

    d_kv_all, mixed, tokens_grad, gain_attn_grad, gain_mlp_grad, dq_pre = layer_tail(
        (d_attn, mb_rows, meta_all, cos_t, sin_t, x_own, scale_attn, gain_attn[None], d_hidden, hidden,
         mlp_gate.reshape(-1, 1), mlp_rows, att_rows, gain_mlp_part, sorter),
        (query, keys, values, bias, turn_slots, query_back, w_query[0], w_k, w_v), n, cid=11)
    w_out_grad = mm_rows(attn, d_obr)[None]
    w_query_grad = mm_rows(picked, dq_pre.reshape(n * CAP, hw))[None]
    w_kv_grad = map_grad(normed_flat, d_kv_all.reshape(n * rows, 2 * hw))
    return (
        mixed, tokens_grad, gain_attn_grad[0], w_kv_grad, w_query_grad, w_out_grad, gain_mlp_grad[0],
        w_gate_grad, w_up_grad, w_down_grad,
    )


def solution(mesh):
    placed = (
        P("dp", None),
        P("dp", None),
        P(),
        P("dp", None),
        P("dp", None),
        P("dp", None),
        P("dp", None),
        P("dp", None),
        P(),
        P(None, None, "tensor"),
        P("dp", None, "tensor"),
        P("dp", "tensor", None),
        P(),
        P("dp", None, "tensor"),
        P("dp", None, "tensor"),
        P("dp", "tensor", None),
    )
    dealt = mesh.shape["dp"] == EXPERTS and mesh.shape["tensor"] == 4
    return jax.shard_map(
        fast_local if dealt else local,
        mesh=mesh,
        in_specs=placed,
        out_specs=(
            P("dp", None),
            P("dp", None),
            P(),
            P(None, None, "tensor"),
            P("dp", None, "tensor"),
            P("dp", "tensor", None),
            P(),
            P("dp", None, "tensor"),
            P("dp", None, "tensor"),
            P("dp", "tensor", None),
        ),
        check_vma=False,
    )
```

```python
import functools
import math

import jax
import jax.numpy as jnp
import numpy as np
from jax import lax
from jax.experimental import pallas as pl
from jax.experimental.pallas import tpu as pltpu
from jax.sharding import PartitionSpec as P

HD = 128
ATT_EXPERTS = 8
EXPERTS = 8
CAP = 64


EPSILON = 1e-05
THETA = 10000.0


def inverse_rms(values_in):
    return lax.rsqrt(jnp.mean(values_in * values_in, axis=-1, keepdims=True) + EPSILON)


def norm_backward(inputs, inv_root, gain, incoming):
    weighted = incoming * gain
    inner_mean = jnp.mean(inputs * weighted, axis=-1, keepdims=True)
    return inv_root * weighted - inputs * (inv_root * inv_root * inv_root) * inner_mean


def rotate(vectors, positions, direction):
    half_dim = vectors.shape[-1] // 2
    frequency = jnp.exp(-math.log(THETA) * jnp.arange(half_dim, dtype=jnp.float32) / half_dim)
    angles = positions.astype(jnp.float32)[:, None] * frequency[None, :]
    target = (vectors.shape[0],) + (1,) * (vectors.ndim - 2) + (half_dim,)
    cosine = jnp.cos(angles).reshape(target)
    sine = direction * jnp.sin(angles).reshape(target)
    former = vectors[..., :half_dim]
    latter = vectors[..., half_dim:]
    return jnp.concatenate(
        [former * cosine - latter * sine, latter * cosine + former * sine], axis=-1
    )


def expert_slots(routes, experts, capacity):
    flattened = routes.reshape(-1)
    pair_count = flattened.shape[0]
    one_hot = (flattened[:, None] == jnp.arange(experts, dtype=jnp.int32)[None, :]).astype(
        jnp.int32
    )
    earlier = jnp.cumsum(one_hot, axis=0) - one_hot
    position = jnp.sum(earlier * one_hot, axis=1)
    slot_table = jnp.full((experts, capacity), pair_count, jnp.int32)
    slot_table = slot_table.at[flattened, position].set(jnp.arange(pair_count, dtype=jnp.int32))
    return (flattened * capacity + position, slot_table)


def pick_rows(source_rows, slot_table):
    padded = jnp.concatenate(
        [source_rows, jnp.zeros((1, source_rows.shape[1]), source_rows.dtype)], axis=0
    )
    return padded[slot_table]


def send_slices(source_rows, slot_table, group_size):
    picked = pick_rows(source_rows, slot_table)
    experts, capacity, features = picked.shape
    divided = picked.reshape(experts, capacity, group_size, features // group_size)
    return divided.transpose(0, 2, 1, 3).reshape(
        experts * group_size, capacity, features // group_size
    )


def send_copies(source_rows, slot_table, group_size):
    picked = pick_rows(source_rows, slot_table)
    experts, capacity, features = picked.shape
    copies = jnp.broadcast_to(picked[:, None], (experts, group_size, capacity, features))
    return copies.reshape(experts * group_size, capacity, features)


def owners_summed(returned, pair_where, group_size):
    owners, capacity, features = returned.shape
    summed = returned.reshape(owners // group_size, group_size, capacity, features).sum(axis=1)
    return summed.reshape(-1, features)[pair_where]


def owners_joined(returned, pair_where, group_size):
    owners, capacity, features = returned.shape
    joined = returned.reshape(owners // group_size, group_size, capacity, features).transpose(
        0, 2, 1, 3
    )
    return joined.reshape(-1, group_size * features)[pair_where]


def query_return(pieces):
    return lax.all_to_all(pieces, "dp", split_axis=0, concat_axis=0, tiled=True)


def output_return(pieces):
    return lax.all_to_all(pieces, "dp", split_axis=0, concat_axis=0, tiled=True)


def expert_return(pieces):
    return lax.all_to_all(pieces, "dp", split_axis=0, concat_axis=0, tiled=True)


def tensor_total(pieces):
    return lax.psum(pieces, "tensor")


def deal_plan(row_place, rows_dev):
    device_count = lax.axis_size("dp")
    my_index = lax.axis_index("dp")
    per_peer = rows_dev // device_count
    every_place = row_place.reshape(device_count, rows_dev)
    my_places = lax.dynamic_index_in_dim(every_place, my_index, 0, keepdims=False)
    counting = jnp.arange(rows_dev, dtype=jnp.int32)
    ordering = jnp.argsort(my_places // rows_dev * rows_dev + counting)
    wanted = every_place // rows_dev == my_index
    chosen = jnp.argsort(
        jnp.where(wanted, counting[None, :], rows_dev + counting[None, :]), axis=1
    )[:, :per_peer]
    placed = jnp.take_along_axis(every_place, chosen, axis=1) % rows_dev
    return (ordering, placed.reshape(-1))


def masked_scores(query_b, keys_b, allowed):
    raw = jnp.einsum(
        "ikjd,mjd->kjim", query_b, keys_b, preferred_element_type=jnp.float32
    ) / math.sqrt(query_b.shape[-1])
    return jnp.where(allowed[None, None], raw, -1e30)


def local(
    tokens,
    out_grad,
    row_place,
    seq_lengths,
    att_routes,
    att_gates,
    mlp_routes,
    mlp_gates,
    gain_attn,
    w_kv,
    w_query,
    w_out,
    gain_mlp,
    w_gate,
    w_up,
    w_down,
):
    rows_dev, features = tokens.shape
    device_count = lax.axis_size("dp")
    group_size = device_count // EXPERTS
    per_peer = rows_dev // device_count
    counting = jnp.arange(rows_dev, dtype=jnp.int32)
    ordering, placed = deal_plan(row_place, rows_dev)
    unplace = jnp.zeros((rows_dev,), jnp.int32).at[placed].set(counting)
    unorder = jnp.zeros((rows_dev,), jnp.int32).at[ordering].set(counting)
    dealt_x, dealt_g = (
        lax.all_to_all(
            tokens[ordering].reshape(device_count, per_peer, features),
            "dp",
            split_axis=0,
            concat_axis=0,
            tiled=True,
        ),
        lax.all_to_all(
            out_grad[ordering].reshape(device_count, per_peer, features),
            "dp",
            split_axis=0,
            concat_axis=0,
            tiled=True,
        ),
    )
    residual = dealt_x.reshape(rows_dev, features)[unplace].astype(jnp.float32)
    top_grad = dealt_g.reshape(rows_dev, features)[unplace].astype(jnp.float32)
    lengths = seq_lengths[0]
    seq_ends = jnp.cumsum(lengths)
    segment = jnp.sum((counting[:, None] >= seq_ends[None, :]).astype(jnp.int32), axis=1)
    starts = seq_ends - lengths
    member = segment[:, None] == jnp.arange(lengths.shape[0], dtype=jnp.int32)[None, :]
    begins = jnp.sum(jnp.where(member, starts[None, :], 0), axis=1)
    positions = counting - begins
    allowed = (segment[:, None] == segment[None, :]) & (counting[None, :] <= counting[:, None])
    head_count = w_kv.shape[2] // HD
    scale_attn = inverse_rms(residual)
    normed = (residual * scale_attn * gain_attn).astype(jnp.bfloat16)
    kv_proj = jnp.einsum("ld,dck->lck", normed, w_kv, preferred_element_type=jnp.float32)
    keys = rotate(kv_proj[:, 0].reshape(rows_dev, head_count, HD), positions, 1.0).astype(
        jnp.bfloat16
    )
    values = kv_proj[:, 1].reshape(rows_dev, head_count, HD).astype(jnp.bfloat16)
    att_where, att_table = expert_slots(att_routes, ATT_EXPERTS, CAP)
    query_rows = lax.all_to_all(
        send_slices(normed, att_table // 2, group_size),
        "dp",
        split_axis=0,
        concat_axis=0,
        tiled=True,
    )
    query_part = jnp.einsum(
        "scd,dh->sch", query_rows, w_query[0], preferred_element_type=jnp.float32
    )
    query_pre = owners_summed(query_return(query_part), att_where, group_size)
    query_rot = rotate(query_pre.reshape(rows_dev, 2, head_count, HD), positions, 1.0).astype(
        jnp.bfloat16
    )
    scores = masked_scores(query_rot, keys, allowed)
    highest = jnp.max(scores, axis=-1, keepdims=True)
    expo = jnp.exp(scores - highest)
    row_total = jnp.sum(expo, axis=-1, keepdims=True)
    log_total = highest + jnp.log(row_total)
    probability = expo / row_total
    attn = jnp.einsum(
        "kjim,mjd->ikjd",
        probability.astype(jnp.bfloat16),
        values,
        preferred_element_type=jnp.float32,
    )
    attn_low = attn.astype(jnp.bfloat16).reshape(rows_dev * 2, head_count * HD)
    out_rows = lax.all_to_all(
        send_copies(attn_low, att_table, group_size), "dp", split_axis=0, concat_axis=0, tiled=True
    )
    out_part = jnp.einsum("sch,hd->scd", out_rows, w_out[0], preferred_element_type=jnp.float32)
    out_pairs = owners_joined(output_return(out_part), att_where, group_size).reshape(
        rows_dev, 2, features
    )
    hidden = residual + tensor_total(jnp.sum(out_pairs * att_gates[:, :, None], axis=1))
    gate_map, up_map, down_map = (w_gate[0], w_up[0], w_down[0])
    scale_mlp = inverse_rms(hidden)
    normed2 = (hidden * scale_mlp * gain_mlp).astype(jnp.bfloat16)
    mlp_where, mlp_table = expert_slots(mlp_routes, EXPERTS, CAP)
    expert_sent = send_copies(normed2, mlp_table // 2, group_size)
    expert_rows = lax.all_to_all(expert_sent, "dp", split_axis=0, concat_axis=0, tiled=True)
    flat_rows = expert_rows.reshape(-1, features)
    gate_act = jnp.dot(flat_rows, gate_map, preferred_element_type=jnp.float32)
    up_act = jnp.dot(flat_rows, up_map, preferred_element_type=jnp.float32)
    inner = (jax.nn.silu(gate_act) * up_act).astype(jnp.bfloat16)
    expert_part = jnp.dot(inner, down_map, preferred_element_type=jnp.float32).reshape(
        expert_rows.shape
    )
    expert_pairs = owners_summed(expert_return(expert_part), mlp_where, group_size).reshape(
        rows_dev, 2, features
    )
    mixed_rows = hidden + tensor_total(jnp.sum(expert_pairs * mlp_gates[:, :, None], axis=1))
    branch_grad = (
        (top_grad[:, None, :] * mlp_gates[:, :, None])
        .astype(jnp.bfloat16)
        .reshape(rows_dev * 2, features)
    )
    grad_sent = send_copies(branch_grad, mlp_table, group_size)
    grad_back, rows_back = (
        lax.all_to_all(grad_sent, "dp", split_axis=0, concat_axis=0, tiled=True),
        lax.all_to_all(expert_sent, "dp", split_axis=0, concat_axis=0, tiled=True),
    )
    grad_rows = grad_back.reshape(-1, features)
    rows_again = rows_back.reshape(-1, features)
    gate_again = jnp.dot(rows_again, gate_map, preferred_element_type=jnp.float32)
    up_again = jnp.dot(rows_again, up_map, preferred_element_type=jnp.float32)
    inner_again = (jax.nn.silu(gate_again) * up_again).astype(jnp.bfloat16)
    contract_rows = (((0,), (0,)), ((), ()))
    contract_cols = (((1,), (1,)), ((), ()))
    d_inner = lax.dot_general(
        grad_rows, down_map, contract_cols, preferred_element_type=jnp.float32
    )
    down_grad_all = lax.dot_general(
        inner_again, grad_rows, contract_rows, preferred_element_type=jnp.float32
    )
    sigmoid_g = jax.nn.sigmoid(gate_again)
    d_up = (d_inner * gate_again * sigmoid_g).astype(jnp.bfloat16)
    d_gate = (d_inner * up_again * sigmoid_g * (1.0 + gate_again * (1.0 - sigmoid_g))).astype(
        jnp.bfloat16
    )
    gate_grad_all = lax.dot_general(
        rows_again, d_gate, contract_rows, preferred_element_type=jnp.float32
    )
    up_grad_all = lax.dot_general(
        rows_again, d_up, contract_rows, preferred_element_type=jnp.float32
    )
    d_rows = lax.dot_general(d_gate, gate_map, contract_cols, preferred_element_type=jnp.float32)
    d_rows = d_rows + lax.dot_general(
        d_up, up_map, contract_cols, preferred_element_type=jnp.float32
    )
    d_pairs = owners_summed(expert_return(d_rows.reshape(expert_rows.shape)), mlp_where, group_size)
    w_gate_grad = gate_grad_all[None]
    w_up_grad = up_grad_all[None]
    w_down_grad = down_grad_all[None]
    d_normed2 = tensor_total(jnp.sum(d_pairs.reshape(rows_dev, 2, features), axis=1))
    d_hidden = top_grad + norm_backward(hidden, scale_mlp, gain_mlp, d_normed2)
    gain_mlp_grad = jnp.sum(d_normed2 * hidden * scale_mlp, axis=0)
    att_grad = (
        (d_hidden[:, None, :] * att_gates[:, :, None])
        .astype(jnp.bfloat16)
        .reshape(rows_dev * 2, features)
    )
    grad_slices = lax.all_to_all(
        send_slices(att_grad, att_table, group_size), "dp", split_axis=0, concat_axis=0, tiled=True
    )
    w_out_grad = jnp.einsum(
        "sch,scd->hd", out_rows, grad_slices, preferred_element_type=jnp.float32
    )
    d_attn_part = jnp.einsum(
        "scd,hd->sch", grad_slices, w_out[0], preferred_element_type=jnp.float32
    )
    d_attn = owners_summed(output_return(d_attn_part), att_where, group_size)
    d_attn = d_attn.astype(jnp.bfloat16).reshape(rows_dev, 2, head_count, HD)
    probability = jnp.exp(masked_scores(query_rot, keys, allowed) - log_total)
    d_prob = jnp.einsum("ikjd,mjd->kjim", d_attn, values, preferred_element_type=jnp.float32)
    d_values = jnp.einsum(
        "kjim,ikjd->mjd",
        probability.astype(jnp.bfloat16),
        d_attn,
        preferred_element_type=jnp.float32,
    )
    delta = jnp.sum(d_prob * probability, axis=-1, keepdims=True)
    d_scores = (probability * (d_prob - delta)).astype(jnp.bfloat16)
    root_hd = math.sqrt(HD)
    d_query = (
        jnp.einsum("kjim,mjd->ikjd", d_scores, keys, preferred_element_type=jnp.float32) / root_hd
    )
    d_keys = (
        jnp.einsum("kjim,ikjd->mjd", d_scores, query_rot, preferred_element_type=jnp.float32)
        / root_hd
    )
    dq_pre = (
        rotate(d_query, positions, -1.0).astype(jnp.bfloat16).reshape(rows_dev * 2, head_count * HD)
    )
    dk_pre = rotate(d_keys, positions, -1.0).reshape(rows_dev, head_count * HD)
    d_kv = jnp.stack([dk_pre, d_values.reshape(rows_dev, head_count * HD)], axis=1).astype(
        jnp.bfloat16
    )
    dq_rows = lax.all_to_all(
        send_copies(dq_pre, att_table, group_size), "dp", split_axis=0, concat_axis=0, tiled=True
    )
    w_query_grad = jnp.einsum(
        "scd,sch->dh", query_rows, dq_rows, preferred_element_type=jnp.float32
    )
    d_slice = jnp.einsum("sch,dh->scd", dq_rows, w_query[0], preferred_element_type=jnp.float32)
    d_norm_query = owners_joined(query_return(d_slice), att_where, group_size)
    d_norm_query = jnp.sum(d_norm_query.reshape(rows_dev, 2, features), axis=1)
    w_kv_grad = jnp.einsum("ld,lck->dck", normed, d_kv, preferred_element_type=jnp.float32)
    d_norm_kv = jnp.einsum("lck,dck->ld", d_kv, w_kv, preferred_element_type=jnp.float32)
    d_normed = tensor_total(d_norm_query + d_norm_kv)
    in_grad = d_hidden + norm_backward(residual, scale_attn, gain_attn, d_normed)
    gain_attn_grad = jnp.sum(d_normed * residual * scale_attn, axis=0)
    w_kv_grad, gain_attn_grad, gain_mlp_grad = (
        lax.psum(w_kv_grad.astype(jnp.bfloat16), "dp").astype(jnp.float32),
        lax.psum(gain_attn_grad.astype(jnp.bfloat16), "dp").astype(jnp.float32),
        lax.psum(gain_mlp_grad.astype(jnp.bfloat16), "dp").astype(jnp.float32),
    )
    send_mixed = mixed_rows.astype(jnp.bfloat16)[placed].reshape(device_count, per_peer, features)
    send_input = in_grad.astype(jnp.bfloat16)[placed].reshape(device_count, per_peer, features)
    back_mixed, back_input = (
        lax.all_to_all(send_mixed, "dp", split_axis=0, concat_axis=0, tiled=True),
        lax.all_to_all(send_input, "dp", split_axis=0, concat_axis=0, tiled=True),
    )
    mixed = back_mixed.reshape(rows_dev, features)[unorder]
    tokens_grad = back_input.reshape(rows_dev, features)[unorder]
    return (
        mixed,
        tokens_grad,
        gain_attn_grad,
        w_kv_grad,
        w_query_grad[None],
        w_out_grad[None],
        gain_mlp_grad,
        w_gate_grad,
        w_up_grad,
        w_down_grad,
    )


MESH = pl.DeviceIdType.MESH
VM = pltpu.VMEM
DMA = pltpu.SemaphoreType.DMA
BF = jnp.bfloat16
F32 = jnp.float32

def rcopy(src, dst, ss, rs, dp, tn):
    return pltpu.make_async_remote_copy(src_ref=src, dst_ref=dst, send_sem=ss, recv_sem=rs,
        device_id={"dp": dp, "tensor": tn}, device_id_type=MESH)

def greet(targets):
    b = pltpu.get_barrier_semaphore()
    for dp, tn in targets:
        pl.semaphore_signal(b, inc=1, device_id={"dp": dp, "tensor": tn}, device_id_type=MESH)
    pl.semaphore_wait(b, len(targets))

def ranks():
    g = lax.axis_index("dp"); t = lax.axis_index("tensor")
    return g, t, lax.rem(t + 2, 4), t + 1 - 2 * lax.rem(t, 2)

def params(cid):
    return pltpu.CompilerParams(collective_id=cid, has_side_effects=True, vmem_limit_bytes=56*2**20)

def gather_body(n, mode, src, out, ssem, rsem, xs, xr, cs, cr, c2s, c2r, lsem):
    g, t, tx, tc = ranks()
    w = src.shape[-1]
    greet([(lax.rem(g + o, n), t) for o in range(1, n)] + [(g, tx), (g, tc)])
    cols = pl.ds(pl.multiple_of(t * w, w), w)
    colsx = pl.ds(pl.multiple_of(tx * w, w), w)
    pick = (lambda d: src.at[d]) if mode == "rows" else (lambda d: src)
    at = (lambda b, cc: out.at[:, b, :, cc]) if mode == "deal" else (lambda b, cc: out.at[b, :, cc])
    sends = []
    for o in range(1, n):
        d = lax.rem(g + o, n)
        c = rcopy(pick(d), at(g, cols), ssem.at[o], rsem.at[o], d, t)
        c.start(); sends.append(c)
    loc = pltpu.make_async_copy(pick(g), at(g, cols), lsem)
    loc.start(); loc.wait()
    fx = []; fc = []; fc2 = []
    for o in range(n):
        b = lax.rem(g - o + n, n)
        if o > 0: sends[o - 1].wait_recv()
        c = rcopy(at(b, cols), at(b, cols), xs.at[o], xr.at[o], g, tx); c.start(); fx.append(c)
        c = rcopy(at(b, cols), at(b, cols), cs.at[o], cr.at[o], g, tc); c.start(); fc.append(c)
    for o in range(n):
        b = lax.rem(g - o + n, n)
        fx[o].wait_recv()
        c = rcopy(at(b, colsx), at(b, colsx), c2s.at[o], c2r.at[o], g, tc); c.start(); fc2.append(c)
    for c in fc + fc2: c.wait_recv()
    for c in sends + fx + fc + fc2: c.wait_send()

def gather(src, n, bcast=False, deal=False, cid=0, space=VM):
    r, w = src.shape[-2:]
    mode = "deal" if deal else "copy" if bcast else "rows"
    shape = (n, n, r, 4 * w) if deal else (n, r, 4 * w)
    return pl.pallas_call(functools.partial(gather_body, n, mode),
        out_shape=jax.ShapeDtypeStruct(shape, src.dtype),
        in_specs=[pl.BlockSpec(memory_space=VM)], out_specs=pl.BlockSpec(memory_space=space),
        scratch_shapes=[DMA((n,))]*8 + [DMA],
        name="gather_rows", compiler_params=params(cid))(src)

def reduce_body(n, nb, src, out, cbuf, cin, xbuf, xin, dbuf, cs, cr, xs, xr, ds_, dr):
    g, t, tx, tc = ranks()
    tcx = lax.rem(tc + 2, 4); w = out.shape[-1]
    greet([(lax.rem(g + o, n), t) for o in range(1, n)] + [(g, tx), (g, tc)])
    sl = lambda q: pl.ds(pl.multiple_of(q * w, w), w)
    order = list(range(1, n)) + [0] + list(range(n, nb))
    at = lambda o: lax.rem(g + o, n) if o < n else o
    C = {}; X = {}; Dd = {}
    for o in order:
        d = at(o)
        cbuf[o, 0] = src[d, :, sl(tc)].astype(BF)
        cbuf[o, 1] = src[d, :, sl(tcx)].astype(BF)
        C[o] = rcopy(cbuf.at[o], cin.at[o], cs.at[o], cr.at[o], g, tc); C[o].start()
    for o in order:
        C[o].wait_recv()
        xbuf[o] = (src[at(o), :, sl(tx)] + cin[o, 1].astype(F32)).astype(BF)
        X[o] = rcopy(xbuf.at[o], xin.at[o], xs.at[o], xr.at[o], g, tx); X[o].start()
    for o in order:
        d = at(o)
        X[o].wait_recv()
        total = (src[d, :, sl(t)] + cin[o, 0].astype(F32) + xin[o].astype(F32)).astype(BF)
        if 0 < o < n:
            dbuf[o] = total
            Dd[o] = rcopy(dbuf.at[o], out.at[g], ds_.at[o], dr.at[o], d, t); Dd[o].start()
        elif o == 0:
            out[g] = total
        else:
            out[o] = total
    for c in Dd.values(): c.wait_recv()
    for c in list(C.values()) + list(X.values()) + list(Dd.values()): c.wait_send()

def reduce(src, n, cid=1):
    nb, r, w = src.shape; w //= 4
    return pl.pallas_call(functools.partial(reduce_body, n, nb),
        out_shape=jax.ShapeDtypeStruct((nb, r, w), BF),
        in_specs=[pl.BlockSpec(memory_space=VM)], out_specs=pl.BlockSpec(memory_space=VM),
        scratch_shapes=[VM((nb,2,r,w),BF), VM((nb,2,r,w),BF), VM((nb,r,w),BF), VM((nb,r,w),BF), VM((n,r,w),BF)] + [DMA((nb,))]*4 + [DMA((n,))]*2,
        name="reduce_rows", compiler_params=params(cid))(src)

def a2a_body(n, src, out, ss, rs):
    g, t, tx, tc = ranks()
    greet([(lax.rem(g + o, n), t) for o in range(1, n)])
    cs = []
    for o in range(1, n):
        d = lax.rem(g + o, n)
        c = rcopy(src.at[d], out.at[g], ss.at[o], rs.at[o], d, t); c.start(); cs.append(c)
    out[g] = src[g]
    for c in cs: c.wait()

def a2a(src, n, cid=2):
    return pl.pallas_call(functools.partial(a2a_body, n),
        out_shape=jax.ShapeDtypeStruct(src.shape, src.dtype),
        in_specs=[pl.BlockSpec(memory_space=VM)], out_specs=pl.BlockSpec(memory_space=VM),
        scratch_shapes=[DMA((n,))]*2,
        name="a2a_rows", compiler_params=params(cid))(src)

def a2a_copy_body(n, src, out, ss, rs):
    g, t, tx, tc = ranks()
    greet([(lax.rem(g + o, n), t) for o in range(1, n)])
    cs = []
    for o in range(1, n):
        d = lax.rem(g + o, n)
        c = rcopy(src, out.at[g], ss.at[o], rs.at[o], d, t); c.start(); cs.append(c)
    out[g] = src[...]
    for c in cs: c.wait()

def a2a_copy(src, n, cid):
    return pl.pallas_call(functools.partial(a2a_copy_body, n),
        out_shape=jax.ShapeDtypeStruct((n,) + src.shape, src.dtype),
        in_specs=[pl.BlockSpec(memory_space=VM)], out_specs=pl.BlockSpec(memory_space=VM),
        scratch_shapes=[DMA((n,))]*2,
        name="copy_rows", compiler_params=params(cid))(src)

def dot(a, b, dims):
    return lax.dot_general(a, b, dims, preferred_element_type=F32)


def mm(a, b):
    return dot(a, b, (((a.ndim - 1,), (0,)), ((), ())))


def mm_t(a, b):
    return dot(a, b, (((1,), (1,)), ((), ())))


def mm_rows(a, b):
    return dot(a, b, (((0,), (0,)), ((), ())))


class Ring:
    def __init__(self, n):
        self.n = n
        self.g, self.t, self.tx, self.tc = ranks()
        self.tcx = lax.rem(self.tc + 2, 4)
        self.tail = []
        self.dest = [lax.rem(self.g + o, n) for o in range(n)]

    def to(self, o):
        return self.dest[o]

    def greet_all(self):
        greet([(self.to(o), self.t) for o in range(1, self.n)] + [(self.g, self.tx), (self.g, self.tc)])

    def greet_everyone(self):
        greet([(self.to(o), self.t) for o in range(1, self.n)] + [(self.g, q) for q in (self.tx, self.tc, self.tcx)])

    def send(self, src, dst, ss, rs, dp, tn):
        c = rcopy(src, dst, ss, rs, dp, tn)
        c.start()
        self.tail.append(c)
        return c

    def finish(self):
        for c in self.tail:
            c.wait_send()
        self.tail = []


def cols_of(q, j, width, cw):
    return pl.ds(pl.multiple_of(q * width + j * cw, cw), cw)


REDUCE_SEMS = lambda nc, n: [DMA((nc,))] * 4 + [DMA((nc, n))] * 2
GATHER_SEMS = lambda nc, n: [DMA((nc, n))] * 2 + [DMA((nc,))] * 6
REDUCE_BUFS = lambda nc, n, r, cw: [
    VM((nc, 2, n, r, cw), BF), VM((nc, 2, n, r, cw), BF), VM((nc, 2, n, r, cw), F32),
    VM((nc, n, r, cw), BF), VM((nc, n, r, cw), BF), VM((nc, n, r, cw), BF), VM((nc, n, r, cw), BF)]


class Reduce:
    def __init__(self, ring, partial, bufs, sems):
        self.ring, self.partial = ring, partial
        self.cbuf, self.cin, self.pbuf, self.xbuf, self.xin, self.dbuf, self.rbuf = bufs
        self.cs, self.cr, self.xs, self.xr, self.ds, self.dr = sems
        self.c, self.x, self.d = {}, {}, {}

    def core(self):
        k = self.ring
        nc, _, n, r, cw = self.cbuf.shape
        for i, q in enumerate((k.tc, k.tcx)):
            v = self.partial(q).astype(BF)
            for j in range(nc):
                self.cbuf[j, i] = v[:, j * cw:(j + 1) * cw].reshape(n, r, cw)
        for j in range(nc):
            self.c[j] = k.send(self.cbuf.at[j], self.cin.at[j], self.cs.at[j], self.cr.at[j], k.g, k.tc)
        for i, q in ((1, k.tx), (0, k.t)):
            v = self.partial(q)
            for j in range(nc):
                self.pbuf[j, i] = v[:, j * cw:(j + 1) * cw].reshape(n, r, cw)
            if i:
                for j in range(nc):
                    self.cross(j)

    def cross(self, j):
        k = self.ring
        self.c[j].wait_recv()
        self.xbuf[j] = (self.pbuf[j, 1] + self.cin[j, 1].astype(F32)).astype(BF)
        self.x[j] = k.send(self.xbuf.at[j], self.xin.at[j], self.xs.at[j], self.xr.at[j], k.g, k.tx)

    def home(self, j):
        k = self.ring
        self.x[j].wait_recv()
        self.dbuf[j] = (self.pbuf[j, 0] + self.cin[j, 0].astype(F32) + self.xin[j].astype(F32)).astype(BF)
        for o in range(1, k.n):
            d = k.to(o)
            self.d[j, o] = k.send(
                self.dbuf.at[j, d], self.rbuf.at[j, k.g], self.ds.at[j, o], self.dr.at[j, o], d, k.t)
        self.rbuf[j, k.g] = self.dbuf[j, k.g]

    def rows(self, j):
        for o in range(1, self.ring.n):
            self.d[j, o].wait_recv()
        return self.rbuf[j].reshape(-1, self.rbuf.shape[-1])


class Gather:
    def __init__(self, ring, width, full, sbuf, sems):
        self.ring, self.full, self.sbuf = ring, full, sbuf
        ss, rs, xs, xr, cs, cr, c2s, c2r = sems
        k, (nc, n, _, cw) = ring, sbuf.shape
        self.d, self.x, self.c, self.c2, self.own = {}, {}, {}, {}, {}
        for j in range(nc):
            cc, cx = cols_of(k.t, j, width, cw), cols_of(k.tx, j, width, cw)
            self.own[j] = cc
            for o in range(1, n):
                d = k.to(o)
                self.d[j, o] = rcopy(sbuf.at[j, d], full.at[k.g, :, cc], ss.at[j, o], rs.at[j, o], d, k.t)
            ref, ref2 = full.at[:, :, cc], full.at[:, :, cx]
            self.x[j] = rcopy(ref, ref, xs.at[j], xr.at[j], k.g, k.tx)
            self.c[j] = rcopy(ref, ref, cs.at[j], cr.at[j], k.g, k.tc)
            self.c2[j] = rcopy(ref2, ref2, c2s.at[j], c2r.at[j], k.g, k.tc)

    def out(self, j, rows):
        self.sbuf[j] = rows.reshape(self.sbuf.shape[1:])
        for o in range(1, self.ring.n):
            self.d[j, o].start()
        self.full[self.ring.g, :, self.own[j]] = self.sbuf[j, self.ring.g]

    def cross(self, j):
        for o in range(1, self.ring.n):
            self.d[j, o].wait_recv()
        self.x[j].start()
        self.c[j].start()

    def core(self, j):
        self.x[j].wait_recv()
        self.c2[j].start()

    def finish(self):
        for c in list(self.c.values()) + list(self.c2.values()):
            c.wait_recv()
        for c in [*self.d.values(), *self.x.values(), *self.c.values(), *self.c2.values()]:
            c.wait_send()


def paired(reduce_one, gather_one, middle, nc):
    reduce_one.core()
    steps = []
    for j in range(nc):
        steps += [(2 * j, 0, lambda j=j: reduce_one.home(j)), (2 * j + 3, 1, lambda j=j: gather_one.out(j, middle(j, reduce_one.rows(j))))]
        steps += [(2 * j + 7, 2, lambda j=j: gather_one.cross(j)), (2 * j + 9, 3, lambda j=j: gather_one.core(j))]
    for _, _, step in sorted(steps, key=lambda s: s[:2]):
        step()
    gather_one.finish()


NC = 4


def split_bf(v):
    high = v.astype(BF)
    return high, (v - high.astype(F32)).astype(BF)


def hidden_body(n, attn, wo, x_own, comb, gates, pick, hidden, full, scale, *scratch):
    bufs, sbuf, sq, sq_in, qs, qr, sems = scratch[:7], *scratch[7:12], scratch[12:]
    ring = Ring(n)
    ring.greet_everyone()
    rows, width = x_own.shape
    shared = []
    cw = width // NC

    def partial(q):
        return mm(attn[...], wo[:, cols_of(q, 0, width, width)])

    def middle(j, rows):
        high, low = split_bf(rows.astype(F32) * gates[...])
        got = x_own[:, j * cw:(j + 1) * cw] + mm(comb[...], high) + mm(comb[...], low)
        hidden[:, j * cw:(j + 1) * cw] = got
        high, low = split_bf(got * got)
        ones = jnp.ones((8, cw), BF)
        squares = mm_t(ones, high) + mm_t(ones, low)
        sq[...] = squares if j == 0 else sq[...] + squares
        if j == NC - 1:
            for i, q in enumerate([ring.tc, ring.tx, ring.tcx]):
                shared.append(ring.send(sq, sq_in.at[i], qs.at[i], qr.at[i], ring.g, q))
        return mm(pick[...], got.astype(BF)).astype(BF)

    red = Reduce(ring, partial, bufs, sems[:6])
    gat = Gather(ring, width, full, sbuf, sems[6:])
    paired(red, gat, middle, NC)
    for c in shared:
        c.wait_recv()
    total = (sq[...] + sq_in[0] + sq_in[1] + sq_in[2])[:1]
    eye = lax.broadcasted_iota(jnp.int32, (rows, rows), 0) == lax.broadcasted_iota(jnp.int32, (rows, rows), 1)
    column = jnp.sum(jnp.where(eye, total, 0.0), axis=1, keepdims=True)
    scale[...] = lax.rsqrt(column / (4 * width) + EPSILON)
    ring.finish()


def hidden_rows(attn, wo, x_own, comb, gates, pick, n, cid):
    slots = attn.shape[0]
    r, (rows, width) = slots // n, x_own.shape
    return pl.pallas_call(
        functools.partial(hidden_body, n),
        out_shape=(
            jax.ShapeDtypeStruct((rows, width), F32), jax.ShapeDtypeStruct((n, r, 4 * width), BF),
            jax.ShapeDtypeStruct((rows, 1), F32)),
        in_specs=[pl.BlockSpec(memory_space=VM)] * 6,
        out_specs=[pl.BlockSpec(memory_space=VM)] * 3,
        scratch_shapes=REDUCE_BUFS(NC, n, r, width // NC) + [VM((NC, n, r, width // NC), BF)]
        + [VM((8, rows), F32), VM((3, 8, rows), F32), DMA((3,)), DMA((3,))]
        + REDUCE_SEMS(NC, n) + GATHER_SEMS(NC, n),
        name="hidden_rows", compiler_params=params(cid),
    )(attn, wo, x_own, comb, gates, pick)


def expert_body(
    n, hid_rows, d_mbr, gain, wg_hbm, wu_hbm, wd_hbm, hidden, dy_own, gain_t, scale, mlp_t, mlp_gates, mlp_rows, att_rows,
    full, d_hidden, mixed, gain_part, n2, inner, d_gate, d_up, *scratch,
):
    ring = Ring(n)
    bufs, bufs2 = scratch[:7], scratch[7:14]
    sbuf, wg, wu, wd, r_own, r_in, r_to, r_back = scratch[14:22]
    wsem, rss, rsr, rds, rdr = scratch[22:27]
    sems = scratch[27:]
    ff = wg.shape[1]
    rows, width = hidden.shape
    slots = n2.shape[0]
    features = 4 * width
    cw = width // NC
    loads = [pltpu.make_async_copy(a, b, wsem.at[i]) for i, (a, b) in enumerate([(wg_hbm, wg), (wu_hbm, wu), (wd_hbm, wd)])]
    for c in loads:
        c.start()
    ring.greet_everyone()

    def norm_rows(i, _):
        at = pl.ds(pl.multiple_of(i * 64, 64), 64)
        v = hid_rows[i].astype(F32)
        s = lax.rsqrt(jnp.mean(v * v, axis=-1, keepdims=True) + EPSILON)
        n2[at, :] = (v * s * gain[...]).astype(BF)
        return _

    lax.fori_loop(0, n, norm_rows, 0)
    for c in loads:
        c.wait()
    r_own[...] = jnp.zeros_like(r_own)

    def units(at, size):
        a = n2[...]
        gate = mm(a, wg[:, at])
        up = mm(a, wu[:, at])
        d_in = mm_t(d_mbr[...], wd[at, :])
        sig = jax.nn.sigmoid(gate)
        silu = gate * sig
        inner[:, at] = (silu * up).astype(BF)
        du = (d_in * silu).astype(BF)
        dg = (d_in * up * sig * (1.0 + gate * (1.0 - sig))).astype(BF)
        d_up[:, at] = du
        d_gate[:, at] = dg
        both = (gate * dg.astype(F32) + up * du.astype(F32)).astype(BF)
        r_own[...] += mm_t(jnp.ones((8, size), BF), both)

    tile = 256

    def unit_tile(i, _):
        units(pl.ds(pl.multiple_of(i * tile, tile), tile), tile)
        return _

    lax.fori_loop(0, ff // tile, unit_tile, 0)
    if ff % tile:
        units(pl.ds(ff // tile * tile, ff % tile), ff % tile)

    others = [ring.tc, ring.tx, ring.tcx]
    r_sends = [ring.send(r_own, r_in.at[i], rss.at[i], rsr.at[i], ring.g, q) for i, q in enumerate(others)]

    def partial(q):
        at = cols_of(q, 0, width, width)
        return mm_t(d_gate[...], wg[at, :]) + mm_t(d_up[...], wu[at, :])

    def partial_mixed(q):
        return mm(inner[...], wd[:, cols_of(q, 0, width, width)])

    pairs = {}

    def share_r():
        for c in r_sends:
            c.wait_recv()
        r_to[...] = r_own[...] + r_in[0] + r_in[1] + r_in[2]
        for o in range(1, n):
            d = ring.to(o)
            half = pl.ds(pl.multiple_of(d // 2 * 128, 128), 128)
            pairs[o] = ring.send(r_to.at[:, half], r_back.at[ring.g], rds.at[o], rdr.at[o], d, ring.t)
        r_back[ring.g] = r_to[:, pl.ds(pl.multiple_of(ring.g // 2 * 128, 128), 128)]

    total_r = {}

    def take_r():
        for o in range(1, n):
            pairs[o].wait_recv()
        odd = lax.rem(ring.g, 2) == 1
        got = jnp.concatenate(
            [jnp.where(odd, r_back[e][:, 64:], r_back[e][:, :64]) for e in range(n)], axis=1)
        high = got.astype(BF)
        low = (got - high.astype(F32)).astype(BF)
        total_r[0] = (mm_t(mlp_t[...], high) + mm_t(mlp_t[...], low))[:, :1] / features

    def middle(j, got):
        if j == 0:
            take_r()
        cc = slice(j * cw, (j + 1) * cw)
        s2, h = scale[...], hidden[:, cc]
        d_n = mm(mlp_t[...], got)
        d_h = dy_own[:, cc] + s2 * (gain_t[:, cc] * d_n) - h * (s2 * s2) * total_r[0]
        d_hidden[:, cc] = d_h
        gain_part[:, cc] = jnp.broadcast_to(jnp.sum(d_n * h * s2, axis=0, keepdims=True), (8, cw))
        return mm(att_rows[...], d_h.astype(BF)).astype(BF)

    red = Reduce(ring, partial, bufs, sems[:6])
    gat = Gather(ring, width, full, sbuf, sems[6:14])
    red2 = Reduce(ring, partial_mixed, bufs2, sems[14:20])

    def settle(j):
        got = red2.rows(j)
        scaled = got.astype(F32) * mlp_gates[...]
        high = scaled.astype(BF)
        low = (scaled - high.astype(F32)).astype(BF)
        cc = slice(j * cw, (j + 1) * cw)
        mixed[:, cc] = (hidden[:, cc] + mm(mlp_t[...], high) + mm(mlp_t[...], low)).astype(BF)

    red.core()
    share_r()
    steps = []
    for j in range(NC):
        steps += [(2 * j, 1, lambda j=j: red.home(j)), (2 * j + 3, 2, lambda j=j: gat.out(j, middle(j, red.rows(j))))]
        steps += [(2 * j + 7, 3, lambda j=j: gat.cross(j)), (2 * j + 9, 4, lambda j=j: gat.core(j))]
        steps += [(2 * j + 12, 7, lambda j=j: red2.home(j)), (2 * j + 16, 8, lambda j=j: settle(j))]
    steps += [(9.5, 5, red2.core)]
    steps.sort(key=lambda s: s[:2])
    for _, _, run in steps:
        run()
    gat.finish()
    ring.finish()


def expert_layer(hid_rows, d_mbr, gain, wg, wu, wd, hidden, dy_own, gain_t, scale, mlp_t, mlp_gates, mlp_rows, att_rows, n, cid):
    r, features = hid_rows.shape[1:]
    ff = wg.shape[1]
    rows, width = hidden.shape
    slots, cw = n * r, width // NC
    any_, vm = pl.BlockSpec(memory_space=pl.ANY), pl.BlockSpec(memory_space=VM)
    sds = jax.ShapeDtypeStruct
    return pl.pallas_call(
        functools.partial(expert_body, n),
        out_shape=(
            sds((n, r, features), BF), sds((rows, width), F32), sds((rows, width), BF), sds((8, width), F32),
            sds((slots, features), BF), sds((slots, ff), BF), sds((slots, ff), BF), sds((slots, ff), BF)),
        in_specs=[vm, vm, vm, any_, any_, any_] + [vm] * 8,
        out_specs=[vm] * 8,
        scratch_shapes=REDUCE_BUFS(NC, n, r, cw) + REDUCE_BUFS(NC, n, r, cw) + [
            VM((NC, n, r, cw), BF), VM((features, ff), BF), VM((features, ff), BF), VM((ff, features), BF),
            VM((8, slots), F32), VM((3, 8, slots), F32), VM((8, slots), F32), VM((n, 8, 128), F32),
            DMA((3,)), DMA((3,)), DMA((3,)), DMA((n,)), DMA((n,))]
        + REDUCE_SEMS(NC, n) + GATHER_SEMS(NC, n) + REDUCE_SEMS(NC, n),
        name="expert_layer", compiler_params=params(cid),
    )(hid_rows, d_mbr, gain, wg, wu, wd, hidden, dy_own, gain_t, scale, mlp_t, mlp_gates, mlp_rows, att_rows)


META = {name: i for i, name in enumerate(
    ("ar0", "ar1", "ag0", "ag1", "mr0", "mr1", "mg0", "mg1", "pos", "seg", "wpos"))}


def iota(shape, dim):
    return lax.broadcasted_iota(jnp.int32, shape, dim)


def slot_table(meta, first, name, cap):
    member = (meta[first:first + 1] == name) | (meta[first + 1:first + 2] == name)
    tokens = meta.shape[1]
    before = jnp.where(iota((tokens, tokens), 0) < iota((tokens, tokens), 1), 1.0, 0.0).astype(BF)
    rank = mm(jnp.broadcast_to(jnp.where(member, 1.0, 0.0), (8, tokens)).astype(BF), before)[:1]
    return jnp.where((rank == iota((cap, tokens), 0).astype(F32)) & member, 1.0, 0.0).astype(BF)


def allowed_pairs(meta, meta_t):
    seg, wpos = META["seg"], META["wpos"]
    same = meta_t[:, seg:seg + 1] == meta[seg:seg + 1]
    return jnp.where(same & (meta[wpos:wpos + 1] <= meta_t[:, wpos:wpos + 1]), 1.0, 0.0).astype(BF)


def position_rows(meta_t):
    pos = META["pos"]
    tokens = meta_t.shape[0]
    return jnp.where(meta_t[:, pos:pos + 1] == iota((tokens, tokens), 1).astype(F32), 1.0, 0.0).astype(BF)


def looked_up(rows, table):
    got = mm(rows, table)
    w = got.shape[1] // 3
    return got[:, :w] + got[:, w:2 * w] + got[:, 2 * w:]


def turned(v, cosine, sine):
    out = []
    for h in range(v.shape[1] // HD):
        u = v[:, h * HD:(h + 1) * HD]
        out.append(u * cosine + pltpu.roll(u, HD // 2, 1) * sine)
    return jnp.concatenate(out, axis=1)


def angle_tables(positions):
    half = HD // 2
    frequency = np.exp(-math.log(THETA) * np.arange(half) / half)
    turned_by = np.arange(positions)[:, None] * frequency[None, :]
    cosine = np.concatenate([np.cos(turned_by)] * 2, axis=1).astype(np.float32)
    sine = np.concatenate([-np.sin(turned_by), np.sin(turned_by)], axis=1).astype(np.float32)

    def parts(v):
        out, left = [], v
        for _ in range(3):
            p = left.astype(jnp.bfloat16)
            out.append(p)
            left = left - p.astype(np.float32)
        return np.concatenate(out, axis=1)

    return jnp.asarray(parts(cosine)), jnp.asarray(parts(sine))


def softmax_rows(scores):
    top = jnp.max(scores, axis=-1, keepdims=True)
    expo = jnp.exp(scores - top)
    return expo / jnp.sum(expo, axis=-1, keepdims=True)


def keys_back_tables(meta, cos_t, sin_t, n, cap):
    m = meta[...]
    m_t = m.T
    tables = jnp.concatenate([slot_table(m, META["ar0"], float(e), cap) for e in range(n)], axis=0)
    at_pos = position_rows(m_t)
    return (mm(tables, allowed_pairs(m, m_t)) - 1.0) * 1e30, looked_up(at_pos, cos_t[...]), looked_up(at_pos, sin_t[...])


def keys_back_heads(part, query, d_attn, keys, values, bias, cosine, sine, d_kv):
    n, cap, hw = query.shape
    heads = hw // HD // 2
    root = math.sqrt(HD)
    for i in range(heads):
        h = part * heads + i
        hh = slice(h * HD, (h + 1) * HD)
        q = query[:, :, hh].reshape(n * cap, HD)
        d_o = d_attn[:, :, hh].reshape(n * cap, HD)
        k, v = keys[:, hh], values[:, hh]
        probs = softmax_rows(mm_t(q, k) / root + bias)
        d_probs = mm_t(d_o, v)
        delta = jnp.sum(d_probs * probs, axis=-1, keepdims=True)
        d_scores = (probs * (d_probs - delta)).astype(BF)
        at = part * hw + i * HD
        d_kv[:, at + hw // 2:at + hw // 2 + HD] = mm_rows(probs.astype(BF), d_o).astype(BF)
        d_k = mm_rows(d_scores, q) / root
        d_kv[:, at:at + HD] = turned(d_k, cosine, -sine).astype(BF)


def map_grad_body(normed, d_kv, out, d_cols):
    hw = d_kv.shape[1] // 2
    tiles = d_kv.shape[1] // 128
    half = tiles // 4

    @pl.when(pl.program_id(0) == 0)
    def _():
        for i in range(hw // 128):
            for c in range(2):
                at = i // half * hw + c * (hw // 2) + i % half * 128
                d_cols[:, (2 * i + c) * 128:(2 * i + c + 1) * 128] = d_kv[:, at:at + 128]

    got = mm_rows(normed[...], d_cols[...])
    for b in range(tiles):
        out[pl.ds(b, got.shape[0], stride=tiles), :] = got[:, b * 128:(b + 1) * 128]


def map_grad(normed, d_kv):
    total, features = normed.shape
    both = d_kv.shape[1]
    size, tiles = 512, both // 128
    out = pl.pallas_call(
        map_grad_body, grid=(features // size,),
        out_shape=jax.ShapeDtypeStruct((features * tiles, 128), F32),
        in_specs=[pl.BlockSpec((total, size), lambda i: (0, i)), pl.BlockSpec((total, both), lambda i: (0, 0))],
        out_specs=pl.BlockSpec((size * tiles, 128), lambda i: (i, 0)), scratch_shapes=[VM((total, both), BF)],
        name="map_grad", compiler_params=pltpu.CompilerParams(vmem_limit_bytes=56 * 2**20),
    )(normed, d_kv)
    return out.reshape(features, tiles // 2, 2, 128).transpose(0, 2, 1, 3).reshape(features, 2, both // 2)


def attention_back(i, d_attn, query, keys, values, bias, turn_slots, dq_pre):
    root = math.sqrt(HD)
    dq = []
    for h in range(query.shape[2] // HD):
        hh = slice(h * HD, (h + 1) * HD)
        k = keys[i, :, hh]
        probs = softmax_rows(mm_t(query[i, :, hh], k) / root + bias[i])
        d_probs = mm_t(d_attn[i, :, hh], values[i, :, hh])
        delta = jnp.sum(d_probs * probs, axis=-1, keepdims=True)
        dq.append(mm((probs * (d_probs - delta)).astype(BF), k) / root)
    dq_pre[i] = turned(jnp.concatenate(dq, axis=1), turn_slots[i, :, :HD], -turn_slots[i, :, HD:]).astype(BF)


def tail_body(
    n, d_attn, mb_rows, meta, cos_t, sin_t, x_own, scale, gain, d_hidden, hidden, mlp_gate, mlp_rows, att_rows, gain_mlp_part, sorter,
    query_hbm, keys_hbm, values_hbm, bias_hbm, turn_hbm, q_back_hbm, wq_hbm, wk_hbm, wv_hbm,
    d_kv_all, mixed_out, grad_out, gain_att_out, gain_mlp_out, dq_pre, *scratch,
):
    ring = Ring(n)
    (at_in, d_kv, kc_out, kc_in, kv_keep, kx_out, kx_in, sbuf, sq, sq_in, g_out, g_in, g_sum, d_norm, mixed, comb, mlp_t,
     query, keys, values, bias, turn_slots, q_back, w_q, w_k, w_v, whole, pbuf, cbuf, cin, back, gains) = scratch[:32]
    xbuf, xin, dbuf, rbuf = scratch[32:36]
    (as_, ar, zs, zr, ws, wr, ys, yr, ks, kr, lxs, lxr, qs, qr, gs, gr, ts, tr, wsem, qsem) = scratch[36:56]
    sems, fsems = scratch[56:62], scratch[62:]
    wanted = [(query_hbm, query), (keys_hbm, keys), (values_hbm, values), (bias_hbm, bias), (turn_hbm, turn_slots), (wq_hbm, w_q),
              (q_back_hbm, q_back), (wk_hbm, w_k), (wv_hbm, w_v)]
    loads = [pltpu.make_async_copy(a, b, wsem.at[i]) for i, (a, b) in enumerate(wanted)]
    cw = x_own.shape[1] // NC
    q_loads = [
        pltpu.make_async_copy(
            wq_hbm.at[pl.ds(q * NC * cw + j * cw, cw), :], w_q.at[pl.ds((j * 4 + q) * cw, cw), :], qsem.at[j * 4 + q])
        for j in range(NC) for q in range(4)]
    for c in loads[:5] + q_loads + loads[6:]:
        c.start()
    rows, width = x_own.shape
    cw = width // NC
    cap = query.shape[1]
    slots = n * cap
    all_keys, all_values = keys, values
    hw = keys.shape[2]
    features = 4 * width
    keys, values, meta, scale = keys.at[ring.g], values.at[ring.g], meta.at[ring.g], scale.at[ring.g]
    z, y = ring.g // 2, lax.rem(ring.g, 2)
    depth = n // 2
    ring.greet_everyone()

    half = hw // 2
    arrive = []
    for c in range(2):
        cc = pl.ds(c * half, half)
        arrive.append([
            ring.send(d_attn.at[ring.to(o), :, cc], at_in.at[ring.g, :, cc], as_.at[c, o], ar.at[c, o], ring.to(o), ring.t)
            for o in range(1, n)])
    at_in[ring.g] = d_attn[ring.g]
    comb[...] = att_rows[...].T
    mlp_t[...] = mlp_rows[...].T
    own_bias, cosine, sine = keys_back_tables(meta, cos_t, sin_t, n, cap)
    for c in loads[:5]:
        c.wait()

    def group_back(i, _):
        attention_back(i, d_attn, query, all_keys, all_values, bias, turn_slots, dq_pre)
        return _

    halves = [(c, slice(c * hw, (c + 1) * hw)) for c in range(2)]
    pairs = lambda zz, yy: zz * 2 + yy
    across = []

    def unit(zz, c):
        return d_kv_all.at[pairs(zz, y), :, pl.ds(c * hw, hw)]

    def step(up, hop, c, first):
        zz = z - hop if up else z + hop
        here = zz >= 0 if up else zz < depth
        ss, rs = (zs, zr) if up else (ws, wr)
        on, back_to = (z + 1, z - 1) if up else (z - 1, z + 1)

        @pl.when(here)
        def _():
            ref = unit(zz, c)
            if not first:
                rcopy(ref, ref, ss.at[hop - 1, c], rs.at[hop - 1, c], pairs(back_to, y), ring.t).wait_recv()

            @pl.when((on < depth) if up else (on >= 0))
            def _():
                rcopy(ref, ref, ss.at[hop, c], rs.at[hop, c], pairs(on, y), ring.t).start()

            if up or not first:
                rcopy(ref, ref, ys.at[zz, c], yr.at[zz, c], pairs(z, 1 - y), ring.t).start()

    def drain(up, hop, c):
        zz = z - hop if up else z + hop
        here = zz >= 0 if up else zz < depth
        ss, rs = (zs, zr) if up else (ws, wr)
        on = z + 1 if up else z - 1

        @pl.when(here & ((on < depth) if up else (on >= 0)))
        def _():
            ref = unit(zz, c)
            rcopy(ref, ref, ss.at[hop, c], rs.at[hop, c], pairs(on, y), ring.t).wait_send()

    def spread(hop, c):
        step(True, hop, c, hop == 0)
        step(False, hop, c, hop == 0)

    def keys_values(c):
        for r in arrive[c]:
            r.wait_recv()
        keys_back_heads(c, q_back, at_in, keys, values, own_bias, cosine, sine, d_kv)
        cc = slice(c * hw, (c + 1) * hw)
        d_kv_all[ring.g, :, cc] = d_kv[:, cc]
        spread(0, c)

    lax.fori_loop(0, n // 2, group_back, 0)
    loads[6].wait()
    keys_values(0)
    lax.fori_loop(n // 2, n, group_back, 0)
    keys_values(1)
    for c in q_loads:
        c.wait()

    def back_cols(j):
        dq = dq_pre[...].reshape(slots, hw)
        return mm_t(dq, w_q[j * 4 * cw:(j + 1) * 4 * cw, :])

    red = ChunkReduce(ring, back_cols, whole, pbuf, (cbuf, xbuf, dbuf), (cin, xin, rbuf), sems)
    red.core(0)
    spread(1, 0)
    for j in range(1, NC):
        red.core(j)
        red.cross(j - 1)
    spread(1, 1)
    red.cross(NC - 1)
    red.home(0)
    red.home(1)
    loads[7].wait()
    loads[8].wait()

    def kv_part(q):
        at = cols_of(q, 0, width, width)
        return sum(
            mm_t(d_kv[:, c * hw:c * hw + half], w_k[at, c * half:(c + 1) * half])
            + mm_t(d_kv[:, c * hw + half:(c + 1) * hw], w_v[at, c * half:(c + 1) * half]) for c in range(2))

    kc_out[0] = kv_part(ring.tc).astype(BF)
    kc_out[1] = kv_part(ring.tcx).astype(BF)
    kc = ring.send(kc_out, kc_in, ks, kr, ring.g, ring.tc)
    red.home(2)
    kv_keep[1] = kv_part(ring.tx)
    kc.wait_recv()
    kx_out[...] = (kv_keep[1] + kc_in[1].astype(F32)).astype(BF)
    kx = ring.send(kx_out, kx_in, lxs, lxr, ring.g, ring.tx)
    kv_keep[0] = kv_part(ring.t)
    red.home(3)
    spread(2, 0)
    kx.wait_recv()
    local = kv_keep[0] + kc_in[0].astype(F32) + kx_in[...].astype(F32)
    spread(2, 1)
    spread(3, 0)
    squares = jnp.zeros((8, rows), F32)
    for j in range(NC):
        cc = slice(j * cw, (j + 1) * cw)
        got = mm(comb[...], red.rows(j)) + local[:, cc]
        d_norm[:, cc] = got
        high, low = split_bf(x_own[:, cc] * gain[:, cols_of(ring.t, j, width, cw)] * got)
        ones = jnp.ones((8, cw), BF)
        squares = squares + mm_t(ones, high) + mm_t(ones, low)
        g_out[:, cc] = jnp.concatenate([
            gain_mlp_part[:1, cc], jnp.sum(got * x_own[:, cc] * scale[...], axis=0, keepdims=True), jnp.zeros((6, cw), F32)], axis=0)
    sq[...] = squares
    shared = [ring.send(sq, sq_in.at[i], qs.at[i], qr.at[i], ring.g, q) for i, q in enumerate([ring.tc, ring.tx, ring.tcx])]
    sums = []
    for o in range(1, n):
        sums.append(ring.send(g_out, g_in.at[ring.g], gs.at[o], gr.at[o], ring.to(o), ring.t))
    g_in[ring.g] = g_out[...]
    for j in range(NC):
        cc = slice(j * cw, (j + 1) * cw)
        high, low = split_bf(mb_rows[j].reshape(slots, cw).astype(F32) * mlp_gate[...])
        mixed[:, cc] = (hidden[:, cc] + mm(mlp_t[...], high) + mm(mlp_t[...], low)).astype(BF)
    for c in shared:
        c.wait_recv()
    total = (sq[...] + sq_in[0] + sq_in[1] + sq_in[2])[:1]
    eye = iota((rows, rows), 0) == iota((rows, rows), 1)
    mean = jnp.sum(jnp.where(eye, total, 0.0), axis=1, keepdims=True) / features
    s = scale[...]
    in_grad = d_hidden[...] + s * (gain[:, cols_of(ring.t, 0, width, width)] * d_norm[...]) - x_own[...] * (s * s * s * mean)
    per = rows // n
    fin = ChunkGather(
        ring, lambda j, q, e: back.at[slice(None) if e is None else e, :, cols_of(q, 0, width, width)], sbuf, fsems)
    fin.out(0, jnp.concatenate(
        [mixed[...].reshape(n, per, width), in_grad.astype(BF).reshape(n, per, width)], axis=1))
    spread(3, 1)
    for c in sums:
        c.wait_recv()
    g_sum[...] = functools.reduce(lambda a, b: a + b, [g_in[e] for e in range(n)])
    at_t = cols_of(ring.t, 0, width, width)
    gains[:, at_t] = g_sum[...]
    told = [ring.send(g_sum, gains.at[:, at_t], ts.at[i], tr.at[i], ring.g, q) for i, q in enumerate([ring.tc, ring.tx, ring.tcx])]
    fin.cross(0)
    fin.core(0)
    fin.here(0)
    for ref, at in ((mixed_out, slice(0, per)), (grad_out, slice(per, 2 * per))):
        ref[...] = mm_rows(sorter[...], back[:, at].reshape(rows, features)).astype(BF)
    for c in told:
        c.wait_recv()
    gain_mlp_out[...] = gains[0:1]
    gain_att_out[...] = gains[1:2]
    for c, _ in halves:
        for zz in range(depth):
            ref = d_kv_all.at[pairs(zz, 1 - y), :, pl.ds(c * hw, hw)]
            rcopy(ref, ref, ys.at[zz, c], yr.at[zz, c], pairs(z, 1 - y), ring.t).wait()
        for hop in range(depth - 1):
            drain(True, hop, c)
            drain(False, hop, c)
    ring.finish()
    fin.sent()
    red.sent_core()
    red.sent_rest()


def layer_tail(args, later, n, cid):
    d_attn, x_own = args[0], args[5]
    rows, width = x_own.shape
    cap, hw = d_attn.shape[1:]
    cw, features, depth = width // NC, 4 * width, n // 2
    slots = n * cap
    sds = jax.ShapeDtypeStruct
    per = 2 * rows // n
    one, two = VM((NC, n, cap, cw), BF), VM((NC, 2, n, cap, cw), BF)
    any_, vm = pl.BlockSpec(memory_space=pl.ANY), pl.BlockSpec(memory_space=VM)
    return pl.pallas_call(
        functools.partial(tail_body, n),
        out_shape=(
            sds((n, rows, 2 * hw), BF), sds((rows, features), BF), sds((rows, features), BF), sds((1, features), F32),
            sds((1, features), F32), sds((n, cap, hw), BF)),
        in_specs=[vm] * len(args) + [any_] * len(later), out_specs=[vm] * 6,
        scratch_shapes=[
            VM((n, cap, hw), BF), VM((rows, 2 * hw), BF), VM((2, rows, width), BF), VM((2, rows, width), BF),
            VM((2, rows, width), F32), VM((rows, width), BF), VM((rows, width), BF), VM((1, n, per, width), BF),
            VM((8, rows), F32), VM((3, 8, rows), F32), VM((8, width), F32), VM((n, 8, width), F32), VM((8, width), F32),
            VM((rows, width), F32), VM((rows, width), BF), VM((rows, slots), BF), VM((rows, slots), BF)]
        + [VM(a.shape, a.dtype) for a in later]
        + [VM((slots, 4 * cw), F32), VM((NC, 2, n, cap, cw), F32), two, two, VM((n, per, features), BF), VM((8, features), F32)]
        + [one] * 4 + [
            DMA((2, n)), DMA((2, n)), DMA((depth, 2)), DMA((depth, 2)), DMA((depth, 2)), DMA((depth, 2)), DMA((depth, 2)), DMA((depth, 2)),
            DMA, DMA, DMA, DMA, DMA((3,)), DMA((3,)), DMA((n,)), DMA((n,)), DMA((3,)), DMA((3,)), DMA((len(later),)), DMA((4 * NC,))]
        + REDUCE_SEMS(NC, n) + GATHER_SEMS(1, n),
        name="layer_tail", compiler_params=pltpu.CompilerParams(
            collective_id=cid, has_side_effects=True, vmem_limit_bytes=63 * 2**20),
    )(*args, *later)


def front_body(
    n, tokens, out_grad, place_r, att_routes, att_gates, mlp_routes, mlp_gates, seq_lengths, gain, cos_t, sin_t, wkv_hbm, wq_hbm,
    dy_own, meta_all, sorter_out, att_rows, att_gate, mlp_rows, mlp_gate, att_in, wk_hbm, wv_hbm, x_own,
    normed_hbm, picked_hbm, keys, values, query, attn, scale, bias, turn_slots, d_mbr,
    x_all, dy_send, w_kv, w_k, w_v, w_q, meta_w, mlp_in, normed, picked, dy_rows, sbuf, ksem, osem, nsem, *sems,
):
    gsems, sems = sems[:8], sems[8:]
    ms, mr, dys, dyr, zs, zr, ws, wr, ys, yr, xs, xr, cs, cr = sems
    ring = Ring(n)
    g, t = ring.g, ring.t
    rows, features = tokens.shape
    width, per = features // 4, rows // n
    z, y, depth = g // 2, lax.rem(g, 2), n // 2
    pairs = lambda zz, yy: zz * 2 + yy
    fetch = pltpu.make_async_copy(wkv_hbm, w_kv, ksem.at[0])
    fetch.start()
    fetch_q = pltpu.make_async_copy(wq_hbm, w_q, ksem.at[1])
    fetch_q.start()
    gw = sbuf.shape[-1]
    gat = ChunkGather(
        ring, lambda j, q, e: dy_rows.at[slice(None) if e is None else e, :, cols_of(q, j, width, gw)], sbuf, gsems)
    ring.greet_all()
    place_c = place_r[...].astype(F32).T.astype(jnp.int32)

    def arrival(row, col):
        g_row, g_col = row // rows, col // rows
        before = (g_col == g_row) & (iota((rows, rows), 0) < iota((rows, rows), 1))
        return g_row, jnp.sum(jnp.where(before, 1.0, 0.0), axis=0, keepdims=True).astype(jnp.int32)

    col_g = jnp.sum(jnp.where(iota((rows, n), 1) == g, place_c, 0), axis=1, keepdims=True)
    g_row, rank = arrival(place_r[pl.ds(g, 1), :], col_g)
    sorter = jnp.where(g_row * per + rank == iota((rows, rows), 0), 1.0, 0.0).astype(BF)
    sorter_out[...] = sorter

    half = width // 2
    chunks = [("b", t, half), ("a", t, 0), ("c", ring.tx, 0)]
    cols = [pl.ds(pl.multiple_of(q * width + off, half), half) for _, q, off in chunks]
    for cc in cols:
        x_all[:, g, :, cc] = mm(sorter, tokens[:, cc]).astype(BF).reshape(n, per, half)

    def unit(zz, yy, c):
        return x_all.at[:, pairs(zz, yy), :, cols[c]]

    def cross(zz, yy, c):
        if chunks[c][0] == "b":
            ref = unit(zz, yy, c)
            rcopy(ref, ref, xs.at[pairs(zz, yy)], xr.at[pairs(zz, yy)], g, ring.tx).start()

    def hop_on(up, hop, c):
        zz = z - hop if up else z + hop
        here = zz >= 0 if up else zz < depth
        ss, rs = (zs, zr) if up else (ws, wr)
        on, source = (z + 1, z - 1) if up else (z - 1, z + 1)

        @pl.when(here)
        def _():
            ref = unit(zz, y, c)
            if hop:
                rcopy(ref, ref, ss.at[hop - 1, c], rs.at[hop - 1, c], pairs(source, y), t).wait_recv()

            @pl.when((on < depth) if up else (on >= 0))
            def _():
                rcopy(ref, ref, ss.at[hop, c], rs.at[hop, c], pairs(on, y), t).start()

            if up or hop:
                rcopy(ref, ref, ys.at[zz, c], yr.at[zz, c], pairs(z, 1 - y), t).start()
                cross(zz, y, c)

    def from_y(zz, c):
        ref = unit(zz, 1 - y, c)
        rcopy(ref, ref, ys.at[zz, c], yr.at[zz, c], pairs(z, 1 - y), t).wait_recv()
        cross(zz, 1 - y, c)

    count = range(len(chunks))
    for c in count:
        hop_on(True, 0, c)
        hop_on(False, 0, c)

    meta_w[...] = jnp.zeros_like(meta_w)
    for name, ref in (("ar0", att_routes), ("ag0", att_gates), ("mr0", mlp_routes), ("mg0", mlp_gates)):
        meta_w[META[name]:META[name] + 2] = ref[...].astype(F32)
    at = iota((1, rows), 1)
    end, segment, begin = jnp.zeros((1, 1), jnp.int32), jnp.zeros((1, rows), jnp.int32), jnp.zeros((1, rows), jnp.int32)
    for k in range(seq_lengths.shape[1]):
        end = end + seq_lengths[:, k:k + 1]
        segment = segment + jnp.where(at >= end, 1, 0)
        begin = jnp.where(at >= end, end, begin)
    for name, v in (("pos", at - begin), ("seg", segment), ("wpos", at)):
        meta_w[META[name]:META[name] + 1] = v.astype(F32)
    spot = jnp.zeros((rows, rows), F32)
    for s in range(n):
        row, col = place_r[s:s + 1, :], place_c[:, s:s + 1]
        s_row, s_rank = arrival(row, col)
        put = jnp.where((s_row == g) & (s_rank + s * per == iota((rows, rows), 0)), 1.0, 0.0).astype(BF)
        work = jnp.where(col - col // rows * rows == iota((rows, rows), 1), 1.0, 0.0).astype(BF)
        spot = spot + mm(put, work)
    spot = spot.astype(BF)
    left, moved = meta_w[...], 0.0
    for _ in range(3):
        piece = left.astype(BF)
        moved = moved + mm_t(piece, spot)
        left = left - piece.astype(F32)
    meta_all[g] = moved
    sent = [ring.send(meta_all.at[g], meta_all.at[g], ms.at[o], mr.at[o], ring.to(o), t) for o in range(1, n)]

    mine = pl.ds(pl.multiple_of(t * width, width), width)
    dy_send[...] = mm(sorter, out_grad[:, mine]).astype(BF).reshape(n, per, width)
    dealt = [ring.send(dy_send.at[ring.to(o)], dy_own.at[g], dys.at[o], dyr.at[o], ring.to(o), t) for o in range(1, n)]
    dy_own[g] = dy_send[g]

    stored = []

    def split(i):
        if i == 0:
            fetch.wait()
        at = pl.ds(i * 256, 256)
        for c, (v, hbm) in enumerate(((w_k, wk_hbm), (w_v, wv_hbm))):
            v[at, :] = w_kv[at, c, :]
            stored.append(pltpu.make_async_copy(v.at[at, :], hbm.at[at, :], osem.at[c, i]))
            stored[-1].start()

    def tables(first, gate, out_rows, out_gate):
        m = meta_all[g]
        for e in range(n):
            out_rows[e] = slot_table(m, first, float(e), CAP)
            out_gate[e] = slot_gates(m, first, gate, float(e), out_rows[e])

    def hops(k):
        for c in count:
            hop_on(True, k, c)
            hop_on(False, k, c)

    tables(META["mr0"], META["mg0"], mlp_rows, mlp_gate)
    hops(1)
    hops(2)
    hops(3)
    for zz in range(depth):
        from_y(zz, 0)
    for c in dealt:
        c.wait_recv()
    slots = mm(mlp_rows[...].reshape(n * CAP, rows), dy_own[...].reshape(rows, width)).astype(BF)
    for j in range(2):
        gat.out(j, slots[:, j * gw:(j + 1) * gw])
    for i in range(4):
        split(i)

    def whole(q, off):
        return x_all.at[:, :, :, pl.ds(pl.multiple_of(q * width + off, half), half)]

    cores = [ring.send(whole(t, half), whole(t, half), cs.at[0], cr.at[0], g, ring.tc)]
    for c in (1, 2):
        split(3 + c)
        for zz in range(depth):
            from_y(zz, c)
        ref = whole(chunks[c][1], 0)
        cores.append(ring.send(ref, ref, cs.at[c], cr.at[c], g, ring.tc))
    for c in sent:
        c.wait_recv()
    me = g.astype(F32)
    split(6)
    split(7)
    for u in range(n):
        ref = x_all.at[:, u, :, pl.ds(pl.multiple_of(ring.tx * width + half, half), half)]
        rcopy(ref, ref, xs.at[u], xr.at[u], g, ring.tx).wait_recv()
    cores.append(ring.send(whole(ring.tx, half), whole(ring.tx, half), cs.at[3], cr.at[3], g, ring.tc))
    x_own[...] = x_all[g, :, :, mine].reshape(rows, width).astype(F32)
    for c in cores:
        c.wait_recv()
    for u in range(n):
        ref = x_all.at[:, u, :, cols[0]]
        rcopy(ref, ref, xs.at[u], xr.at[u], g, ring.tx).wait_send()
    for c in count:
        for zz in range(depth):
            ref = unit(zz, y, c)
            rcopy(ref, ref, ys.at[zz, c], yr.at[zz, c], pairs(z, 1 - y), t).wait_send()
        for hop in range(depth - 1):
            for up in (True, False):
                zz = z - hop if up else z + hop
                on = z + 1 if up else z - 1
                ss, rs = (zs, zr) if up else (ws, wr)

                @pl.when((zz >= 0) & (on < depth) if up else (zz < depth) & (on >= 0))
                def _(zz=zz, on=on, ss=ss, rs=rs, hop=hop, c=c):
                    ref = unit(zz, y, c)
                    rcopy(ref, ref, ss.at[hop, c], rs.at[hop, c], pairs(on, y), t).wait_send()
    fetch_q.wait()

    pair, steps = 2, n // 2
    heads = w_q.shape[1] // HD
    hw = w_q.shape[1]

    def out_copies(i):
        at = pl.ds(pair * i, pair)
        return (pltpu.make_async_copy(normed.at[at], normed_hbm.at[at], nsem.at[0, i]),
                pltpu.make_async_copy(picked.at[at], picked_hbm.at[at], nsem.at[1, i]))

    def two_groups(i, carry):
        @pl.when(i == 0)
        def _():
            gat.cross(0)

        @pl.when(i == 1)
        def _():
            gat.cross(1)

        @pl.when(i == 2)
        def _():
            gat.core(0)

        two = pl.ds(pair * i, pair)
        flat = x_all[two].reshape(pair * rows, features).astype(F32)
        s = lax.rsqrt(jnp.mean(flat * flat, axis=-1, keepdims=True) + EPSILON)
        scale[two] = s.reshape(pair, rows, 1)
        normed[two] = (flat * s * gain[...]).astype(BF).reshape(pair, rows, features)
        low = normed[two].reshape(pair * rows, features)
        k_all, v_all = mm(low, w_k[...]), mm(low, w_v[...])
        for p in range(pair):
            at = pair * i + p
            m = meta_all[at]
            m_t = m.T
            table = slot_table(m, META["ar0"], me, CAP)
            at_pos = position_rows(m_t)
            rr = slice(p * rows, (p + 1) * rows)
            keys[at] = turned(k_all[rr], looked_up(at_pos, cos_t[...]), looked_up(at_pos, sin_t[...])).astype(BF)
            values[at] = v_all[rr].astype(BF)
            picked[at] = mm(table, normed[at]).astype(BF)
            att_in[at] = slot_gates(m, META["ar0"], META["ag0"], me, table)
            mlp_in[at] = slot_gates(m, META["mr0"], META["mg0"], me, slot_table(m, META["mr0"], me, CAP))
            name, mine_m = at.astype(F32), meta_all[g]
            att_rows[at] = slot_table(mine_m, META["ar0"], name, CAP)
            att_gate[at] = slot_gates(mine_m, META["ar0"], META["ag0"], name, att_rows[at])
            slot_pos = mm(table, at_pos).astype(BF)
            turn_slots[at, :, :HD] = looked_up(slot_pos, cos_t[...])
            turn_slots[at, :, HD:] = looked_up(slot_pos, sin_t[...])
            bias[at] = (mm(table, allowed_pairs(m, m_t)) - 1.0) * 1e30
        for c in out_copies(i):
            c.start()
        q_all = mm(picked[two].reshape(pair * CAP, features), w_q[...])
        for p in range(pair):
            at = pair * i + p
            query[at] = turned(q_all[p * CAP:(p + 1) * CAP], turn_slots[at, :, :HD], turn_slots[at, :, HD:]).astype(BF)
        for p in range(pair):
            at = pair * i + p
            for h in range(heads):
                hh = slice(h * HD, (h + 1) * HD)
                scores = mm_t(query[at, :, hh], keys[at, :, hh]) / math.sqrt(HD) + bias[at]
                attn[at, :, hh] = mm(softmax_rows(scores).astype(BF), values[at, :, hh]).astype(BF)
        return carry

    lax.fori_loop(0, steps, two_groups, 0)
    gat.core(1)
    for j in range(2):
        gat.here(j)
    for e in range(n):
        d_mbr[e] = (dy_rows[e].astype(F32) * mlp_in[e]).astype(BF)
    gat.sent()
    for i in range(steps):
        for c in out_copies(i):
            c.wait()
    for c in stored:
        c.wait()
    ring.finish()


def slot_gates(meta, first, gate, name, table):
    per_token = (jnp.where(meta[first:first + 1] == name, meta[gate:gate + 1], 0.0)
                 + jnp.where(meta[first + 1:first + 2] == name, meta[gate + 1:gate + 2], 0.0))
    return jnp.sum(table.astype(F32) * per_token, axis=1, keepdims=True)


def front(tokens, out_grad, place, att_routes, att_gates, mlp_routes, mlp_gates, seq_lengths, gain, cos_t, sin_t, w_kv, w_q, n, cid):
    rows, features = tokens.shape
    width, per, depth = features // 4, rows // n, n // 2
    hw = w_kv.shape[2]
    sds = jax.ShapeDtypeStruct
    vm, any_ = pl.BlockSpec(memory_space=VM), pl.BlockSpec(memory_space=pl.ANY)
    table, gate, plain = sds((n, CAP, rows), BF), sds((n, CAP, 1), F32), sds((features, hw), BF)
    group, slot = sds((n, rows, hw), BF), sds((n, CAP, hw), BF)
    return pl.pallas_call(
        functools.partial(front_body, n),
        out_shape=(
            sds((n, per, width), BF), sds((n, 16, rows), F32), sds((rows, rows), BF), table, gate, table, gate, gate,
            plain, plain, sds((rows, width), F32), sds((n, rows, features), BF), sds((n, CAP, features), BF),
            group, group, slot, slot, sds((n, rows, 1), F32), sds((n, CAP, rows), F32), sds((n, CAP, 2 * HD), F32),
            sds((n, CAP, features), BF)),
        in_specs=[vm] * 11 + [any_] * 2, out_specs=[vm] * 8 + [any_] * 2 + [vm] + [any_] * 2 + [vm] * 8,
        scratch_shapes=[
            VM((n, n, per, features), BF), VM((n, per, width), BF), VM(w_kv.shape, BF), VM((features, hw), BF),
            VM((features, hw), BF), VM((features, hw), BF), VM((16, rows), F32), VM((n, CAP, 1), F32), VM((n, rows, features), BF),
            VM((n, CAP, features), BF), VM((n, CAP, features), BF), VM((2, n, CAP, width // 2), BF),
            DMA((2,)), DMA((2, features // 256)), DMA((2, n // 2))] + GATHER_SEMS(2, n)
        + [DMA((n,))] * 4 + [DMA((depth, 3))] * 6 + [DMA((n,))] * 2 + [DMA((4,))] * 2,
        name="front", compiler_params=pltpu.CompilerParams(
            collective_id=cid, has_side_effects=True, vmem_limit_bytes=63 * 2**20),
    )(tokens, out_grad, place, att_routes, att_gates, mlp_routes, mlp_gates, seq_lengths, gain, cos_t, sin_t, w_kv, w_q)


def tile_list(size, step):
    return [(a, min(step, size - a)) for a in range(0, size, step)]


class ChunkReduce:
    def __init__(self, ring, partial, whole, pbuf, sent, got, sems):
        self.ring, self.partial, self.whole, self.pbuf = ring, partial, whole, pbuf
        self.cbuf, self.xbuf, self.dbuf = sent
        self.cin, self.xin, self.rbuf = got
        cs, cr, xs, xr, ds, dr = sems
        k, (nc, n, _, _) = ring, self.xbuf.shape
        self.c = [rcopy(self.cbuf.at[j], self.cin.at[j], cs.at[j], cr.at[j], k.g, k.tc) for j in range(nc)]
        self.x = [rcopy(self.xbuf.at[j], self.xin.at[j], xs.at[j], xr.at[j], k.g, k.tx) for j in range(nc)]
        self.d = [
            [rcopy(self.dbuf.at[j, k.to(o)], self.rbuf.at[j, k.g], ds.at[j, o], dr.at[j, o], k.to(o), k.t) for o in range(1, n)]
            for j in range(nc)]

    def core(self, j):
        k = self.ring
        n, r, cw = self.xbuf.shape[1:]
        self.whole[...] = self.partial(j)
        take = lambda q: self.whole[:, pl.ds(pl.multiple_of(q * cw, cw), cw)].reshape(n, r, cw)
        self.cbuf[j, 0] = take(k.tc).astype(BF)
        self.cbuf[j, 1] = take(k.tcx).astype(BF)
        self.c[j].start()
        self.pbuf[j, 0] = take(k.t)
        self.pbuf[j, 1] = take(k.tx)

    def cross(self, j):
        self.c[j].wait_recv()
        self.xbuf[j] = (self.pbuf[j, 1] + self.cin[j, 1].astype(F32)).astype(BF)
        self.x[j].start()

    def home(self, j):
        g = self.ring.g
        self.x[j].wait_recv()
        self.dbuf[j] = (self.pbuf[j, 0] + self.cin[j, 0].astype(F32) + self.xin[j].astype(F32)).astype(BF)
        for c in self.d[j]:
            c.start()
        self.rbuf[j, g] = self.dbuf[j, g]

    def rows(self, j):
        for c in self.d[j]:
            c.wait_recv()
        return self.rbuf[j].reshape(-1, self.rbuf.shape[-1])

    def sent_core(self):
        for c in self.c:
            c.wait_send()

    def sent_rest(self):
        for c in self.x + [c for row in self.d for c in row]:
            c.wait_send()


class ChunkGather:
    def __init__(self, ring, place, sbuf, sems):
        self.ring, self.place, self.sbuf = ring, place, sbuf
        ss, rs, xs, xr, cs, cr, c2s, c2r = sems
        k, (nc, n, _, cw) = ring, sbuf.shape
        self.d = [
            [rcopy(sbuf.at[j, k.to(o)], place(j, k.t, k.g), ss.at[j, o], rs.at[j, o], k.to(o), k.t) for o in range(1, n)]
            for j in range(nc)]
        pair = lambda j, q, a, b, to: rcopy(place(j, q, None), place(j, q, None), a.at[j], b.at[j], k.g, to)
        self.x = [pair(j, k.t, xs, xr, k.tx) for j in range(nc)]
        self.c = [pair(j, k.t, cs, cr, k.tc) for j in range(nc)]
        self.c2 = [pair(j, k.tx, c2s, c2r, k.tc) for j in range(nc)]

    def out(self, j, rows):
        self.sbuf[j] = rows.reshape(self.sbuf.shape[1:])
        for c in self.d[j]:
            c.start()
        self.place(j, self.ring.t, self.ring.g)[...] = self.sbuf[j, self.ring.g]

    def cross(self, j):
        for c in self.d[j]:
            c.wait_recv()
        self.x[j].start()
        self.c[j].start()

    def core(self, j):
        self.x[j].wait_recv()
        self.c2[j].start()

    def here(self, j):
        self.c[j].wait_recv()
        self.c2[j].wait_recv()

    def sent(self):
        for c in [c for row in self.d for c in row] + self.x + self.c + self.c2:
            c.wait_send()


def middle_body(
    n, attn, x_own, att_rows, att_gate, att_in, mlp_rows, dy_own, gain, query, dm_hbm, wo_hbm, wg_hbm, wu_hbm, wd_hbm,
    d_attn, d_hidden, hidden, mb_rows, gain_part, n2_hbm, inner_hbm, dg_hbm, du_hbm, obr_hbm, q_back, *scratch,
):
    (d_mbr, wo, wg, wu, wd, inner, d_gate, d_up, d_rows, n2_st, obr_st, xbuf3, mb_sum, cin3, xin3, hid, att_t, mlp_t, whole, gate_acc, up_acc, d_in, pbuf, cbuf, xbuf, dbuf,
     cin1, xin1, rb1, cin2, xin2, rb2, sb1, sb2, sq, sq_in, r_own, r_in, r_to, r_back, s_col) = scratch[:41]
    wsem, qs, qr, as_, ar, rss, rsr, rds, rdr, osem, nsem, bsem = scratch[41:53]
    s1, s2s, s3, g1, g2 = scratch[53:59], scratch[59:65], scratch[65:71], scratch[71:79], scratch[79:87]
    ring = Ring(n)
    g, t = ring.g, ring.t
    rows, width = x_own.shape
    cw = width // NC
    features, ff = 4 * width, wg.shape[1]
    slots = attn.shape[0]

    loads = {"wo": [], "wg": [], "wu": [], "wd": [], "dm": []}
    for j in range(NC):
        for q in range(4):
            to, at = pl.ds((j * 4 + q) * cw, cw), pl.ds(q * width + j * cw, cw)
            i = j * 4 + q
            loads["wo"].append(pltpu.make_async_copy(wo_hbm.at[:, at], wo.at[:, to], wsem.at[0, i]))
            loads["wg"].append(pltpu.make_async_copy(wg_hbm.at[at, :], wg.at[to, :], wsem.at[1, i]))
            loads["wu"].append(pltpu.make_async_copy(wu_hbm.at[at, :], wu.at[to, :], wsem.at[2, i]))
            loads["wd"].append(pltpu.make_async_copy(wd_hbm.at[:, at], wd.at[:, to], wsem.at[3, i]))
            loads["dm"].append(pltpu.make_async_copy(dm_hbm.at[:, at], d_mbr.at[:, to], wsem.at[4, i]))

    def fetch(*names):
        for name in names:
            for c in loads[name]:
                c.start()

    fetch("wo")

    def loaded(name):
        for c in loads[name]:
            c.wait()

    chunk = lambda j: pl.ds(j * 4 * cw, 4 * cw)
    att_t[...] = att_rows[...].T
    mlp_t[...] = mlp_rows[...].T
    ring.greet_everyone()
    asked = [rcopy(query.at[ring.to(o)], q_back.at[g], as_.at[o], ar.at[o], ring.to(o), t) for o in range(1, n)]

    red1 = ChunkReduce(
        ring, lambda j: mm(attn[...], wo[:, chunk(j)]), whole, pbuf, (cbuf, xbuf, dbuf), (cin1, xin1, rb1), s1)
    gat1 = ChunkGather(
        ring, lambda j, q, e: hid.at[j, slice(None) if e is None else e, :, pl.ds(pl.multiple_of(q * cw, cw), cw)], sb1, g1)
    shared = [rcopy(sq, sq_in.at[i], qs.at[i], qr.at[i], g, q) for i, q in enumerate([ring.tc, ring.tx, ring.tcx])]
    ones = jnp.ones((8, cw), BF)

    def hidden_chunk(j):
        high, low = split_bf(red1.rows(j).astype(F32) * att_gate[...])
        got = x_own[:, j * cw:(j + 1) * cw] + mm(att_t[...], high) + mm(att_t[...], low)
        hidden[:, j * cw:(j + 1) * cw] = got
        gat1.out(j, mm(mlp_rows[...], got.astype(BF)).astype(BF))
        high, low = split_bf(got * got)
        squares = mm_t(ones, high) + mm_t(ones, low)
        sq[...] = squares if j == 0 else sq[...] + squares
        if j == NC - 1:
            for c in shared:
                c.start()

    def gain_cols(j):
        return jnp.concatenate([gain[:, q * width + j * cw:q * width + (j + 1) * cw] for q in range(4)], axis=1)

    pieces = tile_list(ff, 512)

    def d_inner(i):
        if i == 0:
            loaded("wd")
            loaded("dm")
        a, w = pieces[i]
        d_in[:, a:a + w] = mm_t(d_mbr[...], wd[a:a + w, :])

    def absorb(j):
        gat1.here(j)
        v = hid[j].reshape(slots, 4 * cw).astype(F32)
        part = jnp.sum(v * v, axis=1, keepdims=True)
        s_col[...] = part if j == 0 else s_col[...] + part
        u = (v * gain_cols(j)).astype(BF)
        for a, w in pieces:
            cc = slice(a, a + w)
            gate, up = mm(u, wg[chunk(j), cc]), mm(u, wu[chunk(j), cc])
            gate_acc[:, cc] = gate if j == 0 else gate_acc[:, cc] + gate
            up_acc[:, cc] = up if j == 0 else up_acc[:, cc] + up

    loaded("wo")
    for j in range(NC):
        red1.core(j)
        if j:
            red1.cross(j - 1)
    red1.cross(NC - 1)
    fetch("wd", "dm", "wg", "wu")
    plan = [(2 * j, 0, functools.partial(red1.home, j)) for j in range(NC)]
    plan += [(2 * j + 3, 1, functools.partial(hidden_chunk, j)) for j in range(NC)]
    plan += [(2 * j + 7, 2, functools.partial(gat1.cross, j)) for j in range(NC)]
    plan += [(2 * j + 9, 3, functools.partial(gat1.core, j)) for j in range(NC)]
    plan += [(2 * i + 1.5, 4, functools.partial(d_inner, i)) for i in range(len(pieces))]
    plan += [(2 * j + 10.5, 5, functools.partial(absorb, j)) for j in range(NC)]
    plan += [(10.2, 0, lambda: (loaded("wg"), loaded("wu")))]
    plan += [(13.2, 0, lambda: [c.start() for c in asked])]
    for _, _, run in sorted(plan, key=lambda s: s[:2]):
        run()

    s_col[...] = lax.rsqrt(s_col[...] / features + EPSILON)
    r_own[...] = jnp.zeros_like(r_own)

    def units(at, size):
        s = s_col[...]
        gate, up, d = gate_acc[:, at] * s, up_acc[:, at] * s, d_in[:, at]
        sig = jax.nn.sigmoid(gate)
        silu = gate * sig
        inner[:, at] = (silu * up).astype(BF)
        du = (d * silu).astype(BF)
        dg = (d * up * sig * (1.0 + gate * (1.0 - sig))).astype(BF)
        d_up[:, at] = du
        d_gate[:, at] = dg
        r_own[...] += mm_t(jnp.ones((8, size), BF), (gate * dg.astype(F32) + up * du.astype(F32)).astype(BF))

    def unit_tile(i, _):
        units(pl.ds(pl.multiple_of(i * 128, 128), 128), 128)
        return _

    lax.fori_loop(0, ff // 128, unit_tile, 0)
    stored = [pltpu.make_async_copy(a, b, osem.at[i]) for i, (a, b) in enumerate(
        [(inner, inner_hbm), (d_gate, dg_hbm), (d_up, du_hbm)])]
    for c in stored:
        c.start()
    red1.sent_core()
    red1.sent_rest()
    for c in shared:
        c.wait_recv()
    total = (sq[...] + sq_in[0] + sq_in[1] + sq_in[2])[:1]
    eye = iota((rows, rows), 0) == iota((rows, rows), 1)
    scale = lax.rsqrt(jnp.sum(jnp.where(eye, total, 0.0), axis=1, keepdims=True) / features + EPSILON)

    told = [rcopy(r_own, r_in.at[i], rss.at[i], rsr.at[i], g, q) for i, q in enumerate([ring.tc, ring.tx, ring.tcx])]
    for c in told:
        c.start()
    half = lambda d: pl.ds(pl.multiple_of(d // 2 * 128, 128), 128)
    pairs = [rcopy(r_to.at[:, half(ring.to(o))], r_back.at[g], rds.at[o], rdr.at[o], ring.to(o), t) for o in range(1, n)]

    def share_r():
        for c in told:
            c.wait_recv()
        r_to[...] = r_own[...] + r_in[0] + r_in[1] + r_in[2]
        for c in pairs:
            c.start()
        r_back[g] = r_to[:, half(g)]

    total_r = {}

    def take_r():
        for c in pairs:
            c.wait_recv()
        odd = lax.rem(g, 2) == 1
        got = jnp.concatenate([jnp.where(odd, r_back[e][:, 64:], r_back[e][:, :64]) for e in range(n)], axis=1)
        high, low = split_bf(got)
        total_r[0] = (mm_t(mlp_t[...], high) + mm_t(mlp_t[...], low))[:, :1] / features

    red2 = ChunkReduce(
        ring, lambda j: mm_t(d_gate[...], wg[chunk(j), :]) + mm_t(d_up[...], wu[chunk(j), :]), whole, pbuf,
        (cbuf, xbuf, dbuf), (cin2, xin2, rb2), s2s)
    gat2 = ChunkGather(
        ring, lambda j, q, e: d_rows.at[slice(None) if e is None else e, :, cols_of(q, j, width, cw)], sb2, g2)

    def mixed_cols(j):
        return mm(inner[...], wd[:, chunk(j)])

    red3 = ChunkReduce(ring, mixed_cols, whole, pbuf, (cbuf, xbuf3, mb_sum), (cin3, xin3, mb_rows), s3)

    def mixed_core(j):
        red2.c[j].wait_send()
        red3.core(j)

    def d_hidden_chunk(j):
        got = red2.rows(j)
        if j == 0:
            take_r()
        cc = slice(j * cw, (j + 1) * cw)
        h = hidden[:, cc]
        d_n = mm(mlp_t[...], got)
        d_h = dy_own[:, cc].astype(F32) + scale * (gain[:, cols_of(t, j, width, cw)] * d_n) - h * (scale * scale) * total_r[0]
        d_hidden[:, cc] = d_h
        gain_part[:, cc] = jnp.broadcast_to(jnp.sum(d_n * h * scale, axis=0, keepdims=True), (8, cw))
        gat2.out(j, mm(att_rows[...], d_h.astype(BF)).astype(BF))

    kept, given = [], []

    def keep_normed(j):
        st = n2_st.at[j % 2]
        if j > 1:
            for c in kept[4 * (j - 2):4 * (j - 1)]:
                c.wait()
        st[...] = (hid[j].reshape(slots, 4 * cw).astype(F32) * s_col[...] * gain_cols(j)).astype(BF)
        for q in range(4):
            kept.append(pltpu.make_async_copy(
                st.at[:, pl.ds(q * cw, cw)], n2_hbm.at[:, pl.ds(q * width + j * cw, cw)], nsem.at[j, q]))
            kept[-1].start()

    def attend_rows(j):
        gat2.here(j)
        st = obr_st.at[j % 2]
        if j > 1:
            for c in given[4 * (j - 2):4 * (j - 1)]:
                c.wait()
        for q in range(4):
            v = d_rows[:, :, q * width + j * cw:q * width + (j + 1) * cw].reshape(slots, cw)
            st[:, q * cw:(q + 1) * cw] = (v.astype(F32) * att_in[...]).astype(BF)
        for q in range(4):
            given.append(pltpu.make_async_copy(
                st.at[:, pl.ds(q * cw, cw)], obr_hbm.at[:, pl.ds(q * width + j * cw, cw)], bsem.at[j, q]))
            given[-1].start()
        got = mm_t(st[...], wo[:, chunk(j)])
        hw = wo.shape[0]
        d_in[:, :hw] = got if j == 0 else d_in[:, :hw] + got

    for j in range(NC):
        red2.core(j)
        if j == 0:
            share_r()
        else:
            red2.cross(j - 1)
    red2.cross(NC - 1)
    plan = [(2 * j, 0, functools.partial(red2.home, j)) for j in range(NC)]
    plan += [(2 * j + 3, 1, functools.partial(d_hidden_chunk, j)) for j in range(NC)]
    plan += [(2 * j + 7, 2, functools.partial(gat2.cross, j)) for j in range(NC)]
    plan += [(2 * j + 9, 3, functools.partial(gat2.core, j)) for j in range(NC)]
    plan += [(2 * j + 1.5, 4, functools.partial(keep_normed, j)) for j in range(NC)]
    plan += [(2 * j + 0.7, 5, functools.partial(mixed_core, j)) for j in range(NC)]
    plan += [(2 * j + 2.7, 6, functools.partial(red3.cross, j)) for j in range(NC)]
    plan += [(2 * j + 8.2, 7, functools.partial(red3.home, j)) for j in range(NC)]
    plan += [(2 * j + 11, 8, functools.partial(attend_rows, j)) for j in range(NC)]
    for _, _, run in sorted(plan, key=lambda s: s[:2]):
        run()
    d_attn[...] = d_in[:, :wo.shape[0]].astype(BF).reshape(d_attn.shape)
    for c in asked + [c for row in red3.d for c in row]:
        c.wait_recv()
    q_back[g] = query[g]
    for c in stored + kept[8:] + given[8:]:
        c.wait()
    for c in asked + shared + told + pairs:
        c.wait_send()
    gat1.sent()
    gat2.sent()
    red2.sent_rest()
    red3.sent_core()
    red3.sent_rest()


def middle(attn, x_own, att_rows, att_gate, att_in, mlp_rows, dy_own, gain, d_mbr, query, wo, wg, wu, wd, n, cid):
    slots, (rows, width) = attn.shape[0], x_own.shape
    r, cw, features, ff, hw = slots // n, width // NC, 4 * width, wg.shape[1], attn.shape[1]
    any_, vm = pl.BlockSpec(memory_space=pl.ANY), pl.BlockSpec(memory_space=VM)
    sds = jax.ShapeDtypeStruct
    one, two = VM((NC, n, r, cw), BF), VM((NC, 2, n, r, cw), BF)
    units = sds((slots, ff), BF)
    return pl.pallas_call(
        functools.partial(middle_body, n),
        out_shape=(
            sds((n, r, hw), BF), sds((rows, width), F32), sds((rows, width), F32), sds((NC, n, r, cw), BF), sds((8, width), F32),
            sds((slots, features), BF), units, units, units, sds((slots, features), BF), sds((n, r, hw), BF)),
        in_specs=[vm] * 9 + [any_] * 5, out_specs=[vm] * 5 + [any_] * 5 + [vm],
        scratch_shapes=[
            VM((slots, features), BF), VM((hw, features), BF), VM((features, ff), BF), VM((features, ff), BF), VM((ff, features), BF),
            VM((slots, ff), BF), VM((slots, ff), BF), VM((slots, ff), BF), VM((n, r, features), BF),
            VM((2, slots, 4 * cw), BF), VM((2, slots, 4 * cw), BF), one, one, two, one,
            VM((NC, n, r, 4 * cw), BF), VM((rows, slots), BF), VM((rows, slots), BF),
            VM((slots, 4 * cw), F32), VM((slots, ff), F32), VM((slots, ff), F32), VM((slots, ff), F32),
            VM((NC, 2, n, r, cw), F32), two, one, one]
        + [two, one, one] * 2 + [one, one]
        + [VM((8, rows), F32), VM((3, 8, rows), F32), VM((8, slots), F32), VM((3, 8, slots), F32), VM((8, slots), F32),
           VM((n, 8, 128), F32), VM((slots, 1), F32)]
        + [DMA((5, 16)), DMA((3,)), DMA((3,)), DMA((n,)), DMA((n,)), DMA((3,)), DMA((3,)), DMA((n,)), DMA((n,)), DMA((3,)),
           DMA((NC, 4)), DMA((NC, 4))]
        + REDUCE_SEMS(NC, n) * 3 + GATHER_SEMS(NC, n) * 2,
        name="middle", compiler_params=pltpu.CompilerParams(
            collective_id=cid, has_side_effects=True, vmem_limit_bytes=63 * 2**20),
    )(attn, x_own, att_rows, att_gate, att_in, mlp_rows, dy_own, gain, query, d_mbr, wo, wg, wu, wd)


def fast_local(
    tokens, out_grad, row_place, seq_lengths, att_routes, att_gates, mlp_routes, mlp_gates,
    gain_attn, w_kv, w_query, w_out, gain_mlp, w_gate, w_up, w_down,
):
    rows, features = tokens.shape
    n = lax.axis_size("dp")
    width = features // 4
    hw = w_kv.shape[2]

    cos_t, sin_t = angle_tables(rows)
    (dy_own, meta_all, sorter, att_out, att_gate, mlp_out, mlp_gate, att_in, w_k, w_v, x_own, normed, picked, keys, values,
     query, attn, scale_attn, bias, turn_slots, d_mbr) = front(
        tokens, out_grad, row_place.reshape(n, rows), att_routes.T, att_gates.T, mlp_routes.T, mlp_gates.T, seq_lengths,
        gain_attn[None], cos_t, sin_t, w_kv, w_query[0], n, cid=12)
    dy_own = dy_own.reshape(rows, width)
    att_rows, mlp_rows = att_out.reshape(n * CAP, rows), mlp_out.reshape(n * CAP, rows)
    normed_flat, picked = normed.reshape(n * rows, features), picked.reshape(n * CAP, features)
    attn = attn.reshape(n * CAP, hw)
    d_mbr = d_mbr.reshape(n * CAP, features)

    d_attn, d_hidden, hidden, mb_rows, gain_mlp_part, normed2, inner, d_gate, d_up, d_obr, query_back = middle(
        attn, x_own, att_rows, att_gate.reshape(-1, 1), att_in.reshape(-1, 1), mlp_rows, dy_own, gain_mlp[None],
        d_mbr, query, w_out[0], w_gate[0], w_up[0], w_down[0], n, cid=9)
    w_gate_grad = mm_rows(normed2, d_gate)[None]
    w_up_grad = mm_rows(normed2, d_up)[None]
    w_down_grad = mm_rows(inner, d_mbr)[None]

    d_kv_all, mixed, tokens_grad, gain_attn_grad, gain_mlp_grad, dq_pre = layer_tail(
        (d_attn, mb_rows, meta_all, cos_t, sin_t, x_own, scale_attn, gain_attn[None], d_hidden, hidden,
         mlp_gate.reshape(-1, 1), mlp_rows, att_rows, gain_mlp_part, sorter),
        (query, keys, values, bias, turn_slots, query_back, w_query[0], w_k, w_v), n, cid=11)
    w_out_grad = mm_rows(attn, d_obr)[None]
    w_query_grad = mm_rows(picked, dq_pre.reshape(n * CAP, hw))[None]
    w_kv_grad = map_grad(normed_flat, d_kv_all.reshape(n * rows, 2 * hw))
    return (
        mixed, tokens_grad, gain_attn_grad[0], w_kv_grad, w_query_grad, w_out_grad, gain_mlp_grad[0],
        w_gate_grad, w_up_grad, w_down_grad,
    )


def solution(mesh):
    placed = (
        P("dp", None),
        P("dp", None),
        P(),
        P("dp", None),
        P("dp", None),
        P("dp", None),
        P("dp", None),
        P("dp", None),
        P(),
        P(None, None, "tensor"),
        P("dp", None, "tensor"),
        P("dp", "tensor", None),
        P(),
        P("dp", None, "tensor"),
        P("dp", None, "tensor"),
        P("dp", "tensor", None),
    )
    dealt = mesh.shape["dp"] == EXPERTS and mesh.shape["tensor"] == 4
    return jax.shard_map(
        fast_local if dealt else local,
        mesh=mesh,
        in_specs=placed,
        out_specs=(
            P("dp", None),
            P("dp", None),
            P(),
            P(None, None, "tensor"),
            P("dp", None, "tensor"),
            P("dp", "tensor", None),
            P(),
            P("dp", None, "tensor"),
            P("dp", None, "tensor"),
            P("dp", "tensor", None),
        ),
        check_vma=False,
    )
```
